32 devices in a mesh: tm: 4 (over y, x), space: 4 (over z), mp: 2 (over core).
Axes of the slice: x: 2, y: 2, z: 4, core: 2. Of those that a mesh axis runs over, the one named last changes fastest.
Arguments:
- video: bfloat16 [2, 8, 16, 16, 1024], P(None, 'tm', 'space')
- cotangent: bfloat16 [2, 8, 16, 16, 1024], P(None, 'tm', 'space'), may hold values from -6 to 6
- text: bfloat16 [2, 128, 4096], P(None, ('tm', 'space')), may hold values from -6 to 6
- video_ids: int32 [2, 8], replicated, may hold values from 0 to 2, as said below
- timesteps: int32 [2, 3], replicated, may hold values from 0 to 999
- text_lengths: int32 [2], replicated, may hold values from 16 to 128
- group_gain: float32 [1024], replicated, may hold values from 0.5 to 1.5
- group_bias: float32 [1024], replicated, may hold values from -2 to 2
- first_conv: bfloat16 [1024, 9, 1024], P('space', None, 'mp'), may hold values from -0.0625 to 0.0625
- film_weight: bfloat16 [1024, 2, 1024], P('space', None, 'mp'), may hold values from -0.1875 to 0.1875
- second_conv: bfloat16 [1024, 9, 1024], P('mp', None, 'space'), may hold values from -0.0625 to 0.0625
- spatial_norm: float32 [1024], replicated, may hold values from 0.5 to 1.5
- spatial_qkv: bfloat16 [1024, 3, 1024], P('space', None, 'mp'), may hold values from -0.1875 to 0.1875
- spatial_out: bfloat16 [1024, 1024], P('mp', 'space'), may hold values from -0.5 to 0.5
- cross_norm: float32 [1024], replicated, may hold values from 0.5 to 1.5
- cross_query: bfloat16 [1024, 1024], P('space', 'mp'), may hold values from -0.1875 to 0.1875
- cross_kv: bfloat16 [4096, 2, 1024], P('space', None, 'mp'), may hold values from -0.09375 to 0.09375
- cross_out: bfloat16 [1024, 1024], P('mp', 'space'), may hold values from -0.5 to 0.5
- temporal_norm: float32 [1024], replicated, may hold values from 0.5 to 1.5
- temporal_qkv: bfloat16 [1024, 3, 1024], P('space', None, 'mp'), may hold values from -0.1875 to 0.1875
- temporal_out: bfloat16 [1024, 1024], P('mp', 'space'), may hold values from -0.375 to 0.375
- offset_bias: float32 [128, 16], P(None, 'mp'), may hold values from -4 to 4
- feed_norm: float32 [1024], replicated, may hold values from 0.5 to 1.5
- feed_in: bfloat16 [1024, 4096], P('space', 'mp'), may hold values from -0.1875 to 0.1875
- feed_out: bfloat16 [4096, 1024], P('mp', 'space'), may hold values from -0.09375 to 0.09375
Outputs:
- mixed: bfloat16 [2, 8, 16, 16, 1024], P(None, 'tm', 'space')
- video_grad: float32 [2, 8, 16, 16, 1024], P(None, 'tm', 'space')
- text_grad: float32 [2, 128, 4096], P(None, ('tm', 'space'), 'mp')
- group_gain_grad: float32 [1024], P(('tm', 'space'))
- group_bias_grad: float32 [1024], P(('tm', 'space'))
- first_conv_grad: float32 [1024, 9, 1024], P(('tm', 'space'), None, 'mp')
- film_weight_grad: float32 [1024, 2, 1024], P(('tm', 'space'), None, 'mp')
- second_conv_grad: float32 [1024, 9, 1024], P('mp', None, ('tm', 'space'))
- spatial_norm_grad: float32 [1024], P(('tm', 'space'))
- spatial_qkv_grad: float32 [1024, 3, 1024], P(('tm', 'space'), None, 'mp')
- spatial_out_grad: float32 [1024, 1024], P('mp', ('tm', 'space'))
- cross_norm_grad: float32 [1024], P(('tm', 'space'))
- cross_query_grad: float32 [1024, 1024], P(('tm', 'space'), 'mp')
- cross_kv_grad: float32 [4096, 2, 1024], P(('tm', 'space'), None, 'mp')
- cross_out_grad: float32 [1024, 1024], P('mp', ('tm', 'space'))
- temporal_norm_grad: float32 [1024], P(('tm', 'space'))
- temporal_qkv_grad: float32 [1024, 3, 1024], P(('tm', 'space'), None, 'mp')
- temporal_out_grad: float32 [1024, 1024], P('mp', ('tm', 'space'))
- offset_bias_grad: float32 [128, 16], P(('tm', 'space'), 'mp')
- feed_norm_grad: float32 [1024], P(('tm', 'space'))
- feed_in_grad: float32 [1024, 4096], P(('tm', 'space'), 'mp')
- feed_out_grad: float32 [4096, 1024], P('mp', ('tm', 'space'))
The draws below stay inside these ranges and needn't reach their ends.
Inputs may be any that keep to these rules, and one draw needn't show every extreme that they name: `video_ids`: within each slot the video number starts at 0 and rises by 0 or 1 from one frame to the next. Some slot holds a single video of all 8 frames, and some slot holds 3 videos.
All inputs are finite; a program needn't handle non-finite values.
Results may differ from the reference program's by a relative error of at most 0.03.
Values may be sent and summed in bfloat16 or wider, within the bound.
A program may use at most 256 MiB of HBM per device.

```python
import math
import jax
import jax.numpy as jnp
from jax import lax

D = 1024
HEADS = 16
HDIM = 64
FFN = 4096
TXT = 128
TXTD = 4096
G = 32
R = 128
VIDS = 3
H = 16
W = 16
B = 2
F = 8


def draw_video(key, part):
    key = jax.random.fold_in(key, 11)
    noise_key = jax.random.fold_in(key, 0)
    row_place = jnp.arange(H, dtype=jnp.float32) / (H - 1)
    base = jax.random.normal(noise_key, (B, F, H, W, D), jnp.float32)
    row_scale = 3.0 ** row_place
    return (base * row_scale[None, None, :, None, None]).astype(jnp.bfloat16)


def draw_video_ids(key, part):
    key = jax.random.fold_in(key, 12)
    pick_key, score_key, extra_key = jax.random.split(key, 3)
    single = jax.random.randint(pick_key, (), 0, B)
    double = (single + 1) % B
    scores = jax.random.randint(score_key, (B, F - 1), 0, 1 << 20) * F + jnp.arange(F - 1, dtype=jnp.int32)[None, :]
    order = jnp.argsort(scores, axis=1, stable=True).astype(jnp.int32) + 1
    first_cut = jnp.minimum(order[:, 0], order[:, 1])
    second_cut = jnp.maximum(order[:, 0], order[:, 1])
    slot_index = jnp.arange(B, dtype=jnp.int32)
    use_second = jnp.maximum(jax.random.randint(extra_key, (B,), 0, 2), (slot_index == double).astype(jnp.int32))
    frame_index = jnp.arange(F, dtype=jnp.int32)[None, :]
    ids_all = (frame_index >= first_cut[:, None]).astype(jnp.int32) + use_second[:, None] * (frame_index >= second_cut[:, None]).astype(jnp.int32)
    return jnp.where(slot_index[:, None] == single, 0, ids_all).astype(jnp.int32)


def with_ends(drawn, key, least, top_value):
    place = [jax.random.randint(jax.random.fold_in(key, axis), (), 0, length) for axis, length in enumerate(drawn.shape)]
    main_axis = drawn.shape.index(max(drawn.shape))
    beside = place[:main_axis] + [(place[main_axis] + 1) % drawn.shape[main_axis]] + place[main_axis + 1:]
    return drawn.at[tuple(place)].set(least).at[tuple(beside)].set(top_value)


def block_scale(own_key, shape, pieces, least, top_value):
    def one(dim, blocks):
        steps = jax.random.uniform(jax.random.fold_in(jax.random.fold_in(own_key, 6), dim), (blocks,), jnp.float32, least / len(pieces), top_value / len(pieces))
        return jnp.repeat(jnp.exp(steps), shape[dim] // blocks).reshape((-1,) + (1,) * (len(shape) - dim - 1))

    level = one(*pieces[0])
    for cut in pieces[1:]:
        level = level * one(*cut)
    return level


def centred(key, dims, scale, limit, pieces=(), kind=jnp.bfloat16):
    drawn = jax.random.normal(key, dims, jnp.float32) * scale
    if len(pieces) > 0:
        drawn = block_scale(key, dims, pieces, -0.22, 0.18) * drawn
    return jnp.clip(drawn, min=-limit, max=limit).astype(kind)


def setup_inputs(seed: int = 0) -> dict:
    seeds = jax.random.split(jax.random.key(seed), 26)
    video = draw_video(jax.random.fold_in(seeds[25], 71), 0)
    cotangent = centred(seeds[1], (B, F, H, W, D), 1.0, 6.0, ((1, 4), (2, 4)))
    text = centred(seeds[2], (B, TXT, TXTD), 1.0, 6.0, ((1, 16),))
    video_ids = draw_video_ids(jax.random.fold_in(seeds[25], 71), 0)
    timesteps = with_ends(jax.random.randint(seeds[4], (B, VIDS), 0, 1000), jax.random.fold_in(seeds[4], 1), 0, 999).astype(jnp.int32)
    text_lengths = jax.random.randint(seeds[5], (B,), TXT // 8, TXT + 1).astype(jnp.int32)
    group_gain = jnp.clip(1.0 + 0.1 * jax.random.normal(seeds[6], (D,), jnp.float32), 0.5, 1.5)
    group_bias = centred(seeds[7], (D,), 0.3, 2.0, (), jnp.float32)
    first_conv = centred(seeds[8], (D, 9, D), (9 * D) ** -0.5, 0.0625, ((0, 4), (2, 2)))
    film_weight = centred(seeds[9], (D, 2, D), D ** -0.5, 0.1875, ((0, 4), (2, 2)))
    second_conv = centred(seeds[10], (D, 9, D), (9 * D) ** -0.5, 0.0625, ((0, 2), (2, 4)))
    spatial_norm = jnp.clip(1.0 + 0.1 * jax.random.normal(seeds[11], (D,), jnp.float32), 0.5, 1.5)
    spatial_qkv = centred(seeds[12], (D, 3, D), D ** -0.5, 0.1875, ((0, 4), (2, 2)))
    spatial_out = centred(seeds[13], (D, D), (D // 8) ** -0.5, 0.5, ((0, 2), (1, 4)))
    cross_norm = jnp.clip(1.0 + 0.1 * jax.random.normal(seeds[14], (D,), jnp.float32), 0.5, 1.5)
    cross_query = centred(seeds[15], (D, D), D ** -0.5, 0.1875, ((0, 4), (1, 2)))
    cross_kv = centred(seeds[16], (TXTD, 2, D), TXTD ** -0.5, 0.09375, ((0, 4), (2, 2)))
    cross_out = centred(seeds[17], (D, D), (D // 8) ** -0.5, 0.5, ((0, 2), (1, 4)))
    temporal_norm = jnp.clip(1.0 + 0.1 * jax.random.normal(seeds[18], (D,), jnp.float32), 0.5, 1.5)
    temporal_qkv = centred(seeds[19], (D, 3, D), D ** -0.5, 0.1875, ((0, 4), (2, 2)))
    temporal_out = centred(seeds[20], (D, D), (D // 4) ** -0.5, 0.375, ((0, 2), (1, 4)))
    offset_bias = centred(seeds[21], (R, HEADS), 1.0, 4.0, ((1, 2),), jnp.float32)
    feed_norm = jnp.clip(1.0 + 0.1 * jax.random.normal(seeds[22], (D,), jnp.float32), 0.5, 1.5)
    feed_in = centred(seeds[23], (D, FFN), D ** -0.5, 0.1875, ((0, 4), (1, 2)))
    feed_out = centred(seeds[24], (FFN, D), FFN ** -0.5, 0.09375, ((0, 2), (1, 4)))
    return dict(video=video, cotangent=cotangent, text=text, video_ids=video_ids, timesteps=timesteps, text_lengths=text_lengths, group_gain=group_gain, group_bias=group_bias, first_conv=first_conv, film_weight=film_weight, second_conv=second_conv, spatial_norm=spatial_norm, spatial_qkv=spatial_qkv, spatial_out=spatial_out, cross_norm=cross_norm, cross_query=cross_query, cross_kv=cross_kv, cross_out=cross_out, temporal_norm=temporal_norm, temporal_qkv=temporal_qkv, temporal_out=temporal_out, offset_bias=offset_bias, feed_norm=feed_norm, feed_in=feed_in, feed_out=feed_out)


@jax.custom_vjp
def low(v):
    return lax.optimization_barrier(v.astype(jnp.bfloat16)).astype(jnp.float32)

@jax.custom_vjp
def low_back(v):
    return v

def low_keep(v):
    return (low(v), None)

def low_pass(kept, grad):
    return (grad,)

def back_keep(v):
    return (v, None)

def back_low(kept, grad):
    return (low(grad),)
low.defvjp(low_keep, low_pass)
low_back.defvjp(back_keep, back_low)
epsilon = 1e-05
highest = lax.Precision.HIGHEST
masked = -1e+30

def group_norm(source):
    full_shape = source.shape
    grouped = source.reshape(full_shape[:-1] + (G, full_shape[-1] // G))
    average = lax.optimization_barrier(jnp.mean(grouped, axis=(1, 2, 4), keepdims=True))
    centered = grouped - average
    variance = lax.optimization_barrier(jnp.mean(centered * centered, axis=(1, 2, 4), keepdims=True))
    return (centered * lax.rsqrt(variance + epsilon)).reshape(full_shape)

def layer_norm(source, norm_gain):
    average = lax.optimization_barrier(jnp.mean(source, axis=-1, keepdims=True))
    centered = source - average
    variance = lax.optimization_barrier(jnp.mean(centered * centered, axis=-1, keepdims=True))
    return centered * lax.rsqrt(variance + epsilon) * norm_gain

def sinusoid(steps_int):
    counted = D // 2
    freqs = jnp.exp(-math.log(10000.0) * jnp.arange(counted, dtype=jnp.float32) / counted)
    angles = steps_int.astype(jnp.float32)[..., None] * freqs
    return jnp.concatenate([jnp.sin(angles), jnp.cos(angles)], axis=-1)

def conv_frames(source, weight):
    kernel = weight.reshape(weight.shape[0], 3, 3, weight.shape[2]).transpose(1, 2, 0, 3)
    return lax.conv_general_dilated(source, kernel, (1, 1), 'SAME', dimension_numbers=('NHWC', 'HWIO', 'NHWC'), precision=highest)

def heads_of(source):
    rounded = low(low_back(source))
    return rounded.reshape(rounded.shape[:-1] + (HEADS, HDIM))

def attention(queries, keys, values_in, forms, bias, valid):
    query_form, key_form, score_form = forms
    score_scale = 1.0 / math.sqrt(HDIM)
    scores = jnp.einsum(query_form + ',' + key_form + '->' + score_form, queries, keys, precision=highest) * score_scale
    if bias is not None:
        scores = scores + bias
    scores = low_back(scores)
    if valid is not None:
        scores = jnp.where(valid, scores, masked)
    probs = jax.nn.softmax(scores, axis=-1)
    return jnp.einsum(score_form + ',' + key_form + '->' + query_form, low(probs), values_in, precision=highest)

def slot_forward(params, video_ids, timesteps, text_length):
    video, text, group_gain, group_bias, first_conv, film_weight, second_conv, spatial_norm, spatial_qkv, spatial_out, cross_norm, cross_query, cross_kv, cross_out, temporal_norm, temporal_qkv, temporal_out, offset_bias, feed_norm, feed_in, feed_out = params
    frames = video.shape[0]
    pixels = video.shape[1] * video.shape[2]
    normal_one = group_norm(video) * group_gain + group_bias
    first_in = low(jax.nn.silu(normal_one))
    hidden = low_back(conv_frames(first_in, first_conv))
    embed = low(sinusoid(timesteps))
    film = jnp.einsum('vc,cjk->vjk', embed, film_weight, precision=highest)
    choose = (video_ids[:, None] == jnp.arange(VIDS, dtype=jnp.int32)[None, :]).astype(jnp.float32)
    frame_film = jnp.einsum('fv,vjk->fjk', choose, film, precision=highest)
    modulated = group_norm(hidden) * (1.0 + frame_film[:, None, None, 0, :]) + frame_film[:, None, None, 1, :]
    second_in = low(jax.nn.silu(modulated))
    stream = video + low_back(conv_frames(second_in, second_conv))
    stream = stream.reshape(frames, pixels, D)
    normed = low(layer_norm(stream, spatial_norm))
    triple = jnp.einsum('fpd,djk->fpjk', normed, spatial_qkv, precision=highest)
    queries = heads_of(triple[:, :, 0])
    keys = heads_of(triple[:, :, 1])
    values_in = heads_of(triple[:, :, 2])
    spatial_mix = attention(queries, keys, values_in, ('fphe', 'fqhe', 'fhpq'), None, None)
    spatial_mix = low(low_back(spatial_mix.reshape(frames, pixels, D)))
    stream = stream + low_back(jnp.einsum('fpc,cd->fpd', spatial_mix, spatial_out, precision=highest))
    flat = stream.reshape(frames * pixels, D)
    normed = low(layer_norm(flat, cross_norm))
    queries = heads_of(jnp.einsum('nd,dk->nk', normed, cross_query, precision=highest))
    text_pairs = jnp.einsum('tc,cjk->tjk', text, cross_kv, precision=highest)
    keys = heads_of(text_pairs[:, 0])
    values_in = heads_of(text_pairs[:, 1])
    valid = (jnp.arange(TXT, dtype=jnp.int32) < text_length)[None, None, :]
    cross_mix = attention(queries, keys, values_in, ('nhe', 'the', 'hnt'), None, valid)
    cross_mix = low(low_back(cross_mix.reshape(frames * pixels, D)))
    flat = flat + low_back(jnp.einsum('nc,cd->nd', cross_mix, cross_out, precision=highest))
    stream = flat.reshape(frames, pixels, D)
    normed = low(layer_norm(stream, temporal_norm))
    triple = jnp.einsum('fpd,djk->fpjk', normed, temporal_qkv, precision=highest)
    queries = heads_of(triple[:, :, 0])
    keys = heads_of(triple[:, :, 1])
    values_in = heads_of(triple[:, :, 2])
    frame_range = jnp.arange(frames, dtype=jnp.int32)
    offsets = jnp.clip(frame_range[:, None] - frame_range[None, :], -(R // 2), R // 2 - 1) + R // 2
    bias = jnp.transpose(offset_bias[offsets], (2, 0, 1))[None]
    valid = (video_ids[:, None] == video_ids[None, :])[None, None]
    temporal_mix = attention(queries, keys, values_in, ('fphe', 'gphe', 'phfg'), bias, valid)
    temporal_mix = low(low_back(temporal_mix.reshape(frames, pixels, D)))
    stream = stream + low_back(jnp.einsum('fpc,cd->fpd', temporal_mix, temporal_out, precision=highest))
    normed = low(layer_norm(stream, feed_norm))
    upper = low_back(jnp.einsum('fpd,dk->fpk', normed, feed_in, precision=highest))
    active = low(jax.nn.gelu(upper))
    stream = stream + low_back(jnp.einsum('fpk,kd->fpd', active, feed_out, precision=highest))
    return stream.reshape(video.shape)

def reference(video, cotangent, text, video_ids, timesteps, text_lengths, group_gain, group_bias, first_conv, film_weight, second_conv, spatial_norm, spatial_qkv, spatial_out, cross_norm, cross_query, cross_kv, cross_out, temporal_norm, temporal_qkv, temporal_out, offset_bias, feed_norm, feed_in, feed_out):
    weights_all = tuple((item.astype(jnp.float32) for item in (group_gain, group_bias, first_conv, film_weight, second_conv, spatial_norm, spatial_qkv, spatial_out, cross_norm, cross_query, cross_kv, cross_out, temporal_norm, temporal_qkv, temporal_out, offset_bias, feed_norm, feed_in, feed_out)))

    def one_slot(totals, slot_inputs):
        video_one, text_one, cotangent_one, ids_one, steps_one, length_one = slot_inputs

        def forward(video_in, text_in, weight_set):
            return slot_forward((video_in, text_in) + weight_set, ids_one, steps_one, length_one)
        result, pullback = jax.vjp(forward, video_one, text_one, weights_all)
        video_back, text_back, weight_back = pullback(cotangent_one)
        totals = jax.tree.map(jnp.add, totals, weight_back)
        return (totals, (result, video_back, text_back))
    zero_set = jax.tree.map(jnp.zeros_like, weights_all)
    totals, (results, video_backs, text_backs) = lax.scan(one_slot, zero_set, (video.astype(jnp.float32), text.astype(jnp.float32), cotangent.astype(jnp.float32), video_ids, timesteps, text_lengths))
    group_gain_grad, group_bias_grad, first_conv_grad, film_weight_grad, second_conv_grad, spatial_norm_grad, spatial_qkv_grad, spatial_out_grad, cross_norm_grad, cross_query_grad, cross_kv_grad, cross_out_grad, temporal_norm_grad, temporal_qkv_grad, temporal_out_grad, offset_bias_grad, feed_norm_grad, feed_in_grad, feed_out_grad = totals
    return (results.astype(jnp.bfloat16), video_backs, text_backs, group_gain_grad, group_bias_grad, first_conv_grad, film_weight_grad, second_conv_grad, spatial_norm_grad, spatial_qkv_grad, spatial_out_grad, cross_norm_grad, cross_query_grad, cross_kv_grad, cross_out_grad, temporal_norm_grad, temporal_qkv_grad, temporal_out_grad, offset_bias_grad, feed_norm_grad, feed_in_grad, feed_out_grad)
```

```python
import math

import jax
import jax.numpy as jnp
from jax import lax
from jax.sharding import PartitionSpec as P

D = 1024
HDIM = 64
TXT = 128
G = 32
R = 128
VIDS = 3
H = 16
W = 16


epsilon = 1e-05
highest = lax.Precision.HIGHEST
masked = -1e30


def mp_sum(partial_sum):
    mine = partial_sum.astype(jnp.bfloat16)
    other = lax.ppermute(mine, "mp", [(0, 1), (1, 0)])
    return mine.astype(jnp.float32) + other.astype(jnp.float32)


def part_of(source, axis_name, dim):
    size = source.shape[dim] // lax.axis_size(axis_name)
    return lax.dynamic_slice_in_dim(source, lax.axis_index(axis_name) * size, size, dim)


def space_to_all(source, split, concat):
    return lax.all_to_all(source, "space", split_axis=split, concat_axis=concat, tiled=True)


def gather_tokens(rows):
    half = part_of(rows, "mp", 1)
    line = lax.all_gather(half, "space", axis=0, tiled=True)
    return lax.all_gather(line, "mp", axis=1, tiled=True)


def scatter_tokens(partial_sum):
    half = lax.psum_scatter(
        partial_sum.astype(jnp.bfloat16), "mp", scatter_dimension=1, tiled=True
    )
    line = lax.psum_scatter(half, "space", scatter_dimension=0, tiled=True)
    return lax.all_gather(line, "mp", axis=1, tiled=True).astype(jnp.float32)


def to_clips(source):
    return lax.all_to_all(source, "tm", split_axis=2, concat_axis=1, tiled=True)


def from_clips(source):
    return lax.all_to_all(source, "tm", split_axis=1, concat_axis=2, tiled=True)


def sum_to_owner(weight_grad, dim):
    return lax.psum_scatter(
        weight_grad.astype(jnp.bfloat16), ("tm", "space"), scatter_dimension=dim, tiled=True
    ).astype(jnp.float32)


def sum_over_frames(weight_grad, dim):
    return lax.psum_scatter(
        weight_grad.astype(jnp.bfloat16), "tm", scatter_dimension=dim, tiled=True
    )


def stationary_to_owner(weight_grad, dim):
    portion = sum_over_frames(weight_grad, dim)
    frames, lines = lax.axis_size("tm"), lax.axis_size("space")
    moves = [(t * lines + s, s * frames + t) for t in range(frames) for s in range(lines)]
    return lax.ppermute(portion, ("tm", "space"), moves).astype(jnp.float32)


def padded_rims(source):
    return jnp.pad(source, ((0, 0), (0, 0), (1, 1), (1, 1), (0, 0)))


def conv_weight(weight):
    return weight.reshape(weight.shape[0], 3, 3, weight.shape[2])


def conv_frames(source, weight, spec, flipped):
    images = source.reshape((-1,) + source.shape[2:])
    kernel = conv_weight(weight)
    if flipped:
        kernel = kernel[:, ::-1, ::-1]
    result = lax.conv_general_dilated(
        images,
        kernel,
        (1, 1),
        "SAME",
        dimension_numbers=("NHWC", spec, "NHWC"),
        preferred_element_type=jnp.float32,
    )
    return result.reshape(source.shape[:4] + (result.shape[-1],))


def conv_weight_grad(source, upstream):
    padded = padded_rims(source)
    rows, cols = source.shape[2], source.shape[3]
    tap_list = []
    for tap in range(9):
        i, j = tap // 3, tap % 3
        tap_list.append(
            jnp.einsum(
                "bfhwc,bfhwk->ck",
                padded[:, :, i : i + rows, j : j + cols],
                upstream,
                preferred_element_type=jnp.float32,
            ).astype(jnp.bfloat16)
        )
    return jnp.stack(tap_list, axis=0)


def grouped_view(source):
    size = D // G
    dims_all = source.shape
    return source.reshape(
        dims_all[0], dims_all[1], dims_all[2] * dims_all[3], dims_all[4] // size, size
    )


def group_forward(source):
    grouped = grouped_view(source)
    average = jnp.mean(grouped, axis=(2, 4), keepdims=True)
    centered = grouped - average
    variance = jnp.mean(centered * centered, axis=(2, 4), keepdims=True)
    inverse = lax.rsqrt(variance + epsilon)
    return ((centered * inverse).reshape(source.shape), inverse)


def group_backward(upstream, normal, inverse):
    grouped_up = grouped_view(upstream)
    grouped_norm = grouped_view(normal)
    first_mean = jnp.mean(grouped_up, axis=(2, 4), keepdims=True)
    second_mean = jnp.mean(grouped_up * grouped_norm, axis=(2, 4), keepdims=True)
    result = inverse * (grouped_up - first_mean - grouped_norm * second_mean)
    return result.reshape(upstream.shape)


def layer_norm(source, norm_gain):
    average = jnp.mean(source, axis=-1, keepdims=True)
    centered = source - average
    variance = jnp.mean(centered * centered, axis=-1, keepdims=True)
    return centered * lax.rsqrt(variance + epsilon) * norm_gain


def layer_back(source, norm_gain, upstream):
    _, pullback = jax.vjp(layer_norm, source, norm_gain)
    return pullback(upstream)


def sinusoid(steps_int):
    counted = D // 2
    freqs = jnp.exp(-math.log(10000.0) * jnp.arange(counted, dtype=jnp.float32) / counted)
    angles = steps_int.astype(jnp.float32)[..., None] * freqs
    return jnp.concatenate([jnp.sin(angles), jnp.cos(angles)], axis=-1)


def offset_onehot(query_start, query_count, key_count):
    distance = (
        query_start
        + jnp.arange(query_count, dtype=jnp.int32)[:, None]
        - jnp.arange(key_count, dtype=jnp.int32)[None, :]
    )
    position = jnp.clip(distance, -(R // 2), R // 2 - 1) + R // 2
    return (position[:, :, None] == jnp.arange(R, dtype=jnp.int32)[None, None, :]).astype(
        jnp.float32
    )


def scores_of(queries, keys, forms, bias, valid):
    query_form, key_form, score_form = forms
    raw_scores = jnp.einsum(
        query_form + "," + key_form + "->" + score_form,
        queries,
        keys,
        preferred_element_type=jnp.float32,
    ) * (1.0 / math.sqrt(HDIM))
    if bias is not None:
        raw_scores = raw_scores + bias
    if valid is not None:
        raw_scores = jnp.where(valid, raw_scores, masked)
    return raw_scores


def attend_forward(queries, keys, values_in, forms, bias, valid):
    query_form, key_form, score_form = forms
    raw_scores = scores_of(queries, keys, forms, bias, valid)
    largest = jnp.max(raw_scores, axis=-1, keepdims=True)
    expos = jnp.exp(raw_scores - largest)
    totals = jnp.sum(expos, axis=-1, keepdims=True)
    probs = (expos / totals).astype(jnp.bfloat16)
    log_total = (largest + jnp.log(totals))[..., 0]
    result = jnp.einsum(
        score_form + "," + key_form + "->" + query_form,
        probs,
        values_in,
        preferred_element_type=jnp.float32,
    )
    return (result.astype(jnp.bfloat16), log_total)


def attend_backward(queries, keys, values_in, forms, bias, valid, log_total, upstream):
    query_form, key_form, score_form = forms
    score_scale = 1.0 / math.sqrt(HDIM)
    raw_scores = scores_of(queries, keys, forms, bias, valid)
    probs = jnp.exp(raw_scores - log_total[..., None])
    low_probs = probs.astype(jnp.bfloat16)
    prob_grad = jnp.einsum(
        query_form + "," + key_form + "->" + score_form,
        upstream,
        values_in,
        preferred_element_type=jnp.float32,
    )
    inner = jnp.sum(probs * prob_grad, axis=-1, keepdims=True)
    score_grad = (probs * (prob_grad - inner)).astype(jnp.bfloat16)
    query_grad = (
        jnp.einsum(
            score_form + "," + key_form + "->" + query_form,
            score_grad,
            keys,
            preferred_element_type=jnp.float32,
        )
        * score_scale
    )
    key_grad = (
        jnp.einsum(
            score_form + "," + query_form + "->" + key_form,
            score_grad,
            queries,
            preferred_element_type=jnp.float32,
        )
        * score_scale
    )
    value_grad = jnp.einsum(
        score_form + "," + query_form + "->" + key_form,
        low_probs,
        upstream,
        preferred_element_type=jnp.float32,
    )
    return (query_grad, key_grad, value_grad, score_grad)


def on_device(
    video,
    cotangent,
    text,
    video_ids,
    timesteps,
    text_lengths,
    group_gain,
    group_bias,
    first_conv,
    film_weight,
    second_conv,
    spatial_norm,
    spatial_qkv,
    spatial_out,
    cross_norm,
    cross_query,
    cross_kv,
    cross_out,
    temporal_norm,
    temporal_qkv,
    temporal_out,
    offset_bias,
    feed_norm,
    feed_in,
    feed_out,
):
    frames_axis, lines = lax.axis_size("tm"), lax.axis_size("space")
    slots, frame_dev, row_dev, columns, channels = video.shape
    half_width = first_conv.shape[2]
    head_local = half_width // HDIM
    pixels_dev = row_dev * columns
    frames_all = frame_dev * frames_axis
    token_rows = slots * frame_dev * pixels_dev
    text_local = text.shape[1]
    pixel_form = ("nqhe", "nkhe", "nhqk")
    frame_form = ("bfphe", "bgphe", "bphfg")
    video_lines = space_to_all(video, 4, 2)
    text_all = lax.all_gather(text, ("tm", "space"), axis=1, tiled=True)
    spatial_out = lax.all_gather(spatial_out, "space", axis=1, tiled=True)
    cross_query = lax.all_gather(cross_query, "space", axis=0, tiled=True)
    cross_out = lax.all_gather(cross_out, "space", axis=1, tiled=True)
    temporal_qkv = lax.all_gather(temporal_qkv, "space", axis=0, tiled=True)
    temporal_out = lax.all_gather(temporal_out, "space", axis=1, tiled=True)
    spatial_qkv = space_to_all(spatial_qkv, 2, 0)
    feed_in = space_to_all(feed_in, 1, 0)
    feed_out = space_to_all(feed_out, 0, 1)
    cot_rows = cotangent.reshape(token_rows, channels)
    cot_line = gather_tokens(cot_rows)

    gain_line = part_of(group_gain, "space", 0)
    bias_line = part_of(group_bias, "space", 0)
    normal_one, inverse_one = group_forward(video_lines.astype(jnp.float32))
    affine_one = normal_one * gain_line + bias_line
    first_in = jax.nn.silu(affine_one).astype(jnp.bfloat16)
    hidden_part = conv_frames(first_in, first_conv, "IHWO", False)
    hidden = lax.psum_scatter(
        hidden_part.astype(jnp.bfloat16), "space", scatter_dimension=4, tiled=True
    ).astype(jnp.float32)
    normal_two, inverse_two = group_forward(hidden)
    embed = sinusoid(timesteps).astype(jnp.bfloat16)
    film_part = jnp.einsum(
        "bvc,cjk->bvjk", part_of(embed, "space", 2), film_weight, preferred_element_type=jnp.float32
    )
    film = lax.psum_scatter(film_part, "space", scatter_dimension=3, tiled=True)
    frame_ids = part_of(video_ids, "tm", 1)
    choose = (frame_ids[:, :, None] == jnp.arange(VIDS, dtype=jnp.int32)[None, None, :]).astype(
        jnp.float32
    )
    frame_film = jnp.einsum("bfv,bvjk->bfjk", choose, film, precision=highest)
    modulated = (
        normal_two * (1.0 + frame_film[:, :, None, None, 0]) + frame_film[:, :, None, None, 1]
    )
    second_in = jax.nn.silu(modulated).astype(jnp.bfloat16)
    second_wide = lax.all_gather(second_in, "space", axis=4, tiled=True)
    conv_part = conv_frames(second_wide, second_conv, "IHWO", False)
    conv_half = lax.psum_scatter(
        conv_part.astype(jnp.bfloat16), "mp", scatter_dimension=4, tiled=True
    )
    conv_rows = space_to_all(conv_half, 2, 4).reshape(token_rows, lines, -1)
    conv_rows = lax.all_gather(conv_rows, "mp", axis=2, tiled=True).reshape(token_rows, channels)
    stream_one = video.astype(jnp.float32).reshape(token_rows, channels) + conv_rows.astype(
        jnp.float32
    )

    spatial_in = layer_norm(stream_one, spatial_norm).astype(jnp.bfloat16)
    spatial_line = gather_tokens(spatial_in)
    head_line = spatial_qkv.shape[2] // HDIM
    spatial_triple = (
        jnp.einsum("rd,djk->rjk", spatial_line, spatial_qkv, preferred_element_type=jnp.float32)
        .astype(jnp.bfloat16)
        .reshape(lines, slots * frame_dev, pixels_dev, 3, head_line, HDIM)
        .transpose(3, 1, 0, 2, 4, 5)
        .reshape(3, slots * frame_dev, H * W, head_line, HDIM)
    )
    spatial_query, spatial_key, spatial_value = spatial_triple
    spatial_mix, spatial_total = attend_forward(
        spatial_query, spatial_key, spatial_value, pixel_form, None, None
    )
    spatial_mix = space_to_all(
        spatial_mix.reshape(slots * frame_dev, H * W, head_line * HDIM), 1, 2
    ).reshape(token_rows, half_width)
    stream_two = stream_one + mp_sum(
        jnp.dot(spatial_mix, spatial_out, preferred_element_type=jnp.float32)
    )
    cross_in = layer_norm(stream_two, cross_norm).astype(jnp.bfloat16)
    cross_rows = jnp.dot(cross_in, cross_query, preferred_element_type=jnp.float32).astype(
        jnp.bfloat16
    )
    text_some = part_of(part_of(text_all, "tm", 1), "space", 2)
    text_pairs = lax.psum_scatter(
        jnp.einsum("btc,cjk->btjk", text_some, cross_kv, preferred_element_type=jnp.float32).astype(
            jnp.bfloat16
        ),
        "space",
        scatter_dimension=1,
        tiled=True,
    )
    text_pairs = lax.all_gather(text_pairs, ("tm", "space"), axis=1, tiled=True)
    cross_queries = cross_rows.reshape(slots, frame_dev * pixels_dev, head_local, HDIM)
    text_key = text_pairs[:, :, 0].reshape(slots, TXT, head_local, HDIM)
    text_value = text_pairs[:, :, 1].reshape(slots, TXT, head_local, HDIM)
    text_valid = (jnp.arange(TXT, dtype=jnp.int32)[None, :] < text_lengths[:, None])[
        :, None, None, :
    ]
    cross_mix, cross_total = attend_forward(
        cross_queries, text_key, text_value, pixel_form, None, text_valid
    )
    cross_mix = cross_mix.reshape(token_rows, half_width)
    stream_three = stream_two + mp_sum(
        jnp.dot(cross_mix, cross_out, preferred_element_type=jnp.float32)
    )
    temporal_in = layer_norm(stream_three, temporal_norm).astype(jnp.bfloat16)
    temporal_triple = (
        jnp.einsum("rd,djk->rjk", temporal_in, temporal_qkv, preferred_element_type=jnp.float32)
        .astype(jnp.bfloat16)
        .reshape(slots, frame_dev, pixels_dev, 3, half_width)
    )
    clip_triple = to_clips(temporal_triple)
    clip_pixels = clip_triple.shape[2]
    clip_query = clip_triple[:, :, :, 0].reshape(slots, frames_all, clip_pixels, head_local, HDIM)
    clip_key = clip_triple[:, :, :, 1].reshape(slots, frames_all, clip_pixels, head_local, HDIM)
    clip_value = clip_triple[:, :, :, 2].reshape(slots, frames_all, clip_pixels, head_local, HDIM)
    offset_table = offset_onehot(0, video_ids.shape[1], frames_all)
    clip_bias = jnp.einsum("qkr,rh->hqk", offset_table, offset_bias, precision=highest)[None, None]
    clip_valid = (video_ids[:, :, None] == video_ids[:, None, :])[:, None, None]
    clip_mix, clip_total = attend_forward(
        clip_query, clip_key, clip_value, frame_form, clip_bias, clip_valid
    )
    temporal_mix = from_clips(clip_mix.reshape(slots, frames_all, clip_pixels, half_width))
    temporal_mix = temporal_mix.reshape(token_rows, half_width)
    stream_four = stream_three + mp_sum(
        jnp.dot(temporal_mix, temporal_out, preferred_element_type=jnp.float32)
    )
    feed_rows = layer_norm(stream_four, feed_norm).astype(jnp.bfloat16)
    feed_line = gather_tokens(feed_rows)
    upper = jnp.dot(feed_line, feed_in, preferred_element_type=jnp.float32)
    active = jax.nn.gelu(upper).astype(jnp.bfloat16)
    final = stream_four + scatter_tokens(
        jnp.dot(active, feed_out, preferred_element_type=jnp.float32)
    )
    mixed = final.astype(jnp.bfloat16).reshape(video.shape)

    feed_out_grad = jnp.einsum("rf,rd->fd", active, cot_line, preferred_element_type=jnp.float32)
    feed_out_grad = space_to_all(sum_over_frames(feed_out_grad, 1), 1, 0).astype(jnp.float32)
    active_grad = jnp.einsum("rd,fd->rf", cot_line, feed_out, preferred_element_type=jnp.float32)
    upper_grad = jax.vjp(jax.nn.gelu, upper)[1](active_grad)[0].astype(jnp.bfloat16)
    feed_in_grad = jnp.einsum(
        "rd,rf->df", feed_line, upper_grad, preferred_element_type=jnp.float32
    )
    feed_in_grad = space_to_all(sum_over_frames(feed_in_grad, 0), 0, 1).astype(jnp.float32)
    normed_grad = scatter_tokens(
        jnp.einsum("rf,df->rd", upper_grad, feed_in, preferred_element_type=jnp.float32)
    )
    stream_grad, feed_norm_grad = layer_back(stream_four, feed_norm, normed_grad)
    upstream = cot_rows.astype(jnp.float32) + stream_grad
    branch_grad = upstream.astype(jnp.bfloat16)
    temporal_out_grad = sum_to_owner(
        jnp.einsum("rc,rd->cd", temporal_mix, branch_grad, preferred_element_type=jnp.float32), 1
    )
    mix_grad = jnp.einsum(
        "rd,cd->rc", branch_grad, temporal_out, preferred_element_type=jnp.float32
    ).astype(jnp.bfloat16)
    clip_up = to_clips(mix_grad.reshape(slots, frame_dev, pixels_dev, half_width)).reshape(
        slots, frames_all, clip_pixels, head_local, HDIM
    )
    query_grad, key_grad, value_grad, score_grad = attend_backward(
        clip_query, clip_key, clip_value, frame_form, clip_bias, clip_valid, clip_total, clip_up
    )
    score_total = jnp.sum(score_grad.astype(jnp.float32), axis=(0, 1))
    offset_bias_grad = jnp.einsum("hqk,qkr->rh", score_total, offset_table, precision=highest)
    clip_grads = (
        jnp.stack([query_grad, key_grad, value_grad], axis=3)
        .astype(jnp.bfloat16)
        .reshape(slots, frames_all, clip_pixels, 3, half_width)
    )
    triple_grad = from_clips(clip_grads)
    triple_grad = triple_grad.reshape(token_rows, 3, half_width)
    temporal_qkv_grad = sum_to_owner(
        jnp.einsum("rd,rjk->djk", temporal_in, triple_grad, preferred_element_type=jnp.float32), 0
    )
    normed_grad = mp_sum(
        jnp.einsum("rjk,djk->rd", triple_grad, temporal_qkv, preferred_element_type=jnp.float32)
    )
    stream_grad, temporal_norm_grad = layer_back(stream_three, temporal_norm, normed_grad)
    upstream = upstream + stream_grad
    branch_grad = upstream.astype(jnp.bfloat16)
    cross_out_grad = sum_to_owner(
        jnp.einsum("rc,rd->cd", cross_mix, branch_grad, preferred_element_type=jnp.float32), 1
    )
    mix_grad = (
        jnp.einsum("rd,cd->rc", branch_grad, cross_out, preferred_element_type=jnp.float32)
        .astype(jnp.bfloat16)
        .reshape(slots, frame_dev * pixels_dev, head_local, HDIM)
    )
    query_grad, key_grad, value_grad, score_grad = attend_backward(
        cross_queries, text_key, text_value, pixel_form, None, text_valid, cross_total, mix_grad
    )
    text_pair_grad = lax.psum_scatter(
        jnp.stack([key_grad, value_grad], axis=2)
        .reshape(slots, TXT, 2, half_width)
        .astype(jnp.bfloat16),
        ("tm", "space"),
        scatter_dimension=1,
        tiled=True,
    )
    text_pair_all = lax.all_gather(text_pair_grad, ("tm", "space"), axis=1, tiled=True)
    cross_kv_grad = jnp.einsum(
        "btc,btjk->cjk",
        part_of(part_of(text_all, "tm", 2), "space", 2),
        text_pair_all,
        preferred_element_type=jnp.float32,
    )
    text_part = jnp.einsum(
        "btjk,cjk->btc",
        part_of(text_pair_all, "tm", 1),
        cross_kv,
        preferred_element_type=jnp.float32,
    ).astype(jnp.bfloat16)
    text_grad = lax.psum_scatter(
        space_to_all(text_part, 1, 2), "mp", scatter_dimension=2, tiled=True
    ).astype(jnp.float32)
    query_rows_grad = query_grad.astype(jnp.bfloat16).reshape(token_rows, half_width)
    cross_query_grad = sum_to_owner(
        jnp.einsum("rd,rk->dk", cross_in, query_rows_grad, preferred_element_type=jnp.float32), 0
    )
    normed_grad = mp_sum(
        jnp.einsum("rk,dk->rd", query_rows_grad, cross_query, preferred_element_type=jnp.float32)
    )
    stream_grad, cross_norm_grad = layer_back(stream_two, cross_norm, normed_grad)
    upstream = upstream + stream_grad
    branch_grad = upstream.astype(jnp.bfloat16)
    spatial_out_grad = sum_to_owner(
        jnp.einsum("rc,rd->cd", spatial_mix, branch_grad, preferred_element_type=jnp.float32), 1
    )
    mix_grad = (
        jnp.einsum("rd,cd->rc", branch_grad, spatial_out, preferred_element_type=jnp.float32)
        .astype(jnp.bfloat16)
        .reshape(slots * frame_dev, pixels_dev, half_width)
    )
    mix_line = space_to_all(mix_grad, 2, 1).reshape(slots * frame_dev, H * W, head_line, HDIM)
    query_grad, key_grad, value_grad, score_grad = attend_backward(
        spatial_query, spatial_key, spatial_value, pixel_form, None, None, spatial_total, mix_line
    )
    triple_grad = (
        jnp.stack([query_grad, key_grad, value_grad], axis=0)
        .astype(jnp.bfloat16)
        .reshape(3, slots * frame_dev, lines, pixels_dev, head_line * HDIM)
        .transpose(2, 1, 3, 0, 4)
        .reshape(lines * token_rows, 3, head_line * HDIM)
    )
    spatial_qkv_grad = jnp.einsum(
        "rd,rjk->djk", spatial_line, triple_grad, preferred_element_type=jnp.float32
    )
    spatial_qkv_grad = space_to_all(sum_over_frames(spatial_qkv_grad, 0), 0, 2).astype(jnp.float32)
    normed_grad = scatter_tokens(
        jnp.einsum("rjk,djk->rd", triple_grad, spatial_qkv, preferred_element_type=jnp.float32)
    )
    stream_grad, spatial_norm_grad = layer_back(stream_one, spatial_norm, normed_grad)
    upstream = upstream + stream_grad
    branch_line = space_to_all(upstream.astype(jnp.bfloat16).reshape(video.shape), 4, 2)
    second_conv_grad = stationary_to_owner(conv_weight_grad(second_wide, branch_line), 2)
    second_part = conv_frames(branch_line, second_conv, "OHWI", True)
    second_in_grad = lax.psum_scatter(
        second_part.astype(jnp.bfloat16), "space", scatter_dimension=4, tiled=True
    ).astype(jnp.float32)
    modulated_grad = jax.vjp(jax.nn.silu, modulated)[1](second_in_grad)[0]
    frame_grads = jnp.stack(
        [jnp.sum(modulated_grad * normal_two, axis=(2, 3)), jnp.sum(modulated_grad, axis=(2, 3))],
        axis=2,
    )
    video_film_grad = jnp.einsum("bfv,bfjk->bvjk", choose, frame_grads, precision=highest)
    video_film_grad = lax.all_gather(
        lax.psum(video_film_grad, "tm"), "space", axis=3, tiled=True
    )
    film_weight_grad = jnp.einsum(
        "bvc,bvjk->cjk",
        part_of(part_of(embed, "tm", 2), "space", 2).astype(jnp.float32),
        video_film_grad,
        precision=highest,
    )
    hidden_grad = group_backward(
        modulated_grad * (1.0 + frame_film[:, :, None, None, 0]), normal_two, inverse_two
    ).astype(jnp.bfloat16)
    hidden_wide = lax.all_gather(hidden_grad, "space", axis=4, tiled=True)
    first_conv_grad = stationary_to_owner(conv_weight_grad(first_in, hidden_wide), 1)
    first_in_grad = mp_sum(conv_frames(hidden_wide, first_conv, "OHWI", True))
    affine_grad = jax.vjp(jax.nn.silu, affine_one)[1](first_in_grad)[0]
    group_gain_grad = jnp.sum(affine_grad * normal_one, axis=(0, 1, 2, 3))
    group_bias_grad = jnp.sum(affine_grad, axis=(0, 1, 2, 3))
    video_line_grad = group_backward(affine_grad * gain_line, normal_one, inverse_one)
    video_grad = upstream.reshape(video.shape) + space_to_all(
        video_line_grad.astype(jnp.bfloat16), 2, 4
    ).astype(jnp.float32)

    def placed(line_grad):
        whole = jnp.zeros((channels,), jnp.float32)
        return lax.dynamic_update_slice_in_dim(
            whole, line_grad, lax.axis_index("space") * line_grad.shape[0], 0
        )

    owners = frames_axis * lines
    small = jnp.concatenate(
        [
            item.reshape(owners, -1)
            for item in (
                placed(group_gain_grad),
                placed(group_bias_grad),
                spatial_norm_grad,
                cross_norm_grad,
                temporal_norm_grad,
                feed_norm_grad,
                offset_bias_grad,
            )
        ],
        axis=1,
    )
    small = lax.psum_scatter(small, ("tm", "space"), scatter_dimension=0, tiled=True)[0]
    gain_size = channels // owners
    gains = [small[i * gain_size : (i + 1) * gain_size] for i in range(6)]
    offset_bias_grad = small[6 * gain_size :].reshape(R // owners, head_local)
    return (
        mixed,
        video_grad,
        text_grad,
        gains[0],
        gains[1],
        first_conv_grad.transpose(1, 0, 2),
        film_weight_grad,
        second_conv_grad.transpose(1, 0, 2),
        gains[2],
        spatial_qkv_grad,
        spatial_out_grad,
        gains[3],
        cross_query_grad,
        cross_kv_grad,
        cross_out_grad,
        gains[4],
        temporal_qkv_grad,
        temporal_out_grad,
        offset_bias_grad,
        gains[5],
        feed_in_grad,
        feed_out_grad,
    )


def solution(mesh):
    return jax.shard_map(
        on_device,
        mesh=mesh,
        in_specs=(
            P(None, "tm", "space", None, None),
            P(None, "tm", "space", None, None),
            P(None, ("tm", "space"), None),
            P(),
            P(),
            P(),
            P(),
            P(),
            P("space", None, "mp"),
            P("space", None, "mp"),
            P("mp", None, "space"),
            P(),
            P("space", None, "mp"),
            P("mp", "space"),
            P(),
            P("space", "mp"),
            P("space", None, "mp"),
            P("mp", "space"),
            P(),
            P("space", None, "mp"),
            P("mp", "space"),
            P(None, "mp"),
            P(),
            P("space", "mp"),
            P("mp", "space"),
        ),
        out_specs=(
            P(None, "tm", "space", None, None),
            P(None, "tm", "space", None, None),
            P(None, ("tm", "space"), "mp"),
            P(("tm", "space")),
            P(("tm", "space")),
            P(("tm", "space"), None, "mp"),
            P(("tm", "space"), None, "mp"),
            P("mp", None, ("tm", "space")),
            P(("tm", "space")),
            P(("tm", "space"), None, "mp"),
            P("mp", ("tm", "space")),
            P(("tm", "space")),
            P(("tm", "space"), "mp"),
            P(("tm", "space"), None, "mp"),
            P("mp", ("tm", "space")),
            P(("tm", "space")),
            P(("tm", "space"), None, "mp"),
            P("mp", ("tm", "space")),
            P(("tm", "space"), "mp"),
            P(("tm", "space")),
            P(("tm", "space"), "mp"),
            P("mp", ("tm", "space")),
        ),
        check_vma=False,
    )
```

```python
import math

import jax
import jax.numpy as jnp
from jax import lax
from jax.experimental import pallas as pl
from jax.experimental.pallas import tpu as pltpu
from jax.sharding import PartitionSpec as P

D = 1024
HDIM = 64
TXT = 128
G = 32
R = 128
VIDS = 3
H = 16
W = 16


epsilon = 1e-05
highest = lax.Precision.HIGHEST
masked = -1e30


def mp_sum(partial_sum):
    mine = partial_sum.astype(jnp.bfloat16)
    other = lax.ppermute(mine, "mp", [(0, 1), (1, 0)])
    return mine.astype(jnp.float32) + other.astype(jnp.float32)


def part_of(source, axis_name, dim):
    size = source.shape[dim] // lax.axis_size(axis_name)
    return lax.dynamic_slice_in_dim(source, lax.axis_index(axis_name) * size, size, dim)


def space_to_all(source, split, concat):
    return lax.all_to_all(source, "space", split_axis=split, concat_axis=concat, tiled=True)


MESH = pl.DeviceIdType.MESH
lane = 128
ANY = pl.BlockSpec(memory_space=pl.ANY)
VMEM = pl.BlockSpec(memory_space=pltpu.VMEM)


def meet(peers):
    gate = pltpu.get_barrier_semaphore()
    for peer in peers:
        pl.semaphore_signal(gate, inc=1, device_id=peer, device_id_type=MESH)
    pl.semaphore_wait(gate, len(peers))


def others(axis_name):
    count = lax.axis_size(axis_name)
    me = lax.axis_index(axis_name)
    return [(step, lax.rem(me + step, count)) for step in range(1, count)]


def send(source, target, send_sem, recv_sem, peer):
    copy = pltpu.make_async_remote_copy(
        src_ref=source,
        dst_ref=target,
        send_sem=send_sem,
        recv_sem=recv_sem,
        device_id=peer,
        device_id_type=MESH,
    )
    copy.start()
    return copy


def keep(source, target, sem):
    copy = pltpu.make_async_copy(source, target, sem)
    copy.start()
    return copy


def cols_of(ref, index, width):
    return ref.at[:, :, pl.ds(pl.multiple_of(index * width, width), width)]


def rows_of(ref, index, width):
    return ref.at[:, pl.ds(pl.multiple_of(index * width, width), width), :]


def talk(kernel, result, operands, scratch, number, specs=None, out_spec=ANY):
    return pl.pallas_call(
        kernel,
        out_shape=result,
        in_specs=[ANY] * len(operands) if specs is None else specs,
        out_specs=out_spec,
        scratch_shapes=scratch,
        compiler_params=pltpu.CompilerParams(
            collective_id=number, has_side_effects=True, vmem_limit_bytes=48 * 1024 * 1024
        ),
    )(*operands)


def dma_sems(*counts):
    return [pltpu.SemaphoreType.DMA((max(count, 1),)) for count in counts]


def flat_index(axes):
    index = 0
    for name in axes:
        index = index * lax.axis_size(name) + lax.axis_index(name)
    return index


def flat_peers(axes):
    count = math.prod(lax.axis_size(name) for name in axes)
    me = flat_index(axes)
    peers = []
    for step in range(1, count):
        peer = lax.rem(me + step, count)
        place, rest = {}, peer
        for name in reversed(axes):
            place[name] = lax.rem(rest, lax.axis_size(name))
            rest = rest // lax.axis_size(name)
        peers.append((step, peer, place))
    return peers


def exchange(source, axes, number):
    count = source.shape[0]

    def kernel(x_ref, out_ref, send_sem, recv_sem, own_sem):
        me = flat_index(axes)
        peers = flat_peers(axes)
        meet([place for _, _, place in peers])
        copies = [
            send(x_ref.at[peer], out_ref.at[me], send_sem.at[i - 1], recv_sem.at[i - 1], place)
            for i, peer, place in peers
        ]
        copies.append(keep(x_ref.at[me], out_ref.at[me], own_sem.at[0]))
        for copy in copies:
            copy.wait()

    result = jax.ShapeDtypeStruct(source.shape, source.dtype)
    return talk(kernel, result, [source], dma_sems(count - 1, count - 1, 1), number)


def share(source, axes, number):
    count = math.prod(lax.axis_size(name) for name in axes)

    def kernel(x_ref, out_ref, send_sem, recv_sem, own_sem):
        me = flat_index(axes)
        peers = flat_peers(axes)
        meet([place for _, _, place in peers])
        copies = [
            send(x_ref, out_ref.at[me], send_sem.at[i - 1], recv_sem.at[i - 1], place)
            for i, _, place in peers
        ]
        copies.append(keep(x_ref, out_ref.at[me], own_sem.at[0]))
        for copy in copies:
            copy.wait()

    result = jax.ShapeDtypeStruct((count,) + source.shape, source.dtype)
    return talk(kernel, result, [source], dma_sems(count - 1, count - 1, 1), number)


class FrameSum:
    def __init__(self, source):
        self.count, self.rows, self.width = source.shape
        self.source = source
        self.result = jax.ShapeDtypeStruct((self.rows, self.width), jnp.bfloat16)
        self.scratch = [
            pltpu.VMEM((max(self.count - 1, 1), self.rows, self.width), jnp.bfloat16),
            pltpu.VMEM((self.rows, self.width), jnp.bfloat16),
        ] + dma_sems(self.count - 1, self.count - 1, 1)

    def peers(self):
        return [{"tm": peer} for _, peer in others("tm")]

    def start(self, w_ref, got_ref, own_ref, send_sem, recv_sem, own_sem):
        me = lax.axis_index("tm")
        self.copies = [
            send(w_ref.at[peer], got_ref.at[i - 1], send_sem.at[i - 1], recv_sem.at[i - 1], {"tm": peer})
            for i, peer in others("tm")
        ]
        self.copies.append(keep(w_ref.at[me], own_ref, own_sem.at[0]))

    def finish(self, out_ref, got_ref, own_ref):
        for copy in self.copies:
            copy.wait()
        block = min(16, self.rows)

        def some(index, carry):
            rows = pl.ds(pl.multiple_of(index * block, block), block)
            total = own_ref[rows, :].astype(jnp.float32)
            for step in range(self.count - 1):
                total = total + got_ref[step, rows, :].astype(jnp.float32)
            out_ref[rows, :] = total.astype(jnp.bfloat16)
            return carry

        lax.fori_loop(0, self.rows // block, some, 0)


def talk_with(kernel, peers, result, operands, scratch, number, extra, specs=None, out_spec=ANY):
    specs = [ANY] * len(operands) if specs is None else specs
    if extra is None:

        def alone(*refs):
            meet(peers())
            kernel(*refs)

        return talk(alone, result, operands, scratch, number, specs, out_spec), None
    inputs, own_scratch = len(operands), len(scratch)

    def both(*refs):
        ins, w_ref = refs[:inputs], refs[inputs]
        out_ref, sum_ref = refs[inputs + 1 : inputs + 3]
        rest = refs[inputs + 3 :]
        mine, theirs = rest[:own_scratch], rest[own_scratch:]
        meet(peers() + extra.peers())
        extra.start(w_ref, *theirs)
        kernel(*ins, out_ref, *mine)
        extra.finish(sum_ref, theirs[0], theirs[1])

    return talk(
        both,
        (result, extra.result),
        operands + [extra.source],
        scratch + extra.scratch,
        number,
        specs + [ANY],
        (out_spec, VMEM),
    )


def line_peers():
    return [{"space": peer} for _, peer in others("space")]


def to_lines(source, per_core, number):
    images, pixels, channels = source.shape
    lines, cores = lax.axis_size("space"), lax.axis_size("mp")
    pieces = lines * cores if per_core else lines
    width = channels // pieces
    if width % lane != 0 or pixels % 16 != 0:
        if per_core:
            parts = source.reshape(images, pixels, lines, cores, width)
            parts = lax.dynamic_index_in_dim(parts, lax.axis_index("mp"), 3, keepdims=False)
            source = parts.reshape(images, pixels, lines * width)
        return lax.all_to_all(source, "space", split_axis=2, concat_axis=1, tiled=True)

    def kernel(x_ref, out_ref, send_sem, recv_sem, own_sem):
        me, core = lax.axis_index("space"), lax.axis_index("mp")
        place = (lambda s: s * cores + core) if per_core else (lambda s: s)
        meet([{"space": peer} for _, peer in others("space")])
        target = rows_of(out_ref, me, pixels)
        copies = [
            send(cols_of(x_ref, place(peer), width), target, send_sem.at[i - 1], recv_sem.at[i - 1], {"space": peer})
            for i, peer in others("space")
        ]
        copies.append(keep(cols_of(x_ref, place(me), width), target, own_sem.at[0]))
        for copy in copies:
            copy.wait()

    result = jax.ShapeDtypeStruct((images, lines * pixels, width), source.dtype)
    return talk(kernel, result, [source], dma_sems(lines - 1, lines - 1, 1), number)


def plain_sum(extra):
    if extra is None:
        return None
    return lax.psum_scatter(extra.source, "tm", scatter_dimension=0, tiled=True)[0]


def from_lines(source, per_core, number, extra=None):
    images, line_pixels, width = source.shape
    lines, cores = lax.axis_size("space"), lax.axis_size("mp")
    pixels = line_pixels // lines
    pieces = lines * cores if per_core else lines
    if width % lane != 0 or pixels % 16 != 0:
        part = lax.all_to_all(source, "space", split_axis=1, concat_axis=2, tiled=True)
        if per_core:
            part = part.reshape(images, pixels, lines, 1, width)
            part = lax.all_gather(part, "mp", axis=3, tiled=True)
        return part.reshape(images, pixels, pieces * width), plain_sum(extra)

    def kernel(x_ref, out_ref, send_sem, recv_sem, pass_sem, gain_sem, own_sem):
        me, core = lax.axis_index("space"), lax.axis_index("mp")
        place = (lambda s: s * cores + core) if per_core else (lambda s: s)
        twin = {"mp": 1 - core}
        target = cols_of(out_ref, place(me), width)
        copies = [
            send(rows_of(x_ref, peer, pixels), target, send_sem.at[i - 1], recv_sem.at[i - 1], {"space": peer})
            for i, peer in others("space")
        ]
        own = keep(rows_of(x_ref, me, pixels), target, own_sem.at[0])
        passed = []
        if per_core:
            passed.append(send(rows_of(x_ref, me, pixels), target, pass_sem.at[0], gain_sem.at[0], twin))
        for step in range(1, lines):
            copies[step - 1].wait_recv()
            if per_core:
                origin = lax.rem(me - step + lines, lines)
                got = cols_of(out_ref, place(origin), width)
                passed.append(send(got, got, pass_sem.at[step], gain_sem.at[step], twin))
        for copy in copies:
            copy.wait_send()
        own.wait()
        for copy in passed:
            copy.wait()

    def peers():
        return line_peers() + ([{"mp": 1 - lax.axis_index("mp")}] if per_core else [])

    result = jax.ShapeDtypeStruct((images, pixels, pieces * width), source.dtype)
    sems = dma_sems(lines - 1, lines - 1, lines, lines, 1)
    return talk_with(kernel, peers, result, [source], sems, number, extra)


def gather_lines(source, number, extra=None):
    images, line_pixels, width = source.shape
    lines = lax.axis_size("space")
    if width % lane != 0:
        return lax.all_gather(source, "space", axis=2, tiled=True), plain_sum(extra)

    def kernel(x_ref, out_ref, send_sem, recv_sem, own_sem):
        me = lax.axis_index("space")
        target = cols_of(out_ref, me, width)
        copies = [
            send(x_ref, target, send_sem.at[i - 1], recv_sem.at[i - 1], {"space": peer})
            for i, peer in others("space")
        ]
        copies.append(keep(x_ref, target, own_sem.at[0]))
        for copy in copies:
            copy.wait()

    result = jax.ShapeDtypeStruct((images, line_pixels, lines * width), source.dtype)
    sems = dma_sems(lines - 1, lines - 1, 1)
    return talk_with(kernel, line_peers, result, [source], sems, number, extra)


def gather_cores(source, number):
    images, line_pixels, width = source.shape
    cores = lax.axis_size("mp")
    if width % lane != 0:
        return lax.all_gather(source, "mp", axis=2, tiled=True)

    def kernel(x_ref, out_ref, send_sem, recv_sem, own_sem):
        core = lax.axis_index("mp")
        twin = {"mp": 1 - core}
        meet([twin])
        target = cols_of(out_ref, core, width)
        copy = send(x_ref, target, send_sem.at[0], recv_sem.at[0], twin)
        own = keep(x_ref, target, own_sem.at[0])
        copy.wait()
        own.wait()

    result = jax.ShapeDtypeStruct((images, line_pixels, cores * width), source.dtype)
    return talk(kernel, result, [source], dma_sems(1, 1, 1), number)


def sum_lines(source, number, extra=None):
    images, line_pixels, channels = source.shape
    lines = lax.axis_size("space")
    width = channels // lines
    if width % lane != 0:
        total = lax.psum_scatter(source, "space", scatter_dimension=2, tiled=True)
        return total.astype(jnp.float32), plain_sum(extra)

    def kernel(x_ref, out_ref, got_ref, send_sem, recv_sem):
        me = lax.axis_index("space")
        copies = [
            send(cols_of(x_ref, peer, width), got_ref.at[i - 1], send_sem.at[i - 1], recv_sem.at[i - 1], {"space": peer})
            for i, peer in others("space")
        ]
        mine = pl.ds(pl.multiple_of(me * width, width), width)
        for copy in copies:
            copy.wait()
        for image in range(images):
            total = x_ref[image, :, mine].astype(jnp.float32)
            for step in range(lines - 1):
                total = total + got_ref[step, image].astype(jnp.float32)
            out_ref[image] = total

    result = jax.ShapeDtypeStruct((images, line_pixels, width), jnp.float32)
    scratch = [pltpu.VMEM((lines - 1, images, line_pixels, width), source.dtype)]
    scratch = scratch + dma_sems(lines - 1, lines - 1)
    return talk_with(
        kernel, line_peers, result, [source], scratch, number, extra, [VMEM], VMEM
    )


def sum_cores(source, number):
    images, line_pixels, channels = source.shape
    cores = lax.axis_size("mp")
    width = channels // cores
    if width % lane != 0:
        return lax.psum_scatter(source, "mp", scatter_dimension=2, tiled=True).astype(jnp.float32)

    def kernel(x_ref, out_ref, got_ref, send_sem, recv_sem):
        core = lax.axis_index("mp")
        twin = {"mp": 1 - core}
        meet([twin])
        copy = send(cols_of(x_ref, 1 - core, width), got_ref, send_sem.at[0], recv_sem.at[0], twin)
        mine = pl.ds(pl.multiple_of(core * width, width), width)
        copy.wait()
        for image in range(images):
            out_ref[image] = x_ref[image, :, mine].astype(jnp.float32) + got_ref[image].astype(
                jnp.float32
            )

    result = jax.ShapeDtypeStruct((images, line_pixels, width), jnp.float32)
    scratch = [pltpu.VMEM((images, line_pixels, width), source.dtype)]
    return talk(kernel, result, [source], scratch + dma_sems(1, 1), number, [VMEM], VMEM)


def gather_tokens(rows, number):
    count, channels = rows.shape
    lines, cores = lax.axis_size("space"), lax.axis_size("mp")
    width = channels // cores
    source = rows.reshape(1, count, channels)

    def kernel(x_ref, out_ref, send_sem, recv_sem, pass_sem, gain_sem, own_sem):
        me, core = lax.axis_index("space"), lax.axis_index("mp")
        twin = {"mp": 1 - core}
        meet([{"space": peer} for _, peer in others("space")] + [twin])

        def spot(origin):
            return cols_of(rows_of(out_ref, origin, count), core, width)

        copies = [
            send(cols_of(x_ref, core, width), spot(me), send_sem.at[i - 1], recv_sem.at[i - 1], {"space": peer})
            for i, peer in others("space")
        ]
        own = keep(x_ref, rows_of(out_ref, me, count), own_sem.at[0])
        passed = []
        for step in range(1, lines):
            copies[step - 1].wait_recv()
            got = spot(lax.rem(me - step + lines, lines))
            passed.append(send(got, got, pass_sem.at[step - 1], gain_sem.at[step - 1], twin))
        for copy in copies:
            copy.wait_send()
        own.wait()
        for copy in passed:
            copy.wait()

    result = jax.ShapeDtypeStruct((1, lines * count, channels), rows.dtype)
    sems = dma_sems(lines - 1, lines - 1, lines - 1, lines - 1, 1)
    return talk(kernel, result, [source], sems, number).reshape(lines * count, channels)


def scatter_tokens(partial_sum, number, extra=None):
    all_rows, channels = partial_sum.shape
    lines, cores = lax.axis_size("space"), lax.axis_size("mp")
    count, width = all_rows // lines, channels // cores
    source = partial_sum.astype(jnp.bfloat16).reshape(lines, count, channels)

    def kernel(x_ref, out_ref, twin_ref, sum_ref, got_ref, s_sem, r_sem, s2_sem, r2_sem, s3_sem, r3_sem):
        me, core = lax.axis_index("space"), lax.axis_index("mp")
        twin = {"mp": 1 - core}
        theirs = pl.ds(pl.multiple_of((1 - core) * width, width), width)
        mine = pl.ds(pl.multiple_of(core * width, width), width)
        order = [(i, peer) for i, peer in others("space")] + [(0, me)]
        first = [
            send(x_ref.at[target, :, theirs], twin_ref.at[i], s_sem.at[i], r_sem.at[i], twin)
            for i, target in order
        ]
        second = []
        for (i, target), copy in zip(order, first):
            copy.wait_recv()
            total = x_ref[target, :, mine].astype(jnp.float32) + twin_ref[i].astype(jnp.float32)
            if i == 0:
                own = total
            else:
                sum_ref[i - 1] = total.astype(jnp.bfloat16)
                second.append(
                    send(sum_ref.at[i - 1], got_ref.at[i - 1], s2_sem.at[i - 1], r2_sem.at[i - 1], {"space": target})
                )
        for copy in second:
            copy.wait_recv()
        for i in range(lines - 1):
            own = own + got_ref[i].astype(jnp.float32)
        out_ref[:, mine] = own.astype(jnp.bfloat16)
        third = send(out_ref.at[:, mine], out_ref.at[:, mine], s3_sem.at[0], r3_sem.at[0], twin)
        for copy in first + second:
            copy.wait_send()
        third.wait()

    result = jax.ShapeDtypeStruct((count, channels), jnp.bfloat16)
    scratch = [
        pltpu.VMEM((lines, count, width), jnp.bfloat16),
        pltpu.VMEM((max(lines - 1, 1), count, width), jnp.bfloat16),
        pltpu.VMEM((max(lines - 1, 1), count, width), jnp.bfloat16),
    ]
    sems = dma_sems(lines, lines, lines - 1, lines - 1, 1, 1)

    def peers():
        return line_peers() + [{"mp": 1 - lax.axis_index("mp")}]

    total, other = talk_with(
        kernel, peers, result, [source], scratch + sems, number, extra, [VMEM], VMEM
    )
    return total.astype(jnp.float32), other


def to_clips(source, number):
    slots, frames, pixels, channels = source.shape
    count = lax.axis_size("tm")
    few = pixels // count
    if few % 16 != 0:
        return lax.all_to_all(source, "tm", split_axis=2, concat_axis=1, tiled=True)

    def kernel(x_ref, out_ref, send_sem, recv_sem, own_sem):
        me = lax.axis_index("tm")
        meet([{"tm": peer} for _, peer in others("tm")])
        target = out_ref.at[:, pl.ds(me * frames, frames)]

        def part(index):
            return x_ref.at[:, :, pl.ds(pl.multiple_of(index * few, few), few)]

        copies = [
            send(part(peer), target, send_sem.at[i - 1], recv_sem.at[i - 1], {"tm": peer})
            for i, peer in others("tm")
        ]
        copies.append(keep(part(me), target, own_sem.at[0]))
        for copy in copies:
            copy.wait()

    result = jax.ShapeDtypeStruct((slots, count * frames, few, channels), source.dtype)
    return talk(kernel, result, [source], dma_sems(count - 1, count - 1, 1), number)


def from_clips(source, number):
    slots, all_frames, few, channels = source.shape
    count = lax.axis_size("tm")
    frames = all_frames // count
    if few % 16 != 0:
        return lax.all_to_all(source, "tm", split_axis=1, concat_axis=2, tiled=True)

    def kernel(x_ref, out_ref, send_sem, recv_sem, own_sem):
        me = lax.axis_index("tm")
        meet([{"tm": peer} for _, peer in others("tm")])
        target = out_ref.at[:, :, pl.ds(pl.multiple_of(me * few, few), few)]

        def part(index):
            return x_ref.at[:, pl.ds(index * frames, frames)]

        copies = [
            send(part(peer), target, send_sem.at[i - 1], recv_sem.at[i - 1], {"tm": peer})
            for i, peer in others("tm")
        ]
        copies.append(keep(part(me), target, own_sem.at[0]))
        for copy in copies:
            copy.wait()

    result = jax.ShapeDtypeStruct((slots, frames, count * few, channels), source.dtype)
    return talk(kernel, result, [source], dma_sems(count - 1, count - 1, 1), number)


def sum_to_owner(weight_grad):
    return lax.psum_scatter(weight_grad, ("tm", "space"), scatter_dimension=0, tiled=True)


def by_frames(weight_grad):
    return FrameSum(weight_grad.reshape(lax.axis_size("tm"), -1, weight_grad.shape[1]))


def to_owner(portion):
    frames, lines = lax.axis_size("tm"), lax.axis_size("space")
    moves = [(t * lines + s, s * frames + t) for t in range(frames) for s in range(lines)]
    return lax.ppermute(portion, ("tm", "space"), moves)


def padded_rims(source):
    return jnp.pad(source, ((0, 0), (0, 0), (1, 1), (1, 1), (0, 0)))


def conv_weight(weight):
    return weight.reshape(weight.shape[0], 3, 3, weight.shape[2])


def conv_frames(source, weight, spec, flipped):
    images = source.reshape((-1,) + source.shape[2:])
    kernel = conv_weight(weight)
    if flipped:
        kernel = kernel[:, ::-1, ::-1]
    result = lax.conv_general_dilated(
        images,
        kernel,
        (1, 1),
        "SAME",
        dimension_numbers=("NHWC", spec, "NHWC"),
        preferred_element_type=jnp.float32,
    )
    return result.reshape(source.shape[:4] + (result.shape[-1],))


def conv_weight_grad(source, upstream, form):
    padded = padded_rims(source)
    rows, cols = source.shape[2], source.shape[3]
    tap_list = []
    for tap in range(9):
        i, j = tap // 3, tap % 3
        tap_list.append(
            jnp.einsum(
                "bfhwc,bfhwk->" + form,
                padded[:, :, i : i + rows, j : j + cols],
                upstream,
                preferred_element_type=jnp.float32,
            ).astype(jnp.bfloat16)
        )
    return jnp.concatenate(tap_list, axis=1)


def grouped_view(source):
    size = D // G
    dims_all = source.shape
    return source.reshape(
        dims_all[0], dims_all[1], dims_all[2] * dims_all[3], dims_all[4] // size, size
    )


def group_forward(source):
    grouped = grouped_view(source)
    average = jnp.mean(grouped, axis=(2, 4), keepdims=True)
    centered = grouped - average
    variance = jnp.mean(centered * centered, axis=(2, 4), keepdims=True)
    inverse = lax.rsqrt(variance + epsilon)
    return ((centered * inverse).reshape(source.shape), inverse)


def group_backward(upstream, normal, inverse):
    grouped_up = grouped_view(upstream)
    grouped_norm = grouped_view(normal)
    first_mean = jnp.mean(grouped_up, axis=(2, 4), keepdims=True)
    second_mean = jnp.mean(grouped_up * grouped_norm, axis=(2, 4), keepdims=True)
    result = inverse * (grouped_up - first_mean - grouped_norm * second_mean)
    return result.reshape(upstream.shape)


def layer_norm(source, norm_gain):
    average = jnp.mean(source, axis=-1, keepdims=True)
    centered = source - average
    variance = jnp.mean(centered * centered, axis=-1, keepdims=True)
    return centered * lax.rsqrt(variance + epsilon) * norm_gain


def layer_back(source, norm_gain, upstream):
    _, pullback = jax.vjp(layer_norm, source, norm_gain)
    return pullback(upstream)


def sinusoid(steps_int):
    counted = D // 2
    freqs = jnp.exp(-math.log(10000.0) * jnp.arange(counted, dtype=jnp.float32) / counted)
    angles = steps_int.astype(jnp.float32)[..., None] * freqs
    return jnp.concatenate([jnp.sin(angles), jnp.cos(angles)], axis=-1)


def offset_onehot(query_start, query_count, key_count):
    distance = (
        query_start
        + jnp.arange(query_count, dtype=jnp.int32)[:, None]
        - jnp.arange(key_count, dtype=jnp.int32)[None, :]
    )
    position = jnp.clip(distance, -(R // 2), R // 2 - 1) + R // 2
    return (position[:, :, None] == jnp.arange(R, dtype=jnp.int32)[None, None, :]).astype(
        jnp.float32
    )


def scores_of(queries, keys, forms, bias, valid):
    query_form, key_form, score_form = forms
    raw_scores = jnp.einsum(
        query_form + "," + key_form + "->" + score_form,
        queries,
        keys,
        preferred_element_type=jnp.float32,
    ) * (1.0 / math.sqrt(HDIM))
    if bias is not None:
        raw_scores = raw_scores + bias
    if valid is not None:
        raw_scores = jnp.where(valid, raw_scores, masked)
    return raw_scores


def attend_forward(queries, keys, values_in, forms, bias, valid):
    query_form, key_form, score_form = forms
    raw_scores = scores_of(queries, keys, forms, bias, valid)
    largest = jnp.max(raw_scores, axis=-1, keepdims=True)
    expos = jnp.exp(raw_scores - largest)
    totals = jnp.sum(expos, axis=-1, keepdims=True)
    probs = (expos / totals).astype(jnp.bfloat16)
    log_total = (largest + jnp.log(totals))[..., 0]
    result = jnp.einsum(
        score_form + "," + key_form + "->" + query_form,
        probs,
        values_in,
        preferred_element_type=jnp.float32,
    )
    return (result.astype(jnp.bfloat16), log_total)


def attend_backward(queries, keys, values_in, forms, bias, valid, log_total, upstream):
    query_form, key_form, score_form = forms
    score_scale = 1.0 / math.sqrt(HDIM)
    raw_scores = scores_of(queries, keys, forms, bias, valid)
    probs = jnp.exp(raw_scores - log_total[..., None])
    low_probs = probs.astype(jnp.bfloat16)
    prob_grad = jnp.einsum(
        query_form + "," + key_form + "->" + score_form,
        upstream,
        values_in,
        preferred_element_type=jnp.float32,
    )
    inner = jnp.sum(probs * prob_grad, axis=-1, keepdims=True)
    score_grad = (probs * (prob_grad - inner)).astype(jnp.bfloat16)
    query_grad = (
        jnp.einsum(
            score_form + "," + key_form + "->" + query_form,
            score_grad,
            keys,
            preferred_element_type=jnp.float32,
        )
        * score_scale
    )
    key_grad = (
        jnp.einsum(
            score_form + "," + query_form + "->" + key_form,
            score_grad,
            queries,
            preferred_element_type=jnp.float32,
        )
        * score_scale
    )
    value_grad = jnp.einsum(
        score_form + "," + query_form + "->" + key_form,
        low_probs,
        upstream,
        preferred_element_type=jnp.float32,
    )
    return (query_grad, key_grad, value_grad, score_grad)


def on_device(
    video,
    cotangent,
    text,
    video_ids,
    timesteps,
    text_lengths,
    group_gain,
    group_bias,
    first_conv,
    film_weight,
    second_conv,
    spatial_norm,
    spatial_qkv,
    spatial_out,
    cross_norm,
    cross_query,
    cross_kv,
    cross_out,
    temporal_norm,
    temporal_qkv,
    temporal_out,
    offset_bias,
    feed_norm,
    feed_in,
    feed_out,
):
    frames_axis, lines = lax.axis_size("tm"), lax.axis_size("space")
    slots, frame_dev, row_dev, columns, channels = video.shape
    half_width = first_conv.shape[2]
    head_local = half_width // HDIM
    pixels_dev = row_dev * columns
    frames_all = frame_dev * frames_axis
    token_rows = slots * frame_dev * pixels_dev
    text_local = text.shape[1]
    pixel_form = ("nqhe", "nkhe", "nhqk")
    frame_form = ("bfphe", "bgphe", "bphfg")
    images = slots * frame_dev
    core_shape = (slots, frame_dev, H, W, -1)
    video_lines = to_lines(video.reshape(images, pixels_dev, channels), True, 1).reshape(core_shape)
    everyone = ("tm", "space")
    owners = frames_axis * lines
    out_piece = part_of(jnp.concatenate([spatial_out, cross_out, temporal_out], axis=1), "tm", 0)
    out_all = lax.all_gather(out_piece, everyone, axis=0, tiled=False)
    out_all = out_all.reshape(frames_axis, lines, -1, 3, channels // lines)
    out_all = out_all.transpose(3, 0, 2, 1, 4).reshape(3, half_width, channels)
    spatial_out, cross_out, temporal_out = out_all[0], out_all[1], out_all[2]
    in_piece = jnp.concatenate([cross_query, temporal_qkv.reshape(-1, 3 * half_width)], axis=1)
    in_all = lax.all_gather(part_of(in_piece, "tm", 1), everyone, axis=0, tiled=False)
    in_all = in_all.reshape(frames_axis, channels, -1)
    if in_all.shape[2] == half_width:
        cross_query, temporal_qkv = in_all[0], in_all[1:]
    else:
        in_all = in_all.transpose(1, 0, 2).reshape(channels, 4, half_width).transpose(1, 0, 2)
        cross_query, temporal_qkv = in_all[0], in_all[1:]
    text_rows = slots * text_local
    text_flat = text.reshape(text_rows, -1)
    text_width = text_flat.shape[1]
    spatial_qkv = space_to_all(spatial_qkv, 2, 0)
    feed_in = space_to_all(feed_in, 1, 0)
    feed_out = space_to_all(feed_out, 0, 1)
    cot_rows = cotangent.reshape(token_rows, channels)
    cot_line = gather_tokens(cot_rows, 2)

    gain_line = part_of(part_of(group_gain, "space", 0), "mp", 0)
    bias_line = part_of(part_of(group_bias, "space", 0), "mp", 0)
    normal_one, inverse_one = group_forward(video_lines.astype(jnp.float32))
    affine_one = normal_one * gain_line + bias_line
    first_in = jax.nn.silu(affine_one).astype(jnp.bfloat16)
    first_in = gather_cores(first_in.reshape(images, H * W, -1), 3).reshape(core_shape)
    hidden_part = conv_frames(first_in, first_conv, "IHWO", False)
    hidden = sum_lines(hidden_part.astype(jnp.bfloat16).reshape(images, H * W, half_width), 4)
    hidden = hidden[0].reshape(core_shape)
    normal_two, inverse_two = group_forward(hidden)
    embed = sinusoid(timesteps).astype(jnp.bfloat16)
    film_part = jnp.einsum(
        "bvc,cjk->bvjk", part_of(embed, "space", 2), film_weight, preferred_element_type=jnp.float32
    )
    film = lax.psum_scatter(film_part, "space", scatter_dimension=3, tiled=True)
    frame_ids = part_of(video_ids, "tm", 1)
    choose = (frame_ids[:, :, None] == jnp.arange(VIDS, dtype=jnp.int32)[None, None, :]).astype(
        jnp.float32
    )
    frame_film = jnp.einsum("bfv,bvjk->bfjk", choose, film, precision=highest)
    modulated = (
        normal_two * (1.0 + frame_film[:, :, None, None, 0]) + frame_film[:, :, None, None, 1]
    )
    second_in = jax.nn.silu(modulated).astype(jnp.bfloat16)
    second_wide = gather_lines(second_in.reshape(images, H * W, -1), 5)[0].reshape(core_shape)
    conv_part = conv_frames(second_wide, second_conv, "IHWO", False)
    conv_half = sum_cores(conv_part.astype(jnp.bfloat16).reshape(images, H * W, -1), 6)
    conv_rows = from_lines(conv_half.astype(jnp.bfloat16), True, 7)[0]
    conv_rows = conv_rows.reshape(token_rows, channels)
    stream_one = video.astype(jnp.float32).reshape(token_rows, channels) + conv_rows.astype(
        jnp.float32
    )

    spatial_in = layer_norm(stream_one, spatial_norm).astype(jnp.bfloat16)
    spatial_line = gather_tokens(spatial_in, 8)
    head_line = spatial_qkv.shape[2] // HDIM
    spatial_triple = (
        jnp.einsum("rd,djk->rjk", spatial_line, spatial_qkv, preferred_element_type=jnp.float32)
        .astype(jnp.bfloat16)
        .reshape(lines, slots * frame_dev, pixels_dev, 3, head_line, HDIM)
        .transpose(3, 1, 0, 2, 4, 5)
        .reshape(3, slots * frame_dev, H * W, head_line, HDIM)
    )
    spatial_query, spatial_key, spatial_value = spatial_triple
    spatial_mix, spatial_total = attend_forward(
        spatial_query, spatial_key, spatial_value, pixel_form, None, None
    )
    spatial_mix = from_lines(
        spatial_mix.reshape(slots * frame_dev, H * W, head_line * HDIM), False, 9
    )[0].reshape(token_rows, half_width)
    stream_two = stream_one + mp_sum(
        jnp.dot(spatial_mix, spatial_out, preferred_element_type=jnp.float32)
    )
    cross_in = layer_norm(stream_two, cross_norm).astype(jnp.bfloat16)
    cross_rows = jnp.dot(cross_in, cross_query, preferred_element_type=jnp.float32).astype(
        jnp.bfloat16
    )
    text_line = to_lines(text_flat[None], False, 24)[0]
    text_part = jnp.dot(
        text_line, cross_kv.reshape(cross_kv.shape[0], -1), preferred_element_type=jnp.float32
    )
    text_part = exchange(
        text_part.astype(jnp.bfloat16).reshape(lines, text_rows, -1), ("space",), 25
    )
    text_part = jnp.sum(text_part.astype(jnp.float32), axis=0).astype(jnp.bfloat16)
    text_pairs = (
        share(text_part, everyone, 26)
        .reshape(owners, slots, text_local, 2, half_width)
        .transpose(1, 0, 2, 3, 4)
        .reshape(slots, TXT, 2, half_width)
    )
    cross_queries = cross_rows.reshape(slots, frame_dev * pixels_dev, head_local, HDIM)
    text_key = text_pairs[:, :, 0].reshape(slots, TXT, head_local, HDIM)
    text_value = text_pairs[:, :, 1].reshape(slots, TXT, head_local, HDIM)
    text_valid = (jnp.arange(TXT, dtype=jnp.int32)[None, :] < text_lengths[:, None])[
        :, None, None, :
    ]
    cross_mix, cross_total = attend_forward(
        cross_queries, text_key, text_value, pixel_form, None, text_valid
    )
    cross_mix = cross_mix.reshape(token_rows, half_width)
    stream_three = stream_two + mp_sum(
        jnp.dot(cross_mix, cross_out, preferred_element_type=jnp.float32)
    )
    temporal_in = layer_norm(stream_three, temporal_norm).astype(jnp.bfloat16)
    temporal_triple = (
        jnp.einsum("rd,jdk->rjk", temporal_in, temporal_qkv, preferred_element_type=jnp.float32)
        .astype(jnp.bfloat16)
        .reshape(slots, frame_dev, pixels_dev, 3, half_width)
    )
    clip_triple = to_clips(temporal_triple.reshape(slots, frame_dev, pixels_dev, 3 * half_width), 10)
    clip_pixels = clip_triple.shape[2]
    clip_triple = clip_triple.reshape(slots, frames_all, clip_pixels, 3, half_width)
    clip_query = clip_triple[:, :, :, 0].reshape(slots, frames_all, clip_pixels, head_local, HDIM)
    clip_key = clip_triple[:, :, :, 1].reshape(slots, frames_all, clip_pixels, head_local, HDIM)
    clip_value = clip_triple[:, :, :, 2].reshape(slots, frames_all, clip_pixels, head_local, HDIM)
    offset_table = offset_onehot(0, video_ids.shape[1], frames_all)
    clip_bias = jnp.einsum("qkr,rh->hqk", offset_table, offset_bias, precision=highest)[None, None]
    clip_valid = (video_ids[:, :, None] == video_ids[:, None, :])[:, None, None]
    clip_mix, clip_total = attend_forward(
        clip_query, clip_key, clip_value, frame_form, clip_bias, clip_valid
    )
    temporal_mix = from_clips(clip_mix.reshape(slots, frames_all, clip_pixels, half_width), 11)
    temporal_mix = temporal_mix.reshape(token_rows, half_width)
    stream_four = stream_three + mp_sum(
        jnp.dot(temporal_mix, temporal_out, preferred_element_type=jnp.float32)
    )
    feed_rows = layer_norm(stream_four, feed_norm).astype(jnp.bfloat16)
    feed_line = gather_tokens(feed_rows, 12)
    upper = jnp.dot(feed_line, feed_in, preferred_element_type=jnp.float32)
    active = jax.nn.gelu(upper).astype(jnp.bfloat16)
    final = stream_four + scatter_tokens(
        jnp.dot(active, feed_out, preferred_element_type=jnp.float32), 13
    )[0]
    mixed = final.astype(jnp.bfloat16).reshape(video.shape)

    feed_out_grad = jnp.einsum("rf,rd->df", active, cot_line, preferred_element_type=jnp.float32)
    active_grad = jnp.einsum("rd,fd->rf", cot_line, feed_out, preferred_element_type=jnp.float32)
    upper_grad = jax.vjp(jax.nn.gelu, upper)[1](active_grad)[0].astype(jnp.bfloat16)
    feed_in_grad = jnp.einsum(
        "rd,rf->df", feed_line, upper_grad, preferred_element_type=jnp.float32
    )
    feed_grads = jnp.concatenate(
        [feed_in_grad.astype(jnp.bfloat16), feed_out_grad.astype(jnp.bfloat16)], axis=1
    )
    normed_grad, feed_grads = scatter_tokens(
        jnp.einsum("rf,df->rd", upper_grad, feed_in, preferred_element_type=jnp.float32),
        14,
        by_frames(feed_grads),
    )
    stream_grad, feed_norm_grad = layer_back(stream_four, feed_norm, normed_grad)
    upstream = cot_rows.astype(jnp.float32) + stream_grad
    branch_grad = upstream.astype(jnp.bfloat16)
    temporal_out_grad = jnp.einsum(
        "rc,rd->dc", temporal_mix, branch_grad, preferred_element_type=jnp.float32
    ).astype(jnp.bfloat16)
    mix_grad = jnp.einsum(
        "rd,cd->rc", branch_grad, temporal_out, preferred_element_type=jnp.float32
    ).astype(jnp.bfloat16)
    clip_up = to_clips(mix_grad.reshape(slots, frame_dev, pixels_dev, half_width), 15).reshape(
        slots, frames_all, clip_pixels, head_local, HDIM
    )
    query_grad, key_grad, value_grad, score_grad = attend_backward(
        clip_query, clip_key, clip_value, frame_form, clip_bias, clip_valid, clip_total, clip_up
    )
    score_total = jnp.sum(score_grad.astype(jnp.float32), axis=(0, 1))
    offset_bias_grad = jnp.einsum("hqk,qkr->rh", score_total, offset_table, precision=highest)
    clip_grads = (
        jnp.stack([query_grad, key_grad, value_grad], axis=3)
        .astype(jnp.bfloat16)
        .reshape(slots, frames_all, clip_pixels, 3 * half_width)
    )
    triple_grad = from_clips(clip_grads, 16)
    triple_grad = triple_grad.reshape(token_rows, 3, half_width)
    temporal_qkv_grad = jnp.dot(
        temporal_in.T,
        triple_grad.reshape(token_rows, 3 * half_width),
        preferred_element_type=jnp.float32,
    ).astype(jnp.bfloat16)
    temporal_grads = sum_to_owner(
        jnp.concatenate([temporal_qkv_grad, temporal_out_grad], axis=1)
    )
    normed_grad = mp_sum(
        jnp.einsum("rjk,jdk->rd", triple_grad, temporal_qkv, preferred_element_type=jnp.float32)
    )
    stream_grad, temporal_norm_grad = layer_back(stream_three, temporal_norm, normed_grad)
    upstream = upstream + stream_grad
    branch_grad = upstream.astype(jnp.bfloat16)
    cross_out_grad = jnp.einsum(
        "rc,rd->dc", cross_mix, branch_grad, preferred_element_type=jnp.float32
    ).astype(jnp.bfloat16)
    mix_grad = (
        jnp.einsum("rd,cd->rc", branch_grad, cross_out, preferred_element_type=jnp.float32)
        .astype(jnp.bfloat16)
        .reshape(slots, frame_dev * pixels_dev, head_local, HDIM)
    )
    query_grad, key_grad, value_grad, score_grad = attend_backward(
        cross_queries, text_key, text_value, pixel_form, None, text_valid, cross_total, mix_grad
    )
    pair_grad = (
        jnp.stack([key_grad, value_grad], axis=2)
        .astype(jnp.bfloat16)
        .reshape(slots, owners, text_local, 2 * half_width)
        .transpose(1, 0, 2, 3)
        .reshape(owners, text_rows, 2 * half_width)
    )
    pair_grad = exchange(pair_grad, everyone, 27)
    pair_grad = jnp.sum(pair_grad.astype(jnp.float32), axis=0).astype(jnp.bfloat16)
    pair_all = share(pair_grad, everyone, 28)
    text_cols = text_flat.reshape(text_rows, owners, -1).transpose(1, 0, 2)
    text_cols = exchange(text_cols, everyone, 29)
    cross_kv_grad = jnp.einsum(
        "prc,prk->ck", text_cols, pair_all, preferred_element_type=jnp.float32
    ).reshape(-1, 2, half_width)
    text_part = jnp.einsum(
        "srk,ck->src",
        part_of(pair_all, "tm", 0),
        cross_kv.reshape(cross_kv.shape[0], -1),
        preferred_element_type=jnp.float32,
    ).astype(jnp.bfloat16)
    text_part = exchange(text_part, ("space",), 30).transpose(1, 0, 2).reshape(text_rows, -1)
    text_half = part_of(mp_sum(text_part), "mp", 1)
    text_grad = text_half.reshape(slots, text_local, -1)
    query_rows_grad = query_grad.astype(jnp.bfloat16).reshape(token_rows, half_width)
    cross_query_grad = jnp.einsum(
        "rd,rk->dk", cross_in, query_rows_grad, preferred_element_type=jnp.float32
    ).astype(jnp.bfloat16)
    normed_grad = mp_sum(
        jnp.einsum("rk,dk->rd", query_rows_grad, cross_query, preferred_element_type=jnp.float32)
    )
    stream_grad, cross_norm_grad = layer_back(stream_two, cross_norm, normed_grad)
    upstream = upstream + stream_grad
    branch_grad = upstream.astype(jnp.bfloat16)
    spatial_out_grad = jnp.einsum(
        "rc,rd->dc", spatial_mix, branch_grad, preferred_element_type=jnp.float32
    ).astype(jnp.bfloat16)
    cross_grads = sum_to_owner(
        jnp.concatenate([cross_query_grad, cross_out_grad, spatial_out_grad], axis=1)
    )
    mix_grad = (
        jnp.einsum("rd,cd->rc", branch_grad, spatial_out, preferred_element_type=jnp.float32)
        .astype(jnp.bfloat16)
        .reshape(slots * frame_dev, pixels_dev, half_width)
    )
    mix_line = to_lines(mix_grad, False, 17).reshape(slots * frame_dev, H * W, head_line, HDIM)
    query_grad, key_grad, value_grad, score_grad = attend_backward(
        spatial_query, spatial_key, spatial_value, pixel_form, None, None, spatial_total, mix_line
    )
    triple_grad = (
        jnp.stack([query_grad, key_grad, value_grad], axis=0)
        .astype(jnp.bfloat16)
        .reshape(3, slots * frame_dev, lines, pixels_dev, head_line * HDIM)
        .transpose(2, 1, 3, 0, 4)
        .reshape(lines * token_rows, 3, head_line * HDIM)
    )
    spatial_qkv_grad = jnp.dot(
        spatial_line.T,
        triple_grad.reshape(lines * token_rows, -1),
        preferred_element_type=jnp.float32,
    ).astype(jnp.bfloat16)
    normed_grad = scatter_tokens(
        jnp.einsum("rjk,djk->rd", triple_grad, spatial_qkv, preferred_element_type=jnp.float32), 18
    )[0]
    stream_grad, spatial_norm_grad = layer_back(stream_one, spatial_norm, normed_grad)
    upstream = upstream + stream_grad
    branch_line = upstream.astype(jnp.bfloat16).reshape(images, pixels_dev, channels)
    branch_line = to_lines(branch_line, False, 19).reshape(core_shape)
    second_conv_grad = conv_weight_grad(second_wide, branch_line, "kc")
    second_part = conv_frames(branch_line, second_conv, "OHWI", True)
    second_in_grad, spatial_qkv_grad = sum_lines(
        second_part.astype(jnp.bfloat16).reshape(images, H * W, half_width),
        20,
        by_frames(spatial_qkv_grad),
    )
    second_in_grad = second_in_grad.reshape(core_shape)
    modulated_grad = jax.vjp(jax.nn.silu, modulated)[1](second_in_grad)[0]
    frame_grads = jnp.stack(
        [jnp.sum(modulated_grad * normal_two, axis=(2, 3)), jnp.sum(modulated_grad, axis=(2, 3))],
        axis=2,
    )
    video_film_grad = jnp.einsum("bfv,bfjk->bvjk", choose, frame_grads, precision=highest)
    film_shares = share(
        video_film_grad.reshape(slots * VIDS * 2, -1), everyone, 31
    ).reshape(frames_axis, lines, slots, VIDS, 2, -1)
    video_film_grad = (
        jnp.sum(film_shares, axis=0)
        .transpose(1, 2, 3, 0, 4)
        .reshape(slots, VIDS, 2, half_width)
    )
    film_weight_grad = jnp.einsum(
        "bvc,bvjk->cjk",
        part_of(part_of(embed, "tm", 2), "space", 2).astype(jnp.float32),
        video_film_grad,
        precision=highest,
    )
    hidden_grad = group_backward(
        modulated_grad * (1.0 + frame_film[:, :, None, None, 0]), normal_two, inverse_two
    ).astype(jnp.bfloat16)
    hidden_wide, second_conv_grad = gather_lines(
        hidden_grad.reshape(images, H * W, -1), 21, by_frames(second_conv_grad)
    )
    hidden_wide = hidden_wide.reshape(core_shape)
    first_conv_grad = conv_weight_grad(first_in, hidden_wide, "ck")
    first_in_grad = conv_frames(hidden_wide, first_conv, "OHWI", True).astype(jnp.bfloat16)
    first_in_grad = sum_cores(first_in_grad.reshape(images, H * W, -1), 22).reshape(core_shape)
    affine_grad = jax.vjp(jax.nn.silu, affine_one)[1](first_in_grad)[0]
    group_gain_grad = jnp.sum(affine_grad * normal_one, axis=(0, 1, 2, 3))
    group_bias_grad = jnp.sum(affine_grad, axis=(0, 1, 2, 3))
    video_line_grad = group_backward(affine_grad * gain_line, normal_one, inverse_one)
    video_rows_grad, first_conv_grad = from_lines(
        video_line_grad.astype(jnp.bfloat16).reshape(images, H * W, -1),
        True,
        23,
        by_frames(first_conv_grad),
    )
    video_grad = upstream.reshape(video.shape) + video_rows_grad.reshape(video.shape).astype(
        jnp.float32
    )

    def placed(line_grad):
        whole = jnp.zeros((channels,), jnp.float32)
        return lax.dynamic_update_slice_in_dim(
            whole,
            line_grad,
            (lax.axis_index("space") * cores + lax.axis_index("mp")) * line_grad.shape[0],
            0,
        )

    cores = lax.axis_size("mp")
    small = jnp.concatenate(
        [
            item.reshape(owners, -1)
            for item in (
                placed(group_gain_grad),
                placed(group_bias_grad),
                spatial_norm_grad,
                cross_norm_grad,
                temporal_norm_grad,
                feed_norm_grad,
                offset_bias_grad,
            )
        ],
        axis=1,
    )
    small = jnp.sum(exchange(small[:, None], everyone, 32), axis=(0, 1))
    small_twin = lax.ppermute(small, "mp", [(0, 1), (1, 0)])
    gain_size = channels // owners
    gains = [small[i * gain_size : (i + 1) * gain_size] for i in range(6)]
    for i in range(2):
        gains[i] = gains[i] + small_twin[i * gain_size : (i + 1) * gain_size]
    local = jnp.concatenate([feed_grads, spatial_qkv_grad], axis=1)
    local = exchange(local.reshape(lines, -1, local.shape[1]), ("space",), 33).astype(jnp.float32)
    feed_width = feed_in.shape[1]
    local_rows = local.shape[1]
    feed_in_grad = local[:, :, :feed_width].transpose(1, 0, 2).reshape(local_rows, -1)
    feed_out_grad = local[:, :, feed_width : 2 * feed_width].transpose(0, 2, 1)
    feed_out_grad = feed_out_grad.reshape(-1, local_rows)
    spatial_qkv_grad = (
        local[:, :, 2 * feed_width :]
        .reshape(lines, local_rows, 3, -1)
        .transpose(1, 2, 0, 3)
        .reshape(local_rows, 3, half_width)
    )
    first_conv_grad = to_owner(first_conv_grad).astype(jnp.float32)
    second_conv_grad = to_owner(second_conv_grad).astype(jnp.float32)
    temporal_grads = temporal_grads.astype(jnp.float32)
    cross_grads = cross_grads.astype(jnp.float32)
    temporal_qkv_grad = temporal_grads[:, : 3 * half_width].reshape(-1, 3, half_width)
    temporal_out_grad = temporal_grads[:, 3 * half_width :].T
    cross_query_grad = cross_grads[:, :half_width]
    cross_out_grad = cross_grads[:, half_width : 2 * half_width].T
    spatial_out_grad = cross_grads[:, 2 * half_width :].T
    offset_bias_grad = small[6 * gain_size :].reshape(R // owners, head_local)
    return (
        mixed,
        video_grad,
        text_grad,
        gains[0],
        gains[1],
        first_conv_grad.reshape(-1, 9, half_width),
        film_weight_grad,
        second_conv_grad.reshape(-1, 9, half_width).transpose(2, 1, 0),
        gains[2],
        spatial_qkv_grad,
        spatial_out_grad,
        gains[3],
        cross_query_grad,
        cross_kv_grad,
        cross_out_grad,
        gains[4],
        temporal_qkv_grad,
        temporal_out_grad,
        offset_bias_grad,
        gains[5],
        feed_in_grad,
        feed_out_grad,
    )


def solution(mesh):
    return jax.shard_map(
        on_device,
        mesh=mesh,
        in_specs=(
            P(None, "tm", "space", None, None),
            P(None, "tm", "space", None, None),
            P(None, ("tm", "space"), None),
            P(),
            P(),
            P(),
            P(),
            P(),
            P("space", None, "mp"),
            P("space", None, "mp"),
            P("mp", None, "space"),
            P(),
            P("space", None, "mp"),
            P("mp", "space"),
            P(),
            P("space", "mp"),
            P("space", None, "mp"),
            P("mp", "space"),
            P(),
            P("space", None, "mp"),
            P("mp", "space"),
            P(None, "mp"),
            P(),
            P("space", "mp"),
            P("mp", "space"),
        ),
        out_specs=(
            P(None, "tm", "space", None, None),
            P(None, "tm", "space", None, None),
            P(None, ("tm", "space"), "mp"),
            P(("tm", "space")),
            P(("tm", "space")),
            P(("tm", "space"), None, "mp"),
            P(("tm", "space"), None, "mp"),
            P("mp", None, ("tm", "space")),
            P(("tm", "space")),
            P(("tm", "space"), None, "mp"),
            P("mp", ("tm", "space")),
            P(("tm", "space")),
            P(("tm", "space"), "mp"),
            P(("tm", "space"), None, "mp"),
            P("mp", ("tm", "space")),
            P(("tm", "space")),
            P(("tm", "space"), None, "mp"),
            P("mp", ("tm", "space")),
            P(("tm", "space"), "mp"),
            P(("tm", "space")),
            P(("tm", "space"), "mp"),
            P("mp", ("tm", "space")),
        ),
        check_vma=False,
    )
```

```python
import math

import jax
import jax.numpy as jnp
from jax import lax
from jax.experimental import pallas as pl
from jax.experimental.pallas import tpu as pltpu
from jax.sharding import PartitionSpec as P

D = 1024
HDIM = 64
TXT = 128
G = 32
R = 128
VIDS = 3
H = 16
W = 16


epsilon = 1e-05
highest = lax.Precision.HIGHEST
masked = -1e30


def twin_add(partial_sum):
    mine = partial_sum.astype(jnp.bfloat16)
    other = lax.ppermute(mine, "mp", [(0, 1), (1, 0)])
    return mine.astype(jnp.float32) + other.astype(jnp.float32)


def part_of(source, axis_name, dim):
    size = source.shape[dim] // lax.axis_size(axis_name)
    return lax.dynamic_slice_in_dim(source, lax.axis_index(axis_name) * size, size, dim)


MESH = pl.DeviceIdType.MESH
lane = 128
ANY = pl.BlockSpec(memory_space=pl.ANY)
VMEM = pl.BlockSpec(memory_space=pltpu.VMEM)


def meet(peers):
    gate = pltpu.get_barrier_semaphore()
    for peer in peers:
        pl.semaphore_signal(gate, inc=1, device_id=peer, device_id_type=MESH)
    pl.semaphore_wait(gate, len(peers))


def others(axis_name):
    count = lax.axis_size(axis_name)
    me = lax.axis_index(axis_name)
    return [(step, lax.rem(me + step, count)) for step in range(1, count)]


def send(source, target, send_sem, recv_sem, peer):
    copy = pltpu.make_async_remote_copy(
        src_ref=source,
        dst_ref=target,
        send_sem=send_sem,
        recv_sem=recv_sem,
        device_id=peer,
        device_id_type=MESH,
    )
    copy.start()
    return copy


def keep(source, target, sem):
    copy = pltpu.make_async_copy(source, target, sem)
    copy.start()
    return copy


def cols_of(ref, index, width):
    return ref.at[:, :, pl.ds(pl.multiple_of(index * width, width), width)]


def rows_of(ref, index, width):
    return ref.at[:, pl.ds(pl.multiple_of(index * width, width), width), :]


def talk(kernel, result, operands, scratch, number, specs=None, out_spec=ANY):
    return pl.pallas_call(
        kernel,
        out_shape=result,
        in_specs=[ANY] * len(operands) if specs is None else specs,
        out_specs=out_spec,
        scratch_shapes=scratch,
        compiler_params=pltpu.CompilerParams(
            collective_id=number, has_side_effects=True, vmem_limit_bytes=48 * 1024 * 1024
        ),
    )(*operands)


def dma_sems(*counts):
    return [pltpu.SemaphoreType.DMA((max(count, 1),)) for count in counts]


def flat_index(axes):
    index = 0
    for name in axes:
        index = index * lax.axis_size(name) + lax.axis_index(name)
    return index


def flat_peers(axes):
    count = math.prod(lax.axis_size(name) for name in axes)
    me = flat_index(axes)
    peers = []
    for step in range(1, count):
        peer = lax.rem(me + step, count)
        place, rest = {}, peer
        for name in reversed(axes):
            place[name] = lax.rem(rest, lax.axis_size(name))
            rest = rest // lax.axis_size(name)
        peers.append((step, peer, place))
    return peers


class Rider:
    scratch = ()
    result_spec = ANY

    def peers(self):
        return [place for _, _, place in flat_peers(self.axes)]


class Exchange(Rider):
    def __init__(self, source, axes):
        self.source, self.axes = source, axes
        count = source.shape[0]
        self.result = jax.ShapeDtypeStruct(source.shape, source.dtype)
        self.scratch = dma_sems(count - 1, count - 1, 1)

    def plain(self):
        return lax.all_to_all(self.source, self.axes, split_axis=0, concat_axis=0, tiled=True)

    def start(self, x_ref, out_ref, send_sem, recv_sem, own_sem):
        me = flat_index(self.axes)
        self.copies = [
            send(x_ref.at[peer], out_ref.at[me], send_sem.at[i - 1], recv_sem.at[i - 1], place)
            for i, peer, place in flat_peers(self.axes)
        ]
        self.copies.append(keep(x_ref.at[me], out_ref.at[me], own_sem.at[0]))

    def finish(self, *refs):
        for copy in self.copies:
            copy.wait()


class Share(Rider):
    def __init__(self, source, axes, first=0, size=None):
        self.source, self.axes = source, axes
        self.first, self.size = first, size
        count = math.prod(lax.axis_size(name) for name in axes)
        shape = source.shape if size is None else (size,) + source.shape[1:]
        self.result = jax.ShapeDtypeStruct((count,) + shape, source.dtype)
        self.scratch = dma_sems(count - 1, count - 1, 1)

    def plain(self):
        source = self.source
        if self.size is not None:
            source = source[self.first : self.first + self.size]
        return lax.all_gather(source, self.axes, axis=0, tiled=False)

    def start(self, x_ref, out_ref, send_sem, recv_sem, own_sem):
        me = flat_index(self.axes)
        part = x_ref if self.size is None else x_ref.at[pl.ds(self.first, self.size)]
        self.copies = [
            send(part, out_ref.at[me], send_sem.at[i - 1], recv_sem.at[i - 1], place)
            for i, _, place in flat_peers(self.axes)
        ]
        self.copies.append(keep(part, out_ref.at[me], own_sem.at[0]))

    def finish(self, *refs):
        for copy in self.copies:
            copy.wait()


class JoinCores(Rider):
    def __init__(self, source):
        self.source = source
        self.rows, self.width = source.shape
        shape = (self.rows, self.width * lax.axis_size("mp"))
        self.result = jax.ShapeDtypeStruct(shape, source.dtype)
        self.scratch = dma_sems(1, 1, 1)

    def peers(self):
        return twin_peers()

    def plain(self):
        return lax.all_gather(self.source, "mp", axis=1, tiled=True)

    def start(self, x_ref, out_ref, send_sem, recv_sem, own_sem):
        core = lax.axis_index("mp")
        mine = out_ref.at[:, pl.ds(pl.multiple_of(core * self.width, self.width), self.width)]
        self.copies = [
            send(x_ref, mine, send_sem.at[0], recv_sem.at[0], {"mp": 1 - core}),
            keep(x_ref, mine, own_sem.at[0]),
        ]

    def finish(self, *refs):
        for copy in self.copies:
            copy.wait()


class LineColumns(Rider):
    axes = ("space",)

    def __init__(self, source):
        self.source = source
        lines = lax.axis_size("space")
        self.width = source.shape[1] // lines
        shape = (lines, source.shape[0], self.width)
        self.result = jax.ShapeDtypeStruct(shape, source.dtype)
        self.scratch = dma_sems(lines - 1, lines - 1, 1)

    def plain(self):
        return lax.all_to_all(
            self.source[None], "space", split_axis=2, concat_axis=0, tiled=True
        )

    def start(self, x_ref, out_ref, send_sem, recv_sem, own_sem):
        me = lax.axis_index("space")

        def part(index):
            return x_ref.at[:, pl.ds(pl.multiple_of(index * self.width, self.width), self.width)]

        self.copies = [
            send(part(peer), out_ref.at[me], send_sem.at[i - 1], recv_sem.at[i - 1], {"space": peer})
            for i, peer in others("space")
        ]
        self.copies.append(keep(part(me), out_ref.at[me], own_sem.at[0]))

    def finish(self, *refs):
        for copy in self.copies:
            copy.wait()


class FrameSum(Rider):
    axes = ("tm",)
    result_spec = VMEM

    def __init__(self, source):
        self.count, self.rows, self.width = source.shape
        self.source = source
        self.result = jax.ShapeDtypeStruct((self.rows, self.width), jnp.bfloat16)
        self.scratch = [
            pltpu.VMEM((max(self.count - 1, 1), self.rows, self.width), jnp.bfloat16),
            pltpu.VMEM((self.rows, self.width), jnp.bfloat16),
        ] + dma_sems(self.count - 1, self.count - 1, 1)

    def plain(self):
        return lax.psum_scatter(self.source, "tm", scatter_dimension=0, tiled=True)[0]

    def start(self, w_ref, out_ref, got_ref, own_ref, send_sem, recv_sem, own_sem):
        me = lax.axis_index("tm")
        self.copies = [
            send(w_ref.at[peer], got_ref.at[i - 1], send_sem.at[i - 1], recv_sem.at[i - 1], {"tm": peer})
            for i, peer in others("tm")
        ]
        self.copies.append(keep(w_ref.at[me], own_ref, own_sem.at[0]))

    def finish(self, w_ref, out_ref, got_ref, own_ref, *sems):
        for copy in self.copies:
            copy.wait()
        block = min(16, self.rows)

        def some(index, carry):
            rows = pl.ds(pl.multiple_of(index * block, block), block)
            total = own_ref[rows, :].astype(jnp.float32)
            for step in range(self.count - 1):
                total = total + got_ref[step, rows, :].astype(jnp.float32)
            out_ref[rows, :] = total.astype(jnp.bfloat16)
            return carry

        lax.fori_loop(0, self.rows // block, some, 0)


class Keep(Rider):
    def __init__(self, source):
        self.source = source
        self.result = jax.ShapeDtypeStruct(source.shape, source.dtype)
        self.scratch = dma_sems(1)

    def peers(self):
        return []

    def plain(self):
        return self.source

    def start(self, x_ref, out_ref, own_sem):
        self.copy = keep(x_ref, out_ref, own_sem.at[0])

    def finish(self, *refs):
        self.copy.wait()


class TapSum(Rider):
    axes = ("tm",)
    result_spec = VMEM

    def __init__(self, source):
        self.taps, all_rows, self.width = source.shape
        self.count = lax.axis_size("tm")
        self.rows = all_rows // self.count
        self.source = source
        shape = (self.taps, self.rows, self.width)
        self.result = jax.ShapeDtypeStruct(shape, jnp.bfloat16)
        self.scratch = [
            pltpu.VMEM((max(self.count - 1, 1),) + shape, jnp.bfloat16),
            pltpu.VMEM(shape, jnp.bfloat16),
        ] + dma_sems(self.count - 1, self.count - 1, 1)

    def plain(self):
        return lax.psum_scatter(self.source, "tm", scatter_dimension=1, tiled=True)

    def start(self, w_ref, out_ref, got_ref, own_ref, send_sem, recv_sem, own_sem):
        me = lax.axis_index("tm")
        self.copies = [
            send(rows_of(w_ref, peer, self.rows), got_ref.at[i - 1], send_sem.at[i - 1], recv_sem.at[i - 1], {"tm": peer})
            for i, peer in others("tm")
        ]
        self.copies.append(keep(rows_of(w_ref, me, self.rows), own_ref, own_sem.at[0]))

    def finish(self, w_ref, out_ref, got_ref, own_ref, *sems):
        for copy in self.copies:
            copy.wait()

        def some(tap, carry):
            total = own_ref[tap].astype(jnp.float32)
            for step in range(self.count - 1):
                total = total + got_ref[step, tap].astype(jnp.float32)
            out_ref[tap] = total.astype(jnp.bfloat16)
            return carry

        lax.fori_loop(0, self.taps, some, 0)


def plain_all(riders):
    return [rider.plain() for rider in riders]


def talk_with(kernel, peers, result, operands, scratch, number, riders, specs=None, out_spec=ANY):
    specs = [ANY] * len(operands) if specs is None else specs
    inputs, own_scratch, count = len(operands), len(scratch), len(riders)

    def whole(*refs):
        ins, rider_ins = refs[:inputs], refs[inputs : inputs + count]
        out_ref = refs[inputs + count]
        rider_outs = refs[inputs + count + 1 : inputs + 2 * count + 1]
        rest = refs[inputs + 2 * count + 1 :]
        mine, rest = rest[:own_scratch], rest[own_scratch:]
        packs = []
        for rider, x_ref, y_ref in zip(riders, rider_ins, rider_outs):
            packs.append((x_ref, y_ref) + tuple(rest[: len(rider.scratch)]))
            rest = rest[len(rider.scratch) :]
        meet(peers() + [peer for rider in riders for peer in rider.peers()])
        for rider, pack in zip(riders, packs):
            rider.start(*pack)
        kernel(*ins, out_ref, *mine)
        for rider, pack in zip(riders, packs):
            rider.finish(*pack)

    results = talk(
        whole,
        (result,) + tuple(rider.result for rider in riders),
        operands + [rider.source for rider in riders],
        scratch + [item for rider in riders for item in rider.scratch],
        number,
        specs + [ANY] * count,
        (out_spec,) + tuple(rider.result_spec for rider in riders),
    )
    return results[0], list(results[1:])


def line_peers():
    return [{"space": peer} for _, peer in others("space")]


def frame_peers():
    return [{"tm": peer} for _, peer in others("tm")]


def twin_peers():
    return [{"mp": 1 - lax.axis_index("mp")}]


def to_lines(source, per_core, number, riders=(), join=False):
    images, pixels, channels = source.shape
    lines, cores = lax.axis_size("space"), lax.axis_size("mp")
    pieces = lines * cores if per_core or join else lines
    width = channels // pieces
    if width % lane != 0 or pixels % 16 != 0:
        if per_core:
            parts = source.reshape(images, pixels, lines, cores, width)
            parts = lax.dynamic_index_in_dim(parts, lax.axis_index("mp"), 3, keepdims=False)
            source = parts.reshape(images, pixels, lines * width)
        moved = lax.all_to_all(source, "space", split_axis=2, concat_axis=1, tiled=True)
        return moved, plain_all(riders)

    def kernel(x_ref, out_ref, send_sem, recv_sem, pass_sem, gain_sem, own_sem):
        me, core = lax.axis_index("space"), lax.axis_index("mp")
        twin = {"mp": 1 - core}
        place = (lambda s: s * cores + core) if per_core or join else (lambda s: s)

        def spot(origin):
            rows = rows_of(out_ref, origin, pixels)
            return cols_of(rows, core, width) if join else rows

        copies = [
            send(cols_of(x_ref, place(peer), width), spot(me), send_sem.at[i - 1], recv_sem.at[i - 1], {"space": peer})
            for i, peer in others("space")
        ]
        if join:
            own_width = cores * width
            own = keep(cols_of(x_ref, me, own_width), rows_of(out_ref, me, pixels), own_sem.at[0])
        else:
            own = keep(cols_of(x_ref, place(me), width), spot(me), own_sem.at[0])
        passed = []
        for step in range(1, lines):
            copies[step - 1].wait_recv()
            if join:
                got = spot(lax.rem(me - step + lines, lines))
                passed.append(send(got, got, pass_sem.at[step - 1], gain_sem.at[step - 1], twin))
        for copy in copies:
            copy.wait_send()
        own.wait()
        for copy in passed:
            copy.wait()

    def peers():
        return line_peers() + (twin_peers() if join else [])

    held = cores * width if join else width
    result = jax.ShapeDtypeStruct((images, lines * pixels, held), source.dtype)
    sems = dma_sems(lines - 1, lines - 1, lines - 1, lines - 1, 1)
    return talk_with(kernel, peers, result, [source], sems, number, riders)


def from_lines(source, per_core, number, riders=()):
    images, line_pixels, width = source.shape
    lines, cores = lax.axis_size("space"), lax.axis_size("mp")
    pixels = line_pixels // lines
    pieces = lines * cores if per_core else lines
    if width % lane != 0 or pixels % 16 != 0:
        part = lax.all_to_all(source, "space", split_axis=1, concat_axis=2, tiled=True)
        if per_core:
            part = part.reshape(images, pixels, lines, 1, width)
            part = lax.all_gather(part, "mp", axis=3, tiled=True)
        return part.reshape(images, pixels, pieces * width), plain_all(riders)

    def kernel(x_ref, out_ref, send_sem, recv_sem, pass_sem, gain_sem, own_sem):
        me, core = lax.axis_index("space"), lax.axis_index("mp")
        place = (lambda s: s * cores + core) if per_core else (lambda s: s)
        twin = {"mp": 1 - core}
        target = cols_of(out_ref, place(me), width)
        copies = [
            send(rows_of(x_ref, peer, pixels), target, send_sem.at[i - 1], recv_sem.at[i - 1], {"space": peer})
            for i, peer in others("space")
        ]
        own = keep(rows_of(x_ref, me, pixels), target, own_sem.at[0])
        passed = []
        if per_core:
            passed.append(send(rows_of(x_ref, me, pixels), target, pass_sem.at[0], gain_sem.at[0], twin))
        for step in range(1, lines):
            copies[step - 1].wait_recv()
            if per_core:
                origin = lax.rem(me - step + lines, lines)
                got = cols_of(out_ref, place(origin), width)
                passed.append(send(got, got, pass_sem.at[step], gain_sem.at[step], twin))
        for copy in copies:
            copy.wait_send()
        own.wait()
        for copy in passed:
            copy.wait()

    def peers():
        return line_peers() + ([{"mp": 1 - lax.axis_index("mp")}] if per_core else [])

    result = jax.ShapeDtypeStruct((images, pixels, pieces * width), source.dtype)
    sems = dma_sems(lines - 1, lines - 1, lines, lines, 1)
    return talk_with(kernel, peers, result, [source], sems, number, riders)


def gather_lines(source, number, riders=()):
    images, line_pixels, width = source.shape
    lines = lax.axis_size("space")
    if width % lane != 0:
        return lax.all_gather(source, "space", axis=2, tiled=True), plain_all(riders)

    def kernel(x_ref, out_ref, send_sem, recv_sem, own_sem):
        me = lax.axis_index("space")
        target = cols_of(out_ref, me, width)
        copies = [
            send(x_ref, target, send_sem.at[i - 1], recv_sem.at[i - 1], {"space": peer})
            for i, peer in others("space")
        ]
        copies.append(keep(x_ref, target, own_sem.at[0]))
        for copy in copies:
            copy.wait()

    result = jax.ShapeDtypeStruct((images, line_pixels, lines * width), source.dtype)
    sems = dma_sems(lines - 1, lines - 1, 1)
    return talk_with(kernel, line_peers, result, [source], sems, number, riders)


def gather_cores(source, number, riders=()):
    images, line_pixels, width = source.shape
    cores = lax.axis_size("mp")
    if width % lane != 0:
        return lax.all_gather(source, "mp", axis=2, tiled=True), plain_all(riders)

    def kernel(x_ref, out_ref, send_sem, recv_sem, own_sem):
        core = lax.axis_index("mp")
        twin = {"mp": 1 - core}
        target = cols_of(out_ref, core, width)
        copy = send(x_ref, target, send_sem.at[0], recv_sem.at[0], twin)
        own = keep(x_ref, target, own_sem.at[0])
        copy.wait()
        own.wait()

    result = jax.ShapeDtypeStruct((images, line_pixels, cores * width), source.dtype)
    return talk_with(kernel, twin_peers, result, [source], dma_sems(1, 1, 1), number, riders)


def sum_lines(source, number, riders=()):
    images, line_pixels, channels = source.shape
    lines = lax.axis_size("space")
    width = channels // lines
    if width % lane != 0:
        total = lax.psum_scatter(source, "space", scatter_dimension=2, tiled=True)
        return total.astype(jnp.float32), plain_all(riders)

    def kernel(x_ref, out_ref, got_ref, send_sem, recv_sem):
        me = lax.axis_index("space")
        copies = [
            send(cols_of(x_ref, peer, width), got_ref.at[i - 1], send_sem.at[i - 1], recv_sem.at[i - 1], {"space": peer})
            for i, peer in others("space")
        ]
        mine = pl.ds(pl.multiple_of(me * width, width), width)
        for copy in copies:
            copy.wait()
        for image in range(images):
            total = x_ref[image, :, mine].astype(jnp.float32)
            for step in range(lines - 1):
                total = total + got_ref[step, image].astype(jnp.float32)
            out_ref[image] = total

    result = jax.ShapeDtypeStruct((images, line_pixels, width), jnp.float32)
    scratch = [pltpu.VMEM((lines - 1, images, line_pixels, width), source.dtype)]
    scratch = scratch + dma_sems(lines - 1, lines - 1)
    return talk_with(
        kernel, line_peers, result, [source], scratch, number, riders, [VMEM], VMEM
    )


def sum_cores(source, number, riders=()):
    images, line_pixels, channels = source.shape
    cores = lax.axis_size("mp")
    width = channels // cores
    if width % lane != 0:
        total = lax.psum_scatter(source, "mp", scatter_dimension=2, tiled=True)
        return total.astype(jnp.float32), plain_all(riders)

    def kernel(x_ref, out_ref, got_ref, send_sem, recv_sem):
        core = lax.axis_index("mp")
        twin = {"mp": 1 - core}
        copy = send(cols_of(x_ref, 1 - core, width), got_ref, send_sem.at[0], recv_sem.at[0], twin)
        mine = pl.ds(pl.multiple_of(core * width, width), width)
        copy.wait()
        for image in range(images):
            out_ref[image] = x_ref[image, :, mine].astype(jnp.float32) + got_ref[image].astype(
                jnp.float32
            )

    result = jax.ShapeDtypeStruct((images, line_pixels, width), jnp.float32)
    scratch = [pltpu.VMEM((images, line_pixels, width), source.dtype)]
    scratch = scratch + dma_sems(1, 1)
    return talk_with(
        kernel, twin_peers, result, [source], scratch, number, riders, [VMEM], VMEM
    )


def gather_tokens(rows, number, riders=()):
    count, channels = rows.shape
    lines, cores = lax.axis_size("space"), lax.axis_size("mp")
    width = channels // cores
    source = rows.reshape(1, count, channels)

    def kernel(x_ref, out_ref, send_sem, recv_sem, pass_sem, gain_sem, own_sem):
        me, core = lax.axis_index("space"), lax.axis_index("mp")
        twin = {"mp": 1 - core}

        def spot(origin):
            return cols_of(rows_of(out_ref, origin, count), core, width)

        copies = [
            send(cols_of(x_ref, core, width), spot(me), send_sem.at[i - 1], recv_sem.at[i - 1], {"space": peer})
            for i, peer in others("space")
        ]
        own = keep(x_ref, rows_of(out_ref, me, count), own_sem.at[0])
        passed = []
        for step in range(1, lines):
            copies[step - 1].wait_recv()
            got = spot(lax.rem(me - step + lines, lines))
            passed.append(send(got, got, pass_sem.at[step - 1], gain_sem.at[step - 1], twin))
        for copy in copies:
            copy.wait_send()
        own.wait()
        for copy in passed:
            copy.wait()

    result = jax.ShapeDtypeStruct((1, lines * count, channels), rows.dtype)
    sems = dma_sems(lines - 1, lines - 1, lines - 1, lines - 1, 1)

    def peers():
        return line_peers() + twin_peers()

    line, others_done = talk_with(kernel, peers, result, [source], sems, number, riders)
    return line.reshape(lines * count, channels), others_done


def scatter_tokens(partial_sum, number, riders=()):
    all_rows, channels = partial_sum.shape
    lines, cores = lax.axis_size("space"), lax.axis_size("mp")
    count, width = all_rows // lines, channels // cores
    source = partial_sum.astype(jnp.bfloat16).reshape(lines, count, channels)

    def kernel(x_ref, out_ref, twin_ref, sum_ref, got_ref, s_sem, r_sem, s2_sem, r2_sem, s3_sem, r3_sem):
        me, core = lax.axis_index("space"), lax.axis_index("mp")
        twin = {"mp": 1 - core}
        theirs = pl.ds(pl.multiple_of((1 - core) * width, width), width)
        mine = pl.ds(pl.multiple_of(core * width, width), width)
        order = [(i, peer) for i, peer in others("space")] + [(0, me)]
        first = [
            send(x_ref.at[target, :, theirs], twin_ref.at[i], s_sem.at[i], r_sem.at[i], twin)
            for i, target in order
        ]
        second = []
        for (i, target), copy in zip(order, first):
            copy.wait_recv()
            total = x_ref[target, :, mine].astype(jnp.float32) + twin_ref[i].astype(jnp.float32)
            if i == 0:
                own = total
            else:
                sum_ref[i - 1] = total.astype(jnp.bfloat16)
                second.append(
                    send(sum_ref.at[i - 1], got_ref.at[i - 1], s2_sem.at[i - 1], r2_sem.at[i - 1], {"space": target})
                )
        for copy in second:
            copy.wait_recv()
        for i in range(lines - 1):
            own = own + got_ref[i].astype(jnp.float32)
        out_ref[:, mine] = own.astype(jnp.bfloat16)
        third = send(out_ref.at[:, mine], out_ref.at[:, mine], s3_sem.at[0], r3_sem.at[0], twin)
        for copy in first + second:
            copy.wait_send()
        third.wait()

    result = jax.ShapeDtypeStruct((count, channels), jnp.bfloat16)
    scratch = [
        pltpu.VMEM((lines, count, width), jnp.bfloat16),
        pltpu.VMEM((max(lines - 1, 1), count, width), jnp.bfloat16),
        pltpu.VMEM((max(lines - 1, 1), count, width), jnp.bfloat16),
    ]
    sems = dma_sems(lines, lines, lines - 1, lines - 1, 1, 1)

    def peers():
        return line_peers() + [{"mp": 1 - lax.axis_index("mp")}]

    total, other = talk_with(
        kernel, peers, result, [source], scratch + sems, number, riders, [VMEM], VMEM
    )
    return total, other


def to_clips(source, number, riders=()):
    slots, frames, pixels, channels = source.shape
    count = lax.axis_size("tm")
    few = pixels // count
    if few % 16 != 0:
        return lax.all_to_all(source, "tm", split_axis=2, concat_axis=1, tiled=True), plain_all(riders)

    def kernel(x_ref, out_ref, send_sem, recv_sem, own_sem):
        me = lax.axis_index("tm")
        target = out_ref.at[:, pl.ds(me * frames, frames)]

        def part(index):
            return x_ref.at[:, :, pl.ds(pl.multiple_of(index * few, few), few)]

        copies = [
            send(part(peer), target, send_sem.at[i - 1], recv_sem.at[i - 1], {"tm": peer})
            for i, peer in others("tm")
        ]
        copies.append(keep(part(me), target, own_sem.at[0]))
        for copy in copies:
            copy.wait()

    result = jax.ShapeDtypeStruct((slots, count * frames, few, channels), source.dtype)
    sems = dma_sems(count - 1, count - 1, 1)
    return talk_with(kernel, frame_peers, result, [source], sems, number, riders)


def from_clips(source, number, riders=()):
    slots, all_frames, few, channels = source.shape
    count = lax.axis_size("tm")
    frames = all_frames // count
    if few % 16 != 0:
        return lax.all_to_all(source, "tm", split_axis=1, concat_axis=2, tiled=True), plain_all(riders)

    def kernel(x_ref, out_ref, send_sem, recv_sem, own_sem):
        me = lax.axis_index("tm")
        target = out_ref.at[:, :, pl.ds(pl.multiple_of(me * few, few), few)]

        def part(index):
            return x_ref.at[:, pl.ds(index * frames, frames)]

        copies = [
            send(part(peer), target, send_sem.at[i - 1], recv_sem.at[i - 1], {"tm": peer})
            for i, peer in others("tm")
        ]
        copies.append(keep(part(me), target, own_sem.at[0]))
        for copy in copies:
            copy.wait()

    result = jax.ShapeDtypeStruct((slots, frames, count * few, channels), source.dtype)
    sems = dma_sems(count - 1, count - 1, 1)
    return talk_with(kernel, frame_peers, result, [source], sems, number, riders)


def by_owner_line(source, owners, lines):
    parts = source.reshape(source.shape[:-1] + (owners // lines, lines, -1))
    return parts.swapaxes(-3, -2).reshape(source.shape)


def by_frames(weight_grad):
    return FrameSum(weight_grad.reshape(lax.axis_size("tm"), -1, weight_grad.shape[1]))


def padded_rims(source):
    return jnp.pad(source, ((0, 0), (0, 0), (1, 1), (1, 1), (0, 0)))


def conv_weight(weight):
    return weight.reshape(weight.shape[0], 3, 3, weight.shape[2])


def conv_frames(source, weight, spec, flipped):
    images = source.reshape((-1,) + source.shape[2:])
    kernel = conv_weight(weight)
    if flipped:
        kernel = kernel[:, ::-1, ::-1]
    result = lax.conv_general_dilated(
        images,
        kernel,
        (1, 1),
        "SAME",
        dimension_numbers=("NHWC", spec, "NHWC"),
        preferred_element_type=jnp.float32,
    )
    return result.reshape(source.shape[:4] + (result.shape[-1],))


def conv_weight_grad(source, upstream, form):
    padded = padded_rims(source)
    rows, cols = source.shape[2], source.shape[3]
    tap_list = []
    for tap in range(9):
        i, j = tap // 3, tap % 3
        tap_list.append(
            jnp.einsum(
                "bfhwc,bfhwk->" + form,
                padded[:, :, i : i + rows, j : j + cols],
                upstream,
                preferred_element_type=jnp.float32,
            ).astype(jnp.bfloat16)
        )
    return jnp.stack(tap_list)


def sinusoid(steps_int):
    counted = D // 2
    freqs = jnp.exp(-math.log(10000.0) * jnp.arange(counted, dtype=jnp.float32) / counted)
    angles = steps_int.astype(jnp.float32)[..., None] * freqs
    return jnp.concatenate([jnp.sin(angles), jnp.cos(angles)], axis=-1)


def offset_onehot(query_start, query_count, key_count):
    distance = (
        query_start
        + jnp.arange(query_count, dtype=jnp.int32)[:, None]
        - jnp.arange(key_count, dtype=jnp.int32)[None, :]
    )
    position = jnp.clip(distance, -(R // 2), R // 2 - 1) + R // 2
    return (position[:, :, None] == jnp.arange(R, dtype=jnp.int32)[None, None, :]).astype(
        jnp.float32
    )


def local(kernel, results, operands, grid, in_specs, out_specs, scratch=()):
    return pl.pallas_call(
        kernel,
        out_shape=results,
        grid=grid,
        in_specs=in_specs,
        out_specs=out_specs,
        scratch_shapes=list(scratch),
        compiler_params=pltpu.CompilerParams(vmem_limit_bytes=48 * 1024 * 1024),
    )(*operands)


def dot(a, b):
    return jnp.dot(a, b, preferred_element_type=jnp.float32)


def dot_nt(a, b):
    return lax.dot_general(a, b, (((1,), (1,)), ((), ())), preferred_element_type=jnp.float32)


def dot_tn(a, b):
    return lax.dot_general(a, b, (((0,), (0,)), ((), ())), preferred_element_type=jnp.float32)


def low(value):
    return value.astype(jnp.bfloat16)


def head_probs(query, key, bias, valid):
    scores = dot_nt(query, key) * (1.0 / math.sqrt(HDIM))
    if bias is not None:
        scores = scores + bias
    if valid is not None:
        scores = jnp.where(valid, scores, masked)
    expos = jnp.exp(scores - jnp.max(scores, axis=-1, keepdims=True))
    return expos / jnp.sum(expos, axis=-1, keepdims=True)


def head_forward(query, key, value, bias, valid):
    return dot(low(head_probs(query, key, bias, valid)), value)


def head_backward(query, key, value, bias, valid, upstream):
    probs = head_probs(query, key, bias, valid)
    prob_grad = dot_nt(upstream, value)
    inner = jnp.sum(probs * prob_grad, axis=-1, keepdims=True)
    score_grad = low(probs * (prob_grad - inner))
    scale = 1.0 / math.sqrt(HDIM)
    return (
        dot(score_grad, key) * scale,
        dot_tn(score_grad, query) * scale,
        dot_tn(low(probs), upstream),
        score_grad,
    )


def norm_forward(source, gain):
    centered = source - jnp.mean(source, axis=-1, keepdims=True)
    variance = jnp.mean(centered * centered, axis=-1, keepdims=True)
    return centered * lax.rsqrt(variance + epsilon) * gain


def norm_backward(source, gain, upstream):
    centered = source - jnp.mean(source, axis=-1, keepdims=True)
    variance = jnp.mean(centered * centered, axis=-1, keepdims=True)
    inverse = lax.rsqrt(variance + epsilon)
    normal = centered * inverse
    gain_grad = jnp.sum(upstream * normal, axis=0, keepdims=True)
    scaled = upstream * gain
    first = jnp.mean(scaled, axis=-1, keepdims=True)
    second = jnp.mean(scaled * normal, axis=-1, keepdims=True)
    return inverse * (scaled - first - normal * second), gain_grad


def in_weight(halves, index):
    per = halves[0].shape[0] // 4
    return jnp.concatenate(
        [
            jnp.concatenate([half[t, s] for half in halves for s in range(half.shape[1])], axis=0)
            for t in range(index * per, (index + 1) * per)
        ],
        axis=1,
    )


def out_weight(halves, index):
    frames, width = halves[0].shape[0], halves[0].shape[3] // 3
    cols = slice(index * width, (index + 1) * width)
    return jnp.concatenate(
        [
            jnp.concatenate([half[t, s, :, cols] for t in range(frames)], axis=0)
            for half in halves
            for s in range(half.shape[1])
        ],
        axis=1,
    )


def spatial_forward(rows, weight):
    lines, images, pixels, channels = rows.shape
    width = weight.shape[2]
    count = lines * pixels

    def kernel(x_ref, w_ref, triple_ref, mix_ref):
        x = x_ref[...].reshape(count, channels)
        for j in range(3):
            triple_ref[0, j] = low(dot(x, w_ref[j]))
        for head in range(width // HDIM):
            cols = slice(head * HDIM, (head + 1) * HDIM)
            query, key, value = (triple_ref[0, j, :, cols] for j in range(3))
            mix_ref[0, :, cols] = low(head_forward(query, key, value, None, None))

    return local(
        kernel,
        (
            jax.ShapeDtypeStruct((images, 3, count, width), jnp.bfloat16),
            jax.ShapeDtypeStruct((images, count, width), jnp.bfloat16),
        ),
        (rows, weight),
        (images,),
        [
            pl.BlockSpec((lines, 1, pixels, channels), lambda i: (0, i, 0, 0)),
            pl.BlockSpec(weight.shape, lambda i: (0, 0, 0)),
        ],
        (
            pl.BlockSpec((1, 3, count, width), lambda i: (i, 0, 0, 0)),
            pl.BlockSpec((1, count, width), lambda i: (i, 0, 0)),
        ),
    )


def spatial_backward(rows, weight, triple, upstream):
    lines, images, pixels, channels = rows.shape
    width = weight.shape[2]
    count = lines * pixels

    def kernel(x_ref, w_ref, triple_ref, up_ref, grad_ref, dw_ref, grads_ref, total_ref):
        step = pl.program_id(0)
        x = x_ref[...].reshape(count, channels)
        for head in range(width // HDIM):
            cols = slice(head * HDIM, (head + 1) * HDIM)
            query, key, value = (triple_ref[0, j, :, cols] for j in range(3))
            grads = head_backward(query, key, value, None, None, up_ref[0, :, cols])
            for j in range(3):
                grads_ref[j, :, cols] = low(grads[j])
        part = dot_nt(grads_ref[0], w_ref[0])
        part = part + dot_nt(grads_ref[1], w_ref[1])
        part = part + dot_nt(grads_ref[2], w_ref[2])
        grad_ref[...] = low(part).reshape(lines, 1, pixels, channels)

        @pl.when(step == 0)
        def _():
            total_ref[...] = jnp.zeros_like(total_ref)

        for j in range(3):
            total_ref[j] += dot_tn(x, grads_ref[j])

        @pl.when(step == images - 1)
        def _():
            for j in range(3):
                dw_ref[:, j * width : (j + 1) * width] = low(total_ref[j])

    return local(
        kernel,
        (
            jax.ShapeDtypeStruct((lines, images, pixels, channels), jnp.bfloat16),
            jax.ShapeDtypeStruct((channels, 3 * width), jnp.bfloat16),
        ),
        (rows, weight, triple, upstream),
        (images,),
        [
            pl.BlockSpec((lines, 1, pixels, channels), lambda i: (0, i, 0, 0)),
            pl.BlockSpec(weight.shape, lambda i: (0, 0, 0)),
            pl.BlockSpec((1, 3, count, width), lambda i: (i, 0, 0, 0)),
            pl.BlockSpec((1, count, width), lambda i: (i, 0, 0)),
        ],
        (
            pl.BlockSpec((lines, 1, pixels, channels), lambda i: (0, i, 0, 0)),
            pl.BlockSpec((channels, 3 * width), lambda i: (0, 0)),
        ),
        [
            pltpu.VMEM((3, count, width), jnp.bfloat16),
            pltpu.VMEM((3, channels, width), jnp.float32),
        ],
    )


def dot_exact(a, b):
    return jnp.dot(a, b, preferred_element_type=jnp.float32, precision=highest)


def clip_masks(rows, few, ids_ref, turned_ref):
    across = lax.broadcasted_iota(jnp.int32, (rows, rows), 1)
    down = lax.broadcasted_iota(jnp.int32, (rows, rows), 0)
    return (lax.rem(across, few) == lax.rem(down, few)) & (ids_ref[0] == turned_ref[0])


def temporal_forward(clip, bias, ids, few):
    slots, rows, triple = clip.shape
    width = triple // 3

    def kernel(x_ref, bias_ref, ids_ref, turned_ref, mix_ref):
        valid = clip_masks(rows, few, ids_ref, turned_ref)
        for head in range(width // HDIM):
            at = head * HDIM
            query, key, value = (
                x_ref[0, :, j * width + at : j * width + at + HDIM] for j in range(3)
            )
            mix = head_forward(query, key, value, bias_ref[head], valid)
            mix_ref[0, :, at : at + HDIM] = low(mix)

    return local(
        kernel,
        jax.ShapeDtypeStruct((slots, rows, width), jnp.bfloat16),
        (clip, bias, ids[:, :, None], ids[:, None, :]),
        (slots,),
        [
            pl.BlockSpec((1, rows, triple), lambda i: (i, 0, 0)),
            pl.BlockSpec(bias.shape, lambda i: (0, 0, 0)),
            pl.BlockSpec((1, rows, 1), lambda i: (i, 0, 0)),
            pl.BlockSpec((1, 1, rows), lambda i: (i, 0, 0)),
        ],
        pl.BlockSpec((1, rows, width), lambda i: (i, 0, 0)),
    )


def temporal_backward(clip, bias, ids, few, upstream):
    slots, rows, triple = clip.shape
    width = triple // 3
    frames = rows // few

    def kernel(x_ref, bias_ref, ids_ref, turned_ref, up_ref, grad_ref, score_ref):
        step = pl.program_id(0)
        valid = clip_masks(rows, few, ids_ref, turned_ref)
        frame = lax.broadcasted_iota(jnp.int32, (frames, rows), 0)
        row = lax.broadcasted_iota(jnp.int32, (frames, rows), 1)
        gather = low((row // few == frame).astype(jnp.float32))

        @pl.when(step == 0)
        def _():
            score_ref[...] = jnp.zeros_like(score_ref)

        for head in range(width // HDIM):
            at = head * HDIM
            query, key, value = (
                x_ref[0, :, j * width + at : j * width + at + HDIM] for j in range(3)
            )
            grads = head_backward(
                query, key, value, bias_ref[head], valid, up_ref[0, :, at : at + HDIM]
            )
            for j in range(3):
                grad_ref[0, :, j * width + at : j * width + at + HDIM] = low(grads[j])
            score_ref[head] += dot(gather, grads[3])

    return local(
        kernel,
        (
            jax.ShapeDtypeStruct((slots, rows, triple), jnp.bfloat16),
            jax.ShapeDtypeStruct((bias.shape[0], frames, rows), jnp.float32),
        ),
        (clip, bias, ids[:, :, None], ids[:, None, :], upstream),
        (slots,),
        [
            pl.BlockSpec((1, rows, triple), lambda i: (i, 0, 0)),
            pl.BlockSpec(bias.shape, lambda i: (0, 0, 0)),
            pl.BlockSpec((1, rows, 1), lambda i: (i, 0, 0)),
            pl.BlockSpec((1, 1, rows), lambda i: (i, 0, 0)),
            pl.BlockSpec((1, rows, width), lambda i: (i, 0, 0)),
        ],
        (
            pl.BlockSpec((1, rows, triple), lambda i: (i, 0, 0)),
            pl.BlockSpec((bias.shape[0], frames, rows), lambda i: (0, 0, 0)),
        ),
    )


def gelu_pair(upper):
    rate = math.sqrt(2.0 / math.pi)
    square = upper * upper
    bend = jnp.tanh(rate * (upper + 0.044715 * square * upper))
    half = 0.5 * (1.0 + bend)
    slope = half + 0.5 * upper * (1.0 - bend * bend) * rate * (1.0 + 3.0 * 0.044715 * square)
    return upper * half, slope


def feed_both(rows, cot, w_in, w_out):
    lines, count, channels = rows.shape
    hidden = w_in.shape[1]

    def kernel(x_ref, cot_ref, in_ref, out_ref, y_ref, grad_ref, dw_ref, first_ref, second_ref):
        step = pl.program_id(0)
        x, up = x_ref[0], cot_ref[0]
        active, slope = gelu_pair(dot(x, in_ref[...]))
        active = low(active)
        upper_grad = low(dot_nt(up, out_ref[...]) * slope)
        y_ref[0] = low(dot(active, out_ref[...]))
        grad_ref[0] = low(dot_nt(upper_grad, in_ref[...]))

        @pl.when(step == 0)
        def _():
            first_ref[...] = dot_tn(x, upper_grad)
            second_ref[...] = dot_tn(up, active)

        @pl.when(step > 0)
        def _():
            first_ref[...] += dot_tn(x, upper_grad)
            second_ref[...] += dot_tn(up, active)

        @pl.when(step == lines - 1)
        def _():
            dw_ref[:, :hidden] = low(first_ref[...])
            dw_ref[:, hidden:] = low(second_ref[...])

    block = pl.BlockSpec((1, count, channels), lambda i: (i, 0, 0))
    return local(
        kernel,
        (
            jax.ShapeDtypeStruct(rows.shape, jnp.bfloat16),
            jax.ShapeDtypeStruct(rows.shape, jnp.bfloat16),
            jax.ShapeDtypeStruct((channels, 2 * hidden), jnp.bfloat16),
        ),
        (rows, cot, w_in, w_out),
        (lines,),
        [
            block,
            block,
            pl.BlockSpec(w_in.shape, lambda i: (0, 0)),
            pl.BlockSpec(w_out.shape, lambda i: (0, 0)),
        ],
        (block, block, pl.BlockSpec((channels, 2 * hidden), lambda i: (0, 0))),
        [
            pltpu.VMEM((channels, hidden), jnp.float32),
            pltpu.VMEM((channels, hidden), jnp.float32),
        ],
    )


def twin_sum(partial_sum, mine_ref, theirs_ref, send_sem, recv_sem, work=None):
    mine_ref[...] = low(partial_sum)
    copy = send(mine_ref, theirs_ref, send_sem, recv_sem, {"mp": 1 - lax.axis_index("mp")})
    if work is not None:
        work()
    copy.wait()
    return mine_ref[...].astype(jnp.float32) + theirs_ref[...].astype(jnp.float32)


def chat(kernel, results, operands, rows, channels, swaps, number, scratch=()):
    own = [
        pltpu.VMEM((swaps, rows, channels), jnp.bfloat16),
        pltpu.VMEM((swaps, rows, channels), jnp.bfloat16),
    ] + dma_sems(swaps, swaps)
    count = len(operands) + len(results)

    def whole(*refs):
        mine_ref, theirs_ref, send_sem, recv_sem = refs[count : count + 4]
        meet(twin_peers())

        def swap(index, partial_sum, work=None):
            return twin_sum(
                partial_sum,
                mine_ref.at[index],
                theirs_ref.at[index],
                send_sem.at[index],
                recv_sem.at[index],
                work,
            )

        kernel(swap, *refs[:count], *refs[count + 4 :])

    return talk(
        whole,
        tuple(results),
        operands,
        own + list(scratch),
        number,
        [VMEM] * len(operands),
        tuple([VMEM] * len(results)),
    )


def group_means(totals, count):
    channels = totals.shape[1]
    down = lax.broadcasted_iota(jnp.int32, (channels, channels), 0)
    across = lax.broadcasted_iota(jnp.int32, (channels, channels), 1)
    size = D // G
    same = (down // size == across // size).astype(jnp.float32)
    return dot_exact(totals, same) * (1.0 / (count * size))


def group_normal(source):
    count = source.shape[0]
    centered = source - group_means(jnp.sum(source, axis=0, keepdims=True), count)
    spread = group_means(jnp.sum(centered * centered, axis=0, keepdims=True), count)
    inverse = lax.rsqrt(spread + epsilon)
    return centered * inverse, inverse


def group_step(upstream, normal, inverse):
    count = upstream.shape[0]
    first = group_means(jnp.sum(upstream, axis=0, keepdims=True), count)
    second = group_means(jnp.sum(upstream * normal, axis=0, keepdims=True), count)
    return inverse * (upstream - first - normal * second)


def silu(value):
    return value * jax.nn.sigmoid(value)


def silu_slope(value):
    gate = jax.nn.sigmoid(value)
    return gate * (1.0 + value * (1.0 - gate))


def image_block(shape):
    return pl.BlockSpec((1,) + shape[1:], lambda i: (i, 0, 0))


def group_forward(source, scale, shift):
    def kernel(x_ref, scale_ref, shift_ref, out_ref):
        normal, _ = group_normal(x_ref[0].astype(jnp.float32))
        out_ref[0] = low(silu(normal * scale_ref[0] + shift_ref[0]))

    return local(
        kernel,
        jax.ShapeDtypeStruct(source.shape, jnp.bfloat16),
        (source, scale, shift),
        (source.shape[0],),
        [image_block(source.shape), image_block(scale.shape), image_block(shift.shape)],
        image_block(source.shape),
    )


def group_backward(source, scale, shift, upstream):
    def kernel(x_ref, scale_ref, shift_ref, up_ref, grad_ref, scale_grad_ref, shift_grad_ref):
        normal, inverse = group_normal(x_ref[0].astype(jnp.float32))
        grad = up_ref[0] * silu_slope(normal * scale_ref[0] + shift_ref[0])
        scale_grad_ref[0] = jnp.sum(grad * normal, axis=0, keepdims=True)
        shift_grad_ref[0] = jnp.sum(grad, axis=0, keepdims=True)
        grad_ref[0] = low(group_step(grad * scale_ref[0], normal, inverse))

    return local(
        kernel,
        (
            jax.ShapeDtypeStruct(source.shape, jnp.bfloat16),
            jax.ShapeDtypeStruct(scale.shape, jnp.float32),
            jax.ShapeDtypeStruct(shift.shape, jnp.float32),
        ),
        (source, scale, shift, upstream),
        (source.shape[0],),
        [
            image_block(source.shape),
            image_block(scale.shape),
            image_block(shift.shape),
            image_block(upstream.shape),
        ],
        (image_block(source.shape), image_block(scale.shape), image_block(shift.shape)),
    )


def flat_call(kernel, results, operands):
    return pl.pallas_call(
        kernel,
        out_shape=tuple(results),
        in_specs=[VMEM] * len(operands),
        out_specs=tuple([VMEM] * len(results)),
        compiler_params=pltpu.CompilerParams(vmem_limit_bytes=48 * 1024 * 1024),
    )(*operands)


def store_both(both_ref, value, owners, lines):
    both_ref[0] = value
    if (value.shape[1] // owners) % HDIM != 0:
        return
    size = value.shape[1] // owners
    frames = owners // lines
    both_ref[1] = jnp.concatenate(
        [
            value[:, (t * lines + s) * size : (t * lines + s + 1) * size]
            for s in range(lines)
            for t in range(frames)
        ],
        axis=1,
    )


def both_orders(rows, owners, lines):
    if (rows.shape[1] // owners) % HDIM != 0:
        return jnp.stack([rows, by_owner_line(rows, owners, lines)])

    def kernel(x_ref, both_ref):
        store_both(both_ref, x_ref[...], owners, lines)

    return flat_call(kernel, [jax.ShapeDtypeStruct((2,) + rows.shape, rows.dtype)], [rows])[0]


def first_norm(rows, branch, gain):
    def kernel(x_ref, branch_ref, gain_ref, one_ref, normed_ref):
        one = x_ref[...].astype(jnp.float32) + branch_ref[...].astype(jnp.float32)
        one_ref[...] = one
        normed_ref[...] = low(norm_forward(one, gain_ref[...]))

    return flat_call(
        kernel,
        [
            jax.ShapeDtypeStruct(rows.shape, jnp.float32),
            jax.ShapeDtypeStruct(rows.shape, jnp.bfloat16),
        ],
        [rows, branch, gain],
    )


def first_norm_backward(stream, gain, normed_grad, upstream, owners, lines):
    def kernel(x_ref, gain_ref, normed_ref, up_ref, grad_ref, both_ref, dg_ref):
        step, gain_grad = norm_backward(
            x_ref[...], gain_ref[...], normed_ref[...].astype(jnp.float32)
        )
        grad = up_ref[...] + step
        grad_ref[...] = grad
        dg_ref[...] = gain_grad
        store_both(both_ref, low(grad), owners, lines)

    grad, both, gain_grad = flat_call(
        kernel,
        [
            jax.ShapeDtypeStruct(stream.shape, jnp.float32),
            jax.ShapeDtypeStruct((2,) + stream.shape, jnp.bfloat16),
            jax.ShapeDtypeStruct(gain.shape, jnp.float32),
        ],
        [stream, gain, normed_grad, upstream],
    )
    if (stream.shape[1] // owners) % HDIM != 0:
        both = jnp.stack([both[0], by_owner_line(both[0], owners, lines)])
    return grad, both, gain_grad


def middle_forward(mix, stream, out_halves, in_halves, pairs, valid, gains, number):
    rows, channels = stream.shape
    width = mix.shape[1]
    slots = pairs.shape[0]
    part = rows // slots

    def kernel(
        swap, mix_ref, x_ref, out_ref, out_rest, in_ref, in_rest, pairs_ref, valid_ref, gain_ref,
        two_ref, normed_ref, query_ref, cross_ref, three_ref, last_ref, triple_ref,
    ):
        outs, ins = (out_ref, out_rest), (in_ref, in_rest)
        two = x_ref[...] + swap(0, dot(mix_ref[...], out_weight(outs, 0)))
        two_ref[...] = two
        normed_ref[...] = low(norm_forward(two, gain_ref[0:1, :]))
        query_ref[...] = low(dot(normed_ref[...], in_weight(ins, 0)))
        for slot in range(slots):
            here = slice(slot * part, (slot + 1) * part)
            good = valid_ref[slot] > 0.5
            for head in range(width // HDIM):
                at = head * HDIM
                cross = head_forward(
                    query_ref[here, at : at + HDIM],
                    pairs_ref[slot, :, at : at + HDIM],
                    pairs_ref[slot, :, width + at : width + at + HDIM],
                    None,
                    good,
                )
                cross_ref[here, at : at + HDIM] = low(cross)
        three = two_ref[...] + swap(1, dot(cross_ref[...], out_weight(outs, 1)))
        three_ref[...] = three
        last_ref[...] = low(norm_forward(three, gain_ref[1:2, :]))
        for j in range(3):
            triple_ref[:, j * width : (j + 1) * width] = low(dot(last_ref[...], in_weight(ins, 1 + j)))

    wide = jax.ShapeDtypeStruct((rows, channels), jnp.float32)
    wide_low = jax.ShapeDtypeStruct((rows, channels), jnp.bfloat16)
    thin = jax.ShapeDtypeStruct((rows, width), jnp.bfloat16)
    return chat(
        kernel,
        [wide, wide_low, thin, thin, wide, wide_low, jax.ShapeDtypeStruct((rows, 3 * width), jnp.bfloat16)],
        [mix, stream, *out_halves, *in_halves, pairs, valid, gains],
        rows,
        channels,
        2,
        number,
    )


def late_forward(mix, stream, out_halves, gain, number):
    rows, channels = stream.shape

    def kernel(swap, mix_ref, x_ref, out_ref, out_rest, gain_ref, four_ref, normed_ref):
        four = x_ref[...] + swap(0, dot(mix_ref[...], out_weight((out_ref, out_rest), 2)))
        four_ref[...] = four
        normed_ref[...] = low(norm_forward(four, gain_ref[...]))

    return chat(
        kernel,
        [
            jax.ShapeDtypeStruct((rows, channels), jnp.float32),
            jax.ShapeDtypeStruct((rows, channels), jnp.bfloat16),
        ],
        [mix, stream, *out_halves, gain],
        rows,
        channels,
        1,
        number,
    )


def late_backward(cot, normed_grad, stream, gain, mix, out_halves):
    rows, channels = stream.shape
    width = mix.shape[1]

    def kernel(
        cot_ref, up_ref, x_ref, gain_ref, mix_ref, out_ref, out_rest, grad_ref, mix_grad_ref, dw_ref, dg_ref
    ):
        step, gain_grad = norm_backward(
            x_ref[...], gain_ref[...], up_ref[...].astype(jnp.float32)
        )
        grad = cot_ref[...].astype(jnp.float32) + step
        grad_ref[...] = grad
        dg_ref[...] = gain_grad
        branch = low(grad)
        mix_grad_ref[...] = low(dot_nt(branch, out_weight((out_ref, out_rest), 2)))
        dw_ref[...] = low(dot_tn(branch, mix_ref[...]))

    return pl.pallas_call(
        kernel,
        out_shape=(
            jax.ShapeDtypeStruct((rows, channels), jnp.float32),
            jax.ShapeDtypeStruct((rows, width), jnp.bfloat16),
            jax.ShapeDtypeStruct((channels, width), jnp.bfloat16),
            jax.ShapeDtypeStruct((1, channels), jnp.float32),
        ),
        in_specs=[VMEM] * 7,
        out_specs=tuple([VMEM] * 4),
        compiler_params=pltpu.CompilerParams(vmem_limit_bytes=48 * 1024 * 1024),
    )(cot, normed_grad, stream, gain, mix, *out_halves)


def middle_backward(
    triple, upstream, three, two, last, normed, query, cross, mix, out_halves, in_halves, pairs, valid, gains, number
):
    rows, channels = three.shape
    width = mix.shape[1]
    slots, keys = pairs.shape[0], pairs.shape[1]
    part = rows // slots

    def kernel(
        swap, triple_ref, up_ref, three_ref, two_ref, last_ref, normed_ref, query_ref, cross_ref, mix_ref,
        out_ref, out_rest, in_ref, in_rest, pairs_ref, valid_ref, gain_ref,
        grad_ref, mix_grad_ref, pair_grad_ref, query_dw_ref, pair_dw_ref, cross_dw_ref, outs_dw_ref, dg_ref,
        cross_up_ref, dq_ref,
    ):
        outs, ins = (out_ref, out_rest), (in_ref, in_rest)

        def temporal_weights():
            query_dw_ref[...] = low(dot_tn(last_ref[...], triple_ref[:, :width]))
            pair_dw_ref[...] = low(dot_tn(last_ref[...], triple_ref[:, width:]))

        part_sum = dot_nt(triple_ref[:, :width], in_weight(ins, 1))
        part_sum = part_sum + dot_nt(triple_ref[:, width : 2 * width], in_weight(ins, 2))
        part_sum = part_sum + dot_nt(triple_ref[:, 2 * width :], in_weight(ins, 3))
        normed_grad = swap(0, part_sum, temporal_weights)
        step, gain_grad = norm_backward(three_ref[...], gain_ref[1:2, :], normed_grad)
        dg_ref[1:2, :] = gain_grad
        grad = up_ref[...] + step
        grad_ref[...] = grad
        branch = low(grad)
        cross_up_ref[...] = low(dot_nt(branch, out_weight(outs, 1)))
        for slot in range(slots):
            here = slice(slot * part, (slot + 1) * part)
            good = valid_ref[slot] > 0.5
            for head in range(width // HDIM):
                at = head * HDIM
                grads = head_backward(
                    query_ref[here, at : at + HDIM],
                    pairs_ref[slot, :, at : at + HDIM],
                    pairs_ref[slot, :, width + at : width + at + HDIM],
                    None,
                    good,
                    cross_up_ref[here, at : at + HDIM],
                )
                dq_ref[here, at : at + HDIM] = low(grads[0])
                pair_grad_ref[slot, :, at : at + HDIM] = low(grads[1])
                pair_grad_ref[slot, :, width + at : width + at + HDIM] = low(grads[2])

        def cross_weights():
            cross_dw_ref[...] = low(dot_tn(normed_ref[...], dq_ref[...]))
            outs_dw_ref[:, :width] = low(dot_tn(low(grad_ref[...]), cross_ref[...]))

        normed_grad = swap(1, dot_nt(dq_ref[...], in_weight(ins, 0)), cross_weights)
        step, gain_grad = norm_backward(two_ref[...], gain_ref[0:1, :], normed_grad)
        dg_ref[0:1, :] = gain_grad
        grad = grad_ref[...] + step
        grad_ref[...] = grad
        branch = low(grad)
        mix_grad_ref[...] = low(dot_nt(branch, out_weight(outs, 0)))
        outs_dw_ref[:, width:] = low(dot_tn(branch, mix_ref[...]))

    return chat(
        kernel,
        [
            jax.ShapeDtypeStruct((rows, channels), jnp.float32),
            jax.ShapeDtypeStruct((rows, width), jnp.bfloat16),
            jax.ShapeDtypeStruct((slots, keys, 2 * width), jnp.bfloat16),
            jax.ShapeDtypeStruct((channels, width), jnp.bfloat16),
            jax.ShapeDtypeStruct((channels, 2 * width), jnp.bfloat16),
            jax.ShapeDtypeStruct((channels, width), jnp.bfloat16),
            jax.ShapeDtypeStruct((channels, 2 * width), jnp.bfloat16),
            jax.ShapeDtypeStruct((2, channels), jnp.float32),
        ],
        [triple, upstream, three, two, last, normed, query, cross, mix, *out_halves, *in_halves, pairs, valid, gains],
        rows,
        channels,
        2,
        number,
        [pltpu.VMEM((rows, width), jnp.bfloat16), pltpu.VMEM((rows, width), jnp.bfloat16)],
    )


def on_device(
    video,
    cotangent,
    text,
    video_ids,
    timesteps,
    text_lengths,
    group_gain,
    group_bias,
    first_conv,
    film_weight,
    second_conv,
    spatial_norm,
    spatial_qkv,
    spatial_out,
    cross_norm,
    cross_query,
    cross_kv,
    cross_out,
    temporal_norm,
    temporal_qkv,
    temporal_out,
    offset_bias,
    feed_norm,
    feed_in,
    feed_out,
):
    frames_axis, lines, cores = (lax.axis_size(name) for name in ("tm", "space", "mp"))
    slots, frame_dev, row_dev, columns, channels = video.shape
    half_width = first_conv.shape[2]
    head_local = half_width // HDIM
    pixels_dev = row_dev * columns
    frames_all = frame_dev * frames_axis
    token_rows = slots * frame_dev * pixels_dev
    text_local = text.shape[1]
    images = slots * frame_dev
    frame_shape = (-1, frame_dev, H, W)
    everyone = ("tm", "space")
    owners = frames_axis * lines
    line_half = lines // 2
    feed_width = feed_in.shape[1] // lines
    text_rows = slots * text_local

    def wide(source):
        return source.reshape(frame_shape + source.shape[2:])

    out_piece = part_of(jnp.concatenate([spatial_out, cross_out, temporal_out], axis=1), "tm", 0)
    if frames_axis == 4:
        in_piece = jnp.concatenate([cross_query[None], temporal_qkv.transpose(1, 0, 2)], axis=0)
        in_piece = lax.dynamic_index_in_dim(in_piece, lax.axis_index("tm"), 0, keepdims=False)
    else:
        in_piece = jnp.concatenate([cross_query, temporal_qkv.reshape(-1, 3 * half_width)], axis=1)
        in_piece = part_of(in_piece, "tm", 1)
    qkv_piece = part_of(spatial_qkv.transpose(1, 0, 2), "tm", 1)
    qkv_piece = qkv_piece.reshape(3, -1, lines, half_width // lines).transpose(2, 0, 1, 3)
    in_quarter = part_of(feed_in, "tm", 0)
    in_quarter = in_quarter.reshape(-1, lines, feed_width).transpose(1, 0, 2)
    out_quarter = part_of(feed_out.reshape(lines, feed_width, -1), "tm", 1)
    cot_rows = cotangent.reshape(token_rows, channels)
    text_flat = text.reshape(text_rows, -1)
    cross_kv = cross_kv.reshape(cross_kv.shape[0], -1)

    video_rows = video.reshape(token_rows, channels)
    in_groups = (channels // owners) % (D // G) == 0
    video_both = both_orders(video_rows, owners, lines) if in_groups else video_rows
    video_lines, (text_line, qkv_piece, out_piece) = to_lines(
        video_both.reshape(-1, pixels_dev, channels),
        True,
        1,
        [
            LineColumns(text_flat),
            Exchange(qkv_piece, ("space",)),
            Share(out_piece, ("space",)),
        ],
    )

    def line_gains(whole):
        own = part_of(part_of(whole, "space", 0), "mp", 0)
        if not in_groups:
            return jnp.broadcast_to(own, (images, 1, own.shape[0]))
        owned = part_of(part_of(by_owner_line(whole, owners, lines), "space", 0), "mp", 0)
        return jnp.repeat(jnp.stack([own, owned]), images, axis=0)[:, None]

    gain_line, bias_line = line_gains(group_gain), line_gains(group_bias)
    first_in = group_forward(video_lines, gain_line, bias_line)
    text_part = jnp.dot(
        text_line.reshape(lines * text_rows, -1), cross_kv, preferred_element_type=jnp.float32
    )
    text_part = text_part.astype(jnp.bfloat16).reshape(lines, text_rows, -1)
    first_in, (text_part, in_piece) = gather_cores(
        first_in, 3, [Exchange(text_part, ("space",)), Share(in_piece, ("space",))]
    )
    if in_groups:
        first_in, first_owned = first_in[:images], first_in[images:]
    else:
        blocks = first_in.reshape(first_in.shape[:2] + (-1, lines, channels // owners))
        blocks = blocks.swapaxes(2, 3).reshape(first_in.shape)
        first_owned = lax.all_to_all(blocks, "space", split_axis=2, concat_axis=2, tiled=True)
    text_part = jnp.sum(text_part.astype(jnp.float32), axis=0).astype(jnp.bfloat16)
    hidden_part = conv_frames(wide(first_in), first_conv, "IHWO", False).astype(jnp.bfloat16)
    hidden, (out_first, text_part) = sum_lines(
        hidden_part.reshape(images, H * W, half_width),
        4,
        [Share(out_piece, ("tm",), 0, line_half), Share(text_part, ("space",))],
    )

    embed = sinusoid(timesteps).astype(jnp.bfloat16)
    film_part = jnp.einsum(
        "bvc,cjk->bvjk", part_of(embed, "space", 2), film_weight, preferred_element_type=jnp.float32
    )
    film = lax.psum_scatter(film_part, "space", scatter_dimension=3, tiled=True)
    frame_ids = part_of(video_ids, "tm", 1)
    choose = (frame_ids[:, :, None] == jnp.arange(VIDS, dtype=jnp.int32)[None, None, :]).astype(
        jnp.float32
    )
    frame_film = jnp.einsum("bfv,bvjk->jbfk", choose, film, precision=highest)
    frame_film = frame_film.reshape(2, images, 1, -1)
    film_scale, film_shift = 1.0 + frame_film[0], frame_film[1]
    second_in = group_forward(hidden, film_scale, film_shift)
    second_wide, (text_pairs, in_first) = gather_lines(
        second_in, 5, [Share(text_part, ("tm",)), Share(in_piece, ("tm",), 0, line_half)]
    )
    text_pairs = (
        text_pairs.reshape(owners, slots, text_local, 2 * half_width)
        .transpose(1, 0, 2, 3)
        .reshape(slots, TXT, 2 * half_width)
    )
    conv_part = conv_frames(wide(second_wide), second_conv, "IHWO", False).astype(jnp.bfloat16)
    conv_half, _ = sum_cores(conv_part.reshape(images, H * W, -1), 6)
    text_cols = text_flat.reshape(text_rows, owners, -1).transpose(1, 0, 2)
    conv_rows, (text_cols, qkv_piece) = from_lines(
        conv_half.astype(jnp.bfloat16),
        True,
        7,
        [Exchange(text_cols, everyone), Share(qkv_piece, ("tm",))],
    )
    spatial_qkv = qkv_piece.transpose(2, 1, 0, 3, 4).reshape(3, channels, -1)

    spatial_gain = spatial_norm[None]
    stream_one, spatial_in = first_norm(
        video_rows, conv_rows.reshape(token_rows, channels), spatial_gain
    )
    spatial_line, (in_rest,) = gather_tokens(
        spatial_in, 8, [Share(in_piece, ("tm",), line_half, lines - line_half)]
    )
    spatial_line = spatial_line.reshape(lines, images, pixels_dev, channels)
    spatial_triple, spatial_mix = spatial_forward(spatial_line, spatial_qkv)
    spatial_mix, (out_rest, cot_late) = from_lines(
        spatial_mix,
        False,
        9,
        [Share(out_piece, ("tm",), line_half, lines - line_half), Keep(cot_rows)],
    )
    cot_half = lax.all_gather(part_of(cot_late, "mp", 1), "space", axis=0, tiled=True)

    spatial_mix = spatial_mix.reshape(token_rows, half_width)
    out_all, in_all = (out_first, out_rest), (in_first, in_rest)
    text_valid = (jnp.arange(TXT, dtype=jnp.int32)[None, :] < text_lengths[:, None])[:, None, :]
    text_valid = text_valid.astype(jnp.float32)
    two_gains = jnp.stack([cross_norm, temporal_norm])
    stream_two, cross_in, cross_queries, cross_mix, stream_three, temporal_in, temporal_triple = (
        middle_forward(
            spatial_mix, stream_one, out_all, in_all, text_pairs, text_valid, two_gains, 34
        )
    )

    clip_triple, (in_quarter, out_quarter) = to_clips(
        temporal_triple.reshape(slots, frame_dev, pixels_dev, 3 * half_width),
        10,
        [Exchange(in_quarter, ("space",)), Exchange(out_quarter, ("space",))],
    )
    clip_pixels = clip_triple.shape[2]
    clip_rows = frames_all * clip_pixels
    clip_triple = clip_triple.reshape(slots, clip_rows, 3 * half_width)
    offset_table = offset_onehot(0, frames_all, frames_all)
    clip_frames = jnp.arange(clip_rows, dtype=jnp.int32)[:, None] // clip_pixels
    clip_frames = (clip_frames == jnp.arange(frames_all, dtype=jnp.int32)[None, :]).astype(
        jnp.float32
    )
    clip_bias = jnp.einsum("qkr,rh->hqk", offset_table, offset_bias, precision=highest)
    clip_bias = jnp.einsum("hqk,ck->hqc", clip_bias, clip_frames, precision=highest)
    clip_bias = jnp.einsum("rq,hqc->hrc", clip_frames, clip_bias, precision=highest)
    clip_ids = jnp.repeat(video_ids, clip_pixels, axis=1)
    clip_mix = temporal_forward(clip_triple, clip_bias, clip_ids, clip_pixels)
    temporal_mix, (cot_line,) = from_clips(
        clip_mix.reshape(slots, frames_all, clip_pixels, half_width), 11, [JoinCores(cot_half)]
    )
    temporal_mix = temporal_mix.reshape(token_rows, half_width)

    feed_gain = feed_norm[None]
    stream_four, feed_rows = late_forward(temporal_mix, stream_three, out_all, feed_gain, 35)
    feed_line, (feed_in, feed_out) = gather_tokens(
        feed_rows, 12, [Share(in_quarter, ("tm",)), Share(out_quarter, ("tm",))]
    )
    feed_in = feed_in.transpose(1, 0, 2, 3).reshape(channels, feed_width)
    feed_out = feed_out.transpose(0, 2, 1, 3).reshape(feed_width, channels)
    line_shape = (lines, token_rows, channels)
    final_part, feed_part, feed_grads = feed_both(
        feed_line.reshape(line_shape), cot_line.reshape(line_shape), feed_in, feed_out
    )
    normed_grad, (feed_grads,) = scatter_tokens(
        feed_part.reshape(lines * token_rows, channels), 14, [by_frames(feed_grads)]
    )

    upstream, mix_grad, temporal_out_grad, feed_norm_grad = late_backward(
        cot_rows, normed_grad, stream_four, feed_gain, temporal_mix, out_all
    )
    clip_up, (feed_grads,) = to_clips(
        mix_grad.reshape(slots, frame_dev, pixels_dev, half_width),
        15,
        [Exchange(feed_grads.reshape(lines, -1, 2 * feed_width), ("space",))],
    )
    clip_grads, score_total = temporal_backward(
        clip_triple,
        clip_bias,
        clip_ids,
        clip_pixels,
        clip_up.reshape(slots, clip_rows, half_width),
    )
    score_total = jnp.einsum("hqc,ck->hqk", score_total, clip_frames, precision=highest)
    offset_bias_grad = jnp.einsum("hqk,qkr->rh", score_total, offset_table, precision=highest)
    triple_grad, _ = from_clips(
        clip_grads.reshape(slots, frames_all, clip_pixels, 3 * half_width), 16
    )

    (
        upstream,
        mix_grad,
        pair_grad,
        temporal_query_grad,
        temporal_pair_grad,
        cross_query_grad,
        outs_grad,
        two_grads,
    ) = middle_backward(
        triple_grad.reshape(token_rows, 3 * half_width),
        upstream,
        stream_three,
        stream_two,
        temporal_in,
        cross_in,
        cross_queries,
        cross_mix,
        spatial_mix,
        out_all,
        in_all,
        text_pairs,
        text_valid,
        two_gains,
        36,
    )
    final_rows, (first_grads, second_grads) = scatter_tokens(
        final_part.reshape(lines * token_rows, channels),
        13,
        [by_frames(temporal_out_grad), by_frames(temporal_query_grad)],
    )
    mixed = (stream_four + final_rows.astype(jnp.float32)).astype(jnp.bfloat16)
    pair_grad = (
        pair_grad.reshape(slots, frames_axis, lines, text_local, 2 * half_width)
        .transpose(1, 2, 0, 3, 4)
        .reshape(frames_axis, lines * text_rows, 2 * half_width)
    )

    mix_line, (pair_grad,) = to_lines(
        mix_grad.reshape(images, pixels_dev, half_width), False, 17, [FrameSum(pair_grad)]
    )
    spatial_part, spatial_qkv_grad = spatial_backward(
        spatial_line, spatial_qkv, spatial_triple, mix_line
    )
    normed_grad, (pair_grad, third_grads) = scatter_tokens(
        spatial_part.reshape(lines * token_rows, channels),
        18,
        [
            Exchange(pair_grad.reshape(lines, text_rows, 2 * half_width), ("space",)),
            by_frames(temporal_pair_grad),
        ],
    )
    pair_grad = jnp.sum(pair_grad.astype(jnp.float32), axis=0).astype(jnp.bfloat16)
    upstream, branch_both, spatial_norm_grad = first_norm_backward(
        stream_one, spatial_gain, normed_grad, upstream, owners, lines
    )

    branch_line, (fourth_grads, pair_line) = to_lines(
        branch_both.reshape(-1, pixels_dev, channels),
        False,
        19,
        [by_frames(cross_query_grad), Share(pair_grad, ("space",))],
        join=True,
    )
    branch_line, branch_owned = branch_line[:images], branch_line[images:]
    second_conv_grad = conv_weight_grad(wide(second_wide), wide(branch_owned), "kc")
    second_part = conv_frames(wide(branch_line), second_conv, "OHWI", True).astype(jnp.bfloat16)
    second_in_grad, (fifth_grads, pair_all) = sum_lines(
        second_part.reshape(images, H * W, half_width),
        20,
        [by_frames(outs_grad), Share(pair_line, ("tm",))],
    )
    hidden_grad, scale_grad, shift_grad = group_backward(
        hidden, film_scale, film_shift, second_in_grad
    )
    frame_grads = jnp.stack([scale_grad, shift_grad], axis=1).reshape(slots, frame_dev, 2, -1)
    film_rows = jnp.einsum("bfv,bfjk->bvjk", choose, frame_grads, precision=highest)
    film_rows = film_rows.reshape(slots * VIDS * 2, -1)
    text_part = jnp.dot(
        pair_line.reshape(lines * text_rows, -1), cross_kv.T, preferred_element_type=jnp.float32
    )
    text_part = text_part.astype(jnp.bfloat16).reshape(lines, text_rows, -1)

    hidden_wide, (second_conv_grad, film_shares, text_part) = gather_lines(
        hidden_grad,
        21,
        [TapSum(second_conv_grad), Share(film_rows, everyone), Exchange(text_part, ("space",))],
    )
    first_conv_grad = conv_weight_grad(wide(first_owned), wide(hidden_wide), "ck")
    first_part = conv_frames(wide(hidden_wide), first_conv, "OHWI", True).astype(jnp.bfloat16)
    gathered_grads = jnp.concatenate(
        [first_grads, second_grads, third_grads, fourth_grads, fifth_grads], axis=1
    )
    first_in_grad, (first_conv_grad, spatial_qkv_grad, gathered_grads) = sum_cores(
        first_part.reshape(images, H * W, -1),
        22,
        [
            TapSum(first_conv_grad),
            by_frames(spatial_qkv_grad),
            Exchange(gathered_grads.reshape(lines, -1, gathered_grads.shape[1]), ("space",)),
        ],
    )
    video_line_grad, gain_grad, bias_grad = group_backward(
        video_lines[:images], gain_line[:images], bias_line[:images], first_in_grad
    )

    def placed(line_grad):
        whole = jnp.zeros((channels,), jnp.float32)
        size = line_grad.shape[2]
        place = (lax.axis_index("space") * cores + lax.axis_index("mp")) * size
        return lax.dynamic_update_slice_in_dim(whole, jnp.sum(line_grad, axis=(0, 1)), place, 0)

    small = jnp.concatenate(
        [
            item.reshape(owners, -1)
            for item in (
                placed(gain_grad),
                placed(bias_grad),
                spatial_norm_grad,
                two_grads[0],
                two_grads[1],
                feed_norm_grad,
                offset_bias_grad,
            )
        ],
        axis=1,
    )
    video_rows_grad, (small, qkv_part) = from_lines(
        video_line_grad,
        True,
        23,
        [
            Exchange(small[:, None], everyone),
            Exchange(spatial_qkv_grad.reshape(lines, -1, spatial_qkv_grad.shape[1]), ("space",)),
        ],
    )
    video_grad = upstream + video_rows_grad.reshape(token_rows, channels).astype(jnp.float32)

    film_shares = film_shares.reshape(frames_axis, lines, slots, VIDS, 2, -1)
    video_film_grad = (
        jnp.sum(film_shares, axis=0)
        .transpose(1, 2, 3, 0, 4)
        .reshape(slots, VIDS, 2, half_width)
    )
    film_weight_grad = jnp.einsum(
        "bvc,bvjk->cjk",
        part_of(part_of(embed, "tm", 2), "space", 2).astype(jnp.float32),
        video_film_grad,
        precision=highest,
    )
    cross_kv_grad = jnp.einsum(
        "prc,prk->ck",
        text_cols,
        pair_all.reshape(owners, text_rows, 2 * half_width),
        preferred_element_type=jnp.float32,
    )
    text_half = part_of(
        twin_add(text_part.transpose(1, 0, 2).reshape(text_rows, -1)), "mp", 1
    )
    small = jnp.sum(small, axis=(0, 1))
    small_twin = lax.ppermute(small, "mp", [(0, 1), (1, 0)])
    gain_size = channels // owners
    gains = [small[i * gain_size : (i + 1) * gain_size] for i in range(6)]
    for i in range(2):
        gains[i] = gains[i] + small_twin[i * gain_size : (i + 1) * gain_size]
    feed_grads, qkv_part = feed_grads.astype(jnp.float32), qkv_part.astype(jnp.float32)
    owner_rows = feed_grads.shape[1]
    gathered_grads = jnp.sum(gathered_grads.astype(jnp.float32), axis=0)
    owner_parts = [
        gathered_grads[:, i * half_width : (i + 1) * half_width] for i in range(7)
    ]
    return (
        mixed.reshape(video.shape),
        video_grad.reshape(video.shape),
        text_half.reshape(slots, text_local, -1),
        gains[0],
        gains[1],
        first_conv_grad.astype(jnp.float32).transpose(1, 0, 2),
        film_weight_grad,
        second_conv_grad.astype(jnp.float32).transpose(2, 0, 1),
        gains[2],
        qkv_part.reshape(lines, owner_rows, 3, -1)
        .transpose(1, 2, 0, 3)
        .reshape(owner_rows, 3, half_width),
        owner_parts[6].T,
        gains[3],
        owner_parts[4],
        cross_kv_grad.reshape(-1, 2, half_width),
        owner_parts[5].T,
        gains[4],
        gathered_grads[:, half_width : 4 * half_width].reshape(-1, 3, half_width),
        owner_parts[0].T,
        small[6 * gain_size :].reshape(R // owners, head_local),
        gains[5],
        feed_grads[:, :, :feed_width].transpose(1, 0, 2).reshape(owner_rows, -1),
        feed_grads[:, :, feed_width:].transpose(0, 2, 1).reshape(-1, owner_rows),
    )


def solution(mesh):
    return jax.shard_map(
        on_device,
        mesh=mesh,
        in_specs=(
            P(None, "tm", "space", None, None),
            P(None, "tm", "space", None, None),
            P(None, ("tm", "space"), None),
            P(),
            P(),
            P(),
            P(),
            P(),
            P("space", None, "mp"),
            P("space", None, "mp"),
            P("mp", None, "space"),
            P(),
            P("space", None, "mp"),
            P("mp", "space"),
            P(),
            P("space", "mp"),
            P("space", None, "mp"),
            P("mp", "space"),
            P(),
            P("space", None, "mp"),
            P("mp", "space"),
            P(None, "mp"),
            P(),
            P("space", "mp"),
            P("mp", "space"),
        ),
        out_specs=(
            P(None, "tm", "space", None, None),
            P(None, "tm", "space", None, None),
            P(None, ("tm", "space"), "mp"),
            P(("tm", "space")),
            P(("tm", "space")),
            P(("tm", "space"), None, "mp"),
            P(("tm", "space"), None, "mp"),
            P("mp", None, ("tm", "space")),
            P(("tm", "space")),
            P(("tm", "space"), None, "mp"),
            P("mp", ("tm", "space")),
            P(("tm", "space")),
            P(("tm", "space"), "mp"),
            P(("tm", "space"), None, "mp"),
            P("mp", ("tm", "space")),
            P(("tm", "space")),
            P(("tm", "space"), None, "mp"),
            P("mp", ("tm", "space")),
            P(("tm", "space"), "mp"),
            P(("tm", "space")),
            P(("tm", "space"), "mp"),
            P("mp", ("tm", "space")),
        ),
        check_vma=False,
    )
```

```python
import math

import jax
import jax.numpy as jnp
from jax import lax
from jax.experimental import pallas as pl
from jax.experimental.pallas import tpu as pltpu
from jax.sharding import PartitionSpec as P

D = 1024
HDIM = 64
TXT = 128
G = 32
R = 128
VIDS = 3
H = 16
W = 16


epsilon = 1e-05
highest = lax.Precision.HIGHEST
masked = -1e30


def twin_add(partial_sum):
    mine = partial_sum.astype(jnp.bfloat16)
    other = lax.ppermute(mine, "mp", [(0, 1), (1, 0)])
    return mine.astype(jnp.float32) + other.astype(jnp.float32)


def part_of(source, axis_name, dim):
    size = source.shape[dim] // lax.axis_size(axis_name)
    return lax.dynamic_slice_in_dim(source, lax.axis_index(axis_name) * size, size, dim)


MESH = pl.DeviceIdType.MESH
lane = 128
ANY = pl.BlockSpec(memory_space=pl.ANY)
VMEM = pl.BlockSpec(memory_space=pltpu.VMEM)


def meet(peers):
    gate = pltpu.get_barrier_semaphore()
    for peer in peers:
        pl.semaphore_signal(gate, inc=1, device_id=peer, device_id_type=MESH)
    pl.semaphore_wait(gate, len(peers))


def others(axis_name):
    count = lax.axis_size(axis_name)
    me = lax.axis_index(axis_name)
    return [(step, lax.rem(me + step, count)) for step in range(1, count)]


def send(source, target, send_sem, recv_sem, peer):
    copy = pltpu.make_async_remote_copy(
        src_ref=source,
        dst_ref=target,
        send_sem=send_sem,
        recv_sem=recv_sem,
        device_id=peer,
        device_id_type=MESH,
    )
    copy.start()
    return copy


def keep(source, target, sem):
    copy = pltpu.make_async_copy(source, target, sem)
    copy.start()
    return copy


def cols_of(ref, index, width):
    return ref.at[:, :, pl.ds(pl.multiple_of(index * width, width), width)]


def rows_of(ref, index, width):
    return ref.at[:, pl.ds(pl.multiple_of(index * width, width), width), :]


def talk(kernel, result, operands, scratch, number, specs=None, out_spec=ANY, grant=32):
    return pl.pallas_call(
        kernel,
        out_shape=result,
        in_specs=[ANY] * len(operands) if specs is None else specs,
        out_specs=out_spec,
        scratch_shapes=scratch,
        compiler_params=pltpu.CompilerParams(
            collective_id=number, has_side_effects=True, vmem_limit_bytes=grant * 1024 * 1024
        ),
    )(*operands)


def dma_sems(*counts):
    return [pltpu.SemaphoreType.DMA((max(count, 1),)) for count in counts]


def flat_index(axes):
    index = 0
    for name in axes:
        index = index * lax.axis_size(name) + lax.axis_index(name)
    return index


def flat_peers(axes):
    count = math.prod(lax.axis_size(name) for name in axes)
    me = flat_index(axes)
    peers = []
    for step in range(1, count):
        peer = lax.rem(me + step, count)
        place, rest = {}, peer
        for name in reversed(axes):
            place[name] = lax.rem(rest, lax.axis_size(name))
            rest = rest // lax.axis_size(name)
        peers.append((step, peer, place))
    return peers


class Rider:
    scratch = ()
    source_spec = ANY
    result_spec = ANY

    def peers(self):
        return [place for _, _, place in flat_peers(self.axes)]

    def middle(self, *refs):
        pass


def square_places():
    me = lax.axis_index("tm")
    near = me + 1 - 2 * lax.rem(me, 2)
    far = me + 2 - 4 * (me // 2)
    return me, near, far, 3 - me


class Exchange(Rider):
    def __init__(self, source, axes, pick=None, cut=None):
        self.source, self.axes, self.cut = source, axes, cut
        self.pick = (lambda ref, place: ref.at[place]) if pick is None else pick
        stack = source if cut is None else jax.eval_shape(cut, source)
        count = math.prod(lax.axis_size(name) for name in axes)
        self.result = jax.ShapeDtypeStruct(stack.shape, stack.dtype)
        self.scratch = dma_sems(count - 1, count - 1, 1)

    def plain(self):
        stack = self.source if self.cut is None else self.cut(self.source)
        return lax.all_to_all(stack, self.axes, split_axis=0, concat_axis=0, tiled=True)

    def start(self, x_ref, out_ref, send_sem, recv_sem, own_sem):
        me = flat_index(self.axes)
        self.copies = [
            send(self.pick(x_ref, peer), out_ref.at[me], send_sem.at[i - 1], recv_sem.at[i - 1], place)
            for i, peer, place in flat_peers(self.axes)
        ]
        self.copies.append(keep(self.pick(x_ref, me), out_ref.at[me], own_sem.at[0]))

    def finish(self, *refs):
        for copy in self.copies:
            copy.wait()


def span(index, size):
    return pl.ds(pl.multiple_of(index * size, size), size)


class LineSum(Rider):
    axes = ("space",)
    source_spec = VMEM
    result_spec = VMEM

    def __init__(self, source):
        self.source = source
        self.lines = lax.axis_size("space")
        self.rows, self.width = source.shape[0] // self.lines, source.shape[1]
        self.result = jax.ShapeDtypeStruct((self.rows, self.width), jnp.bfloat16)
        self.scratch = [
            pltpu.VMEM((self.lines - 1, self.rows, self.width), jnp.bfloat16)
        ] + dma_sems(self.lines - 1, self.lines - 1)

    def plain(self):
        return lax.psum_scatter(self.source, "space", scatter_dimension=0, tiled=True)

    def start(self, x_ref, out_ref, got_ref, send_sem, recv_sem):
        self.copies = [
            send(x_ref.at[span(peer, self.rows)], got_ref.at[i - 1], send_sem.at[i - 1], recv_sem.at[i - 1], {"space": peer})
            for i, peer in others("space")
        ]

    def finish(self, x_ref, out_ref, got_ref, *sems):
        for copy in self.copies:
            copy.wait()
        total = x_ref[span(lax.axis_index("space"), self.rows)].astype(jnp.float32)
        for step in range(self.lines - 1):
            total = total + got_ref[step].astype(jnp.float32)
        out_ref[...] = total.astype(jnp.bfloat16)


class Share(Rider):
    def __init__(self, source, axes, first=0, size=None, cols=None):
        self.source, self.axes = source, axes
        self.first, self.size, self.cols = first, size, cols
        count = math.prod(lax.axis_size(name) for name in axes)
        shape = source.shape if size is None else (size,) + source.shape[1:]
        if cols is not None:
            shape = shape[:-1] + (cols[1] - cols[0],)
        self.shape = shape
        self.result = jax.ShapeDtypeStruct((count,) + shape, source.dtype)
        even = (len(shape) > 2 and shape[0] % 2 == 0) or shape[-2] % 32 == 0
        self.square = axes == ("tm",) and count == 4 and even
        copies = 4 if self.square else count - 1
        self.scratch = dma_sems(copies, copies, 1)

    def plain(self):
        source = self.source
        if self.size is not None:
            source = source[self.first : self.first + self.size]
        if self.cols is not None:
            source = source[..., self.cols[0] : self.cols[1]]
        return lax.all_gather(source, self.axes, axis=0, tiled=False)

    def half(self, ref, index):
        if len(self.shape) > 2 and self.shape[0] % 2 == 0:
            size = self.shape[0] // 2
            return ref.at[pl.ds(index * size, size)]
        size = self.shape[-2] // 2
        rows = pl.ds(index * size, size)
        return ref.at[:, rows] if len(self.shape) == 3 else ref.at[rows]

    def start(self, x_ref, out_ref, send_sem, recv_sem, own_sem):
        part = x_ref if self.size is None else x_ref.at[pl.ds(self.first, self.size)]
        if self.cols is not None:
            part = part.at[:, :, pl.ds(self.cols[0], self.cols[1] - self.cols[0])]
        if self.square:
            me, near, far, _ = square_places()
            self.copies = [
                send(part, out_ref.at[me], send_sem.at[i], recv_sem.at[i], {"tm": peer})
                for i, peer in enumerate((near, far))
            ]
        else:
            me = flat_index(self.axes)
            self.copies = [
                send(part, out_ref.at[me], send_sem.at[i - 1], recv_sem.at[i - 1], place)
                for i, _, place in flat_peers(self.axes)
            ]
        self.own = keep(part, out_ref.at[me], own_sem.at[0])

    def middle(self, x_ref, out_ref, send_sem, recv_sem, own_sem):
        if not self.square:
            return
        _, near, far, _ = square_places()
        from_near, from_far = self.copies
        from_far.wait_recv()
        got = self.half(out_ref.at[far], 0)
        to_near = send(got, got, send_sem.at[2], recv_sem.at[2], {"tm": near})
        from_near.wait_recv()
        got = self.half(out_ref.at[near], 1)
        to_far = send(got, got, send_sem.at[3], recv_sem.at[3], {"tm": far})
        self.passed = [to_near, to_far]

    def finish(self, *refs):
        if self.square:
            for copy in self.copies:
                copy.wait_send()
            for copy in self.passed:
                copy.wait()
        else:
            for copy in self.copies:
                copy.wait()
        self.own.wait()


class JoinCores(Rider):
    def __init__(self, source):
        self.source = source
        self.rows, self.width = source.shape
        shape = (self.rows, self.width * lax.axis_size("mp"))
        self.result = jax.ShapeDtypeStruct(shape, source.dtype)
        self.scratch = dma_sems(1, 1, 1)

    def peers(self):
        return twin_peers()

    def plain(self):
        return lax.all_gather(self.source, "mp", axis=1, tiled=True)

    def start(self, x_ref, out_ref, send_sem, recv_sem, own_sem):
        core = lax.axis_index("mp")
        mine = out_ref.at[:, pl.ds(pl.multiple_of(core * self.width, self.width), self.width)]
        self.copies = [
            send(x_ref, mine, send_sem.at[0], recv_sem.at[0], {"mp": 1 - core}),
            keep(x_ref, mine, own_sem.at[0]),
        ]

    def finish(self, *refs):
        for copy in self.copies:
            copy.wait()


class LineColumns(Rider):
    axes = ("space",)

    def __init__(self, source):
        self.source = source
        lines = lax.axis_size("space")
        self.width = source.shape[1] // lines
        shape = (lines, source.shape[0], self.width)
        self.result = jax.ShapeDtypeStruct(shape, source.dtype)
        self.scratch = dma_sems(lines - 1, lines - 1, 1)

    def plain(self):
        return lax.all_to_all(
            self.source[None], "space", split_axis=2, concat_axis=0, tiled=True
        )

    def start(self, x_ref, out_ref, send_sem, recv_sem, own_sem):
        me = lax.axis_index("space")

        def part(index):
            return x_ref.at[:, pl.ds(pl.multiple_of(index * self.width, self.width), self.width)]

        self.copies = [
            send(part(peer), out_ref.at[me], send_sem.at[i - 1], recv_sem.at[i - 1], {"space": peer})
            for i, peer in others("space")
        ]
        self.copies.append(keep(part(me), out_ref.at[me], own_sem.at[0]))

    def finish(self, *refs):
        for copy in self.copies:
            copy.wait()


class FrameSum(Rider):
    axes = ("tm",)
    result_spec = VMEM

    def __init__(self, source, taps=False):
        self.taps = taps
        self.count = lax.axis_size("tm")
        if taps:
            self.layers, all_rows, self.width = source.shape
            self.rows = all_rows // self.count
        else:
            self.layers, (_, self.rows, self.width) = 1, source.shape
        self.source = source
        shape = (self.layers, self.rows, self.width)
        self.result = jax.ShapeDtypeStruct(shape if taps else shape[1:], jnp.bfloat16)
        self.square = self.count == 4 and self.rows % 32 == 0
        self.split = self.rows // 2 if self.square else self.rows
        half = (self.layers, self.split, self.width)
        if self.square:
            self.scratch = [
                pltpu.VMEM((2, 2) + half, jnp.bfloat16),
                pltpu.VMEM((2,) + half, jnp.bfloat16),
                pltpu.VMEM((2, 2) + half, jnp.bfloat16),
            ] + dma_sems(4, 6, 6)
        else:
            self.scratch = [
                pltpu.VMEM((max(self.count - 1, 1),) + half, jnp.bfloat16),
                pltpu.VMEM((1, 1) + half, jnp.bfloat16),
            ] + dma_sems(1, self.count - 1, self.count - 1)

    def plain(self):
        dim = 1 if self.taps else 0
        total = lax.psum_scatter(self.source, "tm", scatter_dimension=dim, tiled=True)
        return total if self.taps else total[0]

    def view(self, w_ref, place, half):
        if self.taps:
            start = pl.multiple_of(place * self.rows + half * self.split, self.split)
            return w_ref.at[:, pl.ds(start, self.split)]
        return w_ref.at[pl.ds(place, 1), pl.ds(half * self.split, self.split)]

    def add(self, target_ref, first, *rest):
        block = min(16, self.split)
        steps = self.split // block

        def some(index, carry):
            layer = index // steps
            rows = pl.ds(pl.multiple_of(lax.rem(index, steps) * block, block), block)
            total = first[layer, rows].astype(jnp.float32)
            for other in rest:
                total = total + other[layer, rows].astype(jnp.float32)
            target_ref[layer, rows] = total.astype(jnp.bfloat16)
            return carry

        lax.fori_loop(0, self.layers * steps, some, 0)

    def out_view(self, out_ref, half):
        rows = pl.ds(half * self.split, self.split)
        if self.taps:
            return out_ref.at[:, rows]
        return out_ref.reshape(1, self.rows, self.width).at[:, rows]

    def start(self, w_ref, out_ref, got_ref, *rest):
        near_ref, own_sem, send_sem, recv_sem = rest[-4:]
        if not self.square:
            me = lax.axis_index("tm")
            self.copies = [
                send(self.view(w_ref, peer, 0), got_ref.at[i - 1], send_sem.at[i - 1], recv_sem.at[i - 1], {"tm": peer})
                for i, peer in others("tm")
            ]
            self.own = [keep(self.view(w_ref, me, 0), near_ref.at[0, 0], own_sem.at[0])]
            return
        me, near, far, across = square_places()
        self.copies = [
            send(self.view(w_ref, place, half), got_ref.at[half, i], send_sem.at[2 * half + i], recv_sem.at[2 * half + i], {"tm": peer})
            for half, peer in ((0, near), (1, far))
            for i, place in ((1, across), (0, peer))
        ]
        self.own = [
            keep(self.view(w_ref, place, half), near_ref.at[half, i], own_sem.at[2 * half + i])
            for half, peer in ((0, far), (1, near))
            for i, place in ((0, me), (1, peer))
        ]

    def middle(self, w_ref, out_ref, got_ref, *rest):
        if not self.square:
            return
        last_ref, near_ref, _, send_sem, recv_sem = rest
        _, near, far, _ = square_places()
        self.passed = []
        for half, peer in ((0, far), (1, near)):
            self.copies[2 * half].wait_recv()
            self.own[2 * half + 1].wait()
            self.add(got_ref.at[half, 1], near_ref.at[half, 1], got_ref.at[half, 1])
            self.passed.append(
                send(got_ref.at[half, 1], last_ref.at[half], send_sem.at[4 + half], recv_sem.at[4 + half], {"tm": peer})
            )

    def finish(self, w_ref, out_ref, got_ref, *rest):
        near_ref = rest[-4]
        if not self.square:
            for copy in self.copies + self.own:
                copy.wait()
            parts = [got_ref.at[i] for i in range(self.count - 1)]
            self.add(self.out_view(out_ref, 0), near_ref.at[0, 0], *parts)
            return
        last_ref = rest[0]
        for half in range(2):
            self.copies[2 * half].wait_send()
            self.copies[2 * half + 1].wait()
            self.own[2 * half].wait()
            self.passed[half].wait()
            self.add(
                self.out_view(out_ref, half),
                near_ref.at[half, 0],
                got_ref.at[half, 0],
                last_ref.at[half],
            )


class SmallSum(Rider):
    source_spec = VMEM
    result_spec = VMEM

    def __init__(self, source):
        self.source = source
        self.frames, self.lines = source.shape[:2]
        part = source.shape[1:]
        self.result = jax.ShapeDtypeStruct(part[1:], source.dtype)
        self.scratch = [
            pltpu.VMEM((self.frames - 1,) + part, source.dtype),
            pltpu.VMEM(part, source.dtype),
            pltpu.VMEM((self.lines - 1,) + part[1:], source.dtype),
        ] + dma_sems(self.frames - 1, self.frames - 1, self.lines - 1, self.lines - 1)

    def peers(self):
        return frame_peers() + line_peers()

    def plain(self):
        total = lax.psum_scatter(self.source, "tm", scatter_dimension=0, tiled=True)[0]
        return lax.psum_scatter(total, "space", scatter_dimension=0, tiled=True)[0]

    def start(self, x_ref, out_ref, got_ref, sum_ref, last_ref, send_sem, recv_sem, send2, recv2):
        self.copies = [
            send(x_ref.at[peer], got_ref.at[i - 1], send_sem.at[i - 1], recv_sem.at[i - 1], {"tm": peer})
            for i, peer in others("tm")
        ]

    def middle(self, x_ref, out_ref, got_ref, sum_ref, last_ref, send_sem, recv_sem, send2, recv2):
        total = x_ref[lax.axis_index("tm")]
        for i, copy in enumerate(self.copies):
            copy.wait()
            total = total + got_ref[i]
        sum_ref[...] = total
        self.passed = [
            send(sum_ref.at[peer], last_ref.at[i - 1], send2.at[i - 1], recv2.at[i - 1], {"space": peer})
            for i, peer in others("space")
        ]

    def finish(self, x_ref, out_ref, got_ref, sum_ref, last_ref, *sems):
        total = sum_ref[lax.axis_index("space")]
        for i, copy in enumerate(self.passed):
            copy.wait()
            total = total + last_ref[i]
        out_ref[...] = total


class Keep(Rider):
    def __init__(self, source):
        self.source = source
        self.result = jax.ShapeDtypeStruct(source.shape, source.dtype)
        self.scratch = dma_sems(1)

    def peers(self):
        return []

    def plain(self):
        return self.source

    def start(self, x_ref, out_ref, own_sem):
        self.copy = keep(x_ref, out_ref, own_sem.at[0])

    def finish(self, *refs):
        self.copy.wait()


class TapSum(Rider):
    axes = ("tm",)
    source_spec = VMEM
    result_spec = VMEM

    def __init__(self, source):
        self.taps, all_rows, self.width = source.shape
        self.count = lax.axis_size("tm")
        self.rows = all_rows // self.count
        self.source = source
        shape = (self.taps, self.rows, self.width)
        self.result = jax.ShapeDtypeStruct(shape, jnp.bfloat16)
        self.scratch = [
            pltpu.VMEM((max(self.count - 1, 1),) + shape, jnp.bfloat16),
            pltpu.VMEM(shape, jnp.bfloat16),
        ] + dma_sems(self.count - 1, self.count - 1, 1)

    def plain(self):
        return lax.psum_scatter(self.source, "tm", scatter_dimension=1, tiled=True)

    def start(self, w_ref, out_ref, got_ref, own_ref, send_sem, recv_sem, own_sem):
        me = lax.axis_index("tm")
        self.copies = [
            send(rows_of(w_ref, peer, self.rows), got_ref.at[i - 1], send_sem.at[i - 1], recv_sem.at[i - 1], {"tm": peer})
            for i, peer in others("tm")
        ]
        self.copies.append(keep(rows_of(w_ref, me, self.rows), own_ref, own_sem.at[0]))

    def finish(self, w_ref, out_ref, got_ref, own_ref, *sems):
        for copy in self.copies:
            copy.wait()

        def some(tap, carry):
            total = own_ref[tap].astype(jnp.float32)
            for step in range(self.count - 1):
                total = total + got_ref[step, tap].astype(jnp.float32)
            out_ref[tap] = total.astype(jnp.bfloat16)
            return carry

        lax.fori_loop(0, self.taps, some, 0)


class CoreSum(Rider):
    source_spec = VMEM
    result_spec = VMEM

    def __init__(self, source):
        self.source = source
        rows, channels = source.shape
        self.rows, self.width = rows, channels // lax.axis_size("mp")
        self.result = jax.ShapeDtypeStruct((rows, self.width), jnp.bfloat16)
        self.scratch = [pltpu.VMEM((rows, self.width), jnp.bfloat16)] + dma_sems(1, 1)

    def peers(self):
        return twin_peers()

    def start(self, x_ref, out_ref, got_ref, send_sem, recv_sem):
        core = lax.axis_index("mp")
        theirs = pl.ds(pl.multiple_of((1 - core) * self.width, self.width), self.width)
        self.copy = send(x_ref.at[:, theirs], got_ref, send_sem.at[0], recv_sem.at[0], {"mp": 1 - core})

    def finish(self, x_ref, out_ref, got_ref, *sems):
        self.copy.wait()
        block = min(128, self.rows)
        start = lax.axis_index("mp") * self.width
        mine = pl.ds(pl.multiple_of(start, self.width), self.width)

        def some(index, carry):
            rows = pl.ds(pl.multiple_of(index * block, block), block)
            total = x_ref[rows, mine].astype(jnp.float32) + got_ref[rows, :].astype(jnp.float32)
            out_ref[rows, :] = total.astype(jnp.bfloat16)
            return carry

        lax.fori_loop(0, self.rows // block, some, 0)


def plain_all(riders):
    return [rider.plain() for rider in riders]


def talk_with(kernel, peers, result, operands, scratch, number, riders, specs=None, out_spec=ANY):
    specs = [ANY] * len(operands) if specs is None else specs
    inputs, own_scratch, count = len(operands), len(scratch), len(riders)

    def whole(*refs):
        ins, rider_ins = refs[:inputs], refs[inputs : inputs + count]
        out_ref = refs[inputs + count]
        rider_outs = refs[inputs + count + 1 : inputs + 2 * count + 1]
        rest = refs[inputs + 2 * count + 1 :]
        mine, rest = rest[:own_scratch], rest[own_scratch:]
        packs = []
        for rider, x_ref, y_ref in zip(riders, rider_ins, rider_outs):
            packs.append((x_ref, y_ref) + tuple(rest[: len(rider.scratch)]))
            rest = rest[len(rider.scratch) :]
        meet(peers() + [peer for rider in riders for peer in rider.peers()])
        for rider, pack in zip(riders, packs):
            rider.start(*pack)
        waiting = list(zip(riders, packs))

        def hook():
            while waiting:
                rider, pack = waiting.pop(0)
                rider.middle(*pack)

        kernel(hook, *ins, out_ref, *mine)
        hook()
        for rider, pack in zip(riders, packs):
            rider.finish(*pack)

    results = talk(
        whole,
        (result,) + tuple(rider.result for rider in riders),
        operands + [rider.source for rider in riders],
        scratch + [item for rider in riders for item in rider.scratch],
        number,
        specs + [rider.source_spec for rider in riders],
        (out_spec,) + tuple(rider.result_spec for rider in riders),
    )
    return results[0], list(results[1:])


def line_peers():
    return [{"space": peer} for _, peer in others("space")]


def frame_peers():
    return [{"tm": peer} for _, peer in others("tm")]


def twin_peers():
    return [{"mp": 1 - lax.axis_index("mp")}]


pieces_per_chunk = 2


def relay_gather(lines, own, slot, sems, hook, arrived=None):
    me = lax.axis_index("space")
    right_send, right_recv, left_send, left_recv = sems
    parts = pieces_per_chunk

    def move(step, part, sign, send_sem, recv_sem):
        place = slot(lax.rem(me - sign * step + lines, lines), part)
        at = step * parts + part
        return pltpu.make_async_remote_copy(
            own(part) if step == 0 else place, place, send_sem.at[at], recv_sem.at[at],
            device_id={"space": lax.rem(me + sign + lines, lines)}, device_id_type=MESH,
        )

    def came(step, part, sign, recv_sem, order):
        place = slot(lax.rem(me - sign * (step + 1) + lines, lines), part)
        at = step * parts + part
        pltpu.make_async_remote_copy(
            place, place, recv_sem.at[at], recv_sem.at[at],
            device_id={"space": lax.rem(me + 1, lines)}, device_id_type=MESH,
        ).wait_recv()
        if arrived is not None:
            arrived(place, order * parts + part)

    ways = (
        (1, me, right_send, right_recv, 0),
        (-1, lines - 1 - me, left_send, left_recv, lines - 1),
    )
    for step in range(lines):
        for part in range(parts):
            for sign, rank, send_sem, recv_sem, order in ways:
                if step > 0:

                    @pl.when(rank >= step)
                    def _():
                        came(step - 1, part, sign, recv_sem, order + step - 1)

                if step < lines - 1:

                    @pl.when((rank >= step) & (rank + 1 < lines))
                    def _():
                        move(step, part, sign, send_sem, recv_sem).start()

        if step == min(1, lines - 1):
            hook()
    for step in range(lines - 1):
        for part in range(parts):
            for sign, rank, send_sem, recv_sem, _ in ways:

                @pl.when((rank >= step) & (rank + 1 < lines))
                def _():
                    move(step, part, sign, send_sem, recv_sem).wait_send()


def relay_sum(lines, stage_ref, right_ref, left_ref, sems, hook, ready=None):
    me = lax.axis_index("space")
    right_send, right_recv, left_send, left_recv = sems
    parts, last = pieces_per_chunk, lines - 1

    def move(source, slots, sem_out, sem_in, step, part, peer):
        at = step * parts + part
        return pltpu.make_async_remote_copy(
            source, slots.at[step, part], sem_out.at[at], sem_in.at[at],
            device_id={"space": lax.rem(peer + lines, lines)}, device_id_type=MESH,
        )

    def add(slots, step, part, place):
        total = slots[step, part].astype(jnp.float32) + stage_ref[place, part].astype(jnp.float32)
        slots[step, part] = total.astype(jnp.bfloat16)

    ways = (
        (me, me + 1, right_ref, right_send, right_recv, lambda step: last - step + me),
        (last - me, me - 1, left_ref, left_send, left_recv, lambda step: step - last + me),
    )
    for step in range(last):
        if ready is not None:
            ready(step)
        for part in range(parts):
            for rank, peer, slots, sem_out, sem_in, target in ways:
                place = lax.rem(target(step) + 2 * lines, lines)

                @pl.when(rank == 0)
                def _():
                    move(stage_ref.at[place, part], slots, sem_out, sem_in, step, part, peer).start()

                if step > 0:

                    @pl.when((rank > 0) & (rank <= step))
                    def _():
                        source = stage_ref.at[place, part]
                        move(source, slots, sem_out, sem_in, step - 1, part, peer).wait_recv()
                        add(slots, step - 1, part, place)
                        source = slots.at[step - 1, part]
                        move(source, slots, sem_out, sem_in, step, part, peer).start()

        if step == min(1, last - 1):
            hook()
    for part in range(parts):
        for rank, peer, slots, sem_out, sem_in, target in ways:

            @pl.when(rank > 0)
            def _():
                move(stage_ref.at[0, part], slots, sem_out, sem_in, last - 1, part, peer).wait_recv()

            for step in range(last):

                @pl.when(rank <= step)
                def _():
                    move(stage_ref.at[0, part], slots, sem_out, sem_in, step, part, peer).wait_send()


def to_lines(source, per_core, number, riders=(), join=False):
    images, pixels, channels = source.shape
    lines, cores = lax.axis_size("space"), lax.axis_size("mp")
    pieces = lines * cores if per_core or join else lines
    width = channels // pieces
    if width % lane != 0 or pixels % 16 != 0:
        if per_core:
            parts = source.reshape(images, pixels, lines, cores, width)
            parts = lax.dynamic_index_in_dim(parts, lax.axis_index("mp"), 3, keepdims=False)
            source = parts.reshape(images, pixels, lines * width)
        moved = lax.all_to_all(source, "space", split_axis=2, concat_axis=1, tiled=True)
        return moved, plain_all(riders)

    def kernel(hook, x_ref, out_ref, stage_ref, send_sem, recv_sem, pass_sem, gain_sem, own_sem):
        me, core = lax.axis_index("space"), lax.axis_index("mp")
        twin = {"mp": 1 - core}
        place = (lambda s: s * cores + core) if per_core or join else (lambda s: s)

        def spot(origin):
            rows = rows_of(out_ref, origin, pixels)
            return cols_of(rows, core, width) if join else rows

        copies = []
        for i, peer in others("space"):
            start = pl.multiple_of(place(peer) * width, width)
            stage_ref[i - 1] = x_ref[:, :, pl.ds(start, width)]
            copies.append(
                send(stage_ref.at[i - 1], spot(me), send_sem.at[i - 1], recv_sem.at[i - 1], {"space": peer})
            )
        if join:
            own_width = cores * width
            own = keep(cols_of(x_ref, me, own_width), rows_of(out_ref, me, pixels), own_sem.at[0])
        else:
            own = keep(cols_of(x_ref, place(me), width), spot(me), own_sem.at[0])
        passed = []
        for step in range(1, lines):
            copies[step - 1].wait_recv()
            if join:
                got = spot(lax.rem(me - step + lines, lines))
                passed.append(send(got, got, pass_sem.at[step - 1], gain_sem.at[step - 1], twin))
        for copy in copies:
            copy.wait_send()
        own.wait()
        for copy in passed:
            copy.wait()

    def peers():
        return line_peers() + (twin_peers() if join else [])

    held = cores * width if join else width
    result = jax.ShapeDtypeStruct((images, lines * pixels, held), source.dtype)
    scratch = [pltpu.VMEM((lines - 1, images, pixels, width), source.dtype)]
    scratch = scratch + dma_sems(lines - 1, lines - 1, lines - 1, lines - 1, 1)
    return talk_with(kernel, peers, result, [source], scratch, number, riders, [VMEM])


def from_lines(source, per_core, number, riders=()):
    images, line_pixels, width = source.shape
    lines, cores = lax.axis_size("space"), lax.axis_size("mp")
    pixels = line_pixels // lines
    pieces = lines * cores if per_core else lines
    if width % lane != 0 or pixels % 16 != 0:
        part = lax.all_to_all(source, "space", split_axis=1, concat_axis=2, tiled=True)
        if per_core:
            part = part.reshape(images, pixels, lines, 1, width)
            part = lax.all_gather(part, "mp", axis=3, tiled=True)
        return part.reshape(images, pixels, pieces * width), plain_all(riders)

    def kernel(hook, x_ref, out_ref, got_ref, send_sem, recv_sem, pass_sem, gain_sem):
        me, core = lax.axis_index("space"), lax.axis_index("mp")
        twin = {"mp": 1 - core}
        mine = core if per_core else 0
        copies = [
            send(rows_of(x_ref, peer, pixels), got_ref.at[me, mine], send_sem.at[i - 1], recv_sem.at[i - 1], {"space": peer})
            for i, peer in others("space")
        ]
        passed = []
        if per_core:
            passed.append(
                send(rows_of(x_ref, me, pixels), got_ref.at[me, core], pass_sem.at[0], gain_sem.at[0], twin)
            )
        got_ref[me, mine] = x_ref[:, pl.ds(pl.multiple_of(me * pixels, pixels), pixels), :]
        for step in range(1, lines):
            copies[step - 1].wait_recv()
            if per_core:
                got = got_ref.at[lax.rem(me - step + lines, lines), core]
                passed.append(send(got, got, pass_sem.at[step], gain_sem.at[step], twin))
        for copy in copies:
            copy.wait_send()
        for copy in passed:
            copy.wait()
        each = pieces // lines
        for piece in range(pieces):
            out_ref[:, :, piece * width : (piece + 1) * width] = got_ref[piece // each, piece % each]

    def peers():
        return line_peers() + ([{"mp": 1 - lax.axis_index("mp")}] if per_core else [])

    result = jax.ShapeDtypeStruct((images, pixels, pieces * width), source.dtype)
    scratch = [pltpu.VMEM((lines, pieces // lines, images, pixels, width), source.dtype)]
    scratch = scratch + dma_sems(lines - 1, lines - 1, lines, lines)
    return talk_with(kernel, peers, result, [source], scratch, number, riders, [VMEM], VMEM)


def gather_lines(source, number, riders=()):
    images, line_pixels, width = source.shape
    lines = lax.axis_size("space")
    if width % lane != 0:
        return lax.all_gather(source, "space", axis=2, tiled=True), plain_all(riders)

    def kernel(hook, x_ref, out_ref, got_ref, *sems):
        some = images // pieces_per_chunk

        def own(part):
            return x_ref.at[pl.ds(part * some, some)]

        def slot(index, part):
            return got_ref.at[index, pl.ds(part * some, some)]

        got_ref[lax.axis_index("space")] = x_ref[...]
        relay_gather(lines, own, slot, sems, hook)
        for line in range(lines):
            out_ref[:, :, line * width : (line + 1) * width] = got_ref[line]

    result = jax.ShapeDtypeStruct((images, line_pixels, lines * width), source.dtype)
    scratch = [pltpu.VMEM((lines,) + source.shape, source.dtype)]
    scratch = scratch + dma_sems(*[pieces_per_chunk * (lines - 1)] * 4)
    return talk_with(kernel, line_peers, result, [source], scratch, number, riders, [VMEM], VMEM)


def gather_cores(source, number, riders=()):
    images, line_pixels, width = source.shape
    cores = lax.axis_size("mp")
    if width % lane != 0:
        return lax.all_gather(source, "mp", axis=2, tiled=True), plain_all(riders)

    def kernel(hook, x_ref, out_ref, send_sem, recv_sem, own_sem):
        core = lax.axis_index("mp")
        twin = {"mp": 1 - core}
        target = cols_of(out_ref, core, width)
        copy = send(x_ref, target, send_sem.at[0], recv_sem.at[0], twin)
        own = keep(x_ref, target, own_sem.at[0])
        copy.wait()
        own.wait()

    result = jax.ShapeDtypeStruct((images, line_pixels, cores * width), source.dtype)
    return talk_with(kernel, twin_peers, result, [source], dma_sems(1, 1, 1), number, riders)


def sum_lines(source, number, riders=()):
    images, line_pixels, channels = source.shape
    lines = lax.axis_size("space")
    width = channels // lines
    if width % lane != 0:
        total = lax.psum_scatter(source, "space", scatter_dimension=2, tiled=True)
        return total.astype(jnp.float32), plain_all(riders)

    def kernel(hook, x_ref, out_ref, stage_ref, right_ref, left_ref, *sems):
        me = lax.axis_index("space")
        for line in range(lines):
            for part in range(pieces_per_chunk):
                rows = slice(part * some, (part + 1) * some)
                stage_ref[line, part] = x_ref[rows, :, line * width : (line + 1) * width]
        relay_sum(lines, stage_ref, right_ref, left_ref, sems, hook)
        for part in range(pieces_per_chunk):
            rows = slice(part * some, (part + 1) * some)
            out_ref[rows] = stage_ref[me, part].astype(jnp.float32)

            @pl.when(me > 0)
            def _():
                out_ref[rows] += right_ref[lines - 2, part].astype(jnp.float32)

            @pl.when(me < lines - 1)
            def _():
                out_ref[rows] += left_ref[lines - 2, part].astype(jnp.float32)

    result = jax.ShapeDtypeStruct((images, line_pixels, width), jnp.float32)
    some = images // pieces_per_chunk
    chunk = (pieces_per_chunk, some, line_pixels, width)
    scratch = [
        pltpu.VMEM((lines,) + chunk, source.dtype),
        pltpu.VMEM((lines - 1,) + chunk, source.dtype),
        pltpu.VMEM((lines - 1,) + chunk, source.dtype),
    ] + dma_sems(*[pieces_per_chunk * (lines - 1)] * 4)
    return talk_with(kernel, line_peers, result, [source], scratch, number, riders, [VMEM], VMEM)


def sum_cores(source, number, riders=()):
    images, line_pixels, channels = source.shape
    cores = lax.axis_size("mp")
    width = channels // cores
    if width % lane != 0:
        total = lax.psum_scatter(source, "mp", scatter_dimension=2, tiled=True)
        return total.astype(jnp.float32), plain_all(riders)

    def kernel(hook, x_ref, out_ref, got_ref, send_sem, recv_sem):
        core = lax.axis_index("mp")
        twin = {"mp": 1 - core}
        copy = send(cols_of(x_ref, 1 - core, width), got_ref, send_sem.at[0], recv_sem.at[0], twin)
        mine = pl.ds(pl.multiple_of(core * width, width), width)
        copy.wait()
        for image in range(images):
            out_ref[image] = x_ref[image, :, mine].astype(jnp.float32) + got_ref[image].astype(
                jnp.float32
            )

    result = jax.ShapeDtypeStruct((images, line_pixels, width), jnp.float32)
    scratch = [pltpu.VMEM((images, line_pixels, width), source.dtype)]
    scratch = scratch + dma_sems(1, 1)
    return talk_with(
        kernel, twin_peers, result, [source], scratch, number, riders, [VMEM], VMEM
    )


def gather_tokens(rows, number, riders=()):
    count, channels = rows.shape
    lines, cores = lax.axis_size("space"), lax.axis_size("mp")
    width = channels // cores
    source = rows.reshape(1, count, channels)

    def kernel(hook, x_ref, out_ref, pass_sem, gain_sem, own_sem, *sems):
        me, core = lax.axis_index("space"), lax.axis_index("mp")
        twin = {"mp": 1 - core}

        some = count // pieces_per_chunk

        def spot(origin, part):
            start = pl.multiple_of(origin * count + part * some, some)
            return cols_of(out_ref.at[:, pl.ds(start, some)], core, width)

        def own_part(part):
            return cols_of(x_ref.at[:, pl.ds(part * some, some)], core, width)

        def hand(ref, order):
            return pltpu.make_async_remote_copy(
                ref, ref, pass_sem.at[order], gain_sem.at[order], device_id=twin, device_id_type=MESH
            )

        own = keep(x_ref, rows_of(out_ref, me, count), own_sem.at[0])
        relay_gather(
            lines,
            own_part,
            spot,
            sems,
            hook,
            lambda ref, order: hand(ref, order).start(),
        )
        own.wait()
        parts = pieces_per_chunk
        for step in range(1, lines):
            for part in range(parts):

                @pl.when(me - step >= 0)
                def _():
                    place = spot(lax.rem(me - step + lines, lines), part)
                    hand(place, (step - 1) * parts + part).wait()

                @pl.when(me + step < lines)
                def _():
                    place = spot(lax.rem(me + step, lines), part)
                    hand(place, (lines + step - 2) * parts + part).wait()

    result = jax.ShapeDtypeStruct((1, lines * count, channels), rows.dtype)
    moves = pieces_per_chunk * (lines - 1)
    sems = dma_sems(2 * moves, 2 * moves, 1, *[moves] * 4)

    def peers():
        return line_peers() + twin_peers()

    line, others_done = talk_with(kernel, peers, result, [source], sems, number, riders, [VMEM], VMEM)
    return line.reshape(lines * count, channels), others_done


def scatter_tokens(partial_sum, number, riders=()):
    all_rows, channels = partial_sum.shape
    lines, cores = lax.axis_size("space"), lax.axis_size("mp")
    count, width = all_rows // lines, channels // cores
    source = partial_sum.astype(jnp.bfloat16).reshape(lines, count, channels)

    def kernel(
        hook, x_ref, out_ref, twin_ref, stage_ref, right_ref, left_ref, sum_ref,
        s_sem, r_sem, s3_sem, r3_sem, *sems,
    ):
        me, core = lax.axis_index("space"), lax.axis_index("mp")
        twin = {"mp": 1 - core}
        theirs = pl.ds(pl.multiple_of((1 - core) * width, width), width)
        mine = pl.ds(pl.multiple_of(core * width, width), width)
        order = [lines - 1, 0] + list(range(1, lines - 1))
        first = [
            send(x_ref.at[target, :, theirs], twin_ref.at[target], s_sem.at[target], r_sem.at[target], twin)
            for target in order
        ]

        def ready(step):
            turn = {0: zip(order[:2], first[:2]), 1: zip(order[2:], first[2:])}
            for target, copy in turn.get(step, ()):
                copy.wait_recv()
                total = x_ref[target, :, mine].astype(jnp.float32)
                total = total + twin_ref[target].astype(jnp.float32)
                total = total.astype(jnp.bfloat16)
                for part in range(pieces_per_chunk):
                    stage_ref[target, part] = total[part * some : (part + 1) * some]

        relay_sum(lines, stage_ref, right_ref, left_ref, sems, hook, ready)
        for part in range(pieces_per_chunk):
            sum_ref[part] = stage_ref[me, part].astype(jnp.float32)

            @pl.when(me > 0)
            def _():
                sum_ref[part] += right_ref[lines - 2, part].astype(jnp.float32)

            @pl.when(me < lines - 1)
            def _():
                sum_ref[part] += left_ref[lines - 2, part].astype(jnp.float32)

            out_ref[part * some : (part + 1) * some, mine] = sum_ref[part].astype(jnp.bfloat16)
        third = send(out_ref.at[:, mine], out_ref.at[:, mine], s3_sem.at[0], r3_sem.at[0], twin)
        for copy in first:
            copy.wait_send()
        third.wait()

    result = jax.ShapeDtypeStruct((count, channels), jnp.bfloat16)
    some = count // pieces_per_chunk
    chunk = (pieces_per_chunk, some, width)
    scratch = [
        pltpu.VMEM((lines, count, width), jnp.bfloat16),
        pltpu.VMEM((lines,) + chunk, jnp.bfloat16),
        pltpu.VMEM((lines - 1,) + chunk, jnp.bfloat16),
        pltpu.VMEM((lines - 1,) + chunk, jnp.bfloat16),
        pltpu.VMEM(chunk, jnp.float32),
    ]
    sems = dma_sems(lines, lines, 1, 1, *[pieces_per_chunk * (lines - 1)] * 4)

    def peers():
        return line_peers() + [{"mp": 1 - lax.axis_index("mp")}]

    total, other = talk_with(
        kernel, peers, result, [source], scratch + sems, number, riders, [VMEM], VMEM
    )
    return total, other


def to_clips(source, number, riders=()):
    slots, frames, pixels, channels = source.shape
    count = lax.axis_size("tm")
    few = pixels // count
    if few % 16 != 0:
        return lax.all_to_all(source, "tm", split_axis=2, concat_axis=1, tiled=True), plain_all(riders)

    def kernel(hook, x_ref, out_ref, send_sem, recv_sem, own_sem):
        me = lax.axis_index("tm")
        target = out_ref.at[:, pl.ds(me * frames, frames)]

        def part(index):
            return x_ref.at[:, :, pl.ds(pl.multiple_of(index * few, few), few)]

        copies = [
            send(part(peer), target, send_sem.at[i - 1], recv_sem.at[i - 1], {"tm": peer})
            for i, peer in others("tm")
        ]
        copies.append(keep(part(me), target, own_sem.at[0]))
        for copy in copies:
            copy.wait()

    result = jax.ShapeDtypeStruct((slots, count * frames, few, channels), source.dtype)
    sems = dma_sems(count - 1, count - 1, 1)
    return talk_with(kernel, frame_peers, result, [source], sems, number, riders)


def from_clips(source, number, riders=()):
    slots, all_frames, few, channels = source.shape
    count = lax.axis_size("tm")
    frames = all_frames // count
    if few % 16 != 0:
        return lax.all_to_all(source, "tm", split_axis=1, concat_axis=2, tiled=True), plain_all(riders)

    def kernel(hook, x_ref, out_ref, send_sem, recv_sem, own_sem):
        me = lax.axis_index("tm")
        target = out_ref.at[:, :, pl.ds(pl.multiple_of(me * few, few), few)]

        def part(index):
            return x_ref.at[:, pl.ds(index * frames, frames)]

        copies = [
            send(part(peer), target, send_sem.at[i - 1], recv_sem.at[i - 1], {"tm": peer})
            for i, peer in others("tm")
        ]
        copies.append(keep(part(me), target, own_sem.at[0]))
        for copy in copies:
            copy.wait()

    result = jax.ShapeDtypeStruct((slots, frames, count * few, channels), source.dtype)
    sems = dma_sems(count - 1, count - 1, 1)
    return talk_with(kernel, frame_peers, result, [source], sems, number, riders)


def by_owner_line(source, owners, lines):
    parts = source.reshape(source.shape[:-1] + (owners // lines, lines, -1))
    return parts.swapaxes(-3, -2).reshape(source.shape)


def by_frames(weight_grad):
    return FrameSum(weight_grad.reshape(lax.axis_size("tm"), -1, weight_grad.shape[1]))


def padded_rims(source):
    return jnp.pad(source, ((0, 0), (0, 0), (1, 1), (1, 1), (0, 0)))


def conv_weight(weight):
    return weight.reshape(weight.shape[0], 3, 3, weight.shape[2])


def conv_frames(source, weight, spec, flipped):
    images = source.reshape((-1,) + source.shape[2:])
    kernel = conv_weight(weight)
    if flipped:
        kernel = kernel[:, ::-1, ::-1]
    result = lax.conv_general_dilated(
        images,
        kernel,
        (1, 1),
        "SAME",
        dimension_numbers=("NHWC", spec, "NHWC"),
        preferred_element_type=jnp.float32,
    )
    return result.reshape(source.shape[:4] + (result.shape[-1],))


def conv_weight_grad(source, upstream, form, taps=range(9)):
    padded = padded_rims(source)
    rows, cols = source.shape[2], source.shape[3]
    tap_list = []
    for tap in taps:
        i, j = tap // 3, tap % 3
        tap_list.append(
            jnp.einsum(
                "bfhwc,bfhwk->" + form,
                padded[:, :, i : i + rows, j : j + cols],
                upstream,
                preferred_element_type=jnp.float32,
            ).astype(jnp.bfloat16)
        )
    return jnp.stack(tap_list)


def sinusoid(steps_int):
    counted = D // 2
    freqs = jnp.exp(-math.log(10000.0) * jnp.arange(counted, dtype=jnp.float32) / counted)
    angles = steps_int.astype(jnp.float32)[..., None] * freqs
    return jnp.concatenate([jnp.sin(angles), jnp.cos(angles)], axis=-1)


def offset_onehot(query_start, query_count, key_count):
    distance = (
        query_start
        + jnp.arange(query_count, dtype=jnp.int32)[:, None]
        - jnp.arange(key_count, dtype=jnp.int32)[None, :]
    )
    position = jnp.clip(distance, -(R // 2), R // 2 - 1) + R // 2
    return (position[:, :, None] == jnp.arange(R, dtype=jnp.int32)[None, None, :]).astype(
        jnp.float32
    )


def local(kernel, results, operands, grid, in_specs, out_specs, scratch=()):
    return pl.pallas_call(
        kernel,
        out_shape=results,
        grid=grid,
        in_specs=in_specs,
        out_specs=out_specs,
        scratch_shapes=list(scratch),
        compiler_params=pltpu.CompilerParams(vmem_limit_bytes=32 * 1024 * 1024),
    )(*operands)


def dot(a, b):
    return jnp.dot(a, b, preferred_element_type=jnp.float32)


def dot_nt(a, b):
    return lax.dot_general(a, b, (((1,), (1,)), ((), ())), preferred_element_type=jnp.float32)


def dot_tn(a, b):
    return lax.dot_general(a, b, (((0,), (0,)), ((), ())), preferred_element_type=jnp.float32)


def low(value):
    return value.astype(jnp.bfloat16)


def head_probs(query, key, bias, valid):
    scores = dot_nt(query, key) * (1.0 / math.sqrt(HDIM))
    if bias is not None:
        scores = scores + bias
    if valid is not None:
        scores = jnp.where(valid, scores, masked)
    expos = jnp.exp(scores - jnp.max(scores, axis=-1, keepdims=True))
    return expos / jnp.sum(expos, axis=-1, keepdims=True)


def head_forward(query, key, value, bias, valid):
    return dot(low(head_probs(query, key, bias, valid)), value)


def head_backward(query, key, value, bias, valid, upstream):
    probs = head_probs(query, key, bias, valid)
    prob_grad = dot_nt(upstream, value)
    inner = jnp.sum(probs * prob_grad, axis=-1, keepdims=True)
    score_grad = low(probs * (prob_grad - inner))
    scale = 1.0 / math.sqrt(HDIM)
    return (
        dot(score_grad, key) * scale,
        dot_tn(score_grad, query) * scale,
        dot_tn(low(probs), upstream),
        score_grad,
    )


def norm_forward(source, gain):
    centered = source - jnp.mean(source, axis=-1, keepdims=True)
    variance = jnp.mean(centered * centered, axis=-1, keepdims=True)
    return centered * lax.rsqrt(variance + epsilon) * gain


def norm_backward(source, gain, upstream):
    centered = source - jnp.mean(source, axis=-1, keepdims=True)
    variance = jnp.mean(centered * centered, axis=-1, keepdims=True)
    inverse = lax.rsqrt(variance + epsilon)
    normal = centered * inverse
    gain_grad = jnp.sum(upstream * normal, axis=0, keepdims=True)
    scaled = upstream * gain
    first = jnp.mean(scaled, axis=-1, keepdims=True)
    second = jnp.mean(scaled * normal, axis=-1, keepdims=True)
    return inverse * (scaled - first - normal * second), gain_grad


def in_weight(packs, index, width):
    per = packs[0].shape[0] // 4
    cols = width // per
    return jnp.concatenate(
        [
            jnp.concatenate(
                [
                    pack[t, s, :, i * cols : (i + 1) * cols]
                    for pack in packs
                    for s in range(pack.shape[1])
                    for i in range(pack.shape[3] // cols)
                ],
                axis=0,
            )
            for t in range(index * per, (index + 1) * per)
        ],
        axis=1,
    )


def out_weight(pack, index, count):
    width = pack.shape[3] // count
    return jnp.concatenate(
        [
            jnp.concatenate(
                [pack[t, s, :, index * width : (index + 1) * width] for t in range(pack.shape[0])],
                axis=0,
            )
            for s in range(pack.shape[1])
        ],
        axis=1,
    )


class Fetch:
    def __init__(self, sources, targets, sem):
        self.copies = [keep(*pair, sem.at[i]) for i, pair in enumerate(zip(sources, targets))]
        self.targets, self.here = targets, set()

    def __call__(self, index):
        if index not in self.here:
            self.here.add(index)
            self.copies[index].wait()
        return self.targets[index]


def fetch_scratch(arrays):
    return [pltpu.VMEM(item.shape, item.dtype) for item in arrays] + dma_sems(len(arrays))


def spatial_forward(rows, weight):
    lines, images, pixels, channels = rows.shape
    width = weight.shape[2]
    count = lines * pixels

    def kernel(x_ref, w_ref, triple_ref, mix_ref):
        x = x_ref[...].reshape(count, channels)
        for j in range(3):
            triple_ref[0, j] = low(dot(x, w_ref[j]))
        for head in range(width // HDIM):
            cols = slice(head * HDIM, (head + 1) * HDIM)
            query, key, value = (triple_ref[0, j, :, cols] for j in range(3))
            mix_ref[0, :, cols] = low(head_forward(query, key, value, None, None))

    return local(
        kernel,
        (
            jax.ShapeDtypeStruct((images, 3, count, width), jnp.bfloat16),
            jax.ShapeDtypeStruct((images, count, width), jnp.bfloat16),
        ),
        (rows, weight),
        (images,),
        [
            pl.BlockSpec((lines, 1, pixels, channels), lambda i: (0, i, 0, 0)),
            pl.BlockSpec(weight.shape, lambda i: (0, 0, 0)),
        ],
        (
            pl.BlockSpec((1, 3, count, width), lambda i: (i, 0, 0, 0)),
            pl.BlockSpec((1, count, width), lambda i: (i, 0, 0)),
        ),
    )


def spatial_backward(rows, weight, triple, upstream):
    lines, images, pixels, channels = rows.shape
    width = weight.shape[2]
    count = lines * pixels

    def kernel(x_ref, w_ref, triple_ref, up_ref, grad_ref, dw_ref, grads_ref, total_ref):
        step = pl.program_id(0)
        x = x_ref[...].reshape(count, channels)
        for head in range(width // HDIM):
            cols = slice(head * HDIM, (head + 1) * HDIM)
            query, key, value = (triple_ref[0, j, :, cols] for j in range(3))
            grads = head_backward(query, key, value, None, None, up_ref[0, :, cols])
            for j in range(3):
                grads_ref[j, :, cols] = low(grads[j])
        part = dot_nt(grads_ref[0], w_ref[0])
        part = part + dot_nt(grads_ref[1], w_ref[1])
        part = part + dot_nt(grads_ref[2], w_ref[2])
        grad_ref[...] = low(part).reshape(lines, 1, pixels, channels)

        @pl.when(step == 0)
        def _():
            total_ref[...] = jnp.zeros_like(total_ref)

        for j in range(3):
            total_ref[j] += dot_tn(x, grads_ref[j])

        @pl.when(step == images - 1)
        def _():
            for j in range(3):
                dw_ref[:, j * width : (j + 1) * width] = low(total_ref[j])

    return local(
        kernel,
        (
            jax.ShapeDtypeStruct((lines, images, pixels, channels), jnp.bfloat16),
            jax.ShapeDtypeStruct((channels, 3 * width), jnp.bfloat16),
        ),
        (rows, weight, triple, upstream),
        (images,),
        [
            pl.BlockSpec((lines, 1, pixels, channels), lambda i: (0, i, 0, 0)),
            pl.BlockSpec(weight.shape, lambda i: (0, 0, 0)),
            pl.BlockSpec((1, 3, count, width), lambda i: (i, 0, 0, 0)),
            pl.BlockSpec((1, count, width), lambda i: (i, 0, 0)),
        ],
        (
            pl.BlockSpec((lines, 1, pixels, channels), lambda i: (0, i, 0, 0)),
            pl.BlockSpec((channels, 3 * width), lambda i: (0, 0)),
        ),
        [
            pltpu.VMEM((3, count, width), jnp.bfloat16),
            pltpu.VMEM((3, channels, width), jnp.float32),
        ],
    )


def dot_exact(a, b):
    return jnp.dot(a, b, preferred_element_type=jnp.float32, precision=highest)


def clip_masks(rows, few, ids_ref, turned_ref):
    across = lax.broadcasted_iota(jnp.int32, (rows, rows), 1)
    down = lax.broadcasted_iota(jnp.int32, (rows, rows), 0)
    return (lax.rem(across, few) == lax.rem(down, few)) & (ids_ref[0] == turned_ref[0])


def temporal_forward(clip, bias, ids, few):
    slots, rows, triple = clip.shape
    width = triple // 3

    def kernel(x_ref, bias_ref, ids_ref, turned_ref, mix_ref):
        valid = clip_masks(rows, few, ids_ref, turned_ref)
        for head in range(width // HDIM):
            at = head * HDIM
            query, key, value = (
                x_ref[0, :, j * width + at : j * width + at + HDIM] for j in range(3)
            )
            mix = head_forward(query, key, value, bias_ref[head], valid)
            mix_ref[0, :, at : at + HDIM] = low(mix)

    return local(
        kernel,
        jax.ShapeDtypeStruct((slots, rows, width), jnp.bfloat16),
        (clip, bias, ids[:, :, None], ids[:, None, :]),
        (slots,),
        [
            pl.BlockSpec((1, rows, triple), lambda i: (i, 0, 0)),
            pl.BlockSpec(bias.shape, lambda i: (0, 0, 0)),
            pl.BlockSpec((1, rows, 1), lambda i: (i, 0, 0)),
            pl.BlockSpec((1, 1, rows), lambda i: (i, 0, 0)),
        ],
        pl.BlockSpec((1, rows, width), lambda i: (i, 0, 0)),
    )


def temporal_backward(clip, bias, ids, few, upstream):
    slots, rows, triple = clip.shape
    width = triple // 3
    frames = rows // few

    def kernel(x_ref, bias_ref, ids_ref, turned_ref, up_ref, grad_ref, score_ref):
        step = pl.program_id(0)
        valid = clip_masks(rows, few, ids_ref, turned_ref)
        frame = lax.broadcasted_iota(jnp.int32, (frames, rows), 0)
        row = lax.broadcasted_iota(jnp.int32, (frames, rows), 1)
        gather = low((row // few == frame).astype(jnp.float32))

        @pl.when(step == 0)
        def _():
            score_ref[...] = jnp.zeros_like(score_ref)

        for head in range(width // HDIM):
            at = head * HDIM
            query, key, value = (
                x_ref[0, :, j * width + at : j * width + at + HDIM] for j in range(3)
            )
            grads = head_backward(
                query, key, value, bias_ref[head], valid, up_ref[0, :, at : at + HDIM]
            )
            for j in range(3):
                grad_ref[0, :, j * width + at : j * width + at + HDIM] = low(grads[j])
            score_ref[head] += dot(gather, grads[3])

    return local(
        kernel,
        (
            jax.ShapeDtypeStruct((slots, rows, triple), jnp.bfloat16),
            jax.ShapeDtypeStruct((bias.shape[0], frames, rows), jnp.float32),
        ),
        (clip, bias, ids[:, :, None], ids[:, None, :], upstream),
        (slots,),
        [
            pl.BlockSpec((1, rows, triple), lambda i: (i, 0, 0)),
            pl.BlockSpec(bias.shape, lambda i: (0, 0, 0)),
            pl.BlockSpec((1, rows, 1), lambda i: (i, 0, 0)),
            pl.BlockSpec((1, 1, rows), lambda i: (i, 0, 0)),
            pl.BlockSpec((1, rows, width), lambda i: (i, 0, 0)),
        ],
        (
            pl.BlockSpec((1, rows, triple), lambda i: (i, 0, 0)),
            pl.BlockSpec((bias.shape[0], frames, rows), lambda i: (0, 0, 0)),
        ),
    )


def gelu_pair(upper):
    rate = math.sqrt(2.0 / math.pi)
    square = upper * upper
    bend = jnp.tanh(rate * (upper + 0.044715 * square * upper))
    half = 0.5 * (1.0 + bend)
    slope = half + 0.5 * upper * (1.0 - bend * bend) * rate * (1.0 + 3.0 * 0.044715 * square)
    return upper * half, slope


def feed_both(rows, cot, w_in, w_out):
    lines, count, channels = rows.shape
    hidden = w_in.shape[1]

    def kernel(x_ref, cot_ref, in_ref, out_ref, y_ref, grad_ref, dw_ref, first_ref, second_ref):
        step = pl.program_id(0)
        x, up = x_ref[0], cot_ref[0]
        active, slope = gelu_pair(dot(x, in_ref[...]))
        active = low(active)
        upper_grad = low(dot_nt(up, out_ref[...]) * slope)
        y_ref[0] = low(dot(active, out_ref[...]))
        grad_ref[0] = low(dot_nt(upper_grad, in_ref[...]))

        @pl.when(step == 0)
        def _():
            first_ref[...] = dot_tn(x, upper_grad)
            second_ref[...] = dot_tn(up, active)

        @pl.when(step > 0)
        def _():
            first_ref[...] += dot_tn(x, upper_grad)
            second_ref[...] += dot_tn(up, active)

        @pl.when(step == lines - 1)
        def _():
            dw_ref[:, :hidden] = low(first_ref[...])
            dw_ref[:, hidden:] = low(second_ref[...])

    block = pl.BlockSpec((1, count, channels), lambda i: (i, 0, 0))
    return local(
        kernel,
        (
            jax.ShapeDtypeStruct(rows.shape, jnp.bfloat16),
            jax.ShapeDtypeStruct(rows.shape, jnp.bfloat16),
            jax.ShapeDtypeStruct((channels, 2 * hidden), jnp.bfloat16),
        ),
        (rows, cot, w_in, w_out),
        (lines,),
        [
            block,
            block,
            pl.BlockSpec(w_in.shape, lambda i: (0, 0)),
            pl.BlockSpec(w_out.shape, lambda i: (0, 0)),
        ],
        (block, block, pl.BlockSpec((channels, 2 * hidden), lambda i: (0, 0))),
        [
            pltpu.VMEM((channels, hidden), jnp.float32),
            pltpu.VMEM((channels, hidden), jnp.float32),
        ],
    )


def twin_sum(partial_sum, mine_ref, theirs_ref, send_sem, recv_sem, work=None):
    mine_ref[...] = low(partial_sum)
    copy = send(mine_ref, theirs_ref, send_sem, recv_sem, {"mp": 1 - lax.axis_index("mp")})
    if work is not None:
        work()
    copy.wait()
    return mine_ref[...].astype(jnp.float32) + theirs_ref[...].astype(jnp.float32)


def chat(kernel, results, operands, rows, channels, swaps, number, scratch=(), far=(), late=()):
    own = []
    if swaps > 0:
        own = [
            pltpu.VMEM((swaps, rows, channels), jnp.bfloat16),
            pltpu.VMEM((swaps, rows, channels), jnp.bfloat16),
        ] + dma_sems(swaps, swaps)
    near, fetched = len(operands), len(far)
    count = near + fetched + len(results)
    late = list(late)
    late_scratch = [pltpu.VMEM(results[i].shape, results[i].dtype) for i in late] + dma_sems(
        len(late)
    )

    def whole(*refs):
        ins, sources = refs[:near], refs[near : near + fetched]
        outs = list(refs[near + fetched : count])
        rest = refs[count:]
        swapped, rest = rest[: len(own)], rest[len(own) :]
        targets, sem, rest = rest[:fetched], rest[fetched], rest[fetched + 1 :]
        held, late_sem, rest = rest[: len(late)], rest[len(late)], rest[len(late) + 1 :]
        fetch = Fetch(sources, targets, sem)
        ends = {place: outs[place] for place in late}
        for place, ref in zip(late, held):
            outs[place] = ref
        written = []

        def flush(*places):
            for place in places:
                index = late.index(place)
                written.append(keep(held[index], ends[place], late_sem.at[index]))

        def swap(index, partial_sum, work=None):
            mine_ref, theirs_ref, send_sem, recv_sem = swapped
            return twin_sum(
                partial_sum,
                mine_ref.at[index],
                theirs_ref.at[index],
                send_sem.at[index],
                recv_sem.at[index],
                work,
            )

        if swaps > 0:
            meet(twin_peers())
        kernel(swap, fetch, flush, *ins, *outs, *rest)
        for copy in written:
            copy.wait()

    specs = [VMEM] * near + [ANY] * fetched
    out_specs = tuple(ANY if i in late else VMEM for i in range(len(results)))
    scratch = own + fetch_scratch(far) + late_scratch + list(scratch)
    if swaps > 0:
        return talk(
            whole, tuple(results), list(operands) + list(far), scratch, number, specs, out_specs, 56
        )
    return pl.pallas_call(
        whole,
        out_shape=tuple(results),
        in_specs=specs,
        out_specs=out_specs,
        scratch_shapes=scratch,
        compiler_params=pltpu.CompilerParams(vmem_limit_bytes=56 * 1024 * 1024),
    )(*operands, *far)


def group_means(totals, count):
    channels = totals.shape[1]
    down = lax.broadcasted_iota(jnp.int32, (channels, channels), 0)
    across = lax.broadcasted_iota(jnp.int32, (channels, channels), 1)
    size = D // G
    same = (down // size == across // size).astype(jnp.float32)
    return dot_exact(totals, same) * (1.0 / (count * size))


def group_normal(source):
    count = source.shape[0]
    centered = source - group_means(jnp.sum(source, axis=0, keepdims=True), count)
    spread = group_means(jnp.sum(centered * centered, axis=0, keepdims=True), count)
    inverse = lax.rsqrt(spread + epsilon)
    return centered * inverse, inverse


def group_step(upstream, normal, inverse):
    count = upstream.shape[0]
    first = group_means(jnp.sum(upstream, axis=0, keepdims=True), count)
    second = group_means(jnp.sum(upstream * normal, axis=0, keepdims=True), count)
    return inverse * (upstream - first - normal * second)


def silu(value):
    return value * jax.nn.sigmoid(value)


def silu_slope(value):
    gate = jax.nn.sigmoid(value)
    return gate * (1.0 + value * (1.0 - gate))


def image_block(shape):
    return pl.BlockSpec((1,) + shape[1:], lambda i: (i, 0, 0))


def group_forward(source, scale, shift):
    def kernel(x_ref, scale_ref, shift_ref, out_ref):
        normal, _ = group_normal(x_ref[0].astype(jnp.float32))
        out_ref[0] = low(silu(normal * scale_ref[0] + shift_ref[0]))

    return local(
        kernel,
        jax.ShapeDtypeStruct(source.shape, jnp.bfloat16),
        (source, scale, shift),
        (source.shape[0],),
        [image_block(source.shape), image_block(scale.shape), image_block(shift.shape)],
        image_block(source.shape),
    )


def group_backward(source, scale, shift, upstream):
    def kernel(x_ref, scale_ref, shift_ref, up_ref, grad_ref, scale_grad_ref, shift_grad_ref):
        normal, inverse = group_normal(x_ref[0].astype(jnp.float32))
        grad = up_ref[0] * silu_slope(normal * scale_ref[0] + shift_ref[0])
        scale_grad_ref[0] = jnp.sum(grad * normal, axis=0, keepdims=True)
        shift_grad_ref[0] = jnp.sum(grad, axis=0, keepdims=True)
        grad_ref[0] = low(group_step(grad * scale_ref[0], normal, inverse))

    return local(
        kernel,
        (
            jax.ShapeDtypeStruct(source.shape, jnp.bfloat16),
            jax.ShapeDtypeStruct(scale.shape, jnp.float32),
            jax.ShapeDtypeStruct(shift.shape, jnp.float32),
        ),
        (source, scale, shift, upstream),
        (source.shape[0],),
        [
            image_block(source.shape),
            image_block(scale.shape),
            image_block(shift.shape),
            image_block(upstream.shape),
        ],
        (image_block(source.shape), image_block(scale.shape), image_block(shift.shape)),
    )


def flat_call(kernel, results, operands):
    return pl.pallas_call(
        kernel,
        out_shape=tuple(results),
        in_specs=[VMEM] * len(operands),
        out_specs=tuple([VMEM] * len(results)),
        compiler_params=pltpu.CompilerParams(vmem_limit_bytes=32 * 1024 * 1024),
    )(*operands)


def store_both(both_ref, value, owners, lines):
    both_ref[0] = value
    if (value.shape[1] // owners) % HDIM != 0:
        return
    size = value.shape[1] // owners
    frames = owners // lines
    both_ref[1] = jnp.concatenate(
        [
            value[:, (t * lines + s) * size : (t * lines + s + 1) * size]
            for s in range(lines)
            for t in range(frames)
        ],
        axis=1,
    )


def both_orders(rows, owners, lines):
    if (rows.shape[1] // owners) % HDIM != 0:
        return jnp.stack([rows, by_owner_line(rows, owners, lines)])

    def kernel(x_ref, both_ref):
        store_both(both_ref, x_ref[...], owners, lines)

    return flat_call(kernel, [jax.ShapeDtypeStruct((2,) + rows.shape, rows.dtype)], [rows])[0]


def first_norm(rows, branch, gain):
    def kernel(swap, fetch, flush, branch_ref, gain_ref, one_ref, normed_ref):
        one = fetch(0)[...].astype(jnp.float32) + branch_ref[...].astype(jnp.float32)
        one_ref[...] = one
        flush(0)
        normed_ref[...] = low(norm_forward(one, gain_ref[...]))

    return chat(
        kernel,
        [
            jax.ShapeDtypeStruct(rows.shape, jnp.float32),
            jax.ShapeDtypeStruct(rows.shape, jnp.bfloat16),
        ],
        [branch, gain],
        *rows.shape,
        0,
        0,
        far=[rows],
        late=[0],
    )


def first_norm_backward(stream, gain, normed_grad, upstream, owners, lines):
    def kernel(swap, fetch, flush, gain_ref, normed_ref, grad_ref, both_ref, dg_ref):
        step, gain_grad = norm_backward(
            fetch(0)[...], gain_ref[...], normed_ref[...].astype(jnp.float32)
        )
        grad = fetch(1)[...] + step
        grad_ref[...] = grad
        flush(0)
        dg_ref[...] = gain_grad
        store_both(both_ref, low(grad), owners, lines)

    grad, both, gain_grad = chat(
        kernel,
        [
            jax.ShapeDtypeStruct(stream.shape, jnp.float32),
            jax.ShapeDtypeStruct((2,) + stream.shape, jnp.bfloat16),
            jax.ShapeDtypeStruct(gain.shape, jnp.float32),
        ],
        [gain, normed_grad],
        *stream.shape,
        0,
        0,
        far=[stream, upstream],
        late=[0],
    )
    if (stream.shape[1] // owners) % HDIM != 0:
        both = jnp.stack([both[0], by_owner_line(both[0], owners, lines)])
    return grad, both, gain_grad


def middle_forward(mix, stream, outs, ins, pairs, valid, gains, number):
    rows, channels = stream.shape
    width = mix.shape[1]
    slots = pairs.shape[0]
    part = rows // slots

    def kernel(
        swap, fetch, flush, mix_ref, x_ref, pairs_ref, valid_ref, gain_ref,
        two_ref, normed_ref, query_ref, cross_ref, three_ref, last_ref, triple_ref,
    ):
        two = x_ref[...] + swap(0, dot(mix_ref[...], out_weight(fetch(0), 0, 2)))
        two_ref[...] = two
        normed_ref[...] = low(norm_forward(two, gain_ref[0:1, :]))
        flush(0, 1)
        query_ref[...] = low(dot(normed_ref[...], in_weight((fetch(1), fetch(2)), 0, width)))
        for slot in range(slots):
            here = slice(slot * part, (slot + 1) * part)
            good = valid_ref[slot] > 0.5
            for head in range(width // HDIM):
                at = head * HDIM
                cross = head_forward(
                    query_ref[here, at : at + HDIM],
                    pairs_ref[slot, :, at : at + HDIM],
                    pairs_ref[slot, :, width + at : width + at + HDIM],
                    None,
                    good,
                )
                cross_ref[here, at : at + HDIM] = low(cross)
        flush(2, 3)
        three = two_ref[...] + swap(1, dot(cross_ref[...], out_weight(fetch(0), 1, 2)))
        three_ref[...] = three
        last_ref[...] = low(norm_forward(three, gain_ref[1:2, :]))
        flush(4, 5)
        for j in range(3):
            weight = in_weight((fetch(1), fetch(2)), 1 + j, width)
            triple_ref[:, j * width : (j + 1) * width] = low(dot(last_ref[...], weight))

    wide = jax.ShapeDtypeStruct((rows, channels), jnp.float32)
    wide_low = jax.ShapeDtypeStruct((rows, channels), jnp.bfloat16)
    thin = jax.ShapeDtypeStruct((rows, width), jnp.bfloat16)
    return chat(
        kernel,
        [wide, wide_low, thin, thin, wide, wide_low, jax.ShapeDtypeStruct((rows, 3 * width), jnp.bfloat16)],
        [mix, stream, pairs, valid, gains],
        rows,
        channels,
        2,
        number,
        far=[outs, *ins],
        late=range(6),
    )


def late_forward(mix, stream, out, gain, number):
    rows, channels = stream.shape

    def kernel(swap, fetch, flush, mix_ref, gain_ref, four_ref, normed_ref):
        part = swap(0, dot(mix_ref[...], out_weight(fetch(0), 0, 1)))
        four = fetch(1)[...] + part
        four_ref[...] = four
        flush(0)
        normed_ref[...] = low(norm_forward(four, gain_ref[...]))

    return chat(
        kernel,
        [
            jax.ShapeDtypeStruct((rows, channels), jnp.float32),
            jax.ShapeDtypeStruct((rows, channels), jnp.bfloat16),
        ],
        [mix, gain],
        rows,
        channels,
        1,
        number,
        far=[out, stream],
        late=[0],
    )


def late_backward(cot, normed_grad, stream, gain, mix, out):
    rows, channels = stream.shape
    width = mix.shape[1]

    def kernel(swap, fetch, flush, up_ref, gain_ref, grad_ref, mix_grad_ref, dw_ref, dg_ref):
        step, gain_grad = norm_backward(
            fetch(0)[...], gain_ref[...], up_ref[...].astype(jnp.float32)
        )
        grad = fetch(1)[...].astype(jnp.float32) + step
        grad_ref[...] = grad
        flush(0)
        dg_ref[...] = gain_grad
        branch = low(grad)
        dw_ref[...] = low(dot_tn(branch, fetch(3)[...]))
        flush(2)
        mix_grad_ref[...] = low(dot_nt(branch, out_weight(fetch(2), 0, 1)))

    return chat(
        kernel,
        [
            jax.ShapeDtypeStruct((rows, channels), jnp.float32),
            jax.ShapeDtypeStruct((rows, width), jnp.bfloat16),
            jax.ShapeDtypeStruct((channels, width), jnp.bfloat16),
            jax.ShapeDtypeStruct((1, channels), jnp.float32),
        ],
        [normed_grad, gain],
        rows,
        channels,
        0,
        0,
        far=[stream, cot, out, mix],
        late=[0, 2],
    )


def middle_backward(
    triple, upstream, three, two, last, normed, query, cross, mix, outs, ins, pairs, valid, gains, number
):
    rows, channels = three.shape
    width = mix.shape[1]
    slots, keys = pairs.shape[0], pairs.shape[1]
    part = rows // slots

    def kernel(
        swap, fetch, flush, pairs_ref, valid_ref, gain_ref,
        grad_ref, mix_grad_ref, pair_grad_ref, query_dw_ref, pair_dw_ref, cross_dw_ref, outs_dw_ref, dg_ref,
        cross_up_ref, dq_ref,
    ):
        def weight_in(index):
            return in_weight((fetch(1), fetch(2)), index, width)

        def temporal_weights():
            last_ref = fetch(3)
            query_dw_ref[...] = low(dot_tn(last_ref[...], triple_ref[:, :width]))
            pair_dw_ref[...] = low(dot_tn(last_ref[...], triple_ref[:, width:]))
            flush(3, 4)

        triple_ref = fetch(9)
        part_sum = dot_nt(triple_ref[:, :width], weight_in(1))
        part_sum = part_sum + dot_nt(triple_ref[:, width : 2 * width], weight_in(2))
        part_sum = part_sum + dot_nt(triple_ref[:, 2 * width :], weight_in(3))
        normed_grad = swap(0, part_sum, temporal_weights)
        step, gain_grad = norm_backward(fetch(10)[...], gain_ref[1:2, :], normed_grad)
        dg_ref[1:2, :] = gain_grad
        grad = fetch(11)[...] + step
        grad_ref[...] = grad
        branch = low(grad)
        cross_up_ref[...] = low(dot_nt(branch, out_weight(fetch(0), 1, 2)))
        query_ref, cross_ref, two_ref = fetch(4), fetch(5), fetch(6)
        normed_ref, mix_ref = fetch(7), fetch(8)
        for slot in range(slots):
            here = slice(slot * part, (slot + 1) * part)
            good = valid_ref[slot] > 0.5
            for head in range(width // HDIM):
                at = head * HDIM
                grads = head_backward(
                    query_ref[here, at : at + HDIM],
                    pairs_ref[slot, :, at : at + HDIM],
                    pairs_ref[slot, :, width + at : width + at + HDIM],
                    None,
                    good,
                    cross_up_ref[here, at : at + HDIM],
                )
                dq_ref[here, at : at + HDIM] = low(grads[0])
                pair_grad_ref[slot, :, at : at + HDIM] = low(grads[1])
                pair_grad_ref[slot, :, width + at : width + at + HDIM] = low(grads[2])

        def cross_weights():
            cross_dw_ref[...] = low(dot_tn(normed_ref[...], dq_ref[...]))
            flush(5)
            outs_dw_ref[:, :width] = low(dot_tn(low(grad_ref[...]), cross_ref[...]))

        normed_grad = swap(1, dot_nt(dq_ref[...], weight_in(0)), cross_weights)
        step, gain_grad = norm_backward(two_ref[...], gain_ref[0:1, :], normed_grad)
        dg_ref[0:1, :] = gain_grad
        grad = grad_ref[...] + step
        grad_ref[...] = grad
        flush(0)
        branch = low(grad)
        outs_dw_ref[:, width:] = low(dot_tn(branch, mix_ref[...]))
        flush(6)
        mix_grad_ref[...] = low(dot_nt(branch, out_weight(fetch(0), 0, 2)))

    return chat(
        kernel,
        [
            jax.ShapeDtypeStruct((rows, channels), jnp.float32),
            jax.ShapeDtypeStruct((rows, width), jnp.bfloat16),
            jax.ShapeDtypeStruct((slots, keys, 2 * width), jnp.bfloat16),
            jax.ShapeDtypeStruct((channels, width), jnp.bfloat16),
            jax.ShapeDtypeStruct((channels, 2 * width), jnp.bfloat16),
            jax.ShapeDtypeStruct((channels, width), jnp.bfloat16),
            jax.ShapeDtypeStruct((channels, 2 * width), jnp.bfloat16),
            jax.ShapeDtypeStruct((2, channels), jnp.float32),
        ],
        [pairs, valid, gains],
        rows,
        channels,
        2,
        number,
        [pltpu.VMEM((rows, width), jnp.bfloat16), pltpu.VMEM((rows, width), jnp.bfloat16)],
        [outs, *ins, last, query, cross, two, normed, mix, triple, three, upstream],
        [0, 3, 4, 5, 6],
    )


def on_device(
    video,
    cotangent,
    text,
    video_ids,
    timesteps,
    text_lengths,
    group_gain,
    group_bias,
    first_conv,
    film_weight,
    second_conv,
    spatial_norm,
    spatial_qkv,
    spatial_out,
    cross_norm,
    cross_query,
    cross_kv,
    cross_out,
    temporal_norm,
    temporal_qkv,
    temporal_out,
    offset_bias,
    feed_norm,
    feed_in,
    feed_out,
):
    frames_axis, lines, cores = (lax.axis_size(name) for name in ("tm", "space", "mp"))
    slots, frame_dev, row_dev, columns, channels = video.shape
    half_width = first_conv.shape[2]
    head_local = half_width // HDIM
    pixels_dev = row_dev * columns
    frames_all = frame_dev * frames_axis
    token_rows = slots * frame_dev * pixels_dev
    text_local = text.shape[1]
    images = slots * frame_dev
    frame_shape = (-1, frame_dev, H, W)
    everyone = ("tm", "space")
    owners = frames_axis * lines
    line_half = lines // 2
    feed_width = feed_in.shape[1] // lines
    text_rows = slots * text_local

    def wide(source):
        return source.reshape(frame_shape + source.shape[2:])

    out_piece = part_of(jnp.concatenate([spatial_out, cross_out, temporal_out], axis=1), "tm", 0)
    if frames_axis == 4:
        in_piece = jnp.concatenate([cross_query[None], temporal_qkv.transpose(1, 0, 2)], axis=0)
        in_piece = lax.dynamic_index_in_dim(in_piece, lax.axis_index("tm"), 0, keepdims=False)
    else:
        in_piece = jnp.concatenate([cross_query, temporal_qkv.reshape(-1, 3 * half_width)], axis=1)
        in_piece = part_of(in_piece, "tm", 1)
    picks = channels % (16 * owners) == 0 and (half_width // lines) % lane == 0
    turned_qkv = spatial_qkv.transpose(1, 0, 2)

    def cut_qkv(whole):
        piece = part_of(whole, "tm", 1)
        return piece.reshape(3, -1, lines, half_width // lines).transpose(2, 0, 1, 3)

    def pick_qkv(ref, place):
        rows = span(lax.axis_index("tm"), channels // owners)
        return ref.at[:, rows, span(place, half_width // lines)]

    def cut_in(whole):
        return part_of(whole, "tm", 0).reshape(-1, lines, feed_width).transpose(1, 0, 2)

    def pick_in(ref, place):
        return ref.at[span(lax.axis_index("tm"), channels // owners), span(place, feed_width)]

    def cut_out(whole):
        return part_of(whole.reshape(lines, feed_width, -1), "tm", 1)

    def pick_out(ref, place):
        return ref.at[span(place * frames_axis + lax.axis_index("tm"), feed_width // frames_axis)]

    def cut_text(whole):
        return whole.reshape(text_rows, frames_axis, -1).transpose(1, 0, 2)

    def pick_text(ref, place):
        return ref.at[:, span(place, ref.shape[1] // frames_axis)]

    def cut_cols(whole):
        return whole.reshape(frames_axis, text_rows, lines, -1).transpose(2, 0, 1, 3)

    def pick_cols(ref, place):
        return ref.at[:, :, span(place, ref.shape[2] // lines)]

    def cut_and_send(source, axes, pick, cut):
        return Exchange(source, axes, pick, cut) if picks else Exchange(cut(source), axes)

    cot_rows = cotangent.reshape(token_rows, channels)
    text_flat = text.reshape(text_rows, -1)
    cross_kv = cross_kv.reshape(cross_kv.shape[0], -1)

    folds = in_piece.shape[0] // out_piece.shape[0]
    in_piece = jnp.concatenate(jnp.split(in_piece, folds, axis=0), axis=1)
    out_cols = out_piece.shape[1]
    pack = jnp.concatenate([out_piece, in_piece], axis=1)
    in_cols = (out_cols, pack.shape[1])
    embed = sinusoid(timesteps).astype(jnp.bfloat16)
    film_part = jnp.einsum(
        "bvc,cjk->bvjk", part_of(embed, "space", 2), film_weight, preferred_element_type=jnp.float32
    )
    film_part = film_part.reshape(slots * VIDS * 2, lines, -1).transpose(1, 0, 2)

    video_rows = video.reshape(token_rows, channels)
    in_groups = (channels // owners) % (D // G) == 0
    video_both = both_orders(video_rows, owners, lines) if in_groups else video_rows
    video_lines, (text_line, qkv_piece, film, pack) = to_lines(
        video_both.reshape(-1, pixels_dev, channels),
        True,
        1,
        [
            LineColumns(text_flat),
            cut_and_send(turned_qkv, ("space",), pick_qkv, cut_qkv),
            Exchange(film_part, ("space",)),
            Keep(pack),
        ],
    )
    pack = lax.all_gather(pack, "space", axis=0, tiled=False)

    def line_gains(whole):
        own = part_of(part_of(whole, "space", 0), "mp", 0)
        if not in_groups:
            return jnp.broadcast_to(own, (images, 1, own.shape[0]))
        owned = part_of(part_of(by_owner_line(whole, owners, lines), "space", 0), "mp", 0)
        return jnp.repeat(jnp.stack([own, owned]), images, axis=0)[:, None]

    gain_line, bias_line = line_gains(group_gain), line_gains(group_bias)
    first_in = group_forward(video_lines, gain_line, bias_line)
    text_part = jnp.dot(
        text_line.reshape(lines * text_rows, -1), cross_kv, preferred_element_type=jnp.float32
    )
    text_part = text_part.astype(jnp.bfloat16).reshape(lines, text_rows, -1)
    first_in, (text_part,) = gather_cores(first_in, 3, [Exchange(text_part, ("space",))])
    if in_groups:
        first_in, first_owned = first_in[:images], first_in[images:]
    else:
        blocks = first_in.reshape(first_in.shape[:2] + (-1, lines, channels // owners))
        blocks = blocks.swapaxes(2, 3).reshape(first_in.shape)
        first_owned = lax.all_to_all(blocks, "space", split_axis=2, concat_axis=2, tiled=True)
    text_part = jnp.sum(text_part.astype(jnp.float32), axis=0).astype(jnp.bfloat16)
    hidden_part = conv_frames(wide(first_in), first_conv, "IHWO", False).astype(jnp.bfloat16)
    hidden, (text_part, qkv_piece) = sum_lines(
        hidden_part.reshape(images, H * W, half_width),
        4,
        [Share(text_part, ("space",)), Share(qkv_piece, ("tm",))],
    )

    film = jnp.sum(film, axis=0).reshape(slots, VIDS, 2, -1)
    frame_ids = part_of(video_ids, "tm", 1)
    choose = (frame_ids[:, :, None] == jnp.arange(VIDS, dtype=jnp.int32)[None, None, :]).astype(
        jnp.float32
    )
    frame_film = jnp.einsum("bfv,bvjk->jbfk", choose, film, precision=highest)
    frame_film = frame_film.reshape(2, images, 1, -1)
    film_scale, film_shift = 1.0 + frame_film[0], frame_film[1]
    second_in = group_forward(hidden, film_scale, film_shift)
    second_wide, (text_pairs, in_first) = gather_lines(
        second_in,
        5,
        [Share(text_part, ("tm",)), Share(pack, ("tm",), 0, line_half, in_cols)],
    )
    text_pairs = (
        text_pairs.reshape(owners, slots, text_local, 2 * half_width)
        .transpose(1, 0, 2, 3)
        .reshape(slots, TXT, 2 * half_width)
    )
    conv_part = conv_frames(wide(second_wide), second_conv, "IHWO", False).astype(jnp.bfloat16)
    conv_half, _ = sum_cores(conv_part.reshape(images, H * W, -1), 6)
    conv_rows, (outs_all,) = from_lines(
        conv_half.astype(jnp.bfloat16),
        True,
        7,
        [Share(pack, ("tm",), cols=(0, out_cols // 3 * 2))],
    )
    spatial_qkv = qkv_piece.transpose(2, 1, 0, 3, 4).reshape(3, channels, -1)

    spatial_gain = spatial_norm[None]
    stream_one, spatial_in = first_norm(
        video_rows, conv_rows.reshape(token_rows, channels), spatial_gain
    )
    spatial_line, (in_rest,) = gather_tokens(
        spatial_in, 8, [Share(pack, ("tm",), line_half, lines - line_half, in_cols)]
    )
    spatial_line = spatial_line.reshape(lines, images, pixels_dev, channels)
    spatial_triple, spatial_mix = spatial_forward(spatial_line, spatial_qkv)
    spatial_mix, (out_last, cot_late, text_cols) = from_lines(
        spatial_mix,
        False,
        9,
        [
            Share(pack, ("tm",), cols=(out_cols // 3 * 2, out_cols)),
            Keep(cot_rows),
            cut_and_send(text_flat, ("tm",), pick_text, cut_text),
        ],
    )
    cot_half = lax.all_gather(part_of(cot_late, "mp", 1), "space", axis=0, tiled=True)

    spatial_mix = spatial_mix.reshape(token_rows, half_width)
    in_all = (in_first, in_rest)
    text_valid = (jnp.arange(TXT, dtype=jnp.int32)[None, :] < text_lengths[:, None])[:, None, :]
    text_valid = text_valid.astype(jnp.float32)
    two_gains = jnp.stack([cross_norm, temporal_norm])
    stream_two, cross_in, cross_queries, cross_mix, stream_three, temporal_in, temporal_triple = (
        middle_forward(
            spatial_mix, stream_one, outs_all, in_all, text_pairs, text_valid, two_gains, 34
        )
    )

    clip_triple, (in_quarter, out_quarter) = to_clips(
        temporal_triple.reshape(slots, frame_dev, pixels_dev, 3 * half_width),
        10,
        [
            cut_and_send(feed_in, ("space",), pick_in, cut_in),
            cut_and_send(feed_out, ("space",), pick_out, cut_out),
        ],
    )
    clip_pixels = clip_triple.shape[2]
    clip_rows = frames_all * clip_pixels
    clip_triple = clip_triple.reshape(slots, clip_rows, 3 * half_width)
    offset_table = offset_onehot(0, frames_all, frames_all)
    clip_frames = jnp.arange(clip_rows, dtype=jnp.int32)[:, None] // clip_pixels
    clip_frames = (clip_frames == jnp.arange(frames_all, dtype=jnp.int32)[None, :]).astype(
        jnp.float32
    )
    clip_bias = jnp.einsum("qkr,rh->hqk", offset_table, offset_bias, precision=highest)
    clip_bias = jnp.einsum("hqk,ck->hqc", clip_bias, clip_frames, precision=highest)
    clip_bias = jnp.einsum("rq,hqc->hrc", clip_frames, clip_bias, precision=highest)
    clip_ids = jnp.repeat(video_ids, clip_pixels, axis=1)
    clip_mix = temporal_forward(clip_triple, clip_bias, clip_ids, clip_pixels)
    temporal_mix, (cot_line, text_cols) = from_clips(
        clip_mix.reshape(slots, frames_all, clip_pixels, half_width),
        11,
        [JoinCores(cot_half), cut_and_send(text_cols, ("space",), pick_cols, cut_cols)],
    )
    temporal_mix = temporal_mix.reshape(token_rows, half_width)

    feed_gain = feed_norm[None]
    stream_four, feed_rows = late_forward(temporal_mix, stream_three, out_last, feed_gain, 35)
    feed_line, (feed_in, feed_out) = gather_tokens(
        feed_rows, 12, [Share(in_quarter, ("tm",)), Share(out_quarter, ("tm",))]
    )
    feed_in = feed_in.transpose(1, 0, 2, 3).reshape(channels, feed_width)
    feed_out = feed_out.transpose(0, 2, 1, 3).reshape(feed_width, channels)
    line_shape = (lines, token_rows, channels)
    final_part, feed_part, feed_grads = feed_both(
        feed_line.reshape(line_shape), cot_line.reshape(line_shape), feed_in, feed_out
    )
    normed_grad, (feed_grads, final_half) = scatter_tokens(
        feed_part.reshape(lines * token_rows, channels),
        14,
        [by_frames(feed_grads), CoreSum(final_part.reshape(lines * token_rows, channels))],
    )

    upstream, mix_grad, temporal_out_grad, feed_norm_grad = late_backward(
        cot_rows, normed_grad, stream_four, feed_gain, temporal_mix, out_last
    )
    clip_up, (feed_grads,) = to_clips(
        mix_grad.reshape(slots, frame_dev, pixels_dev, half_width),
        15,
        [Exchange(feed_grads.reshape(lines, -1, 2 * feed_width), ("space",))],
    )
    clip_grads, score_total = temporal_backward(
        clip_triple,
        clip_bias,
        clip_ids,
        clip_pixels,
        clip_up.reshape(slots, clip_rows, half_width),
    )
    score_total = jnp.einsum("hqc,ck->hqk", score_total, clip_frames, precision=highest)
    offset_bias_grad = jnp.einsum("hqk,qkr->rh", score_total, offset_table, precision=highest)
    triple_grad, (first_grads, final_half) = from_clips(
        clip_grads.reshape(slots, frames_all, clip_pixels, 3 * half_width),
        16,
        [by_frames(temporal_out_grad), LineSum(final_half)],
    )

    (
        upstream,
        mix_grad,
        pair_grad,
        temporal_query_grad,
        temporal_pair_grad,
        cross_query_grad,
        outs_grad,
        two_grads,
    ) = middle_backward(
        triple_grad.reshape(token_rows, 3 * half_width),
        upstream,
        stream_three,
        stream_two,
        temporal_in,
        cross_in,
        cross_queries,
        cross_mix,
        spatial_mix,
        outs_all,
        in_all,
        text_pairs,
        text_valid,
        two_gains,
        36,
    )
    pair_grad = (
        pair_grad.reshape(slots, frames_axis, lines, text_local, 2 * half_width)
        .transpose(1, 2, 0, 3, 4)
        .reshape(frames_axis, lines * text_rows, 2 * half_width)
    )

    mix_line, (pair_grad, second_grads, final_rows) = to_lines(
        mix_grad.reshape(images, pixels_dev, half_width),
        False,
        17,
        [FrameSum(pair_grad), by_frames(temporal_query_grad), JoinCores(final_half)],
    )
    mixed = (stream_four + final_rows.astype(jnp.float32)).astype(jnp.bfloat16)
    spatial_part, spatial_qkv_grad = spatial_backward(
        spatial_line, spatial_qkv, spatial_triple, mix_line
    )
    normed_grad, (pair_grad, third_grads) = scatter_tokens(
        spatial_part.reshape(lines * token_rows, channels),
        18,
        [
            Exchange(pair_grad.reshape(lines, text_rows, 2 * half_width), ("space",)),
            by_frames(temporal_pair_grad),
        ],
    )
    temporal_grads = lax.psum_scatter(
        jnp.concatenate([first_grads, second_grads, third_grads], axis=1),
        "space",
        scatter_dimension=0,
        tiled=True,
    )
    pair_grad = jnp.sum(pair_grad.astype(jnp.float32), axis=0).astype(jnp.bfloat16)
    upstream, branch_both, spatial_norm_grad = first_norm_backward(
        stream_one, spatial_gain, normed_grad, upstream, owners, lines
    )

    branch_line, (fourth_grads, pair_line) = to_lines(
        branch_both.reshape(-1, pixels_dev, channels),
        False,
        19,
        [by_frames(cross_query_grad), Share(pair_grad, ("space",))],
        join=True,
    )
    branch_line, branch_owned = branch_line[:images], branch_line[images:]
    second_conv_grad = conv_weight_grad(wide(second_wide), wide(branch_owned), "kc")
    second_part = conv_frames(wide(branch_line), second_conv, "OHWI", True).astype(jnp.bfloat16)
    second_in_grad, (fifth_grads, pair_all) = sum_lines(
        second_part.reshape(images, H * W, half_width),
        20,
        [by_frames(outs_grad), Share(pair_line, ("tm",))],
    )
    hidden_grad, scale_grad, shift_grad = group_backward(
        hidden, film_scale, film_shift, second_in_grad
    )
    frame_grads = jnp.stack([scale_grad, shift_grad], axis=1).reshape(slots, frame_dev, 2, -1)
    film_rows = jnp.einsum("bfv,bfjk->bvjk", choose, frame_grads, precision=highest)
    film_rows = film_rows.reshape(slots * VIDS * 2, -1)
    text_part = jnp.dot(
        pair_line.reshape(lines * text_rows, -1), cross_kv.T, preferred_element_type=jnp.float32
    )
    text_part = text_part.astype(jnp.bfloat16).reshape(lines, text_rows, -1)

    hidden_wide, (second_conv_grad, film_shares, text_part) = gather_lines(
        hidden_grad,
        21,
        [FrameSum(second_conv_grad, True), Share(film_rows, ("tm",)), Exchange(text_part, ("space",))],
    )
    film_rows = jnp.sum(film_shares, axis=0)
    first_conv_some, first_conv_rest = (
        conv_weight_grad(wide(first_owned), wide(hidden_wide), "ck", taps)
        for taps in (range(5), range(5, 9))
    )
    first_part = conv_frames(wide(hidden_wide), first_conv, "OHWI", True).astype(jnp.bfloat16)
    cross_grads = jnp.concatenate([fourth_grads, fifth_grads], axis=1)
    first_in_grad, (first_conv_some, spatial_qkv_grad, cross_grads, film_shares) = sum_cores(
        first_part.reshape(images, H * W, -1),
        22,
        [
            FrameSum(first_conv_some, True),
            by_frames(spatial_qkv_grad),
            Exchange(cross_grads.reshape(lines, -1, cross_grads.shape[1]), ("space",)),
            Share(film_rows, ("space",)),
        ],
    )
    video_line_grad, gain_grad, bias_grad = group_backward(
        video_lines[:images], gain_line[:images], bias_line[:images], first_in_grad
    )

    def placed(line_grad):
        whole = jnp.zeros((channels,), jnp.float32)
        size = line_grad.shape[2]
        place = (lax.axis_index("space") * cores + lax.axis_index("mp")) * size
        return lax.dynamic_update_slice_in_dim(whole, jnp.sum(line_grad, axis=(0, 1)), place, 0)

    small = jnp.concatenate(
        [
            item.reshape(owners, -1)
            for item in (
                placed(gain_grad),
                placed(bias_grad),
                spatial_norm_grad,
                two_grads[0],
                two_grads[1],
                feed_norm_grad,
                offset_bias_grad,
            )
        ],
        axis=1,
    )
    video_rows_grad, (small, qkv_part, first_conv_rest) = from_lines(
        video_line_grad,
        True,
        23,
        [
            SmallSum(small.reshape(frames_axis, lines, 1, -1)),
            Exchange(spatial_qkv_grad.reshape(lines, -1, spatial_qkv_grad.shape[1]), ("space",)),
            FrameSum(first_conv_rest, True),
        ],
    )
    video_grad = upstream + video_rows_grad.reshape(token_rows, channels).astype(jnp.float32)

    video_film_grad = (
        film_shares.reshape(lines, slots, VIDS, 2, -1)
        .transpose(1, 2, 3, 0, 4)
        .reshape(slots, VIDS, 2, half_width)
    )
    film_weight_grad = jnp.einsum(
        "bvc,bvjk->cjk",
        part_of(part_of(embed, "tm", 2), "space", 2).astype(jnp.float32),
        video_film_grad,
        precision=highest,
    )
    cross_kv_grad = jnp.einsum(
        "prc,prk->ck",
        text_cols.transpose(1, 0, 2, 3).reshape(owners, text_rows, -1),
        pair_all.reshape(owners, text_rows, 2 * half_width),
        preferred_element_type=jnp.float32,
    )
    text_half = part_of(
        twin_add(text_part.transpose(1, 0, 2).reshape(text_rows, -1)), "mp", 1
    )
    small = small[0]
    small_twin = lax.ppermute(small, "mp", [(0, 1), (1, 0)])
    gain_size = channels // owners
    gains = [small[i * gain_size : (i + 1) * gain_size] for i in range(6)]
    for i in range(2):
        gains[i] = gains[i] + small_twin[i * gain_size : (i + 1) * gain_size]
    feed_grads, qkv_part = feed_grads.astype(jnp.float32), qkv_part.astype(jnp.float32)
    owner_rows = feed_grads.shape[1]
    temporal_grads = temporal_grads.astype(jnp.float32)
    cross_grads = jnp.sum(cross_grads.astype(jnp.float32), axis=0)
    first_conv_grad = jnp.concatenate([first_conv_some, first_conv_rest])
    return (
        mixed.reshape(video.shape),
        video_grad.reshape(video.shape),
        text_half.reshape(slots, text_local, -1),
        gains[0],
        gains[1],
        first_conv_grad.astype(jnp.float32).transpose(1, 0, 2),
        film_weight_grad,
        second_conv_grad.astype(jnp.float32).transpose(2, 0, 1),
        gains[2],
        qkv_part.reshape(lines, owner_rows, 3, -1)
        .transpose(1, 2, 0, 3)
        .reshape(owner_rows, 3, half_width),
        cross_grads[:, 2 * half_width :].T,
        gains[3],
        cross_grads[:, :half_width],
        cross_kv_grad.reshape(-1, 2, half_width),
        cross_grads[:, half_width : 2 * half_width].T,
        gains[4],
        temporal_grads[:, half_width:].reshape(-1, 3, half_width),
        temporal_grads[:, :half_width].T,
        small[6 * gain_size :].reshape(R // owners, head_local),
        gains[5],
        feed_grads[:, :, :feed_width].transpose(1, 0, 2).reshape(owner_rows, -1),
        feed_grads[:, :, feed_width:].transpose(0, 2, 1).reshape(-1, owner_rows),
    )


def solution(mesh):
    return jax.shard_map(
        on_device,
        mesh=mesh,
        in_specs=(
            P(None, "tm", "space", None, None),
            P(None, "tm", "space", None, None),
            P(None, ("tm", "space"), None),
            P(),
            P(),
            P(),
            P(),
            P(),
            P("space", None, "mp"),
            P("space", None, "mp"),
            P("mp", None, "space"),
            P(),
            P("space", None, "mp"),
            P("mp", "space"),
            P(),
            P("space", "mp"),
            P("space", None, "mp"),
            P("mp", "space"),
            P(),
            P("space", None, "mp"),
            P("mp", "space"),
            P(None, "mp"),
            P(),
            P("space", "mp"),
            P("mp", "space"),
        ),
        out_specs=(
            P(None, "tm", "space", None, None),
            P(None, "tm", "space", None, None),
            P(None, ("tm", "space"), "mp"),
            P(("tm", "space")),
            P(("tm", "space")),
            P(("tm", "space"), None, "mp"),
            P(("tm", "space"), None, "mp"),
            P("mp", None, ("tm", "space")),
            P(("tm", "space")),
            P(("tm", "space"), None, "mp"),
            P("mp", ("tm", "space")),
            P(("tm", "space")),
            P(("tm", "space"), "mp"),
            P(("tm", "space"), None, "mp"),
            P("mp", ("tm", "space")),
            P(("tm", "space")),
            P(("tm", "space"), None, "mp"),
            P("mp", ("tm", "space")),
            P(("tm", "space"), "mp"),
            P(("tm", "space")),
            P(("tm", "space"), "mp"),
            P("mp", ("tm", "space")),
        ),
        check_vma=False,
    )
```

```python
import math

import jax
import jax.numpy as jnp
from jax import lax
from jax.experimental import pallas as pl
from jax.experimental.pallas import tpu as pltpu
from jax.sharding import PartitionSpec as P

D = 1024
HDIM = 64
TXT = 128
G = 32
R = 128
VIDS = 3
H = 16
W = 16


epsilon = 1e-05
highest = lax.Precision.HIGHEST
masked = -1e30


def twin_add(partial_sum):
    mine = partial_sum.astype(jnp.bfloat16)
    other = lax.ppermute(mine, "mp", [(0, 1), (1, 0)])
    return mine.astype(jnp.float32) + other.astype(jnp.float32)


def part_of(source, axis_name, dim):
    size = source.shape[dim] // lax.axis_size(axis_name)
    return lax.dynamic_slice_in_dim(source, lax.axis_index(axis_name) * size, size, dim)


MESH = pl.DeviceIdType.MESH
lane = 128
ANY = pl.BlockSpec(memory_space=pl.ANY)
VMEM = pl.BlockSpec(memory_space=pltpu.VMEM)


def meet(peers):
    gate = pltpu.get_barrier_semaphore()
    for peer in peers:
        pl.semaphore_signal(gate, inc=1, device_id=peer, device_id_type=MESH)
    pl.semaphore_wait(gate, len(peers))


def others(axis_name):
    count = lax.axis_size(axis_name)
    me = lax.axis_index(axis_name)
    return [(step, lax.rem(me + step, count)) for step in range(1, count)]


def send(source, target, send_sem, recv_sem, peer):
    copy = pltpu.make_async_remote_copy(
        src_ref=source,
        dst_ref=target,
        send_sem=send_sem,
        recv_sem=recv_sem,
        device_id=peer,
        device_id_type=MESH,
    )
    copy.start()
    return copy


def keep(source, target, sem):
    copy = pltpu.make_async_copy(source, target, sem)
    copy.start()
    return copy


def cols_of(ref, index, width):
    return ref.at[:, :, pl.ds(pl.multiple_of(index * width, width), width)]


def rows_of(ref, index, width):
    return ref.at[:, pl.ds(pl.multiple_of(index * width, width), width), :]


def talk(kernel, result, operands, scratch, number, specs=None, out_spec=ANY, grant=32):
    return pl.pallas_call(
        kernel,
        out_shape=result,
        in_specs=[ANY] * len(operands) if specs is None else specs,
        out_specs=out_spec,
        scratch_shapes=scratch,
        compiler_params=pltpu.CompilerParams(
            collective_id=number, has_side_effects=True, vmem_limit_bytes=grant * 1024 * 1024
        ),
    )(*operands)


def dma_sems(*counts):
    return [pltpu.SemaphoreType.DMA((max(count, 1),)) for count in counts]


def flat_index(axes):
    index = 0
    for name in axes:
        index = index * lax.axis_size(name) + lax.axis_index(name)
    return index


def flat_peers(axes):
    count = math.prod(lax.axis_size(name) for name in axes)
    me = flat_index(axes)
    peers = []
    for step in range(1, count):
        peer = lax.rem(me + step, count)
        place, rest = {}, peer
        for name in reversed(axes):
            place[name] = lax.rem(rest, lax.axis_size(name))
            rest = rest // lax.axis_size(name)
        peers.append((step, peer, place))
    return peers


class Rider:
    scratch = ()
    source_spec = ANY
    result_spec = ANY

    def peers(self):
        return [place for _, _, place in flat_peers(self.axes)]

    def middle(self, *refs):
        pass


def square_places():
    me = lax.axis_index("tm")
    near = me + 1 - 2 * lax.rem(me, 2)
    far = me + 2 - 4 * (me // 2)
    return me, near, far, 3 - me


class Exchange(Rider):
    def __init__(self, source, axes, pick=None, cut=None):
        self.source, self.axes, self.cut = source, axes, cut
        self.pick = (lambda ref, place: ref.at[place]) if pick is None else pick
        stack = source if cut is None else jax.eval_shape(cut, source)
        count = math.prod(lax.axis_size(name) for name in axes)
        self.result = jax.ShapeDtypeStruct(stack.shape, stack.dtype)
        self.scratch = dma_sems(count - 1, count - 1, 1)

    def plain(self):
        stack = self.source if self.cut is None else self.cut(self.source)
        return lax.all_to_all(stack, self.axes, split_axis=0, concat_axis=0, tiled=True)

    def start(self, x_ref, out_ref, send_sem, recv_sem, own_sem):
        me = flat_index(self.axes)
        self.copies = [
            send(self.pick(x_ref, peer), out_ref.at[me], send_sem.at[i - 1], recv_sem.at[i - 1], place)
            for i, peer, place in flat_peers(self.axes)
        ]
        self.copies.append(keep(self.pick(x_ref, me), out_ref.at[me], own_sem.at[0]))

    def finish(self, *refs):
        for copy in self.copies:
            copy.wait()


class ColumnJoin(Rider):
    axes = ("space",)

    def __init__(self, source, pick, cut):
        self.source, self.pick, self.cut = source, pick, cut
        stack = jax.eval_shape(cut, source)
        self.lines, self.width = stack.shape[0], stack.shape[-1]
        shape = stack.shape[1:-1] + (self.lines * self.width,)
        self.result = jax.ShapeDtypeStruct(shape, stack.dtype)
        self.scratch = dma_sems(self.lines - 1, self.lines - 1, 1)

    def plain(self):
        stack = lax.all_to_all(
            self.cut(self.source), "space", split_axis=0, concat_axis=0, tiled=True
        )
        return jnp.concatenate([stack[i] for i in range(self.lines)], axis=-1)

    def start(self, x_ref, out_ref, send_sem, recv_sem, own_sem):
        me = lax.axis_index("space")
        cols = span(me, self.width)
        target = out_ref.at[:, cols] if len(self.result.shape) == 2 else out_ref.at[:, :, cols]
        self.copies = [
            send(self.pick(x_ref, peer), target, send_sem.at[i - 1], recv_sem.at[i - 1], {"space": peer})
            for i, peer in others("space")
        ]
        self.copies.append(keep(self.pick(x_ref, me), target, own_sem.at[0]))

    def finish(self, *refs):
        for copy in self.copies:
            copy.wait()


def span(index, size):
    return pl.ds(pl.multiple_of(index * size, size), size)


class LineSum(Rider):
    axes = ("space",)
    source_spec = VMEM
    result_spec = VMEM

    def __init__(self, source, kind=jnp.bfloat16):
        self.source = source
        self.lines = lax.axis_size("space")
        self.rows, self.width = source.shape[0] // self.lines, source.shape[1]
        self.result = jax.ShapeDtypeStruct((self.rows, self.width), kind)
        self.scratch = [
            pltpu.VMEM((self.lines - 1, self.rows, self.width), jnp.bfloat16)
        ] + dma_sems(self.lines - 1, self.lines - 1)

    def plain(self):
        total = lax.psum_scatter(self.source, "space", scatter_dimension=0, tiled=True)
        return total.astype(self.result.dtype)

    def start(self, x_ref, out_ref, got_ref, send_sem, recv_sem):
        self.copies = [
            send(x_ref.at[span(peer, self.rows)], got_ref.at[i - 1], send_sem.at[i - 1], recv_sem.at[i - 1], {"space": peer})
            for i, peer in others("space")
        ]

    def finish(self, x_ref, out_ref, got_ref, *sems):
        for copy in self.copies:
            copy.wait()
        total = x_ref[span(lax.axis_index("space"), self.rows)].astype(jnp.float32)
        for step in range(self.lines - 1):
            total = total + got_ref[step].astype(jnp.float32)
        out_ref[...] = total.astype(out_ref.dtype)


class Share(Rider):
    def __init__(self, source, axes, first=0, size=None, cols=None):
        self.source, self.axes = source, axes
        self.first, self.size, self.cols = first, size, cols
        count = math.prod(lax.axis_size(name) for name in axes)
        shape = source.shape if size is None else (size,) + source.shape[1:]
        if cols is not None:
            shape = shape[:-1] + (cols[1] - cols[0],)
        self.shape = shape
        self.result = jax.ShapeDtypeStruct((count,) + shape, source.dtype)
        even = (len(shape) > 2 and shape[0] % 2 == 0) or shape[-2] % 32 == 0
        self.square = axes == ("tm",) and count == 4 and even
        copies = 4 if self.square else count - 1
        self.scratch = dma_sems(copies, copies, 1)

    def plain(self):
        source = self.source
        if self.size is not None:
            source = source[self.first : self.first + self.size]
        if self.cols is not None:
            source = source[..., self.cols[0] : self.cols[1]]
        return lax.all_gather(source, self.axes, axis=0, tiled=False)

    def half(self, ref, index):
        if len(self.shape) > 2 and self.shape[0] % 2 == 0:
            size = self.shape[0] // 2
            return ref.at[pl.ds(index * size, size)]
        size = self.shape[-2] // 2
        rows = pl.ds(index * size, size)
        return ref.at[:, rows] if len(self.shape) == 3 else ref.at[rows]

    def start(self, x_ref, out_ref, send_sem, recv_sem, own_sem):
        part = x_ref if self.size is None else x_ref.at[pl.ds(self.first, self.size)]
        if self.cols is not None:
            part = part.at[:, :, pl.ds(self.cols[0], self.cols[1] - self.cols[0])]
        if self.square:
            me, near, far, _ = square_places()
            self.copies = [
                send(part, out_ref.at[me], send_sem.at[i], recv_sem.at[i], {"tm": peer})
                for i, peer in enumerate((near, far))
            ]
        else:
            me = flat_index(self.axes)
            self.copies = [
                send(part, out_ref.at[me], send_sem.at[i - 1], recv_sem.at[i - 1], place)
                for i, _, place in flat_peers(self.axes)
            ]
        self.own = keep(part, out_ref.at[me], own_sem.at[0])

    def middle(self, x_ref, out_ref, send_sem, recv_sem, own_sem):
        if not self.square:
            return
        _, near, far, _ = square_places()
        from_near, from_far = self.copies
        from_far.wait_recv()
        got = self.half(out_ref.at[far], 0)
        to_near = send(got, got, send_sem.at[2], recv_sem.at[2], {"tm": near})
        from_near.wait_recv()
        got = self.half(out_ref.at[near], 1)
        to_far = send(got, got, send_sem.at[3], recv_sem.at[3], {"tm": far})
        self.passed = [to_near, to_far]

    def finish(self, *refs):
        if self.square:
            for copy in self.copies:
                copy.wait_send()
            for copy in self.passed:
                copy.wait()
        else:
            for copy in self.copies:
                copy.wait()
        self.own.wait()


class JoinCores(Rider):
    def __init__(self, source):
        self.source = source
        self.rows, self.width = source.shape
        shape = (self.rows, self.width * lax.axis_size("mp"))
        self.result = jax.ShapeDtypeStruct(shape, source.dtype)
        self.scratch = dma_sems(1, 1, 1)

    def peers(self):
        return twin_peers()

    def plain(self):
        return lax.all_gather(self.source, "mp", axis=1, tiled=True)

    def start(self, x_ref, out_ref, send_sem, recv_sem, own_sem):
        core = lax.axis_index("mp")
        mine = out_ref.at[:, pl.ds(pl.multiple_of(core * self.width, self.width), self.width)]
        self.copies = [
            send(x_ref, mine, send_sem.at[0], recv_sem.at[0], {"mp": 1 - core}),
            keep(x_ref, mine, own_sem.at[0]),
        ]

    def finish(self, *refs):
        for copy in self.copies:
            copy.wait()


class LineColumns(Rider):
    axes = ("space",)

    def __init__(self, source):
        self.source = source
        lines = lax.axis_size("space")
        self.width = source.shape[1] // lines
        shape = (lines, source.shape[0], self.width)
        self.result = jax.ShapeDtypeStruct(shape, source.dtype)
        self.scratch = dma_sems(lines - 1, lines - 1, 1)

    def plain(self):
        return lax.all_to_all(
            self.source[None], "space", split_axis=2, concat_axis=0, tiled=True
        )

    def start(self, x_ref, out_ref, send_sem, recv_sem, own_sem):
        me = lax.axis_index("space")

        def part(index):
            return x_ref.at[:, pl.ds(pl.multiple_of(index * self.width, self.width), self.width)]

        self.copies = [
            send(part(peer), out_ref.at[me], send_sem.at[i - 1], recv_sem.at[i - 1], {"space": peer})
            for i, peer in others("space")
        ]
        self.copies.append(keep(part(me), out_ref.at[me], own_sem.at[0]))

    def finish(self, *refs):
        for copy in self.copies:
            copy.wait()


class FrameSum(Rider):
    axes = ("tm",)
    result_spec = VMEM

    def __init__(self, source, taps=False, first=0, size=None, kind=jnp.bfloat16):
        self.taps, self.first = taps, first
        self.count = lax.axis_size("tm")
        if taps:
            self.layers, all_rows, self.width = source.shape
            self.layers = self.layers if size is None else size
            self.rows = all_rows // self.count
        else:
            self.layers, (_, self.rows, self.width) = 1, source.shape
        self.source = source
        shape = (self.layers, self.rows, self.width)
        self.result = jax.ShapeDtypeStruct(shape if taps else shape[1:], kind)
        self.square = self.count == 4 and self.rows % 32 == 0
        self.split = self.rows // 2 if self.square else self.rows
        half = (self.layers, self.split, self.width)
        if self.square:
            self.scratch = [
                pltpu.VMEM((2, 2) + half, jnp.bfloat16),
                pltpu.VMEM((2,) + half, jnp.bfloat16),
                pltpu.VMEM((2, 2) + half, jnp.bfloat16),
            ] + dma_sems(4, 6, 6)
        else:
            self.scratch = [
                pltpu.VMEM((max(self.count - 1, 1),) + half, jnp.bfloat16),
                pltpu.VMEM((1, 1) + half, jnp.bfloat16),
            ] + dma_sems(1, self.count - 1, self.count - 1)

    def plain(self):
        dim = 1 if self.taps else 0
        source = self.source
        if self.taps:
            source = source[self.first : self.first + self.layers]
        total = lax.psum_scatter(source, "tm", scatter_dimension=dim, tiled=True)
        return (total if self.taps else total[0]).astype(self.result.dtype)

    def view(self, w_ref, place, half):
        if self.taps:
            start = pl.multiple_of(place * self.rows + half * self.split, self.split)
            return w_ref.at[pl.ds(self.first, self.layers), pl.ds(start, self.split)]
        return w_ref.at[pl.ds(place, 1), pl.ds(half * self.split, self.split)]

    def add(self, target_ref, first, *rest):
        block = min(16, self.split)
        steps = self.split // block

        def some(index, carry):
            layer = index // steps
            rows = pl.ds(pl.multiple_of(lax.rem(index, steps) * block, block), block)
            total = first[layer, rows].astype(jnp.float32)
            for other in rest:
                total = total + other[layer, rows].astype(jnp.float32)
            target_ref[layer, rows] = total.astype(target_ref.dtype)
            return carry

        lax.fori_loop(0, self.layers * steps, some, 0)

    def out_view(self, out_ref, half):
        rows = pl.ds(half * self.split, self.split)
        if self.taps:
            return out_ref.at[:, rows]
        return out_ref.reshape(1, self.rows, self.width).at[:, rows]

    def start(self, w_ref, out_ref, got_ref, *rest):
        near_ref, own_sem, send_sem, recv_sem = rest[-4:]
        if not self.square:
            me = lax.axis_index("tm")
            self.copies = [
                send(self.view(w_ref, peer, 0), got_ref.at[i - 1], send_sem.at[i - 1], recv_sem.at[i - 1], {"tm": peer})
                for i, peer in others("tm")
            ]
            self.own = [keep(self.view(w_ref, me, 0), near_ref.at[0, 0], own_sem.at[0])]
            return
        me, near, far, across = square_places()
        self.copies = [
            send(self.view(w_ref, place, half), got_ref.at[half, i], send_sem.at[2 * half + i], recv_sem.at[2 * half + i], {"tm": peer})
            for half, peer in ((0, near), (1, far))
            for i, place in ((1, across), (0, peer))
        ]
        self.own = [
            keep(self.view(w_ref, place, half), near_ref.at[half, i], own_sem.at[2 * half + i])
            for half, peer in ((0, far), (1, near))
            for i, place in ((0, me), (1, peer))
        ]

    def middle(self, w_ref, out_ref, got_ref, *rest):
        if not self.square:
            return
        last_ref, near_ref, _, send_sem, recv_sem = rest
        _, near, far, _ = square_places()
        self.passed = []
        for half, peer in ((0, far), (1, near)):
            self.copies[2 * half].wait_recv()
            self.own[2 * half + 1].wait()
            self.add(got_ref.at[half, 1], near_ref.at[half, 1], got_ref.at[half, 1])
            self.passed.append(
                send(got_ref.at[half, 1], last_ref.at[half], send_sem.at[4 + half], recv_sem.at[4 + half], {"tm": peer})
            )

    def finish(self, w_ref, out_ref, got_ref, *rest):
        near_ref = rest[-4]
        if not self.square:
            for copy in self.copies + self.own:
                copy.wait()
            parts = [got_ref.at[i] for i in range(self.count - 1)]
            self.add(self.out_view(out_ref, 0), near_ref.at[0, 0], *parts)
            return
        last_ref = rest[0]
        for half in range(2):
            self.copies[2 * half].wait_send()
            self.copies[2 * half + 1].wait()
            self.own[2 * half].wait()
            self.passed[half].wait()
            self.add(
                self.out_view(out_ref, half),
                near_ref.at[half, 0],
                got_ref.at[half, 0],
                last_ref.at[half],
            )


class SmallSum(Rider):
    source_spec = VMEM
    result_spec = VMEM

    def __init__(self, source):
        self.source = source
        self.frames, self.lines = source.shape[:2]
        part = source.shape[1:]
        self.result = jax.ShapeDtypeStruct(part[1:], source.dtype)
        self.scratch = [
            pltpu.VMEM((self.frames - 1,) + part, source.dtype),
            pltpu.VMEM(part, source.dtype),
            pltpu.VMEM((self.lines - 1,) + part[1:], source.dtype),
        ] + dma_sems(self.frames - 1, self.frames - 1, self.lines - 1, self.lines - 1)

    def peers(self):
        return frame_peers() + line_peers()

    def plain(self):
        total = lax.psum_scatter(self.source, "tm", scatter_dimension=0, tiled=True)[0]
        return lax.psum_scatter(total, "space", scatter_dimension=0, tiled=True)[0]

    def start(self, x_ref, out_ref, got_ref, sum_ref, last_ref, send_sem, recv_sem, send2, recv2):
        self.copies = [
            send(x_ref.at[peer], got_ref.at[i - 1], send_sem.at[i - 1], recv_sem.at[i - 1], {"tm": peer})
            for i, peer in others("tm")
        ]

    def middle(self, x_ref, out_ref, got_ref, sum_ref, last_ref, send_sem, recv_sem, send2, recv2):
        total = x_ref[lax.axis_index("tm")]
        for i, copy in enumerate(self.copies):
            copy.wait()
            total = total + got_ref[i]
        sum_ref[...] = total
        self.passed = [
            send(sum_ref.at[peer], last_ref.at[i - 1], send2.at[i - 1], recv2.at[i - 1], {"space": peer})
            for i, peer in others("space")
        ]

    def finish(self, x_ref, out_ref, got_ref, sum_ref, last_ref, *sems):
        total = sum_ref[lax.axis_index("space")]
        for i, copy in enumerate(self.passed):
            copy.wait()
            total = total + last_ref[i]
        out_ref[...] = total


class Keep(Rider):
    def __init__(self, source):
        self.source = source
        self.result = jax.ShapeDtypeStruct(source.shape, source.dtype)
        self.scratch = dma_sems(1)

    def peers(self):
        return []

    def plain(self):
        return self.source

    def start(self, x_ref, out_ref, own_sem):
        self.copy = keep(x_ref, out_ref, own_sem.at[0])

    def finish(self, *refs):
        self.copy.wait()


class CoreSum(Rider):
    source_spec = VMEM
    result_spec = VMEM

    def __init__(self, source):
        self.source = source
        rows, channels = source.shape
        self.rows, self.width = rows, channels // lax.axis_size("mp")
        self.result = jax.ShapeDtypeStruct((rows, self.width), jnp.bfloat16)
        self.scratch = [pltpu.VMEM((rows, self.width), jnp.bfloat16)] + dma_sems(1, 1)

    def peers(self):
        return twin_peers()

    def start(self, x_ref, out_ref, got_ref, send_sem, recv_sem):
        core = lax.axis_index("mp")
        theirs = pl.ds(pl.multiple_of((1 - core) * self.width, self.width), self.width)
        self.copy = send(x_ref.at[:, theirs], got_ref, send_sem.at[0], recv_sem.at[0], {"mp": 1 - core})

    def finish(self, x_ref, out_ref, got_ref, *sems):
        self.copy.wait()
        block = min(128, self.rows)
        start = lax.axis_index("mp") * self.width
        mine = pl.ds(pl.multiple_of(start, self.width), self.width)

        def some(index, carry):
            rows = pl.ds(pl.multiple_of(index * block, block), block)
            total = x_ref[rows, mine].astype(jnp.float32) + got_ref[rows, :].astype(jnp.float32)
            out_ref[rows, :] = total.astype(jnp.bfloat16)
            return carry

        lax.fori_loop(0, self.rows // block, some, 0)


def plain_all(riders):
    return [rider.plain() for rider in riders]


def talk_many(kernel, peers, results, operands, scratch, number, riders, specs, out_specs):
    inputs, outputs, own_scratch, count = len(operands), len(results), len(scratch), len(riders)

    def whole(*refs):
        ins, rider_ins = refs[:inputs], refs[inputs : inputs + count]
        outs = refs[inputs + count : inputs + count + outputs]
        rider_outs = refs[inputs + count + outputs : inputs + 2 * count + outputs]
        rest = refs[inputs + 2 * count + outputs :]
        mine, rest = rest[:own_scratch], rest[own_scratch:]
        packs = []
        for rider, x_ref, y_ref in zip(riders, rider_ins, rider_outs):
            packs.append((x_ref, y_ref) + tuple(rest[: len(rider.scratch)]))
            rest = rest[len(rider.scratch) :]
        meet(peers() + [peer for rider in riders for peer in rider.peers()])
        for rider, pack in zip(riders, packs):
            rider.start(*pack)
        waiting = list(zip(riders, packs))

        def hook():
            while waiting:
                rider, pack = waiting.pop(0)
                rider.middle(*pack)

        kernel(hook, *ins, *outs, *mine)
        hook()
        for rider, pack in zip(riders, packs):
            rider.finish(*pack)

    done = talk(
        whole,
        tuple(results) + tuple(rider.result for rider in riders),
        list(operands) + [rider.source for rider in riders],
        scratch + [item for rider in riders for item in rider.scratch],
        number,
        list(specs) + [rider.source_spec for rider in riders],
        tuple(out_specs) + tuple(rider.result_spec for rider in riders),
    )
    return list(done[:outputs]), list(done[outputs:])


def talk_with(kernel, peers, result, operands, scratch, number, riders, specs=None, out_spec=ANY):
    if number is None:
        return kernel, peers, result, scratch
    specs = [ANY] * len(operands) if specs is None else specs
    done, others_done = talk_many(
        kernel, peers, [result], operands, scratch, number, riders, specs, [out_spec]
    )
    return done[0], others_done


def line_peers():
    return [{"space": peer} for _, peer in others("space")]


def frame_peers():
    return [{"tm": peer} for _, peer in others("tm")]


def twin_peers():
    return [{"mp": 1 - lax.axis_index("mp")}]


pieces_per_chunk = 2


def relay_gather(lines, own, slot, sems, hook, arrived=None):
    me = lax.axis_index("space")
    right_send, right_recv, left_send, left_recv = sems
    parts = pieces_per_chunk

    def move(step, part, sign, send_sem, recv_sem):
        place = slot(lax.rem(me - sign * step + lines, lines), part)
        at = step * parts + part
        return pltpu.make_async_remote_copy(
            own(part) if step == 0 else place, place, send_sem.at[at], recv_sem.at[at],
            device_id={"space": lax.rem(me + sign + lines, lines)}, device_id_type=MESH,
        )

    def came(step, part, sign, recv_sem, order):
        place = slot(lax.rem(me - sign * (step + 1) + lines, lines), part)
        at = step * parts + part
        pltpu.make_async_remote_copy(
            place, place, recv_sem.at[at], recv_sem.at[at],
            device_id={"space": lax.rem(me + 1, lines)}, device_id_type=MESH,
        ).wait_recv()
        if arrived is not None:
            arrived(place, order * parts + part)

    ways = (
        (1, me, right_send, right_recv, 0),
        (-1, lines - 1 - me, left_send, left_recv, lines - 1),
    )
    for step in range(lines):
        for part in range(parts):
            for sign, rank, send_sem, recv_sem, order in ways:
                if step > 0:

                    @pl.when(rank >= step)
                    def _():
                        came(step - 1, part, sign, recv_sem, order + step - 1)

                if step < lines - 1:

                    @pl.when((rank >= step) & (rank + 1 < lines))
                    def _():
                        move(step, part, sign, send_sem, recv_sem).start()

        if step == max(lines - 2, 0):
            hook()
    for step in range(lines - 1):
        for part in range(parts):
            for sign, rank, send_sem, recv_sem, _ in ways:

                @pl.when((rank >= step) & (rank + 1 < lines))
                def _():
                    move(step, part, sign, send_sem, recv_sem).wait_send()


def relay_sum(lines, stage_ref, right_ref, left_ref, sems, hook, ready=None):
    me = lax.axis_index("space")
    right_send, right_recv, left_send, left_recv = sems
    parts, last = pieces_per_chunk, lines - 1

    def move(source, slots, sem_out, sem_in, step, part, peer):
        at = step * parts + part
        return pltpu.make_async_remote_copy(
            source, slots.at[step, part], sem_out.at[at], sem_in.at[at],
            device_id={"space": lax.rem(peer + lines, lines)}, device_id_type=MESH,
        )

    def add(slots, step, part, place):
        total = slots[step, part].astype(jnp.float32) + stage_ref[place, part].astype(jnp.float32)
        slots[step, part] = total.astype(jnp.bfloat16)

    ways = (
        (me, me + 1, right_ref, right_send, right_recv, lambda step: last - step + me),
        (last - me, me - 1, left_ref, left_send, left_recv, lambda step: step - last + me),
    )
    for step in range(last):
        if ready is not None:
            ready(step)
        for part in range(parts):
            for rank, peer, slots, sem_out, sem_in, target in ways:
                place = lax.rem(target(step) + 2 * lines, lines)

                @pl.when(rank == 0)
                def _():
                    move(stage_ref.at[place, part], slots, sem_out, sem_in, step, part, peer).start()

                if step > 0:

                    @pl.when((rank > 0) & (rank <= step))
                    def _():
                        source = stage_ref.at[place, part]
                        move(source, slots, sem_out, sem_in, step - 1, part, peer).wait_recv()
                        add(slots, step - 1, part, place)
                        source = slots.at[step - 1, part]
                        move(source, slots, sem_out, sem_in, step, part, peer).start()

        if step == last - 1:
            hook()
    for part in range(parts):
        for rank, peer, slots, sem_out, sem_in, target in ways:

            @pl.when(rank > 0)
            def _():
                move(stage_ref.at[0, part], slots, sem_out, sem_in, last - 1, part, peer).wait_recv()

            for step in range(last):

                @pl.when(rank <= step)
                def _():
                    move(stage_ref.at[0, part], slots, sem_out, sem_in, step, part, peer).wait_send()


def to_lines(source, per_core, number, riders=(), join=False):
    images, pixels, channels = source.shape
    lines, cores = lax.axis_size("space"), lax.axis_size("mp")
    pieces = lines * cores if per_core or join else lines
    width = channels // pieces
    if width % lane != 0 or pixels % 16 != 0:
        if number is None:
            return None
        if per_core:
            parts = source.reshape(images, pixels, lines, cores, width)
            parts = lax.dynamic_index_in_dim(parts, lax.axis_index("mp"), 3, keepdims=False)
            source = parts.reshape(images, pixels, lines * width)
        moved = lax.all_to_all(source, "space", split_axis=2, concat_axis=1, tiled=True)
        return moved, plain_all(riders)

    def kernel(hook, x_ref, out_ref, stage_ref, send_sem, recv_sem, pass_sem, gain_sem, own_sem):
        me, core = lax.axis_index("space"), lax.axis_index("mp")
        twin = {"mp": 1 - core}
        place = (lambda s: s * cores + core) if per_core or join else (lambda s: s)

        def spot(origin):
            rows = rows_of(out_ref, origin, pixels)
            return cols_of(rows, core, width) if join else rows

        copies = []
        for i, peer in others("space"):
            start = pl.multiple_of(place(peer) * width, width)
            stage_ref[i - 1] = x_ref[:, :, pl.ds(start, width)]
            copies.append(
                send(stage_ref.at[i - 1], spot(me), send_sem.at[i - 1], recv_sem.at[i - 1], {"space": peer})
            )
        if join:
            own_width = cores * width
            own = keep(cols_of(x_ref, me, own_width), rows_of(out_ref, me, pixels), own_sem.at[0])
        else:
            own = keep(cols_of(x_ref, place(me), width), spot(me), own_sem.at[0])
        hook()
        passed = []
        for step in range(1, lines):
            copies[step - 1].wait_recv()
            if join:
                got = spot(lax.rem(me - step + lines, lines))
                passed.append(send(got, got, pass_sem.at[step - 1], gain_sem.at[step - 1], twin))
        for copy in copies:
            copy.wait_send()
        own.wait()
        for copy in passed:
            copy.wait()

    def peers():
        return line_peers() + (twin_peers() if join else [])

    held = cores * width if join else width
    result = jax.ShapeDtypeStruct((images, lines * pixels, held), source.dtype)
    scratch = [pltpu.VMEM((lines - 1, images, pixels, width), source.dtype)]
    scratch = scratch + dma_sems(lines - 1, lines - 1, lines - 1, lines - 1, 1)
    return talk_with(kernel, peers, result, [source], scratch, number, riders, [VMEM])


def from_lines(source, per_core, number, riders=()):
    images, line_pixels, width = source.shape
    lines, cores = lax.axis_size("space"), lax.axis_size("mp")
    pixels = line_pixels // lines
    pieces = lines * cores if per_core else lines
    if width % lane != 0 or pixels % 16 != 0:
        if number is None:
            return None
        part = lax.all_to_all(source, "space", split_axis=1, concat_axis=2, tiled=True)
        if per_core:
            part = part.reshape(images, pixels, lines, 1, width)
            part = lax.all_gather(part, "mp", axis=3, tiled=True)
        return part.reshape(images, pixels, pieces * width), plain_all(riders)

    def kernel(hook, x_ref, out_ref, got_ref, send_sem, recv_sem, pass_sem, gain_sem):
        me, core = lax.axis_index("space"), lax.axis_index("mp")
        twin = {"mp": 1 - core}
        mine = core if per_core else 0
        copies = [
            send(rows_of(x_ref, peer, pixels), got_ref.at[me, mine], send_sem.at[i - 1], recv_sem.at[i - 1], {"space": peer})
            for i, peer in others("space")
        ]
        passed = []
        if per_core:
            passed.append(
                send(rows_of(x_ref, me, pixels), got_ref.at[me, core], pass_sem.at[0], gain_sem.at[0], twin)
            )
        got_ref[me, mine] = x_ref[:, pl.ds(pl.multiple_of(me * pixels, pixels), pixels), :]
        hook()
        for step in range(1, lines):
            copies[step - 1].wait_recv()
            if per_core:
                got = got_ref.at[lax.rem(me - step + lines, lines), core]
                passed.append(send(got, got, pass_sem.at[step], gain_sem.at[step], twin))
        for copy in copies:
            copy.wait_send()
        for copy in passed:
            copy.wait()
        each = pieces // lines
        for piece in range(pieces):
            out_ref[:, :, piece * width : (piece + 1) * width] = got_ref[piece // each, piece % each]

    def peers():
        return line_peers() + ([{"mp": 1 - lax.axis_index("mp")}] if per_core else [])

    result = jax.ShapeDtypeStruct((images, pixels, pieces * width), source.dtype)
    scratch = [pltpu.VMEM((lines, pieces // lines, images, pixels, width), source.dtype)]
    scratch = scratch + dma_sems(lines - 1, lines - 1, lines, lines)
    return talk_with(kernel, peers, result, [source], scratch, number, riders, [VMEM], VMEM)


def gather_lines(source, number, riders=()):
    images, line_pixels, width = source.shape
    lines = lax.axis_size("space")
    if width % lane != 0:
        return lax.all_gather(source, "space", axis=2, tiled=True), plain_all(riders)

    def kernel(hook, x_ref, out_ref, got_ref, *sems):
        some = images // pieces_per_chunk

        def own(part):
            return x_ref.at[pl.ds(part * some, some)]

        def slot(index, part):
            return got_ref.at[index, pl.ds(part * some, some)]

        got_ref[lax.axis_index("space")] = x_ref[...]
        relay_gather(lines, own, slot, sems, hook)
        for line in range(lines):
            out_ref[:, :, line * width : (line + 1) * width] = got_ref[line]

    result = jax.ShapeDtypeStruct((images, line_pixels, lines * width), source.dtype)
    scratch = [pltpu.VMEM((lines,) + source.shape, source.dtype)]
    scratch = scratch + dma_sems(*[pieces_per_chunk * (lines - 1)] * 4)
    return talk_with(kernel, line_peers, result, [source], scratch, number, riders, [VMEM], VMEM)


def gather_cores(source, number, riders=()):
    images, line_pixels, width = source.shape
    cores = lax.axis_size("mp")
    if width % lane != 0:
        return lax.all_gather(source, "mp", axis=2, tiled=True), plain_all(riders)

    def kernel(hook, x_ref, out_ref, send_sem, recv_sem, own_sem):
        core = lax.axis_index("mp")
        twin = {"mp": 1 - core}
        target = cols_of(out_ref, core, width)
        copy = send(x_ref, target, send_sem.at[0], recv_sem.at[0], twin)
        own = keep(x_ref, target, own_sem.at[0])
        hook()
        copy.wait()
        own.wait()

    result = jax.ShapeDtypeStruct((images, line_pixels, cores * width), source.dtype)
    return talk_with(kernel, twin_peers, result, [source], dma_sems(1, 1, 1), number, riders)


def sum_lines(source, number, riders=()):
    images, line_pixels, channels = source.shape
    lines = lax.axis_size("space")
    width = channels // lines
    if width % lane != 0:
        total = lax.psum_scatter(source, "space", scatter_dimension=2, tiled=True)
        return total.astype(jnp.float32), plain_all(riders)

    def kernel(hook, x_ref, out_ref, stage_ref, right_ref, left_ref, *sems):
        me = lax.axis_index("space")
        for line in range(lines):
            for part in range(pieces_per_chunk):
                rows = slice(part * some, (part + 1) * some)
                stage_ref[line, part] = x_ref[rows, :, line * width : (line + 1) * width]
        relay_sum(lines, stage_ref, right_ref, left_ref, sems, hook)
        for part in range(pieces_per_chunk):
            rows = slice(part * some, (part + 1) * some)
            out_ref[rows] = stage_ref[me, part].astype(jnp.float32)

            @pl.when(me > 0)
            def _():
                out_ref[rows] += right_ref[lines - 2, part].astype(jnp.float32)

            @pl.when(me < lines - 1)
            def _():
                out_ref[rows] += left_ref[lines - 2, part].astype(jnp.float32)

    result = jax.ShapeDtypeStruct((images, line_pixels, width), jnp.float32)
    some = images // pieces_per_chunk
    chunk = (pieces_per_chunk, some, line_pixels, width)
    scratch = [
        pltpu.VMEM((lines,) + chunk, source.dtype),
        pltpu.VMEM((lines - 1,) + chunk, source.dtype),
        pltpu.VMEM((lines - 1,) + chunk, source.dtype),
    ] + dma_sems(*[pieces_per_chunk * (lines - 1)] * 4)
    return talk_with(kernel, line_peers, result, [source], scratch, number, riders, [VMEM], VMEM)


def sum_cores(source, number, riders=()):
    images, line_pixels, channels = source.shape
    cores = lax.axis_size("mp")
    width = channels // cores
    if width % lane != 0:
        total = lax.psum_scatter(source, "mp", scatter_dimension=2, tiled=True)
        return total.astype(jnp.float32), plain_all(riders)

    def kernel(hook, x_ref, out_ref, got_ref, send_sem, recv_sem):
        core = lax.axis_index("mp")
        twin = {"mp": 1 - core}
        copy = send(cols_of(x_ref, 1 - core, width), got_ref, send_sem.at[0], recv_sem.at[0], twin)
        mine = pl.ds(pl.multiple_of(core * width, width), width)
        hook()
        copy.wait()
        for image in range(images):
            out_ref[image] = x_ref[image, :, mine].astype(jnp.float32) + got_ref[image].astype(
                jnp.float32
            )

    result = jax.ShapeDtypeStruct((images, line_pixels, width), jnp.float32)
    scratch = [pltpu.VMEM((images, line_pixels, width), source.dtype)]
    scratch = scratch + dma_sems(1, 1)
    return talk_with(
        kernel, twin_peers, result, [source], scratch, number, riders, [VMEM], VMEM
    )


def gather_tokens(rows, number, riders=()):
    count, channels = rows.shape
    lines, cores = lax.axis_size("space"), lax.axis_size("mp")
    width = channels // cores
    source = None if number is None else rows.reshape(1, count, channels)

    def kernel(hook, x_ref, out_ref, pass_sem, gain_sem, own_sem, *sems):
        me, core = lax.axis_index("space"), lax.axis_index("mp")
        twin = {"mp": 1 - core}

        some = count // pieces_per_chunk

        def spot(origin, part):
            start = pl.multiple_of(origin * count + part * some, some)
            return cols_of(out_ref.at[:, pl.ds(start, some)], core, width)

        def own_part(part):
            return cols_of(x_ref.at[:, pl.ds(part * some, some)], core, width)

        def hand(ref, order):
            return pltpu.make_async_remote_copy(
                ref, ref, pass_sem.at[order], gain_sem.at[order], device_id=twin, device_id_type=MESH
            )

        own = keep(x_ref, rows_of(out_ref, me, count), own_sem.at[0])
        relay_gather(
            lines,
            own_part,
            spot,
            sems,
            hook,
            lambda ref, order: hand(ref, order).start(),
        )
        own.wait()
        parts = pieces_per_chunk
        for step in range(1, lines):
            for part in range(parts):

                @pl.when(me - step >= 0)
                def _():
                    place = spot(lax.rem(me - step + lines, lines), part)
                    hand(place, (step - 1) * parts + part).wait()

                @pl.when(me + step < lines)
                def _():
                    place = spot(lax.rem(me + step, lines), part)
                    hand(place, (lines + step - 2) * parts + part).wait()

    result = jax.ShapeDtypeStruct((1, lines * count, channels), rows.dtype)
    moves = pieces_per_chunk * (lines - 1)
    sems = dma_sems(2 * moves, 2 * moves, 1, *[moves] * 4)

    def peers():
        return line_peers() + twin_peers()

    if number is None:
        return kernel, peers, result, sems
    line, others_done = talk_with(kernel, peers, result, [source], sems, number, riders, [VMEM], VMEM)
    return line.reshape(lines * count, channels), others_done


def scatter_tokens(partial_sum, number, riders=()):
    all_rows, channels = partial_sum.shape
    lines, cores = lax.axis_size("space"), lax.axis_size("mp")
    count, width = all_rows // lines, channels // cores
    source = None
    if number is not None:
        source = partial_sum.astype(jnp.bfloat16).reshape(lines, count, channels)

    def kernel(
        hook, x_ref, out_ref, twin_ref, stage_ref, right_ref, left_ref, sum_ref,
        s_sem, r_sem, s3_sem, r3_sem, *sems,
    ):
        me, core = lax.axis_index("space"), lax.axis_index("mp")
        twin = {"mp": 1 - core}
        theirs = pl.ds(pl.multiple_of((1 - core) * width, width), width)
        mine = pl.ds(pl.multiple_of(core * width, width), width)
        order = [lines - 1, 0] + list(range(1, lines - 1))
        first = [
            send(x_ref.at[target, :, theirs], twin_ref.at[target], s_sem.at[target], r_sem.at[target], twin)
            for target in order
        ]

        def ready(step):
            turn = {0: zip(order[:2], first[:2]), 1: zip(order[2:], first[2:])}
            for target, copy in turn.get(step, ()):
                copy.wait_recv()
                total = x_ref[target, :, mine].astype(jnp.float32)
                total = total + twin_ref[target].astype(jnp.float32)
                total = total.astype(jnp.bfloat16)
                for part in range(pieces_per_chunk):
                    stage_ref[target, part] = total[part * some : (part + 1) * some]

        relay_sum(lines, stage_ref, right_ref, left_ref, sems, hook, ready)
        for part in range(pieces_per_chunk):
            sum_ref[part] = stage_ref[me, part].astype(jnp.float32)

            @pl.when(me > 0)
            def _():
                sum_ref[part] += right_ref[lines - 2, part].astype(jnp.float32)

            @pl.when(me < lines - 1)
            def _():
                sum_ref[part] += left_ref[lines - 2, part].astype(jnp.float32)

            out_ref[part * some : (part + 1) * some, mine] = sum_ref[part].astype(jnp.bfloat16)
        third = send(out_ref.at[:, mine], out_ref.at[:, mine], s3_sem.at[0], r3_sem.at[0], twin)
        for copy in first:
            copy.wait_send()
        third.wait()

    result = jax.ShapeDtypeStruct((count, channels), jnp.bfloat16)
    some = count // pieces_per_chunk
    chunk = (pieces_per_chunk, some, width)
    scratch = [
        pltpu.VMEM((lines, count, width), jnp.bfloat16),
        pltpu.VMEM((lines,) + chunk, jnp.bfloat16),
        pltpu.VMEM((lines - 1,) + chunk, jnp.bfloat16),
        pltpu.VMEM((lines - 1,) + chunk, jnp.bfloat16),
        pltpu.VMEM(chunk, jnp.float32),
    ]
    sems = dma_sems(lines, lines, 1, 1, *[pieces_per_chunk * (lines - 1)] * 4)

    def peers():
        return line_peers() + [{"mp": 1 - lax.axis_index("mp")}]

    return talk_with(
        kernel, peers, result, [source], scratch + sems, number, riders, [VMEM], VMEM
    )


def to_clips(source, number, riders=()):
    slots, frames, pixels, channels = source.shape
    count = lax.axis_size("tm")
    few = pixels // count
    if few % 16 != 0:
        if number is None:
            return None
        return lax.all_to_all(source, "tm", split_axis=2, concat_axis=1, tiled=True), plain_all(riders)

    def kernel(hook, x_ref, out_ref, send_sem, recv_sem, own_sem):
        me = lax.axis_index("tm")
        target = out_ref.at[:, pl.ds(me * frames, frames)]

        def part(index):
            return x_ref.at[:, :, pl.ds(pl.multiple_of(index * few, few), few)]

        copies = [
            send(part(peer), target, send_sem.at[i - 1], recv_sem.at[i - 1], {"tm": peer})
            for i, peer in others("tm")
        ]
        copies.append(keep(part(me), target, own_sem.at[0]))
        hook()
        for copy in copies:
            copy.wait()

    result = jax.ShapeDtypeStruct((slots, count * frames, few, channels), source.dtype)
    sems = dma_sems(count - 1, count - 1, 1)
    return talk_with(kernel, frame_peers, result, [source], sems, number, riders)


def from_clips(source, number, riders=()):
    slots, all_frames, few, channels = source.shape
    count = lax.axis_size("tm")
    frames = all_frames // count
    if few % 16 != 0:
        if number is None:
            return None
        return lax.all_to_all(source, "tm", split_axis=1, concat_axis=2, tiled=True), plain_all(riders)

    def kernel(hook, x_ref, out_ref, send_sem, recv_sem, own_sem):
        me = lax.axis_index("tm")
        target = out_ref.at[:, :, pl.ds(pl.multiple_of(me * few, few), few)]

        def part(index):
            return x_ref.at[:, pl.ds(index * frames, frames)]

        copies = [
            send(part(peer), target, send_sem.at[i - 1], recv_sem.at[i - 1], {"tm": peer})
            for i, peer in others("tm")
        ]
        copies.append(keep(part(me), target, own_sem.at[0]))
        hook()
        for copy in copies:
            copy.wait()

    result = jax.ShapeDtypeStruct((slots, frames, count * few, channels), source.dtype)
    sems = dma_sems(count - 1, count - 1, 1)
    return talk_with(kernel, frame_peers, result, [source], sems, number, riders)


def by_owner_line(source, owners, lines):
    parts = source.reshape(source.shape[:-1] + (owners // lines, lines, -1))
    return parts.swapaxes(-3, -2).reshape(source.shape)


def by_frames(weight_grad):
    return FrameSum(weight_grad.reshape(lax.axis_size("tm"), -1, weight_grad.shape[1]))


def padded_rims(source):
    return jnp.pad(source, ((0, 0), (0, 0), (1, 1), (1, 1), (0, 0)))


def conv_weight(weight):
    return weight.reshape(weight.shape[0], 3, 3, weight.shape[2])


def conv_frames(source, weight, spec, flipped):
    images = source.reshape((-1,) + source.shape[2:])
    kernel = conv_weight(weight)
    if flipped:
        kernel = kernel[:, ::-1, ::-1]
    result = lax.conv_general_dilated(
        images,
        kernel,
        (1, 1),
        "SAME",
        dimension_numbers=("NHWC", spec, "NHWC"),
        preferred_element_type=jnp.float32,
    )
    return result.reshape(source.shape[:4] + (result.shape[-1],))


def conv_weight_grad(source, upstream, form, taps=range(9)):
    padded = padded_rims(source)
    rows, cols = source.shape[2], source.shape[3]
    tap_list = []
    for tap in taps:
        i, j = tap // 3, tap % 3
        tap_list.append(
            jnp.einsum(
                "bfhwc,bfhwk->" + form,
                padded[:, :, i : i + rows, j : j + cols],
                upstream,
                preferred_element_type=jnp.float32,
            ).astype(jnp.bfloat16)
        )
    return jnp.stack(tap_list)


def sinusoid(steps_int):
    counted = D // 2
    freqs = jnp.exp(-math.log(10000.0) * jnp.arange(counted, dtype=jnp.float32) / counted)
    angles = steps_int.astype(jnp.float32)[..., None] * freqs
    return jnp.concatenate([jnp.sin(angles), jnp.cos(angles)], axis=-1)


def offset_onehot(query_start, query_count, key_count):
    distance = (
        query_start
        + jnp.arange(query_count, dtype=jnp.int32)[:, None]
        - jnp.arange(key_count, dtype=jnp.int32)[None, :]
    )
    position = jnp.clip(distance, -(R // 2), R // 2 - 1) + R // 2
    return (position[:, :, None] == jnp.arange(R, dtype=jnp.int32)[None, None, :]).astype(
        jnp.float32
    )


def local(kernel, results, operands, grid, in_specs, out_specs, scratch=()):
    return pl.pallas_call(
        kernel,
        out_shape=results,
        grid=grid,
        in_specs=in_specs,
        out_specs=out_specs,
        scratch_shapes=list(scratch),
        compiler_params=pltpu.CompilerParams(vmem_limit_bytes=32 * 1024 * 1024),
    )(*operands)


def dot(a, b):
    return jnp.dot(a, b, preferred_element_type=jnp.float32)


def dot_nt(a, b):
    return lax.dot_general(a, b, (((1,), (1,)), ((), ())), preferred_element_type=jnp.float32)


def dot_tn(a, b):
    return lax.dot_general(a, b, (((0,), (0,)), ((), ())), preferred_element_type=jnp.float32)


def low(value):
    return value.astype(jnp.bfloat16)


def head_probs(query, key, bias, valid):
    scores = dot_nt(query, key) * (1.0 / math.sqrt(HDIM))
    if bias is not None:
        scores = scores + bias
    if valid is not None:
        scores = jnp.where(valid, scores, masked)
    expos = jnp.exp(scores - jnp.max(scores, axis=-1, keepdims=True))
    return expos / jnp.sum(expos, axis=-1, keepdims=True)


def head_forward(query, key, value, bias, valid):
    return dot(low(head_probs(query, key, bias, valid)), value)


def head_backward(query, key, value, bias, valid, upstream):
    probs = head_probs(query, key, bias, valid)
    prob_grad = dot_nt(upstream, value)
    inner = jnp.sum(probs * prob_grad, axis=-1, keepdims=True)
    score_grad = low(probs * (prob_grad - inner))
    scale = 1.0 / math.sqrt(HDIM)
    return (
        dot(score_grad, key) * scale,
        dot_tn(score_grad, query) * scale,
        dot_tn(low(probs), upstream),
        score_grad,
    )


def norm_forward(source, gain):
    centered = source - jnp.mean(source, axis=-1, keepdims=True)
    variance = jnp.mean(centered * centered, axis=-1, keepdims=True)
    return centered * lax.rsqrt(variance + epsilon) * gain


def norm_backward(source, gain, upstream):
    centered = source - jnp.mean(source, axis=-1, keepdims=True)
    variance = jnp.mean(centered * centered, axis=-1, keepdims=True)
    inverse = lax.rsqrt(variance + epsilon)
    normal = centered * inverse
    gain_grad = jnp.sum(upstream * normal, axis=0, keepdims=True)
    scaled = upstream * gain
    first = jnp.mean(scaled, axis=-1, keepdims=True)
    second = jnp.mean(scaled * normal, axis=-1, keepdims=True)
    return inverse * (scaled - first - normal * second), gain_grad


def in_weight(packs, index, width):
    per = packs[0].shape[0] // 4
    cols = width // per
    return jnp.concatenate(
        [
            jnp.concatenate(
                [
                    pack[t, s, :, i * cols : (i + 1) * cols]
                    for pack in packs
                    for s in range(pack.shape[1])
                    for i in range(pack.shape[3] // cols)
                ],
                axis=0,
            )
            for t in range(index * per, (index + 1) * per)
        ],
        axis=1,
    )


def out_weight(pack, index, count):
    width = pack.shape[3] // count
    return jnp.concatenate(
        [
            jnp.concatenate(
                [pack[t, s, :, index * width : (index + 1) * width] for t in range(pack.shape[0])],
                axis=0,
            )
            for s in range(pack.shape[1])
        ],
        axis=1,
    )


class Fetch:
    def __init__(self, sources, targets, sem):
        self.copies = [keep(*pair, sem.at[i]) for i, pair in enumerate(zip(sources, targets))]
        self.targets, self.here = targets, set()

    def __call__(self, index):
        if index not in self.here:
            self.here.add(index)
            self.copies[index].wait()
        return self.targets[index]


def fetch_scratch(arrays):
    return [pltpu.VMEM(item.shape, item.dtype) for item in arrays] + dma_sems(len(arrays))


def spatial_forward(rows, weight):
    lines, images, pixels, channels = rows.shape
    width = weight.shape[1] // 3
    count = lines * pixels

    def kernel(x_ref, w_ref, triple_ref, mix_ref):
        x = x_ref[...].reshape(count, channels)
        triple_ref[0] = low(dot(x, w_ref[...]))
        for head in range(width // HDIM):
            at = head * HDIM
            query, key, value = (
                triple_ref[0, :, j * width + at : j * width + at + HDIM] for j in range(3)
            )
            mix_ref[0, :, at : at + HDIM] = low(head_forward(query, key, value, None, None))

    return local(
        kernel,
        (
            jax.ShapeDtypeStruct((images, count, 3 * width), jnp.bfloat16),
            jax.ShapeDtypeStruct((images, count, width), jnp.bfloat16),
        ),
        (rows, weight),
        (images,),
        [
            pl.BlockSpec((lines, 1, pixels, channels), lambda i: (0, i, 0, 0)),
            pl.BlockSpec(weight.shape, lambda i: (0, 0)),
        ],
        (
            pl.BlockSpec((1, count, 3 * width), lambda i: (i, 0, 0)),
            pl.BlockSpec((1, count, width), lambda i: (i, 0, 0)),
        ),
    )


def spatial_backward(rows, weight, triple, upstream):
    lines, images, pixels, channels = rows.shape
    width = weight.shape[1] // 3
    count = lines * pixels

    def kernel(x_ref, w_ref, triple_ref, up_ref, grad_ref, dw_ref, grads_ref, total_ref):
        step = pl.program_id(0)
        x = x_ref[...].reshape(count, channels)
        for head in range(width // HDIM):
            at = head * HDIM
            query, key, value = (
                triple_ref[0, :, j * width + at : j * width + at + HDIM] for j in range(3)
            )
            grads = head_backward(query, key, value, None, None, up_ref[0, :, at : at + HDIM])
            for j in range(3):
                grads_ref[:, j * width + at : j * width + at + HDIM] = low(grads[j])
        part = dot_nt(grads_ref[...], w_ref[...])
        grad_ref[...] = low(part).reshape(lines, 1, pixels, channels)

        @pl.when(step == 0)
        def _():
            total_ref[...] = jnp.zeros_like(total_ref)

        total_ref[...] += dot_tn(x, grads_ref[...])

        @pl.when(step == images - 1)
        def _():
            dw_ref[...] = low(total_ref[...])

    return local(
        kernel,
        (
            jax.ShapeDtypeStruct((lines, images, pixels, channels), jnp.bfloat16),
            jax.ShapeDtypeStruct((channels, 3 * width), jnp.bfloat16),
        ),
        (rows, weight, triple, upstream),
        (images,),
        [
            pl.BlockSpec((lines, 1, pixels, channels), lambda i: (0, i, 0, 0)),
            pl.BlockSpec(weight.shape, lambda i: (0, 0)),
            pl.BlockSpec((1, count, 3 * width), lambda i: (i, 0, 0)),
            pl.BlockSpec((1, count, width), lambda i: (i, 0, 0)),
        ],
        (
            pl.BlockSpec((lines, 1, pixels, channels), lambda i: (0, i, 0, 0)),
            pl.BlockSpec((channels, 3 * width), lambda i: (0, 0)),
        ),
        [
            pltpu.VMEM((count, 3 * width), jnp.bfloat16),
            pltpu.VMEM((channels, 3 * width), jnp.float32),
        ],
    )


def dot_exact(a, b):
    return jnp.dot(a, b, preferred_element_type=jnp.float32, precision=highest)


def clip_masks(rows, few, ids_ref, turned_ref):
    across = lax.broadcasted_iota(jnp.int32, (rows, rows), 1)
    down = lax.broadcasted_iota(jnp.int32, (rows, rows), 0)
    return (lax.rem(across, few) == lax.rem(down, few)) & (ids_ref[0] == turned_ref[0])


def temporal_forward(clip, bias, ids, few):
    slots, rows, triple = clip.shape
    width = triple // 3

    def kernel(x_ref, bias_ref, ids_ref, turned_ref, mix_ref):
        valid = clip_masks(rows, few, ids_ref, turned_ref)
        for head in range(width // HDIM):
            at = head * HDIM
            query, key, value = (
                x_ref[0, :, j * width + at : j * width + at + HDIM] for j in range(3)
            )
            mix = head_forward(query, key, value, bias_ref[head], valid)
            mix_ref[0, :, at : at + HDIM] = low(mix)

    return local(
        kernel,
        jax.ShapeDtypeStruct((slots, rows, width), jnp.bfloat16),
        (clip, bias, ids[:, :, None], ids[:, None, :]),
        (slots,),
        [
            pl.BlockSpec((1, rows, triple), lambda i: (i, 0, 0)),
            pl.BlockSpec(bias.shape, lambda i: (0, 0, 0)),
            pl.BlockSpec((1, rows, 1), lambda i: (i, 0, 0)),
            pl.BlockSpec((1, 1, rows), lambda i: (i, 0, 0)),
        ],
        pl.BlockSpec((1, rows, width), lambda i: (i, 0, 0)),
    )


def temporal_backward(clip, bias, ids, few, upstream):
    slots, rows, triple = clip.shape
    width = triple // 3
    frames = rows // few

    def kernel(x_ref, bias_ref, ids_ref, turned_ref, up_ref, grad_ref, score_ref):
        step = pl.program_id(0)
        valid = clip_masks(rows, few, ids_ref, turned_ref)
        frame = lax.broadcasted_iota(jnp.int32, (frames, rows), 0)
        row = lax.broadcasted_iota(jnp.int32, (frames, rows), 1)
        gather = low((row // few == frame).astype(jnp.float32))

        @pl.when(step == 0)
        def _():
            score_ref[...] = jnp.zeros_like(score_ref)

        for head in range(width // HDIM):
            at = head * HDIM
            query, key, value = (
                x_ref[0, :, j * width + at : j * width + at + HDIM] for j in range(3)
            )
            grads = head_backward(
                query, key, value, bias_ref[head], valid, up_ref[0, :, at : at + HDIM]
            )
            for j in range(3):
                grad_ref[0, :, j * width + at : j * width + at + HDIM] = low(grads[j])
            score_ref[head] += dot(gather, grads[3])

    return local(
        kernel,
        (
            jax.ShapeDtypeStruct((slots, rows, triple), jnp.bfloat16),
            jax.ShapeDtypeStruct((bias.shape[0], frames, rows), jnp.float32),
        ),
        (clip, bias, ids[:, :, None], ids[:, None, :], upstream),
        (slots,),
        [
            pl.BlockSpec((1, rows, triple), lambda i: (i, 0, 0)),
            pl.BlockSpec(bias.shape, lambda i: (0, 0, 0)),
            pl.BlockSpec((1, rows, 1), lambda i: (i, 0, 0)),
            pl.BlockSpec((1, 1, rows), lambda i: (i, 0, 0)),
            pl.BlockSpec((1, rows, width), lambda i: (i, 0, 0)),
        ],
        (
            pl.BlockSpec((1, rows, triple), lambda i: (i, 0, 0)),
            pl.BlockSpec((bias.shape[0], frames, rows), lambda i: (0, 0, 0)),
        ),
    )


def later():
    pass


def like(*shape):
    return jax.ShapeDtypeStruct(shape, jnp.bfloat16)


def temporal_chain(triple, bias, ids, numbers, riders):
    slots, frames, pixels, channels = triple.shape
    width, count = channels // 3, lax.axis_size("tm")
    few, all_frames = pixels // count, frames * count
    rows = all_frames * few
    first = to_clips(like(*triple.shape), None)
    second = from_clips(like(slots, all_frames, few, width), None)
    if first is None or second is None:
        clip, done = to_clips(triple, numbers[0], riders)
        mix = temporal_forward(clip.reshape(slots, rows, channels), bias, ids, few)
        mix, _ = from_clips(mix.reshape(slots, all_frames, few, width), numbers[1])
        return clip, mix, done

    def kernel(hook, x_ref, bias_ref, ids_ref, turned_ref, clip_ref, out_ref, mix_ref, *scratch):
        first[0](later, x_ref, clip_ref, *scratch[: len(first[3])])
        for slot in range(slots):
            valid = clip_masks(rows, few, ids_ref.at[pl.ds(slot, 1)], turned_ref.at[pl.ds(slot, 1)])
            for head in range(width // HDIM):
                at = head * HDIM
                query, key, value = (
                    clip_ref[slot, :, :, j * width + at : j * width + at + HDIM].reshape(rows, HDIM)
                    for j in range(3)
                )
                mix = low(head_forward(query, key, value, bias_ref[head], valid))
                mix_ref[slot, :, :, at : at + HDIM] = mix.reshape(all_frames, few, HDIM)
        second[0](hook, mix_ref, out_ref, *scratch[len(first[3]) :])

    (clip, mix), done = talk_many(
        kernel,
        frame_peers,
        [first[2], second[2]],
        [triple, bias, ids[:, :, None], ids[:, None, :]],
        [pltpu.VMEM((slots, all_frames, few, width), jnp.bfloat16)] + first[3] + second[3],
        numbers[0],
        riders,
        [VMEM] * 4,
        [VMEM, VMEM],
    )
    return clip, mix, done


def temporal_back_chain(clip, bias, ids, upstream, numbers, riders):
    slots, all_frames, few, channels = clip.shape
    width, rows = channels // 3, all_frames * few
    first = to_clips(like(*upstream.shape), None)
    second = from_clips(like(*clip.shape), None)
    if first is None or second is None:
        up, done = to_clips(upstream, numbers[0], riders)
        grads, score = temporal_backward(
            clip.reshape(slots, rows, channels), bias, ids, few, up.reshape(slots, rows, width)
        )
        grads, _ = from_clips(grads.reshape(clip.shape), numbers[1])
        return grads, score, done

    def kernel(
        hook, up_ref, clip_ref, bias_ref, ids_ref, turned_ref, out_ref, score_ref, line_ref, grad_ref, *scratch
    ):
        first[0](later, up_ref, line_ref, *scratch[: len(first[3])])
        frame = lax.broadcasted_iota(jnp.int32, (all_frames, rows), 0)
        row = lax.broadcasted_iota(jnp.int32, (all_frames, rows), 1)
        gather = low((row // few == frame).astype(jnp.float32))
        score_ref[...] = jnp.zeros_like(score_ref)
        for slot in range(slots):
            valid = clip_masks(rows, few, ids_ref.at[pl.ds(slot, 1)], turned_ref.at[pl.ds(slot, 1)])
            for head in range(width // HDIM):
                at = head * HDIM
                query, key, value = (
                    clip_ref[slot, :, :, j * width + at : j * width + at + HDIM].reshape(rows, HDIM)
                    for j in range(3)
                )
                up = line_ref[slot, :, :, at : at + HDIM].reshape(rows, HDIM)
                grads = head_backward(query, key, value, bias_ref[head], valid, up)
                for j in range(3):
                    grad_ref[slot, :, :, j * width + at : j * width + at + HDIM] = low(
                        grads[j]
                    ).reshape(all_frames, few, HDIM)
                score_ref[head] += dot(gather, grads[3])
        second[0](hook, grad_ref, out_ref, *scratch[len(first[3]) :])

    (grads, score), done = talk_many(
        kernel,
        frame_peers,
        [second[2], jax.ShapeDtypeStruct((bias.shape[0], all_frames, rows), jnp.float32)],
        [upstream, clip, bias, ids[:, :, None], ids[:, None, :]],
        [pltpu.VMEM(first[2].shape, jnp.bfloat16), pltpu.VMEM(clip.shape, jnp.bfloat16)]
        + first[3]
        + second[3],
        numbers[0],
        riders,
        [VMEM] * 5,
        [VMEM, VMEM],
    )
    return grads, score, done


def line_rows(line_ref, image, lines, images, pixels):
    return jnp.concatenate(
        [
            line_ref[0, (s * images + image) * pixels : (s * images + image + 1) * pixels, :]
            for s in range(lines)
        ],
        axis=0,
    )


def spatial_chain(rows, branch, gain, weight, images, numbers, riders):
    count, channels = rows.shape
    lines, width = lax.axis_size("space"), weight.shape[1] // 3
    pixels = count // images
    first = gather_tokens(like(*rows.shape), None)
    second = from_lines(like(images, lines * pixels, width), False, None)
    if second is None:
        stream, normed = first_norm(rows, branch, gain)
        line, done = gather_tokens(normed, numbers[0], riders)
        line = line[None]
        triple, mix = spatial_forward(line.reshape(lines, images, pixels, channels), weight)
        mix, _ = from_lines(mix, False, numbers[1])
        return stream, line, triple, mix, done

    def kernel(
        hook, branch_ref, gain_ref, w_ref, rows_ref, stream_ref, line_ref, triple_ref, out_ref,
        mix_ref, normed_ref, one_ref, here_ref, sem, *scratch,
    ):
        fetch = Fetch([rows_ref], [here_ref], sem)
        one = fetch(0)[...].astype(jnp.float32) + branch_ref[...].astype(jnp.float32)
        one_ref[...] = one
        written = keep(one_ref, stream_ref, sem.at[1])
        normed_ref[0] = low(norm_forward(one, gain_ref[...]))
        first[0](hook, normed_ref, line_ref, *scratch[: len(first[3])])
        for image in range(images):
            x = line_rows(line_ref, image, lines, images, pixels)
            triple_ref[image] = low(dot(x, w_ref[...]))
            for head in range(width // HDIM):
                at = head * HDIM
                query, key, value = (
                    triple_ref[image, :, j * width + at : j * width + at + HDIM] for j in range(3)
                )
                mix = low(head_forward(query, key, value, None, None))
                mix_ref[image, :, at : at + HDIM] = mix
        second[0](hook, mix_ref, out_ref, *scratch[len(first[3]) :])
        written.wait()

    (stream, line, triple, mix), done = talk_many(
        kernel,
        lambda: line_peers() + twin_peers(),
        [
            jax.ShapeDtypeStruct(rows.shape, jnp.float32),
            first[2],
            like(images, lines * pixels, 3 * width),
            second[2],
        ],
        [branch, gain, weight, rows],
        [
            pltpu.VMEM((images, lines * pixels, width), jnp.bfloat16),
            pltpu.VMEM((1,) + rows.shape, jnp.bfloat16),
            pltpu.VMEM(rows.shape, jnp.float32),
            pltpu.VMEM(rows.shape, rows.dtype),
        ]
        + dma_sems(2)
        + first[3]
        + second[3],
        numbers[0],
        riders,
        [VMEM, VMEM, VMEM, ANY],
        [ANY, VMEM, VMEM, VMEM],
    )
    return stream, line, triple, mix, done


def late_chain(mix, stream, out, gain, number, riders):
    rows, channels = stream.shape
    first = gather_tokens(like(*stream.shape), None)

    def kernel(
        hook, mix_ref, gain_ref, out_any, stream_any, four_any, line_ref,
        normed_ref, four_ref, mine_ref, theirs_ref, out_ref, stream_ref, sem, end_sem, send_sem, recv_sem, *scratch,
    ):
        fetch = Fetch([out_any, stream_any], [out_ref, stream_ref], sem)
        part = dot(mix_ref[...], out_weight(fetch(0), 0, 1))
        part = twin_sum(part, mine_ref, theirs_ref, send_sem.at[0], recv_sem.at[0])
        four = fetch(1)[...] + part
        four_ref[...] = four
        written = keep(four_ref, four_any, end_sem.at[0])
        normed_ref[0] = low(norm_forward(four, gain_ref[...]))
        first[0](hook, normed_ref, line_ref, *scratch)
        written.wait()

    (four, line), done = talk_many(
        kernel,
        lambda: line_peers() + twin_peers(),
        [jax.ShapeDtypeStruct(stream.shape, jnp.float32), first[2]],
        [mix, gain, out, stream],
        [
            pltpu.VMEM((1,) + stream.shape, jnp.bfloat16),
            pltpu.VMEM(stream.shape, jnp.float32),
            pltpu.VMEM(stream.shape, jnp.bfloat16),
            pltpu.VMEM(stream.shape, jnp.bfloat16),
            pltpu.VMEM(out.shape, out.dtype),
            pltpu.VMEM(stream.shape, jnp.float32),
        ]
        + dma_sems(2, 1, 1, 1)
        + first[3],
        number,
        riders,
        [VMEM, VMEM, ANY, ANY],
        [ANY, VMEM],
    )
    return four, line, done


def first_back_chain(stream, gain, normed_grad, upstream, owners, images, numbers, riders):
    count, channels = stream.shape
    lines, pixels = lax.axis_size("space"), count // images
    first = to_lines(like(2 * images, pixels, channels), False, None, join=True)
    if first is None or (channels // owners) % HDIM != 0:
        grad, both, gain_grad = first_norm_backward(
            stream, gain, normed_grad, upstream, owners, lines
        )
        line, done = to_lines(
            both.reshape(2 * images, pixels, channels), False, numbers[0], riders, join=True
        )
        return grad, line, gain_grad, done

    def kernel(
        hook, gain_ref, normed_ref, stream_any, up_any, grad_any, line_ref, dg_ref,
        both_ref, rows_ref, grad_ref, stream_ref, up_ref, sem, *scratch,
    ):
        fetch = Fetch([stream_any, up_any], [stream_ref, up_ref], sem)
        step, gain_grad = norm_backward(
            fetch(0)[...], gain_ref[...], normed_ref[...].astype(jnp.float32)
        )
        grad = fetch(1)[...] + step
        grad_ref[...] = grad
        written = keep(grad_ref, grad_any, sem.at[2])
        dg_ref[...] = gain_grad
        store_both(rows_ref, low(grad), owners, lines)
        for half in range(2):
            for image in range(images):
                both_ref[half * images + image] = rows_ref[
                    half, image * pixels : (image + 1) * pixels, :
                ]
        first[0](hook, both_ref, line_ref, *scratch)
        written.wait()

    (grad, line, gain_grad), done = talk_many(
        kernel,
        first[1],
        [
            jax.ShapeDtypeStruct(stream.shape, jnp.float32),
            first[2],
            jax.ShapeDtypeStruct(gain.shape, jnp.float32),
        ],
        [gain, normed_grad, stream, upstream],
        [
            pltpu.VMEM((2 * images, pixels, channels), jnp.bfloat16),
            pltpu.VMEM((2, count, channels), jnp.bfloat16),
            pltpu.VMEM(stream.shape, jnp.float32),
            pltpu.VMEM(stream.shape, jnp.float32),
            pltpu.VMEM(stream.shape, jnp.float32),
        ]
        + dma_sems(3)
        + first[3],
        numbers[0],
        riders,
        [VMEM, VMEM, ANY, ANY],
        [ANY, ANY, VMEM],
    )
    return grad, line, gain_grad, done


def spatial_back_chain(upstream, line, weight, triple, numbers, riders):
    images, pixels, _ = upstream.shape
    lines, (channels, width) = lax.axis_size("space"), weight.shape
    width = width // 3
    count = images * pixels
    first = to_lines(like(*upstream.shape), False, None)
    second = scatter_tokens(like(lines * count, channels), None)
    if first is None:
        up, done = to_lines(upstream, False, numbers[0], riders)
        part, grads = spatial_backward(
            line.reshape(lines, images, pixels, channels), weight, triple, up
        )
        normed, _ = scatter_tokens(part.reshape(lines * count, channels), numbers[1])
        return normed, jnp.stack(jnp.split(grads, 3, axis=1)), done

    def kernel(
        hook, up_ref, line_ref, w_ref, triple_ref, out_ref, dw_ref, upline_ref, part_ref, grads_ref, *scratch
    ):
        first[0](later, up_ref, upline_ref, *scratch[: len(first[3])])
        for image in range(images):
            for head in range(width // HDIM):
                at = head * HDIM
                query, key, value = (
                    triple_ref[image, :, j * width + at : j * width + at + HDIM] for j in range(3)
                )
                up = upline_ref[image, :, at : at + HDIM]
                grads = head_backward(query, key, value, None, None, up)
                for j in range(3):
                    grads_ref[image, :, j * width + at : j * width + at + HDIM] = low(grads[j])
            part = low(dot_nt(grads_ref[image], w_ref[...]))
            for s in range(lines):
                here = slice(image * pixels, (image + 1) * pixels)
                part_ref[s, here, :] = part[s * pixels : (s + 1) * pixels]

        def weights():
            total = None
            for image in range(images):
                x = line_rows(line_ref, image, lines, images, pixels)
                one = dot_tn(x, grads_ref[image])
                total = one if total is None else total + one
            for j in range(3):
                dw_ref[j] = low(total[:, j * width : (j + 1) * width])
            hook()

        second[0](weights, part_ref, out_ref, *scratch[len(first[3]) :])

    (normed, grads), done = talk_many(
        kernel,
        lambda: line_peers() + twin_peers(),
        [second[2], like(3, channels, width)],
        [upstream, line, weight, triple],
        [
            pltpu.VMEM((images, lines * pixels, width), jnp.bfloat16),
            pltpu.VMEM((lines, count, channels), jnp.bfloat16),
            pltpu.VMEM((images, lines * pixels, 3 * width), jnp.bfloat16),
        ]
        + first[3]
        + second[3],
        numbers[0],
        riders,
        [VMEM] * 4,
        [VMEM, VMEM],
    )
    return normed, grads, done


def gelu_pair(upper):
    rate = math.sqrt(2.0 / math.pi)
    square = upper * upper
    bend = jnp.tanh(rate * (upper + 0.044715 * square * upper))
    half = 0.5 * (1.0 + bend)
    slope = half + 0.5 * upper * (1.0 - bend * bend) * rate * (1.0 + 3.0 * 0.044715 * square)
    return upper * half, slope


def feed_both(rows, cot, w_in, w_out):
    lines, count, channels = rows.shape
    hidden = w_in.shape[1]

    def kernel(x_ref, cot_ref, in_ref, out_ref, y_ref, grad_ref, dw_ref, first_ref, second_ref):
        step = pl.program_id(0)
        x, up = x_ref[0], cot_ref[0]
        active, slope = gelu_pair(dot(x, in_ref[...]))
        active = low(active)
        upper_grad = low(dot_nt(up, out_ref[...]) * slope)
        y_ref[0] = low(dot(active, out_ref[...]))
        grad_ref[0] = low(dot_nt(upper_grad, in_ref[...]))

        @pl.when(step == 0)
        def _():
            first_ref[...] = dot_tn(x, upper_grad)
            second_ref[...] = dot_tn(up, active)

        @pl.when(step > 0)
        def _():
            first_ref[...] += dot_tn(x, upper_grad)
            second_ref[...] += dot_tn(up, active)

        @pl.when(step == lines - 1)
        def _():
            dw_ref[:, :hidden] = low(first_ref[...])
            dw_ref[:, hidden:] = low(second_ref[...])

    block = pl.BlockSpec((1, count, channels), lambda i: (i, 0, 0))
    return local(
        kernel,
        (
            jax.ShapeDtypeStruct(rows.shape, jnp.bfloat16),
            jax.ShapeDtypeStruct(rows.shape, jnp.bfloat16),
            jax.ShapeDtypeStruct((channels, 2 * hidden), jnp.bfloat16),
        ),
        (rows, cot, w_in, w_out),
        (lines,),
        [
            block,
            block,
            pl.BlockSpec(w_in.shape, lambda i: (0, 0)),
            pl.BlockSpec(w_out.shape, lambda i: (0, 0)),
        ],
        (block, block, pl.BlockSpec((channels, 2 * hidden), lambda i: (0, 0))),
        [
            pltpu.VMEM((channels, hidden), jnp.float32),
            pltpu.VMEM((channels, hidden), jnp.float32),
        ],
    )


def twin_sum(partial_sum, mine_ref, theirs_ref, send_sem, recv_sem, work=None):
    mine_ref[...] = low(partial_sum)
    copy = send(mine_ref, theirs_ref, send_sem, recv_sem, {"mp": 1 - lax.axis_index("mp")})
    if work is not None:
        work()
    copy.wait()
    return mine_ref[...].astype(jnp.float32) + theirs_ref[...].astype(jnp.float32)


def chat(kernel, results, operands, rows, channels, swaps, number, scratch=(), far=(), late=()):
    own = []
    if swaps > 0:
        own = [
            pltpu.VMEM((swaps, rows, channels), jnp.bfloat16),
            pltpu.VMEM((swaps, rows, channels), jnp.bfloat16),
        ] + dma_sems(swaps, swaps)
    near, fetched = len(operands), len(far)
    count = near + fetched + len(results)
    late = list(late)
    late_scratch = [pltpu.VMEM(results[i].shape, results[i].dtype) for i in late] + dma_sems(
        len(late)
    )

    def whole(*refs):
        ins, sources = refs[:near], refs[near : near + fetched]
        outs = list(refs[near + fetched : count])
        rest = refs[count:]
        swapped, rest = rest[: len(own)], rest[len(own) :]
        targets, sem, rest = rest[:fetched], rest[fetched], rest[fetched + 1 :]
        held, late_sem, rest = rest[: len(late)], rest[len(late)], rest[len(late) + 1 :]
        fetch = Fetch(sources, targets, sem)
        ends = {place: outs[place] for place in late}
        for place, ref in zip(late, held):
            outs[place] = ref
        written = []

        def flush(*places):
            for place in places:
                index = late.index(place)
                written.append(keep(held[index], ends[place], late_sem.at[index]))

        def swap(index, partial_sum, work=None):
            mine_ref, theirs_ref, send_sem, recv_sem = swapped
            return twin_sum(
                partial_sum,
                mine_ref.at[index],
                theirs_ref.at[index],
                send_sem.at[index],
                recv_sem.at[index],
                work,
            )

        if swaps > 0:
            meet(twin_peers())
        kernel(swap, fetch, flush, *ins, *outs, *rest)
        for copy in written:
            copy.wait()

    specs = [VMEM] * near + [ANY] * fetched
    out_specs = tuple(ANY if i in late else VMEM for i in range(len(results)))
    scratch = own + fetch_scratch(far) + late_scratch + list(scratch)
    if swaps > 0:
        return talk(
            whole, tuple(results), list(operands) + list(far), scratch, number, specs, out_specs, 56
        )
    return pl.pallas_call(
        whole,
        out_shape=tuple(results),
        in_specs=specs,
        out_specs=out_specs,
        scratch_shapes=scratch,
        compiler_params=pltpu.CompilerParams(vmem_limit_bytes=56 * 1024 * 1024),
    )(*operands, *far)


def group_means(totals, count):
    channels = totals.shape[1]
    down = lax.broadcasted_iota(jnp.int32, (channels, channels), 0)
    across = lax.broadcasted_iota(jnp.int32, (channels, channels), 1)
    size = D // G
    same = (down // size == across // size).astype(jnp.float32)
    return dot_exact(totals, same) * (1.0 / (count * size))


def group_normal(source):
    count = source.shape[0]
    centered = source - group_means(jnp.sum(source, axis=0, keepdims=True), count)
    spread = group_means(jnp.sum(centered * centered, axis=0, keepdims=True), count)
    inverse = lax.rsqrt(spread + epsilon)
    return centered * inverse, inverse


def group_step(upstream, normal, inverse):
    count = upstream.shape[0]
    first = group_means(jnp.sum(upstream, axis=0, keepdims=True), count)
    second = group_means(jnp.sum(upstream * normal, axis=0, keepdims=True), count)
    return inverse * (upstream - first - normal * second)


def silu(value):
    return value * jax.nn.sigmoid(value)


def silu_slope(value):
    gate = jax.nn.sigmoid(value)
    return gate * (1.0 + value * (1.0 - gate))


def image_block(shape):
    return pl.BlockSpec((1,) + shape[1:], lambda i: (i, 0, 0))


def group_forward(source, scale, shift):
    def kernel(x_ref, scale_ref, shift_ref, out_ref):
        normal, _ = group_normal(x_ref[0].astype(jnp.float32))
        out_ref[0] = low(silu(normal * scale_ref[0] + shift_ref[0]))

    return local(
        kernel,
        jax.ShapeDtypeStruct(source.shape, jnp.bfloat16),
        (source, scale, shift),
        (source.shape[0],),
        [image_block(source.shape), image_block(scale.shape), image_block(shift.shape)],
        image_block(source.shape),
    )


def group_backward(source, scale, shift, upstream):
    def kernel(x_ref, scale_ref, shift_ref, up_ref, grad_ref, scale_grad_ref, shift_grad_ref):
        normal, inverse = group_normal(x_ref[0].astype(jnp.float32))
        grad = up_ref[0] * silu_slope(normal * scale_ref[0] + shift_ref[0])
        scale_grad_ref[0] = jnp.sum(grad * normal, axis=0, keepdims=True)
        shift_grad_ref[0] = jnp.sum(grad, axis=0, keepdims=True)
        grad_ref[0] = low(group_step(grad * scale_ref[0], normal, inverse))

    return local(
        kernel,
        (
            jax.ShapeDtypeStruct(source.shape, jnp.bfloat16),
            jax.ShapeDtypeStruct(scale.shape, jnp.float32),
            jax.ShapeDtypeStruct(shift.shape, jnp.float32),
        ),
        (source, scale, shift, upstream),
        (source.shape[0],),
        [
            image_block(source.shape),
            image_block(scale.shape),
            image_block(shift.shape),
            image_block(upstream.shape),
        ],
        (image_block(source.shape), image_block(scale.shape), image_block(shift.shape)),
    )


def flat_call(kernel, results, operands):
    return pl.pallas_call(
        kernel,
        out_shape=tuple(results),
        in_specs=[VMEM] * len(operands),
        out_specs=tuple([VMEM] * len(results)),
        compiler_params=pltpu.CompilerParams(vmem_limit_bytes=32 * 1024 * 1024),
    )(*operands)


def store_both(both_ref, value, owners, lines):
    both_ref[0] = value
    if (value.shape[1] // owners) % HDIM != 0:
        return
    size = value.shape[1] // owners
    frames = owners // lines
    both_ref[1] = jnp.concatenate(
        [
            value[:, (t * lines + s) * size : (t * lines + s + 1) * size]
            for s in range(lines)
            for t in range(frames)
        ],
        axis=1,
    )


def both_orders(rows, owners, lines):
    if (rows.shape[1] // owners) % HDIM != 0:
        return jnp.stack([rows, by_owner_line(rows, owners, lines)])

    def kernel(x_ref, both_ref):
        store_both(both_ref, x_ref[...], owners, lines)

    return flat_call(kernel, [jax.ShapeDtypeStruct((2,) + rows.shape, rows.dtype)], [rows])[0]


def first_norm(rows, branch, gain):
    def kernel(swap, fetch, flush, branch_ref, gain_ref, one_ref, normed_ref):
        one = fetch(0)[...].astype(jnp.float32) + branch_ref[...].astype(jnp.float32)
        one_ref[...] = one
        flush(0)
        normed_ref[...] = low(norm_forward(one, gain_ref[...]))

    return chat(
        kernel,
        [
            jax.ShapeDtypeStruct(rows.shape, jnp.float32),
            jax.ShapeDtypeStruct(rows.shape, jnp.bfloat16),
        ],
        [branch, gain],
        *rows.shape,
        0,
        0,
        far=[rows],
        late=[0],
    )


def first_norm_backward(stream, gain, normed_grad, upstream, owners, lines):
    def kernel(swap, fetch, flush, gain_ref, normed_ref, grad_ref, both_ref, dg_ref):
        step, gain_grad = norm_backward(
            fetch(0)[...], gain_ref[...], normed_ref[...].astype(jnp.float32)
        )
        grad = fetch(1)[...] + step
        grad_ref[...] = grad
        flush(0)
        dg_ref[...] = gain_grad
        store_both(both_ref, low(grad), owners, lines)

    grad, both, gain_grad = chat(
        kernel,
        [
            jax.ShapeDtypeStruct(stream.shape, jnp.float32),
            jax.ShapeDtypeStruct((2,) + stream.shape, jnp.bfloat16),
            jax.ShapeDtypeStruct(gain.shape, jnp.float32),
        ],
        [gain, normed_grad],
        *stream.shape,
        0,
        0,
        far=[stream, upstream],
        late=[0],
    )
    if (stream.shape[1] // owners) % HDIM != 0:
        both = jnp.stack([both[0], by_owner_line(both[0], owners, lines)])
    return grad, both, gain_grad


def text_mask(rows, valid_ref):
    slots, keys = valid_ref.shape
    slot = lax.broadcasted_iota(jnp.int32, (rows, keys), 0) // (rows // slots)
    good = None
    for index in range(slots):
        own = (slot == index) & (valid_ref[index : index + 1, :] > 0.5)
        good = own if good is None else good | own
    return good


def middle_forward(mix, stream, outs, ins, pairs, valid, gains, number):
    rows, channels = stream.shape
    width = mix.shape[1]

    def kernel(
        swap, fetch, flush, mix_ref, x_ref, pairs_ref, valid_ref, gain_ref,
        two_ref, normed_ref, query_ref, cross_ref, three_ref, last_ref, triple_ref,
    ):
        two = x_ref[...] + swap(0, dot(mix_ref[...], out_weight(fetch(0), 0, 2)))
        two_ref[...] = two
        normed_ref[...] = low(norm_forward(two, gain_ref[0:1, :]))
        flush(0, 1)
        query_ref[...] = low(dot(normed_ref[...], in_weight((fetch(1), fetch(2)), 0, width)))
        good = text_mask(rows, valid_ref)
        for head in range(width // HDIM):
            at = head * HDIM
            cross = head_forward(
                query_ref[:, at : at + HDIM],
                pairs_ref[:, at : at + HDIM],
                pairs_ref[:, width + at : width + at + HDIM],
                None,
                good,
            )
            cross_ref[:, at : at + HDIM] = low(cross)
        flush(2, 3)
        three = two_ref[...] + swap(1, dot(cross_ref[...], out_weight(fetch(0), 1, 2)))
        three_ref[...] = three
        last_ref[...] = low(norm_forward(three, gain_ref[1:2, :]))
        flush(4, 5)
        for j in range(3):
            weight = in_weight((fetch(1), fetch(2)), 1 + j, width)
            triple_ref[:, j * width : (j + 1) * width] = low(dot(last_ref[...], weight))

    wide = jax.ShapeDtypeStruct((rows, channels), jnp.float32)
    wide_low = jax.ShapeDtypeStruct((rows, channels), jnp.bfloat16)
    thin = jax.ShapeDtypeStruct((rows, width), jnp.bfloat16)
    return chat(
        kernel,
        [wide, wide_low, thin, thin, wide, wide_low, jax.ShapeDtypeStruct((rows, 3 * width), jnp.bfloat16)],
        [mix, stream, pairs, valid, gains],
        rows,
        channels,
        2,
        number,
        far=[outs, *ins],
        late=range(6),
    )


def late_forward(mix, stream, out, gain, number):
    rows, channels = stream.shape

    def kernel(swap, fetch, flush, mix_ref, gain_ref, four_ref, normed_ref):
        part = swap(0, dot(mix_ref[...], out_weight(fetch(0), 0, 1)))
        four = fetch(1)[...] + part
        four_ref[...] = four
        flush(0)
        normed_ref[...] = low(norm_forward(four, gain_ref[...]))

    return chat(
        kernel,
        [
            jax.ShapeDtypeStruct((rows, channels), jnp.float32),
            jax.ShapeDtypeStruct((rows, channels), jnp.bfloat16),
        ],
        [mix, gain],
        rows,
        channels,
        1,
        number,
        far=[out, stream],
        late=[0],
    )


def late_backward(cot, normed_grad, stream, gain, mix, out):
    rows, channels = stream.shape
    width = mix.shape[1]

    def kernel(swap, fetch, flush, up_ref, gain_ref, grad_ref, mix_grad_ref, dw_ref, dg_ref):
        step, gain_grad = norm_backward(
            fetch(0)[...], gain_ref[...], up_ref[...].astype(jnp.float32)
        )
        grad = fetch(1)[...].astype(jnp.float32) + step
        grad_ref[...] = grad
        flush(0)
        dg_ref[...] = gain_grad
        branch = low(grad)
        dw_ref[...] = low(dot_tn(branch, fetch(3)[...]))
        flush(2)
        mix_grad_ref[...] = low(dot_nt(branch, out_weight(fetch(2), 0, 1)))

    return chat(
        kernel,
        [
            jax.ShapeDtypeStruct((rows, channels), jnp.float32),
            jax.ShapeDtypeStruct((rows, width), jnp.bfloat16),
            jax.ShapeDtypeStruct((channels, width), jnp.bfloat16),
            jax.ShapeDtypeStruct((1, channels), jnp.float32),
        ],
        [normed_grad, gain],
        rows,
        channels,
        0,
        0,
        far=[stream, cot, out, mix],
        late=[0, 2],
    )


def middle_backward(
    triple, upstream, three, two, last, normed, query, cross, mix, outs, ins, pairs, valid, gains, number
):
    rows, channels = three.shape
    width = mix.shape[1]

    def kernel(
        swap, fetch, flush, pairs_ref, valid_ref, gain_ref,
        grad_ref, mix_grad_ref, pair_grad_ref, query_dw_ref, pair_dw_ref, cross_dw_ref, outs_dw_ref, dg_ref,
        cross_up_ref, dq_ref,
    ):
        def weight_in(index):
            return in_weight((fetch(1), fetch(2)), index, width)

        def temporal_weights():
            last_ref = fetch(3)
            query_dw_ref[...] = low(dot_tn(last_ref[...], triple_ref[:, :width]))
            pair_dw_ref[...] = low(dot_tn(last_ref[...], triple_ref[:, width:]))
            flush(3, 4)

        triple_ref = fetch(9)
        part_sum = dot_nt(triple_ref[:, :width], weight_in(1))
        part_sum = part_sum + dot_nt(triple_ref[:, width : 2 * width], weight_in(2))
        part_sum = part_sum + dot_nt(triple_ref[:, 2 * width :], weight_in(3))
        normed_grad = swap(0, part_sum, temporal_weights)
        step, gain_grad = norm_backward(fetch(10)[...], gain_ref[1:2, :], normed_grad)
        dg_ref[1:2, :] = gain_grad
        grad = fetch(11)[...] + step
        grad_ref[...] = grad
        branch = low(grad)
        cross_up_ref[...] = low(dot_nt(branch, out_weight(fetch(0), 1, 2)))
        query_ref, cross_ref, two_ref = fetch(4), fetch(5), fetch(6)
        normed_ref, mix_ref = fetch(7), fetch(8)
        good = text_mask(rows, valid_ref)
        for head in range(width // HDIM):
            at = head * HDIM
            grads = head_backward(
                query_ref[:, at : at + HDIM],
                pairs_ref[:, at : at + HDIM],
                pairs_ref[:, width + at : width + at + HDIM],
                None,
                good,
                cross_up_ref[:, at : at + HDIM],
            )
            dq_ref[:, at : at + HDIM] = low(grads[0])
            pair_grad_ref[:, at : at + HDIM] = low(grads[1])
            pair_grad_ref[:, width + at : width + at + HDIM] = low(grads[2])
        flush(2)

        def cross_weights():
            cross_dw_ref[...] = low(dot_tn(normed_ref[...], dq_ref[...]))
            flush(5)
            outs_dw_ref[:, :width] = low(dot_tn(low(grad_ref[...]), cross_ref[...]))

        normed_grad = swap(1, dot_nt(dq_ref[...], weight_in(0)), cross_weights)
        step, gain_grad = norm_backward(two_ref[...], gain_ref[0:1, :], normed_grad)
        dg_ref[0:1, :] = gain_grad
        grad = grad_ref[...] + step
        grad_ref[...] = grad
        flush(0)
        branch = low(grad)
        outs_dw_ref[:, width:] = low(dot_tn(branch, mix_ref[...]))
        flush(6)
        mix_grad_ref[...] = low(dot_nt(branch, out_weight(fetch(0), 0, 2)))

    return chat(
        kernel,
        [
            jax.ShapeDtypeStruct((rows, channels), jnp.float32),
            jax.ShapeDtypeStruct((rows, width), jnp.bfloat16),
            jax.ShapeDtypeStruct(pairs.shape, jnp.bfloat16),
            jax.ShapeDtypeStruct((channels, width), jnp.bfloat16),
            jax.ShapeDtypeStruct((channels, 2 * width), jnp.bfloat16),
            jax.ShapeDtypeStruct((channels, width), jnp.bfloat16),
            jax.ShapeDtypeStruct((channels, 2 * width), jnp.bfloat16),
            jax.ShapeDtypeStruct((2, channels), jnp.float32),
        ],
        [pairs, valid, gains],
        rows,
        channels,
        2,
        number,
        [pltpu.VMEM((rows, width), jnp.bfloat16), pltpu.VMEM((rows, width), jnp.bfloat16)],
        [outs, *ins, last, query, cross, two, normed, mix, triple, three, upstream],
        [0, 2, 3, 4, 5, 6],
    )


def on_device(
    video,
    cotangent,
    text,
    video_ids,
    timesteps,
    text_lengths,
    group_gain,
    group_bias,
    first_conv,
    film_weight,
    second_conv,
    spatial_norm,
    spatial_qkv,
    spatial_out,
    cross_norm,
    cross_query,
    cross_kv,
    cross_out,
    temporal_norm,
    temporal_qkv,
    temporal_out,
    offset_bias,
    feed_norm,
    feed_in,
    feed_out,
):
    frames_axis, lines, cores = (lax.axis_size(name) for name in ("tm", "space", "mp"))
    slots, frame_dev, row_dev, columns, channels = video.shape
    half_width = first_conv.shape[2]
    head_local = half_width // HDIM
    pixels_dev = row_dev * columns
    frames_all = frame_dev * frames_axis
    token_rows = slots * frame_dev * pixels_dev
    text_local = text.shape[1]
    images = slots * frame_dev
    frame_shape = (-1, frame_dev, H, W)
    everyone = ("tm", "space")
    owners = frames_axis * lines
    line_half = lines // 2
    feed_width = feed_in.shape[1] // lines
    text_rows = slots * text_local

    def wide(source):
        return source.reshape(frame_shape + source.shape[2:])

    out_piece = part_of(jnp.concatenate([spatial_out, cross_out, temporal_out], axis=1), "tm", 0)
    if frames_axis == 4:
        in_piece = jnp.concatenate([cross_query[None], temporal_qkv.transpose(1, 0, 2)], axis=0)
        in_piece = lax.dynamic_index_in_dim(in_piece, lax.axis_index("tm"), 0, keepdims=False)
    else:
        in_piece = jnp.concatenate([cross_query, temporal_qkv.reshape(-1, 3 * half_width)], axis=1)
        in_piece = part_of(in_piece, "tm", 1)
    picks = channels % (16 * owners) == 0 and (half_width // lines) % lane == 0
    turned_qkv = spatial_qkv.transpose(1, 0, 2)

    def cut_qkv(whole):
        piece = part_of(whole, "tm", 1)
        return piece.reshape(3, -1, lines, half_width // lines).transpose(2, 0, 1, 3)

    def pick_qkv(ref, place):
        rows = span(lax.axis_index("tm"), channels // owners)
        return ref.at[:, rows, span(place, half_width // lines)]

    def cut_in(whole):
        return part_of(whole, "tm", 0).reshape(-1, lines, feed_width).transpose(1, 0, 2)

    def pick_in(ref, place):
        return ref.at[span(lax.axis_index("tm"), channels // owners), span(place, feed_width)]

    def cut_out(whole):
        return part_of(whole.reshape(lines, feed_width, -1), "tm", 1)

    def pick_out(ref, place):
        return ref.at[span(place * frames_axis + lax.axis_index("tm"), feed_width // frames_axis)]

    def cut_text(whole):
        return whole.reshape(text_rows, frames_axis, -1).transpose(1, 0, 2)

    def pick_text(ref, place):
        return ref.at[:, span(place, ref.shape[1] // frames_axis)]

    def cut_cols(whole):
        return whole.reshape(frames_axis, text_rows, lines, -1).transpose(2, 0, 1, 3)

    def pick_cols(ref, place):
        return ref.at[:, :, span(place, ref.shape[2] // lines)]

    def cut_and_send(source, axes, pick, cut):
        return Exchange(source, axes, pick, cut) if picks else Exchange(cut(source), axes)

    cot_rows = cotangent.reshape(token_rows, channels)
    text_flat = text.reshape(text_rows, -1)
    cross_kv = cross_kv.reshape(cross_kv.shape[0], -1)

    folds = in_piece.shape[0] // out_piece.shape[0]
    in_piece = jnp.concatenate(jnp.split(in_piece, folds, axis=0), axis=1)
    out_cols = out_piece.shape[1]
    pack = jnp.concatenate([out_piece, in_piece], axis=1)
    in_cols = (out_cols, pack.shape[1])
    embed = sinusoid(timesteps).astype(jnp.bfloat16)
    film_part = jnp.einsum(
        "bvc,cjk->bvjk", part_of(embed, "space", 2), film_weight, preferred_element_type=jnp.float32
    )
    film_part = film_part.reshape(slots * VIDS * 2, lines, -1).transpose(1, 0, 2)

    video_rows = video.reshape(token_rows, channels)
    in_groups = (channels // owners) % (D // G) == 0
    video_both = both_orders(video_rows, owners, lines) if in_groups else video_rows
    video_lines, (text_line, qkv_piece, film, pack) = to_lines(
        video_both.reshape(-1, pixels_dev, channels),
        True,
        1,
        [
            LineColumns(text_flat),
            cut_and_send(turned_qkv, ("space",), pick_qkv, cut_qkv),
            Exchange(film_part, ("space",)),
            Keep(pack),
        ],
    )
    pack = lax.all_gather(pack, "space", axis=0, tiled=False)

    def line_gains(whole):
        own = part_of(part_of(whole, "space", 0), "mp", 0)
        if not in_groups:
            return jnp.broadcast_to(own, (images, 1, own.shape[0]))
        owned = part_of(part_of(by_owner_line(whole, owners, lines), "space", 0), "mp", 0)
        return jnp.repeat(jnp.stack([own, owned]), images, axis=0)[:, None]

    gain_line, bias_line = line_gains(group_gain), line_gains(group_bias)
    first_in = group_forward(video_lines, gain_line, bias_line)
    text_part = jnp.dot(
        text_line.reshape(lines * text_rows, -1), cross_kv, preferred_element_type=jnp.float32
    )
    text_part = text_part.astype(jnp.bfloat16).reshape(lines, text_rows, -1)
    first_in, (text_part,) = gather_cores(first_in, 3, [Exchange(text_part, ("space",))])
    if in_groups:
        first_in, first_owned = first_in[:images], first_in[images:]
    else:
        blocks = first_in.reshape(first_in.shape[:2] + (-1, lines, channels // owners))
        blocks = blocks.swapaxes(2, 3).reshape(first_in.shape)
        first_owned = lax.all_to_all(blocks, "space", split_axis=2, concat_axis=2, tiled=True)
    text_part = jnp.sum(text_part.astype(jnp.float32), axis=0).astype(jnp.bfloat16)
    hidden_part = conv_frames(wide(first_in), first_conv, "IHWO", False).astype(jnp.bfloat16)
    hidden, (text_part, qkv_piece) = sum_lines(
        hidden_part.reshape(images, H * W, half_width),
        4,
        [Share(text_part, ("space",)), Share(qkv_piece, ("tm",))],
    )

    film = jnp.sum(film, axis=0).reshape(slots, VIDS, 2, -1)
    frame_ids = part_of(video_ids, "tm", 1)
    choose = (frame_ids[:, :, None] == jnp.arange(VIDS, dtype=jnp.int32)[None, None, :]).astype(
        jnp.float32
    )
    frame_film = jnp.einsum("bfv,bvjk->jbfk", choose, film, precision=highest)
    frame_film = frame_film.reshape(2, images, 1, -1)
    film_scale, film_shift = 1.0 + frame_film[0], frame_film[1]
    second_in = group_forward(hidden, film_scale, film_shift)
    second_wide, (text_pairs, in_first, cot_late) = gather_lines(
        second_in,
        5,
        [Share(text_part, ("tm",)), Share(pack, ("tm",), 0, line_half, in_cols), Keep(cot_rows)],
    )
    cot_half = lax.all_gather(part_of(cot_late, "mp", 1), "space", axis=0, tiled=True)
    text_pairs = text_pairs.reshape(owners * text_rows, 2 * half_width)
    conv_part = conv_frames(wide(second_wide), second_conv, "IHWO", False).astype(jnp.bfloat16)
    conv_half, _ = sum_cores(conv_part.reshape(images, H * W, -1), 6)
    conv_rows, (outs_all,) = from_lines(
        conv_half.astype(jnp.bfloat16),
        True,
        7,
        [Share(pack, ("tm",), cols=(0, out_cols // 3 * 2))],
    )
    spatial_qkv = qkv_piece.transpose(1, 0, 3, 2, 4).reshape(channels, -1)

    spatial_gain = spatial_norm[None]
    stream_one, spatial_line, spatial_triple, spatial_mix, (in_rest, out_last, text_cols) = (
        spatial_chain(
            video_rows,
            conv_rows.reshape(token_rows, channels),
            spatial_gain,
            spatial_qkv,
            images,
            (8, 9),
            [
                Share(pack, ("tm",), line_half, lines - line_half, in_cols),
                Share(pack, ("tm",), cols=(out_cols // 3 * 2, out_cols)),
                cut_and_send(text_flat, ("tm",), pick_text, cut_text),
            ],
        )
    )

    spatial_mix = spatial_mix.reshape(token_rows, half_width)
    in_all = (in_first, in_rest)
    key = jnp.arange(owners * text_rows, dtype=jnp.int32)[None, :]
    key_slot = key % text_rows // text_local
    key_place = key // text_rows * text_local + key % text_local
    own_slot = key_slot == jnp.arange(slots, dtype=jnp.int32)[:, None]
    text_valid = (own_slot & (key_place < text_lengths[:, None])).astype(jnp.float32)
    two_gains = jnp.stack([cross_norm, temporal_norm])
    stream_two, cross_in, cross_queries, cross_mix, stream_three, temporal_in, temporal_triple = (
        middle_forward(
            spatial_mix, stream_one, outs_all, in_all, text_pairs, text_valid, two_gains, 34
        )
    )

    clip_pixels = pixels_dev // frames_axis
    clip_rows = frames_all * clip_pixels
    offset_table = offset_onehot(0, frames_all, frames_all)
    clip_frames = jnp.arange(clip_rows, dtype=jnp.int32)[:, None] // clip_pixels
    clip_frames = (clip_frames == jnp.arange(frames_all, dtype=jnp.int32)[None, :]).astype(
        jnp.float32
    )
    clip_bias = jnp.einsum("qkr,rh->hqk", offset_table, offset_bias, precision=highest)
    clip_bias = jnp.einsum("hqk,ck->hqc", clip_bias, clip_frames, precision=highest)
    clip_bias = jnp.einsum("rq,hqc->hrc", clip_frames, clip_bias, precision=highest)
    clip_ids = jnp.repeat(video_ids, clip_pixels, axis=1)
    clip_triple, temporal_mix, (in_quarter, out_quarter, text_cols) = temporal_chain(
        temporal_triple.reshape(slots, frame_dev, pixels_dev, 3 * half_width),
        clip_bias,
        clip_ids,
        (10, 11),
        [
            cut_and_send(feed_in, ("space",), pick_in, cut_in),
            cut_and_send(feed_out, ("space",), pick_out, cut_out),
            cut_and_send(text_cols, ("space",), pick_cols, cut_cols),
        ],
    )
    temporal_mix = temporal_mix.reshape(token_rows, half_width)

    feed_gain = feed_norm[None]
    stream_four, feed_line, (feed_in, feed_out, cot_line) = late_chain(
        temporal_mix,
        stream_three,
        out_last,
        feed_gain,
        12,
        [Share(in_quarter, ("tm",)), Share(out_quarter, ("tm",)), JoinCores(cot_half)],
    )
    feed_in = feed_in.transpose(1, 0, 2, 3).reshape(channels, feed_width)
    feed_out = feed_out.transpose(0, 2, 1, 3).reshape(feed_width, channels)
    line_shape = (lines, token_rows, channels)
    final_part, feed_part, feed_grads = feed_both(
        feed_line.reshape(line_shape), cot_line.reshape(line_shape), feed_in, feed_out
    )
    normed_grad, (feed_grads, final_half) = scatter_tokens(
        feed_part.reshape(lines * token_rows, channels),
        14,
        [by_frames(feed_grads), CoreSum(final_part.reshape(lines * token_rows, channels))],
    )

    upstream, mix_grad, temporal_out_grad, feed_norm_grad = late_backward(
        cot_rows, normed_grad, stream_four, feed_gain, temporal_mix, out_last
    )

    def cut_feed(half):
        cols = slice(half * feed_width, (half + 1) * feed_width)
        return lambda whole: whole[:, cols].reshape(lines, -1, feed_width)

    def pick_feed(half):
        cols = pl.ds(half * feed_width, feed_width)
        return lambda ref, place: ref.at[span(place, channels // owners), cols]

    (
        triple_grad,
        score_total,
        (feed_in_grad, feed_out_grad, first_grads, final_half),
    ) = temporal_back_chain(
        clip_triple,
        clip_bias,
        clip_ids,
        mix_grad.reshape(slots, frame_dev, pixels_dev, half_width),
        (15, 16),
        [
            ColumnJoin(feed_grads, pick_feed(0), cut_feed(0)),
            ColumnJoin(feed_grads, pick_feed(1), cut_feed(1)),
            by_frames(temporal_out_grad),
            LineSum(final_half),
        ],
    )
    score_total = jnp.einsum("hqc,ck->hqk", score_total, clip_frames, precision=highest)
    offset_bias_grad = jnp.einsum("hqk,qkr->rh", score_total, offset_table, precision=highest)

    (
        upstream,
        mix_grad,
        pair_grad,
        temporal_query_grad,
        temporal_pair_grad,
        cross_query_grad,
        outs_grad,
        two_grads,
    ) = middle_backward(
        triple_grad.reshape(token_rows, 3 * half_width),
        upstream,
        stream_three,
        stream_two,
        temporal_in,
        cross_in,
        cross_queries,
        cross_mix,
        spatial_mix,
        outs_all,
        in_all,
        text_pairs,
        text_valid,
        two_gains,
        36,
    )
    pair_grad = pair_grad.reshape(frames_axis, lines * text_rows, 2 * half_width)

    (
        normed_grad,
        spatial_qkv_grad,
        (pair_grad, second_grads, final_rows, temporal_out_grad, third_grads),
    ) = spatial_back_chain(
        mix_grad.reshape(images, pixels_dev, half_width),
        spatial_line,
        spatial_qkv,
        spatial_triple,
        (17, 18),
        [
            FrameSum(pair_grad),
            by_frames(temporal_query_grad),
            JoinCores(final_half),
            LineSum(first_grads, jnp.float32),
            by_frames(temporal_pair_grad),
        ],
    )
    mixed = (stream_four + final_rows.astype(jnp.float32)).astype(jnp.bfloat16)
    (
        upstream,
        branch_line,
        spatial_norm_grad,
        (fourth_grads, pair_grad, temporal_query_grad),
    ) = first_back_chain(
        stream_one,
        spatial_gain,
        normed_grad,
        upstream,
        owners,
        images,
        (19,),
        [
            by_frames(cross_query_grad),
            Exchange(pair_grad.reshape(lines, text_rows, 2 * half_width), ("space",)),
            LineSum(second_grads, jnp.float32),
        ],
    )
    branch_line, branch_owned = branch_line[:images], branch_line[images:]
    pair_grad = jnp.sum(pair_grad.astype(jnp.float32), axis=0).astype(jnp.bfloat16)
    second_conv_grad = conv_weight_grad(wide(second_wide), wide(branch_owned), "kc")
    second_part = conv_frames(wide(branch_line), second_conv, "OHWI", True).astype(jnp.bfloat16)
    second_in_grad, (fifth_grads, pair_line) = sum_lines(
        second_part.reshape(images, H * W, half_width),
        20,
        [by_frames(outs_grad), Share(pair_grad, ("space",))],
    )
    hidden_grad, scale_grad, shift_grad = group_backward(
        hidden, film_scale, film_shift, second_in_grad
    )
    frame_grads = jnp.stack([scale_grad, shift_grad], axis=1).reshape(slots, frame_dev, 2, -1)
    film_rows = jnp.einsum("bfv,bfjk->bvjk", choose, frame_grads, precision=highest)
    film_rows = film_rows.reshape(slots * VIDS * 2, -1)
    text_part = jnp.dot(
        pair_line.reshape(lines * text_rows, -1), cross_kv.T, preferred_element_type=jnp.float32
    )
    text_part = text_part.astype(jnp.bfloat16).reshape(lines, text_rows, -1)

    hidden_wide, (second_conv_grad, film_shares, text_part, pair_all) = gather_lines(
        hidden_grad,
        21,
        [FrameSum(second_conv_grad, True, kind=jnp.float32), Share(film_rows, ("tm",)), Exchange(text_part, ("space",)), Share(pair_line, ("tm",))],
    )
    film_rows = jnp.sum(film_shares, axis=0)
    first_conv_grad = conv_weight_grad(wide(first_owned), wide(hidden_wide), "ck")
    first_part = conv_frames(wide(hidden_wide), first_conv, "OHWI", True).astype(jnp.bfloat16)
    (
        first_in_grad,
        (first_conv_some, spatial_qkv_grad, cross_query_grad, outs_grad, film_shares),
    ) = sum_cores(
        first_part.reshape(images, H * W, -1),
        22,
        [
            FrameSum(first_conv_grad, True, 0, 5),
            FrameSum(spatial_qkv_grad, True),
            LineSum(fourth_grads, jnp.float32),
            LineSum(fifth_grads, jnp.float32),
            Share(film_rows, ("space",)),
        ],
    )
    video_line_grad, gain_grad, bias_grad = group_backward(
        video_lines[:images], gain_line[:images], bias_line[:images], first_in_grad
    )

    def placed(line_grad):
        whole = jnp.zeros((channels,), jnp.float32)
        size = line_grad.shape[2]
        place = (lax.axis_index("space") * cores + lax.axis_index("mp")) * size
        return lax.dynamic_update_slice_in_dim(whole, jnp.sum(line_grad, axis=(0, 1)), place, 0)

    small = jnp.concatenate(
        [
            item.reshape(owners, -1)
            for item in (
                placed(gain_grad),
                placed(bias_grad),
                spatial_norm_grad,
                two_grads[0],
                two_grads[1],
                feed_norm_grad,
                offset_bias_grad,
            )
        ],
        axis=1,
    )
    owner_rows = channels // owners

    def cut_qkv_rows(whole):
        return whole.reshape(3, lines, owner_rows, -1).transpose(1, 0, 2, 3)

    video_rows_grad, (small, qkv_part, first_conv_rest, temporal_pair_grad) = from_lines(
        video_line_grad,
        True,
        23,
        [
            SmallSum(small.reshape(frames_axis, lines, 1, -1)),
            ColumnJoin(
                spatial_qkv_grad,
                lambda ref, place: ref.at[:, span(place, owner_rows)],
                cut_qkv_rows,
            ),
            FrameSum(first_conv_grad, True, 5, 4),
            LineSum(third_grads, jnp.float32),
        ],
    )
    video_grad = upstream + video_rows_grad.reshape(token_rows, channels).astype(jnp.float32)

    video_film_grad = (
        film_shares.reshape(lines, slots, VIDS, 2, -1)
        .transpose(1, 2, 3, 0, 4)
        .reshape(slots, VIDS, 2, half_width)
    )
    film_weight_grad = jnp.einsum(
        "bvc,bvjk->cjk",
        part_of(part_of(embed, "tm", 2), "space", 2).astype(jnp.float32),
        video_film_grad,
        precision=highest,
    )
    cross_kv_grad = jnp.einsum(
        "prc,prk->ck",
        text_cols.transpose(1, 0, 2, 3).reshape(owners, text_rows, -1),
        pair_all.reshape(owners, text_rows, 2 * half_width),
        preferred_element_type=jnp.float32,
    )
    text_half = part_of(
        twin_add(text_part.transpose(1, 0, 2).reshape(text_rows, -1)), "mp", 1
    )
    small = small[0]
    small_twin = lax.ppermute(small, "mp", [(0, 1), (1, 0)])
    gain_size = channels // owners
    gains = [small[i * gain_size : (i + 1) * gain_size] for i in range(6)]
    for i in range(2):
        gains[i] = gains[i] + small_twin[i * gain_size : (i + 1) * gain_size]
    first_conv_grad = jnp.concatenate([first_conv_some, first_conv_rest])
    temporal_triple_grad = jnp.stack(
        [temporal_query_grad, *jnp.split(temporal_pair_grad, 2, axis=1)], axis=1
    )
    return (
        mixed.reshape(video.shape),
        video_grad.reshape(video.shape),
        text_half.reshape(slots, text_local, -1),
        gains[0],
        gains[1],
        first_conv_grad.astype(jnp.float32).transpose(1, 0, 2),
        film_weight_grad,
        second_conv_grad.transpose(2, 0, 1),
        gains[2],
        qkv_part.astype(jnp.float32).transpose(1, 0, 2),
        outs_grad[:, half_width:].T,
        gains[3],
        cross_query_grad,
        cross_kv_grad.reshape(-1, 2, half_width),
        outs_grad[:, :half_width].T,
        gains[4],
        temporal_triple_grad,
        temporal_out_grad.T,
        small[6 * gain_size :].reshape(R // owners, head_local),
        gains[5],
        feed_in_grad.astype(jnp.float32),
        feed_out_grad.astype(jnp.float32).T,
    )


def solution(mesh):
    return jax.shard_map(
        on_device,
        mesh=mesh,
        in_specs=(
            P(None, "tm", "space", None, None),
            P(None, "tm", "space", None, None),
            P(None, ("tm", "space"), None),
            P(),
            P(),
            P(),
            P(),
            P(),
            P("space", None, "mp"),
            P("space", None, "mp"),
            P("mp", None, "space"),
            P(),
            P("space", None, "mp"),
            P("mp", "space"),
            P(),
            P("space", "mp"),
            P("space", None, "mp"),
            P("mp", "space"),
            P(),
            P("space", None, "mp"),
            P("mp", "space"),
            P(None, "mp"),
            P(),
            P("space", "mp"),
            P("mp", "space"),
        ),
        out_specs=(
            P(None, "tm", "space", None, None),
            P(None, "tm", "space", None, None),
            P(None, ("tm", "space"), "mp"),
            P(("tm", "space")),
            P(("tm", "space")),
            P(("tm", "space"), None, "mp"),
            P(("tm", "space"), None, "mp"),
            P("mp", None, ("tm", "space")),
            P(("tm", "space")),
            P(("tm", "space"), None, "mp"),
            P("mp", ("tm", "space")),
            P(("tm", "space")),
            P(("tm", "space"), "mp"),
            P(("tm", "space"), None, "mp"),
            P("mp", ("tm", "space")),
            P(("tm", "space")),
            P(("tm", "space"), None, "mp"),
            P("mp", ("tm", "space")),
            P(("tm", "space"), "mp"),
            P(("tm", "space")),
            P(("tm", "space"), "mp"),
            P("mp", ("tm", "space")),
        ),
        check_vma=False,
    )
```

```python
import math

import jax
import jax.numpy as jnp
from jax import lax
from jax.experimental import pallas as pl
from jax.experimental.pallas import tpu as pltpu
from jax.sharding import PartitionSpec as P

D = 1024
HDIM = 64
TXT = 128
G = 32
R = 128
VIDS = 3
H = 16
W = 16


epsilon = 1e-05
highest = lax.Precision.HIGHEST
masked = -1e30


def twin_add(partial_sum):
    mine = partial_sum.astype(jnp.bfloat16)
    other = lax.ppermute(mine, "mp", [(0, 1), (1, 0)])
    return mine.astype(jnp.float32) + other.astype(jnp.float32)


def part_of(source, axis_name, dim):
    size = source.shape[dim] // lax.axis_size(axis_name)
    return lax.dynamic_slice_in_dim(source, lax.axis_index(axis_name) * size, size, dim)


MESH = pl.DeviceIdType.MESH
lane = 128
ANY = pl.BlockSpec(memory_space=pl.ANY)
VMEM = pl.BlockSpec(memory_space=pltpu.VMEM)


def meet(peers):
    gate = pltpu.get_barrier_semaphore()
    for peer in peers:
        pl.semaphore_signal(gate, inc=1, device_id=peer, device_id_type=MESH)
    pl.semaphore_wait(gate, len(peers))


def others(axis_name):
    count = lax.axis_size(axis_name)
    me = lax.axis_index(axis_name)
    return [(step, lax.rem(me + step, count)) for step in range(1, count)]


def send(source, target, send_sem, recv_sem, peer):
    copy = pltpu.make_async_remote_copy(
        src_ref=source,
        dst_ref=target,
        send_sem=send_sem,
        recv_sem=recv_sem,
        device_id=peer,
        device_id_type=MESH,
    )
    copy.start()
    return copy


def keep(source, target, sem):
    copy = pltpu.make_async_copy(source, target, sem)
    copy.start()
    return copy


def cols_of(ref, index, width):
    return ref.at[:, :, pl.ds(pl.multiple_of(index * width, width), width)]


def rows_of(ref, index, width):
    return ref.at[:, pl.ds(pl.multiple_of(index * width, width), width), :]


def talk(kernel, result, operands, scratch, number, specs=None, out_spec=ANY, grant=32):
    return pl.pallas_call(
        kernel,
        out_shape=result,
        in_specs=[ANY] * len(operands) if specs is None else specs,
        out_specs=out_spec,
        scratch_shapes=scratch,
        compiler_params=pltpu.CompilerParams(
            collective_id=number, has_side_effects=True, vmem_limit_bytes=grant * 1024 * 1024
        ),
    )(*operands)


def dma_sems(*counts):
    return [pltpu.SemaphoreType.DMA((max(count, 1),)) for count in counts]


def flat_index(axes):
    index = 0
    for name in axes:
        index = index * lax.axis_size(name) + lax.axis_index(name)
    return index


def flat_peers(axes):
    count = math.prod(lax.axis_size(name) for name in axes)
    me = flat_index(axes)
    peers = []
    for step in range(1, count):
        peer = lax.rem(me + step, count)
        place, rest = {}, peer
        for name in reversed(axes):
            place[name] = lax.rem(rest, lax.axis_size(name))
            rest = rest // lax.axis_size(name)
        peers.append((step, peer, place))
    return peers


class Rider:
    scratch = ()
    source_spec = ANY
    result_spec = ANY

    def peers(self):
        return [place for _, _, place in flat_peers(self.axes)]

    def middle(self, *refs):
        pass


def square_places():
    me = lax.axis_index("tm")
    near = me + 1 - 2 * lax.rem(me, 2)
    far = me + 2 - 4 * (me // 2)
    return me, near, far, 3 - me


class Exchange(Rider):
    def __init__(self, source, axes, pick=None, cut=None):
        self.source, self.axes, self.cut = source, axes, cut
        self.pick = (lambda ref, place: ref.at[place]) if pick is None else pick
        stack = source if cut is None else jax.eval_shape(cut, source)
        count = math.prod(lax.axis_size(name) for name in axes)
        self.result = jax.ShapeDtypeStruct(stack.shape, stack.dtype)
        self.scratch = dma_sems(count - 1, count - 1, 1)

    def plain(self):
        stack = self.source if self.cut is None else self.cut(self.source)
        return lax.all_to_all(stack, self.axes, split_axis=0, concat_axis=0, tiled=True)

    def start(self, x_ref, out_ref, send_sem, recv_sem, own_sem):
        me = flat_index(self.axes)
        self.copies = [
            send(self.pick(x_ref, peer), out_ref.at[me], send_sem.at[i - 1], recv_sem.at[i - 1], place)
            for i, peer, place in flat_peers(self.axes)
        ]
        self.copies.append(keep(self.pick(x_ref, me), out_ref.at[me], own_sem.at[0]))

    def finish(self, *refs):
        for copy in self.copies:
            copy.wait()


class ColumnJoin(Rider):
    axes = ("space",)

    def __init__(self, source, pick, cut):
        self.source, self.pick, self.cut = source, pick, cut
        stack = jax.eval_shape(cut, source)
        self.lines, self.width = stack.shape[0], stack.shape[-1]
        shape = stack.shape[1:-1] + (self.lines * self.width,)
        self.result = jax.ShapeDtypeStruct(shape, stack.dtype)
        self.scratch = dma_sems(self.lines - 1, self.lines - 1, 1)

    def plain(self):
        stack = lax.all_to_all(
            self.cut(self.source), "space", split_axis=0, concat_axis=0, tiled=True
        )
        return jnp.concatenate([stack[i] for i in range(self.lines)], axis=-1)

    def start(self, x_ref, out_ref, send_sem, recv_sem, own_sem):
        me = lax.axis_index("space")
        cols = span(me, self.width)
        target = out_ref.at[:, cols] if len(self.result.shape) == 2 else out_ref.at[:, :, cols]
        self.copies = [
            send(self.pick(x_ref, peer), target, send_sem.at[i - 1], recv_sem.at[i - 1], {"space": peer})
            for i, peer in others("space")
        ]
        self.copies.append(keep(self.pick(x_ref, me), target, own_sem.at[0]))

    def finish(self, *refs):
        for copy in self.copies:
            copy.wait()


def span(index, size):
    return pl.ds(pl.multiple_of(index * size, size), size)


class LineSum(Rider):
    axes = ("space",)
    source_spec = VMEM
    result_spec = VMEM

    def __init__(self, source, kind=jnp.bfloat16):
        self.source = source
        self.lines = lax.axis_size("space")
        self.rows, self.width = source.shape[0] // self.lines, source.shape[1]
        self.result = jax.ShapeDtypeStruct((self.rows, self.width), kind)
        self.scratch = [
            pltpu.VMEM((self.lines - 1, self.rows, self.width), jnp.bfloat16)
        ] + dma_sems(self.lines - 1, self.lines - 1)

    def plain(self):
        total = lax.psum_scatter(self.source, "space", scatter_dimension=0, tiled=True)
        return total.astype(self.result.dtype)

    def start(self, x_ref, out_ref, got_ref, send_sem, recv_sem):
        self.copies = [
            send(x_ref.at[span(peer, self.rows)], got_ref.at[i - 1], send_sem.at[i - 1], recv_sem.at[i - 1], {"space": peer})
            for i, peer in others("space")
        ]

    def finish(self, x_ref, out_ref, got_ref, *sems):
        for copy in self.copies:
            copy.wait()
        total = x_ref[span(lax.axis_index("space"), self.rows)].astype(jnp.float32)
        for step in range(self.lines - 1):
            total = total + got_ref[step].astype(jnp.float32)
        out_ref[...] = total.astype(out_ref.dtype)


class Share(Rider):
    def __init__(self, source, axes, first=0, size=None, cols=None):
        self.source, self.axes = source, axes
        self.first, self.size, self.cols = first, size, cols
        count = math.prod(lax.axis_size(name) for name in axes)
        shape = source.shape if size is None else (size,) + source.shape[1:]
        if cols is not None:
            shape = shape[:-1] + (cols[1] - cols[0],)
        self.shape = shape
        self.result = jax.ShapeDtypeStruct((count,) + shape, source.dtype)
        even = (len(shape) > 2 and shape[0] % 2 == 0) or shape[-2] % 32 == 0
        self.square = axes == ("tm",) and count == 4 and even
        copies = 4 if self.square else count - 1
        self.scratch = dma_sems(copies, copies, 1)

    def plain(self):
        source = self.source
        if self.size is not None:
            source = source[self.first : self.first + self.size]
        if self.cols is not None:
            source = source[..., self.cols[0] : self.cols[1]]
        return lax.all_gather(source, self.axes, axis=0, tiled=False)

    def half(self, ref, index):
        if len(self.shape) > 2 and self.shape[0] % 2 == 0:
            size = self.shape[0] // 2
            return ref.at[pl.ds(index * size, size)]
        size = self.shape[-2] // 2
        rows = pl.ds(index * size, size)
        return ref.at[:, rows] if len(self.shape) == 3 else ref.at[rows]

    def start(self, x_ref, out_ref, send_sem, recv_sem, own_sem):
        part = x_ref if self.size is None else x_ref.at[pl.ds(self.first, self.size)]
        if self.cols is not None:
            part = part.at[:, :, pl.ds(self.cols[0], self.cols[1] - self.cols[0])]
        if self.square:
            me, near, far, _ = square_places()
            self.copies = [
                send(part, out_ref.at[me], send_sem.at[i], recv_sem.at[i], {"tm": peer})
                for i, peer in enumerate((near, far))
            ]
        else:
            me = flat_index(self.axes)
            self.copies = [
                send(part, out_ref.at[me], send_sem.at[i - 1], recv_sem.at[i - 1], place)
                for i, _, place in flat_peers(self.axes)
            ]
        self.own = keep(part, out_ref.at[me], own_sem.at[0])

    def middle(self, x_ref, out_ref, send_sem, recv_sem, own_sem):
        if not self.square:
            return
        _, near, far, _ = square_places()
        from_near, from_far = self.copies
        from_far.wait_recv()
        got = self.half(out_ref.at[far], 0)
        to_near = send(got, got, send_sem.at[2], recv_sem.at[2], {"tm": near})
        from_near.wait_recv()
        got = self.half(out_ref.at[near], 1)
        to_far = send(got, got, send_sem.at[3], recv_sem.at[3], {"tm": far})
        self.passed = [to_near, to_far]

    def finish(self, *refs):
        if self.square:
            for copy in self.copies:
                copy.wait_send()
            for copy in self.passed:
                copy.wait()
        else:
            for copy in self.copies:
                copy.wait()
        self.own.wait()


class JoinCores(Rider):
    def __init__(self, source):
        self.source = source
        self.rows, self.width = source.shape
        shape = (self.rows, self.width * lax.axis_size("mp"))
        self.result = jax.ShapeDtypeStruct(shape, source.dtype)
        self.scratch = dma_sems(1, 1, 1)

    def peers(self):
        return twin_peers()

    def plain(self):
        return lax.all_gather(self.source, "mp", axis=1, tiled=True)

    def start(self, x_ref, out_ref, send_sem, recv_sem, own_sem):
        core = lax.axis_index("mp")
        mine = out_ref.at[:, pl.ds(pl.multiple_of(core * self.width, self.width), self.width)]
        self.copies = [
            send(x_ref, mine, send_sem.at[0], recv_sem.at[0], {"mp": 1 - core}),
            keep(x_ref, mine, own_sem.at[0]),
        ]

    def finish(self, *refs):
        for copy in self.copies:
            copy.wait()


class LineColumns(Rider):
    axes = ("space",)

    def __init__(self, source):
        self.source = source
        lines = lax.axis_size("space")
        self.width = source.shape[1] // lines
        shape = (lines, source.shape[0], self.width)
        self.result = jax.ShapeDtypeStruct(shape, source.dtype)
        self.scratch = dma_sems(lines - 1, lines - 1, 1)

    def plain(self):
        return lax.all_to_all(
            self.source[None], "space", split_axis=2, concat_axis=0, tiled=True
        )

    def start(self, x_ref, out_ref, send_sem, recv_sem, own_sem):
        me = lax.axis_index("space")

        def part(index):
            return x_ref.at[:, pl.ds(pl.multiple_of(index * self.width, self.width), self.width)]

        self.copies = [
            send(part(peer), out_ref.at[me], send_sem.at[i - 1], recv_sem.at[i - 1], {"space": peer})
            for i, peer in others("space")
        ]
        self.copies.append(keep(part(me), out_ref.at[me], own_sem.at[0]))

    def finish(self, *refs):
        for copy in self.copies:
            copy.wait()


class FrameSum(Rider):
    axes = ("tm",)
    result_spec = VMEM

    def __init__(self, source, taps=False, first=0, size=None, kind=jnp.bfloat16):
        self.taps, self.first = taps, first
        self.count = lax.axis_size("tm")
        if taps:
            self.layers, all_rows, self.width = source.shape
            self.layers = self.layers if size is None else size
            self.rows = all_rows // self.count
        else:
            self.layers, (_, self.rows, self.width) = 1, source.shape
        self.source = source
        shape = (self.layers, self.rows, self.width)
        self.result = jax.ShapeDtypeStruct(shape if taps else shape[1:], kind)
        self.square = self.count == 4 and self.rows % 32 == 0
        self.split = self.rows // 2 if self.square else self.rows
        half = (self.layers, self.split, self.width)
        if self.square:
            self.scratch = [
                pltpu.VMEM((2, 2) + half, jnp.bfloat16),
                pltpu.VMEM((2,) + half, jnp.bfloat16),
                pltpu.VMEM((2, 2) + half, jnp.bfloat16),
            ] + dma_sems(4, 6, 6)
        else:
            self.scratch = [
                pltpu.VMEM((max(self.count - 1, 1),) + half, jnp.bfloat16),
                pltpu.VMEM((1, 1) + half, jnp.bfloat16),
            ] + dma_sems(1, self.count - 1, self.count - 1)

    def plain(self):
        dim = 1 if self.taps else 0
        source = self.source
        if self.taps:
            source = source[self.first : self.first + self.layers]
        total = lax.psum_scatter(source, "tm", scatter_dimension=dim, tiled=True)
        return (total if self.taps else total[0]).astype(self.result.dtype)

    def view(self, w_ref, place, half):
        if self.taps:
            start = pl.multiple_of(place * self.rows + half * self.split, self.split)
            return w_ref.at[pl.ds(self.first, self.layers), pl.ds(start, self.split)]
        return w_ref.at[pl.ds(place, 1), pl.ds(half * self.split, self.split)]

    def add(self, target_ref, first, *rest):
        block = min(16, self.split)
        steps = self.split // block

        def some(index, carry):
            layer = index // steps
            rows = pl.ds(pl.multiple_of(lax.rem(index, steps) * block, block), block)
            total = first[layer, rows].astype(jnp.float32)
            for other in rest:
                total = total + other[layer, rows].astype(jnp.float32)
            target_ref[layer, rows] = total.astype(target_ref.dtype)
            return carry

        lax.fori_loop(0, self.layers * steps, some, 0)

    def out_view(self, out_ref, half):
        rows = pl.ds(half * self.split, self.split)
        if self.taps:
            return out_ref.at[:, rows]
        return out_ref.reshape(1, self.rows, self.width).at[:, rows]

    def start(self, w_ref, out_ref, got_ref, *rest):
        near_ref, own_sem, send_sem, recv_sem = rest[-4:]
        if not self.square:
            me = lax.axis_index("tm")
            self.copies = [
                send(self.view(w_ref, peer, 0), got_ref.at[i - 1], send_sem.at[i - 1], recv_sem.at[i - 1], {"tm": peer})
                for i, peer in others("tm")
            ]
            self.own = [keep(self.view(w_ref, me, 0), near_ref.at[0, 0], own_sem.at[0])]
            return
        me, near, far, across = square_places()
        self.copies = [
            send(self.view(w_ref, place, half), got_ref.at[half, i], send_sem.at[2 * half + i], recv_sem.at[2 * half + i], {"tm": peer})
            for half, peer in ((0, near), (1, far))
            for i, place in ((1, across), (0, peer))
        ]
        self.own = [
            keep(self.view(w_ref, place, half), near_ref.at[half, i], own_sem.at[2 * half + i])
            for half, peer in ((0, far), (1, near))
            for i, place in ((0, me), (1, peer))
        ]

    def middle(self, w_ref, out_ref, got_ref, *rest):
        if not self.square:
            return
        last_ref, near_ref, _, send_sem, recv_sem = rest
        _, near, far, _ = square_places()
        self.passed = []
        for half, peer in ((0, far), (1, near)):
            self.copies[2 * half].wait_recv()
            self.own[2 * half + 1].wait()
            self.add(got_ref.at[half, 1], near_ref.at[half, 1], got_ref.at[half, 1])
            self.passed.append(
                send(got_ref.at[half, 1], last_ref.at[half], send_sem.at[4 + half], recv_sem.at[4 + half], {"tm": peer})
            )

    def finish(self, w_ref, out_ref, got_ref, *rest):
        near_ref = rest[-4]
        if not self.square:
            for copy in self.copies + self.own:
                copy.wait()
            parts = [got_ref.at[i] for i in range(self.count - 1)]
            self.add(self.out_view(out_ref, 0), near_ref.at[0, 0], *parts)
            return
        last_ref = rest[0]
        for half in range(2):
            self.copies[2 * half].wait_send()
            self.copies[2 * half + 1].wait()
            self.own[2 * half].wait()
            self.passed[half].wait()
            self.add(
                self.out_view(out_ref, half),
                near_ref.at[half, 0],
                got_ref.at[half, 0],
                last_ref.at[half],
            )


class SmallSum(Rider):
    source_spec = VMEM
    result_spec = VMEM

    def __init__(self, source):
        self.source = source
        self.frames, self.lines = source.shape[:2]
        part = source.shape[1:]
        self.result = jax.ShapeDtypeStruct(part[1:], source.dtype)
        self.scratch = [
            pltpu.VMEM((self.frames - 1,) + part, source.dtype),
            pltpu.VMEM(part, source.dtype),
            pltpu.VMEM((self.lines - 1,) + part[1:], source.dtype),
        ] + dma_sems(self.frames - 1, self.frames - 1, self.lines - 1, self.lines - 1)

    def peers(self):
        return frame_peers() + line_peers()

    def plain(self):
        total = lax.psum_scatter(self.source, "tm", scatter_dimension=0, tiled=True)[0]
        return lax.psum_scatter(total, "space", scatter_dimension=0, tiled=True)[0]

    def start(self, x_ref, out_ref, got_ref, sum_ref, last_ref, send_sem, recv_sem, send2, recv2):
        self.copies = [
            send(x_ref.at[peer], got_ref.at[i - 1], send_sem.at[i - 1], recv_sem.at[i - 1], {"tm": peer})
            for i, peer in others("tm")
        ]

    def middle(self, x_ref, out_ref, got_ref, sum_ref, last_ref, send_sem, recv_sem, send2, recv2):
        total = x_ref[lax.axis_index("tm")]
        for i, copy in enumerate(self.copies):
            copy.wait()
            total = total + got_ref[i]
        sum_ref[...] = total
        self.passed = [
            send(sum_ref.at[peer], last_ref.at[i - 1], send2.at[i - 1], recv2.at[i - 1], {"space": peer})
            for i, peer in others("space")
        ]

    def finish(self, x_ref, out_ref, got_ref, sum_ref, last_ref, *sems):
        total = sum_ref[lax.axis_index("space")]
        for i, copy in enumerate(self.passed):
            copy.wait()
            total = total + last_ref[i]
        out_ref[...] = total


class Keep(Rider):
    def __init__(self, source):
        self.source = source
        self.result = jax.ShapeDtypeStruct(source.shape, source.dtype)
        self.scratch = dma_sems(1)

    def peers(self):
        return []

    def plain(self):
        return self.source

    def start(self, x_ref, out_ref, own_sem):
        self.copy = keep(x_ref, out_ref, own_sem.at[0])

    def finish(self, *refs):
        self.copy.wait()


class CoreSum(Rider):
    source_spec = VMEM
    result_spec = VMEM

    def __init__(self, source):
        self.source = source
        rows, channels = source.shape
        self.rows, self.width = rows, channels // lax.axis_size("mp")
        self.result = jax.ShapeDtypeStruct((rows, self.width), jnp.bfloat16)
        self.scratch = [pltpu.VMEM((rows, self.width), jnp.bfloat16)] + dma_sems(1, 1)

    def peers(self):
        return twin_peers()

    def start(self, x_ref, out_ref, got_ref, send_sem, recv_sem):
        core = lax.axis_index("mp")
        theirs = pl.ds(pl.multiple_of((1 - core) * self.width, self.width), self.width)
        self.copy = send(x_ref.at[:, theirs], got_ref, send_sem.at[0], recv_sem.at[0], {"mp": 1 - core})

    def finish(self, x_ref, out_ref, got_ref, *sems):
        self.copy.wait()
        block = min(128, self.rows)
        start = lax.axis_index("mp") * self.width
        mine = pl.ds(pl.multiple_of(start, self.width), self.width)

        def some(index, carry):
            rows = pl.ds(pl.multiple_of(index * block, block), block)
            total = x_ref[rows, mine].astype(jnp.float32) + got_ref[rows, :].astype(jnp.float32)
            out_ref[rows, :] = total.astype(jnp.bfloat16)
            return carry

        lax.fori_loop(0, self.rows // block, some, 0)


def plain_all(riders):
    return [rider.plain() for rider in riders]


def talk_many(
    kernel, peers, results, operands, scratch, number, riders, specs, out_specs, grant=32
):
    inputs, outputs, own_scratch, count = len(operands), len(results), len(scratch), len(riders)

    def whole(*refs):
        ins, rider_ins = refs[:inputs], refs[inputs : inputs + count]
        outs = refs[inputs + count : inputs + count + outputs]
        rider_outs = refs[inputs + count + outputs : inputs + 2 * count + outputs]
        rest = refs[inputs + 2 * count + outputs :]
        mine, rest = rest[:own_scratch], rest[own_scratch:]
        packs = []
        for rider, x_ref, y_ref in zip(riders, rider_ins, rider_outs):
            packs.append((x_ref, y_ref) + tuple(rest[: len(rider.scratch)]))
            rest = rest[len(rider.scratch) :]
        meet(peers() + [peer for rider in riders for peer in rider.peers()])
        for rider, pack in zip(riders, packs):
            rider.start(*pack)
        waiting = list(zip(riders, packs))

        def hook():
            while waiting:
                rider, pack = waiting.pop(0)
                rider.middle(*pack)

        kernel(hook, *ins, *outs, *mine)
        hook()
        for rider, pack in zip(riders, packs):
            rider.finish(*pack)

    done = talk(
        whole,
        tuple(results) + tuple(rider.result for rider in riders),
        list(operands) + [rider.source for rider in riders],
        scratch + [item for rider in riders for item in rider.scratch],
        number,
        list(specs) + [rider.source_spec for rider in riders],
        tuple(out_specs) + tuple(rider.result_spec for rider in riders),
        grant,
    )
    return list(done[:outputs]), list(done[outputs:])


def talk_with(
    kernel, peers, result, operands, scratch, number, riders, specs=None, out_spec=ANY, grant=32
):
    if number is None:
        return kernel, peers, result, scratch
    specs = [ANY] * len(operands) if specs is None else specs
    done, others_done = talk_many(
        kernel, peers, [result], operands, scratch, number, riders, specs, [out_spec], grant
    )
    return done[0], others_done


def line_peers():
    return [{"space": peer} for _, peer in others("space")]


def frame_peers():
    return [{"tm": peer} for _, peer in others("tm")]


def twin_peers():
    return [{"mp": 1 - lax.axis_index("mp")}]


pieces_per_chunk = 2


def relay_gather(lines, own, slot, sems, hook, arrived=None):
    me = lax.axis_index("space")
    right_send, right_recv, left_send, left_recv = sems
    parts = pieces_per_chunk

    def move(step, part, sign, send_sem, recv_sem):
        place = slot(lax.rem(me - sign * step + lines, lines), part)
        at = step * parts + part
        return pltpu.make_async_remote_copy(
            own(part) if step == 0 else place, place, send_sem.at[at], recv_sem.at[at],
            device_id={"space": lax.rem(me + sign + lines, lines)}, device_id_type=MESH,
        )

    def came(step, part, sign, recv_sem, order):
        place = slot(lax.rem(me - sign * (step + 1) + lines, lines), part)
        at = step * parts + part
        pltpu.make_async_remote_copy(
            place, place, recv_sem.at[at], recv_sem.at[at],
            device_id={"space": lax.rem(me + 1, lines)}, device_id_type=MESH,
        ).wait_recv()
        if arrived is not None:
            arrived(place, order * parts + part)

    ways = (
        (1, me, right_send, right_recv, 0),
        (-1, lines - 1 - me, left_send, left_recv, lines - 1),
    )
    for step in range(lines):
        for part in range(parts):
            for sign, rank, send_sem, recv_sem, order in ways:
                if step > 0:

                    @pl.when(rank >= step)
                    def _():
                        came(step - 1, part, sign, recv_sem, order + step - 1)

                if step < lines - 1:

                    @pl.when((rank >= step) & (rank + 1 < lines))
                    def _():
                        move(step, part, sign, send_sem, recv_sem).start()

        if step == max(lines - 2, 0):
            hook()
    for step in range(lines - 1):
        for part in range(parts):
            for sign, rank, send_sem, recv_sem, _ in ways:

                @pl.when((rank >= step) & (rank + 1 < lines))
                def _():
                    move(step, part, sign, send_sem, recv_sem).wait_send()


def relay_sum(lines, stage_ref, right_ref, left_ref, sems, hook, ready=None):
    me = lax.axis_index("space")
    right_send, right_recv, left_send, left_recv = sems
    parts, last = pieces_per_chunk, lines - 1

    def move(source, slots, sem_out, sem_in, step, part, peer):
        at = step * parts + part
        return pltpu.make_async_remote_copy(
            source, slots.at[step, part], sem_out.at[at], sem_in.at[at],
            device_id={"space": lax.rem(peer + lines, lines)}, device_id_type=MESH,
        )

    def add(slots, step, part, place):
        total = slots[step, part].astype(jnp.float32) + stage_ref[place, part].astype(jnp.float32)
        slots[step, part] = total.astype(jnp.bfloat16)

    ways = (
        (me, me + 1, right_ref, right_send, right_recv, lambda step: last - step + me),
        (last - me, me - 1, left_ref, left_send, left_recv, lambda step: step - last + me),
    )
    for step in range(last):
        if ready is not None:
            ready(step)
        for part in range(parts):
            for rank, peer, slots, sem_out, sem_in, target in ways:
                place = lax.rem(target(step) + 2 * lines, lines)

                @pl.when(rank == 0)
                def _():
                    move(stage_ref.at[place, part], slots, sem_out, sem_in, step, part, peer).start()

                if step > 0:

                    @pl.when((rank > 0) & (rank <= step))
                    def _():
                        source = stage_ref.at[place, part]
                        move(source, slots, sem_out, sem_in, step - 1, part, peer).wait_recv()
                        add(slots, step - 1, part, place)
                        source = slots.at[step - 1, part]
                        move(source, slots, sem_out, sem_in, step, part, peer).start()

        if step == last - 1:
            hook()
    for part in range(parts):
        for rank, peer, slots, sem_out, sem_in, target in ways:

            @pl.when(rank > 0)
            def _():
                move(stage_ref.at[0, part], slots, sem_out, sem_in, last - 1, part, peer).wait_recv()

            for step in range(last):

                @pl.when(rank <= step)
                def _():
                    move(stage_ref.at[0, part], slots, sem_out, sem_in, step, part, peer).wait_send()


def to_lines(source, per_core, number, riders=(), join=False):
    images, pixels, channels = source.shape
    lines, cores = lax.axis_size("space"), lax.axis_size("mp")
    pieces = lines * cores if per_core or join else lines
    width = channels // pieces
    if width % lane != 0 or pixels % 16 != 0:
        if number is None:
            return None
        if per_core:
            parts = source.reshape(images, pixels, lines, cores, width)
            parts = lax.dynamic_index_in_dim(parts, lax.axis_index("mp"), 3, keepdims=False)
            source = parts.reshape(images, pixels, lines * width)
        moved = lax.all_to_all(source, "space", split_axis=2, concat_axis=1, tiled=True)
        return moved, plain_all(riders)

    def kernel(hook, x_ref, out_ref, stage_ref, send_sem, recv_sem, pass_sem, gain_sem, own_sem):
        me, core = lax.axis_index("space"), lax.axis_index("mp")
        twin = {"mp": 1 - core}
        place = (lambda s: s * cores + core) if per_core or join else (lambda s: s)

        def spot(origin):
            rows = rows_of(out_ref, origin, pixels)
            return cols_of(rows, core, width) if join else rows

        copies = []
        for i, peer in others("space"):
            start = pl.multiple_of(place(peer) * width, width)
            stage_ref[i - 1] = x_ref[:, :, pl.ds(start, width)]
            copies.append(
                send(stage_ref.at[i - 1], spot(me), send_sem.at[i - 1], recv_sem.at[i - 1], {"space": peer})
            )
        if join:
            own_width = cores * width
            own = keep(cols_of(x_ref, me, own_width), rows_of(out_ref, me, pixels), own_sem.at[0])
        else:
            own = keep(cols_of(x_ref, place(me), width), spot(me), own_sem.at[0])
        hook()
        passed = []
        for step in range(1, lines):
            copies[step - 1].wait_recv()
            if join:
                got = spot(lax.rem(me - step + lines, lines))
                passed.append(send(got, got, pass_sem.at[step - 1], gain_sem.at[step - 1], twin))
        for copy in copies:
            copy.wait_send()
        own.wait()
        for copy in passed:
            copy.wait()

    def peers():
        return line_peers() + (twin_peers() if join else [])

    held = cores * width if join else width
    result = jax.ShapeDtypeStruct((images, lines * pixels, held), source.dtype)
    scratch = [pltpu.VMEM((lines - 1, images, pixels, width), source.dtype)]
    scratch = scratch + dma_sems(lines - 1, lines - 1, lines - 1, lines - 1, 1)
    return talk_with(kernel, peers, result, [source], scratch, number, riders, [VMEM], ANY, 58)


def from_lines(source, per_core, number, riders=()):
    images, line_pixels, width = source.shape
    lines, cores = lax.axis_size("space"), lax.axis_size("mp")
    pixels = line_pixels // lines
    pieces = lines * cores if per_core else lines
    if width % lane != 0 or pixels % 16 != 0:
        if number is None:
            return None
        part = lax.all_to_all(source, "space", split_axis=1, concat_axis=2, tiled=True)
        if per_core:
            part = part.reshape(images, pixels, lines, 1, width)
            part = lax.all_gather(part, "mp", axis=3, tiled=True)
        return part.reshape(images, pixels, pieces * width), plain_all(riders)

    def kernel(hook, x_ref, out_ref, got_ref, send_sem, recv_sem, pass_sem, gain_sem):
        me, core = lax.axis_index("space"), lax.axis_index("mp")
        twin = {"mp": 1 - core}
        mine = core if per_core else 0
        copies = [
            send(rows_of(x_ref, peer, pixels), got_ref.at[me, mine], send_sem.at[i - 1], recv_sem.at[i - 1], {"space": peer})
            for i, peer in others("space")
        ]
        passed = []
        if per_core:
            passed.append(
                send(rows_of(x_ref, me, pixels), got_ref.at[me, core], pass_sem.at[0], gain_sem.at[0], twin)
            )
        got_ref[me, mine] = x_ref[:, pl.ds(pl.multiple_of(me * pixels, pixels), pixels), :]
        hook()
        for step in range(1, lines):
            copies[step - 1].wait_recv()
            if per_core:
                got = got_ref.at[lax.rem(me - step + lines, lines), core]
                passed.append(send(got, got, pass_sem.at[step], gain_sem.at[step], twin))
        for copy in copies:
            copy.wait_send()
        for copy in passed:
            copy.wait()
        each = pieces // lines
        for piece in range(pieces):
            out_ref[:, :, piece * width : (piece + 1) * width] = got_ref[piece // each, piece % each]

    def peers():
        return line_peers() + ([{"mp": 1 - lax.axis_index("mp")}] if per_core else [])

    result = jax.ShapeDtypeStruct((images, pixels, pieces * width), source.dtype)
    scratch = [pltpu.VMEM((lines, pieces // lines, images, pixels, width), source.dtype)]
    scratch = scratch + dma_sems(lines - 1, lines - 1, lines, lines)
    return talk_with(kernel, peers, result, [source], scratch, number, riders, [VMEM], VMEM)


def gather_lines(source, number, riders=()):
    images, line_pixels, width = source.shape
    lines = lax.axis_size("space")
    if width % lane != 0:
        return lax.all_gather(source, "space", axis=2, tiled=True), plain_all(riders)

    def kernel(hook, x_ref, out_ref, got_ref, *sems):
        some = images // pieces_per_chunk

        def own(part):
            return x_ref.at[pl.ds(part * some, some)]

        def slot(index, part):
            return got_ref.at[index, pl.ds(part * some, some)]

        got_ref[lax.axis_index("space")] = x_ref[...]
        relay_gather(lines, own, slot, sems, hook)
        for line in range(lines):
            out_ref[:, :, line * width : (line + 1) * width] = got_ref[line]

    result = jax.ShapeDtypeStruct((images, line_pixels, lines * width), source.dtype)
    scratch = [pltpu.VMEM((lines,) + source.shape, source.dtype)]
    scratch = scratch + dma_sems(*[pieces_per_chunk * (lines - 1)] * 4)
    return talk_with(kernel, line_peers, result, [source], scratch, number, riders, [VMEM], VMEM)


def gather_cores(source, number, riders=()):
    images, line_pixels, width = source.shape
    cores = lax.axis_size("mp")
    if width % lane != 0:
        return lax.all_gather(source, "mp", axis=2, tiled=True), plain_all(riders)

    def kernel(hook, x_ref, out_ref, send_sem, recv_sem, own_sem):
        core = lax.axis_index("mp")
        twin = {"mp": 1 - core}
        target = cols_of(out_ref, core, width)
        copy = send(x_ref, target, send_sem.at[0], recv_sem.at[0], twin)
        own = keep(x_ref, target, own_sem.at[0])
        hook()
        copy.wait()
        own.wait()

    result = jax.ShapeDtypeStruct((images, line_pixels, cores * width), source.dtype)
    return talk_with(kernel, twin_peers, result, [source], dma_sems(1, 1, 1), number, riders)


def sum_lines(source, number, riders=()):
    images, line_pixels, channels = source.shape
    lines = lax.axis_size("space")
    width = channels // lines
    if width % lane != 0:
        total = lax.psum_scatter(source, "space", scatter_dimension=2, tiled=True)
        return total.astype(jnp.float32), plain_all(riders)

    def kernel(hook, x_ref, out_ref, stage_ref, right_ref, left_ref, *sems):
        me = lax.axis_index("space")
        for line in range(lines):
            for part in range(pieces_per_chunk):
                rows = slice(part * some, (part + 1) * some)
                stage_ref[line, part] = x_ref[rows, :, line * width : (line + 1) * width]
        relay_sum(lines, stage_ref, right_ref, left_ref, sems, hook)
        for part in range(pieces_per_chunk):
            rows = slice(part * some, (part + 1) * some)
            out_ref[rows] = stage_ref[me, part].astype(jnp.float32)

            @pl.when(me > 0)
            def _():
                out_ref[rows] += right_ref[lines - 2, part].astype(jnp.float32)

            @pl.when(me < lines - 1)
            def _():
                out_ref[rows] += left_ref[lines - 2, part].astype(jnp.float32)

    result = jax.ShapeDtypeStruct((images, line_pixels, width), jnp.float32)
    some = images // pieces_per_chunk
    chunk = (pieces_per_chunk, some, line_pixels, width)
    scratch = [
        pltpu.VMEM((lines,) + chunk, source.dtype),
        pltpu.VMEM((lines - 1,) + chunk, source.dtype),
        pltpu.VMEM((lines - 1,) + chunk, source.dtype),
    ] + dma_sems(*[pieces_per_chunk * (lines - 1)] * 4)
    return talk_with(kernel, line_peers, result, [source], scratch, number, riders, [VMEM], VMEM)


def sum_cores(source, number, riders=()):
    images, line_pixels, channels = source.shape
    cores = lax.axis_size("mp")
    width = channels // cores
    if width % lane != 0:
        total = lax.psum_scatter(source, "mp", scatter_dimension=2, tiled=True)
        return total.astype(jnp.float32), plain_all(riders)

    def kernel(hook, x_ref, out_ref, got_ref, send_sem, recv_sem):
        core = lax.axis_index("mp")
        twin = {"mp": 1 - core}
        copy = send(cols_of(x_ref, 1 - core, width), got_ref, send_sem.at[0], recv_sem.at[0], twin)
        mine = pl.ds(pl.multiple_of(core * width, width), width)
        hook()
        copy.wait()
        for image in range(images):
            out_ref[image] = x_ref[image, :, mine].astype(jnp.float32) + got_ref[image].astype(
                jnp.float32
            )

    result = jax.ShapeDtypeStruct((images, line_pixels, width), jnp.float32)
    scratch = [pltpu.VMEM((images, line_pixels, width), source.dtype)]
    scratch = scratch + dma_sems(1, 1)
    return talk_with(
        kernel, twin_peers, result, [source], scratch, number, riders, [VMEM], VMEM
    )


def gather_tokens(rows, number, riders=()):
    count, channels = rows.shape
    lines, cores = lax.axis_size("space"), lax.axis_size("mp")
    width = channels // cores
    source = None if number is None else rows.reshape(1, count, channels)

    def kernel(hook, x_ref, out_ref, pass_sem, gain_sem, own_sem, *sems):
        me, core = lax.axis_index("space"), lax.axis_index("mp")
        twin = {"mp": 1 - core}

        some = count // pieces_per_chunk

        def spot(origin, part):
            start = pl.multiple_of(origin * count + part * some, some)
            return cols_of(out_ref.at[:, pl.ds(start, some)], core, width)

        def own_part(part):
            return cols_of(x_ref.at[:, pl.ds(part * some, some)], core, width)

        def hand(ref, order):
            return pltpu.make_async_remote_copy(
                ref, ref, pass_sem.at[order], gain_sem.at[order], device_id=twin, device_id_type=MESH
            )

        own = keep(x_ref, rows_of(out_ref, me, count), own_sem.at[0])
        relay_gather(
            lines,
            own_part,
            spot,
            sems,
            hook,
            lambda ref, order: hand(ref, order).start(),
        )
        own.wait()
        parts = pieces_per_chunk
        for step in range(1, lines):
            for part in range(parts):

                @pl.when(me - step >= 0)
                def _():
                    place = spot(lax.rem(me - step + lines, lines), part)
                    hand(place, (step - 1) * parts + part).wait()

                @pl.when(me + step < lines)
                def _():
                    place = spot(lax.rem(me + step, lines), part)
                    hand(place, (lines + step - 2) * parts + part).wait()

    result = jax.ShapeDtypeStruct((1, lines * count, channels), rows.dtype)
    moves = pieces_per_chunk * (lines - 1)
    sems = dma_sems(2 * moves, 2 * moves, 1, *[moves] * 4)

    def peers():
        return line_peers() + twin_peers()

    if number is None:
        return kernel, peers, result, sems
    line, others_done = talk_with(kernel, peers, result, [source], sems, number, riders, [VMEM], VMEM)
    return line.reshape(lines * count, channels), others_done


def scatter_tokens(partial_sum, number, riders=()):
    all_rows, channels = partial_sum.shape
    lines, cores = lax.axis_size("space"), lax.axis_size("mp")
    count, width = all_rows // lines, channels // cores
    source = None
    if number is not None:
        source = partial_sum.astype(jnp.bfloat16).reshape(lines, count, channels)

    def kernel(
        hook, x_ref, out_ref, twin_ref, stage_ref, right_ref, left_ref, sum_ref,
        s_sem, r_sem, s3_sem, r3_sem, *sems,
    ):
        me, core = lax.axis_index("space"), lax.axis_index("mp")
        twin = {"mp": 1 - core}
        theirs = pl.ds(pl.multiple_of((1 - core) * width, width), width)
        mine = pl.ds(pl.multiple_of(core * width, width), width)
        order = [lines - 1, 0] + list(range(1, lines - 1))
        first = [
            send(x_ref.at[target, :, theirs], twin_ref.at[target], s_sem.at[target], r_sem.at[target], twin)
            for target in order
        ]

        def ready(step):
            turn = {0: zip(order[:2], first[:2]), 1: zip(order[2:], first[2:])}
            for target, copy in turn.get(step, ()):
                copy.wait_recv()
                total = x_ref[target, :, mine].astype(jnp.float32)
                total = total + twin_ref[target].astype(jnp.float32)
                total = total.astype(jnp.bfloat16)
                for part in range(pieces_per_chunk):
                    stage_ref[target, part] = total[part * some : (part + 1) * some]

        relay_sum(lines, stage_ref, right_ref, left_ref, sems, hook, ready)
        for part in range(pieces_per_chunk):
            sum_ref[part] = stage_ref[me, part].astype(jnp.float32)

            @pl.when(me > 0)
            def _():
                sum_ref[part] += right_ref[lines - 2, part].astype(jnp.float32)

            @pl.when(me < lines - 1)
            def _():
                sum_ref[part] += left_ref[lines - 2, part].astype(jnp.float32)

            out_ref[part * some : (part + 1) * some, mine] = sum_ref[part].astype(jnp.bfloat16)
        third = send(out_ref.at[:, mine], out_ref.at[:, mine], s3_sem.at[0], r3_sem.at[0], twin)
        for copy in first:
            copy.wait_send()
        third.wait()

    result = jax.ShapeDtypeStruct((count, channels), jnp.bfloat16)
    some = count // pieces_per_chunk
    chunk = (pieces_per_chunk, some, width)
    scratch = [
        pltpu.VMEM((lines, count, width), jnp.bfloat16),
        pltpu.VMEM((lines,) + chunk, jnp.bfloat16),
        pltpu.VMEM((lines - 1,) + chunk, jnp.bfloat16),
        pltpu.VMEM((lines - 1,) + chunk, jnp.bfloat16),
        pltpu.VMEM(chunk, jnp.float32),
    ]
    sems = dma_sems(lines, lines, 1, 1, *[pieces_per_chunk * (lines - 1)] * 4)

    def peers():
        return line_peers() + [{"mp": 1 - lax.axis_index("mp")}]

    return talk_with(
        kernel, peers, result, [source], scratch + sems, number, riders, [VMEM], VMEM
    )


def to_clips(source, number, riders=()):
    slots, frames, pixels, channels = source.shape
    count = lax.axis_size("tm")
    few = pixels // count
    if few % 16 != 0:
        if number is None:
            return None
        return lax.all_to_all(source, "tm", split_axis=2, concat_axis=1, tiled=True), plain_all(riders)

    def kernel(hook, x_ref, out_ref, send_sem, recv_sem, own_sem):
        me = lax.axis_index("tm")
        target = out_ref.at[:, pl.ds(me * frames, frames)]

        def part(index):
            return x_ref.at[:, :, pl.ds(pl.multiple_of(index * few, few), few)]

        copies = [
            send(part(peer), target, send_sem.at[i - 1], recv_sem.at[i - 1], {"tm": peer})
            for i, peer in others("tm")
        ]
        copies.append(keep(part(me), target, own_sem.at[0]))
        hook()
        for copy in copies:
            copy.wait()

    result = jax.ShapeDtypeStruct((slots, count * frames, few, channels), source.dtype)
    sems = dma_sems(count - 1, count - 1, 1)
    return talk_with(kernel, frame_peers, result, [source], sems, number, riders)


def from_clips(source, number, riders=()):
    slots, all_frames, few, channels = source.shape
    count = lax.axis_size("tm")
    frames = all_frames // count
    if few % 16 != 0:
        if number is None:
            return None
        return lax.all_to_all(source, "tm", split_axis=1, concat_axis=2, tiled=True), plain_all(riders)

    def kernel(hook, x_ref, out_ref, send_sem, recv_sem, own_sem):
        me = lax.axis_index("tm")
        target = out_ref.at[:, :, pl.ds(pl.multiple_of(me * few, few), few)]

        def part(index):
            return x_ref.at[:, pl.ds(index * frames, frames)]

        copies = [
            send(part(peer), target, send_sem.at[i - 1], recv_sem.at[i - 1], {"tm": peer})
            for i, peer in others("tm")
        ]
        copies.append(keep(part(me), target, own_sem.at[0]))
        hook()
        for copy in copies:
            copy.wait()

    result = jax.ShapeDtypeStruct((slots, frames, count * few, channels), source.dtype)
    sems = dma_sems(count - 1, count - 1, 1)
    return talk_with(kernel, frame_peers, result, [source], sems, number, riders)


def by_owner_line(source, owners, lines):
    parts = source.reshape(source.shape[:-1] + (owners // lines, lines, -1))
    return parts.swapaxes(-3, -2).reshape(source.shape)


def by_frames(weight_grad):
    return FrameSum(weight_grad.reshape(lax.axis_size("tm"), -1, weight_grad.shape[1]))


def padded_rims(source):
    return jnp.pad(source, ((0, 0), (0, 0), (1, 1), (1, 1), (0, 0)))


def conv_weight(weight):
    return weight.reshape(weight.shape[0], 3, 3, weight.shape[2])


def conv_frames(source, weight, spec, flipped):
    images = source.reshape((-1,) + source.shape[2:])
    kernel = conv_weight(weight)
    if flipped:
        kernel = kernel[:, ::-1, ::-1]
    result = lax.conv_general_dilated(
        images,
        kernel,
        (1, 1),
        "SAME",
        dimension_numbers=("NHWC", spec, "NHWC"),
        preferred_element_type=jnp.float32,
    )
    return result.reshape(source.shape[:4] + (result.shape[-1],))


def conv_weight_grad(source, upstream, form, taps=range(9)):
    padded = padded_rims(source)
    rows, cols = source.shape[2], source.shape[3]
    tap_list = []
    for tap in taps:
        i, j = tap // 3, tap % 3
        tap_list.append(
            jnp.einsum(
                "bfhwc,bfhwk->" + form,
                padded[:, :, i : i + rows, j : j + cols],
                upstream,
                preferred_element_type=jnp.float32,
            ).astype(jnp.bfloat16)
        )
    return jnp.stack(tap_list)


def sinusoid(steps_int):
    counted = D // 2
    freqs = jnp.exp(-math.log(10000.0) * jnp.arange(counted, dtype=jnp.float32) / counted)
    angles = steps_int.astype(jnp.float32)[..., None] * freqs
    return jnp.concatenate([jnp.sin(angles), jnp.cos(angles)], axis=-1)


def offset_onehot(query_start, query_count, key_count):
    distance = (
        query_start
        + jnp.arange(query_count, dtype=jnp.int32)[:, None]
        - jnp.arange(key_count, dtype=jnp.int32)[None, :]
    )
    position = jnp.clip(distance, -(R // 2), R // 2 - 1) + R // 2
    return (position[:, :, None] == jnp.arange(R, dtype=jnp.int32)[None, None, :]).astype(
        jnp.float32
    )


def local(kernel, results, operands, grid, in_specs, out_specs, scratch=()):
    return pl.pallas_call(
        kernel,
        out_shape=results,
        grid=grid,
        in_specs=in_specs,
        out_specs=out_specs,
        scratch_shapes=list(scratch),
        compiler_params=pltpu.CompilerParams(vmem_limit_bytes=32 * 1024 * 1024),
    )(*operands)


def dot(a, b):
    return jnp.dot(a, b, preferred_element_type=jnp.float32)


def dot_nt(a, b):
    return lax.dot_general(a, b, (((1,), (1,)), ((), ())), preferred_element_type=jnp.float32)


def dot_tn(a, b):
    return lax.dot_general(a, b, (((0,), (0,)), ((), ())), preferred_element_type=jnp.float32)


def low(value):
    return value.astype(jnp.bfloat16)


def head_probs(query, key, bias, valid):
    scores = dot_nt(query, key) * (1.0 / math.sqrt(HDIM))
    if bias is not None:
        scores = scores + bias
    if valid is not None:
        scores = jnp.where(valid, scores, masked)
    expos = jnp.exp(scores - jnp.max(scores, axis=-1, keepdims=True))
    return expos / jnp.sum(expos, axis=-1, keepdims=True)


def head_forward(query, key, value, bias, valid):
    return dot(low(head_probs(query, key, bias, valid)), value)


def head_backward(query, key, value, bias, valid, upstream):
    probs = head_probs(query, key, bias, valid)
    prob_grad = dot_nt(upstream, value)
    inner = jnp.sum(probs * prob_grad, axis=-1, keepdims=True)
    score_grad = low(probs * (prob_grad - inner))
    scale = 1.0 / math.sqrt(HDIM)
    return (
        dot(score_grad, key) * scale,
        dot_tn(score_grad, query) * scale,
        dot_tn(low(probs), upstream),
        score_grad,
    )


def norm_forward(source, gain):
    centered = source - jnp.mean(source, axis=-1, keepdims=True)
    variance = jnp.mean(centered * centered, axis=-1, keepdims=True)
    return centered * lax.rsqrt(variance + epsilon) * gain


def norm_backward(source, gain, upstream):
    centered = source - jnp.mean(source, axis=-1, keepdims=True)
    variance = jnp.mean(centered * centered, axis=-1, keepdims=True)
    inverse = lax.rsqrt(variance + epsilon)
    normal = centered * inverse
    gain_grad = jnp.sum(upstream * normal, axis=0, keepdims=True)
    scaled = upstream * gain
    first = jnp.mean(scaled, axis=-1, keepdims=True)
    second = jnp.mean(scaled * normal, axis=-1, keepdims=True)
    return inverse * (scaled - first - normal * second), gain_grad


def in_weight(packs, index, width):
    per = packs[0].shape[0] // 4
    cols = width // per
    return jnp.concatenate(
        [
            jnp.concatenate(
                [
                    pack[t, s, :, i * cols : (i + 1) * cols]
                    for pack in packs
                    for s in range(pack.shape[1])
                    for i in range(pack.shape[3] // cols)
                ],
                axis=0,
            )
            for t in range(index * per, (index + 1) * per)
        ],
        axis=1,
    )


def out_weight(pack, index, count):
    width = pack.shape[3] // count
    return jnp.concatenate(
        [
            jnp.concatenate(
                [pack[t, s, :, index * width : (index + 1) * width] for t in range(pack.shape[0])],
                axis=0,
            )
            for s in range(pack.shape[1])
        ],
        axis=1,
    )


class Fetch:
    def __init__(self, sources, targets, sem):
        self.copies = [keep(*pair, sem.at[i]) for i, pair in enumerate(zip(sources, targets))]
        self.targets, self.here = targets, set()

    def __call__(self, index):
        if index not in self.here:
            self.here.add(index)
            self.copies[index].wait()
        return self.targets[index]


def fetch_scratch(arrays):
    return [pltpu.VMEM(item.shape, item.dtype) for item in arrays] + dma_sems(len(arrays))


def spatial_forward(rows, weight):
    lines, images, pixels, channels = rows.shape
    width = weight.shape[1] // 3
    count = lines * pixels

    def kernel(x_ref, w_ref, triple_ref, mix_ref):
        x = x_ref[...].reshape(count, channels)
        triple_ref[0] = low(dot(x, w_ref[...]))
        for head in range(width // HDIM):
            at = head * HDIM
            query, key, value = (
                triple_ref[0, :, j * width + at : j * width + at + HDIM] for j in range(3)
            )
            mix_ref[0, :, at : at + HDIM] = low(head_forward(query, key, value, None, None))

    return local(
        kernel,
        (
            jax.ShapeDtypeStruct((images, count, 3 * width), jnp.bfloat16),
            jax.ShapeDtypeStruct((images, count, width), jnp.bfloat16),
        ),
        (rows, weight),
        (images,),
        [
            pl.BlockSpec((lines, 1, pixels, channels), lambda i: (0, i, 0, 0)),
            pl.BlockSpec(weight.shape, lambda i: (0, 0)),
        ],
        (
            pl.BlockSpec((1, count, 3 * width), lambda i: (i, 0, 0)),
            pl.BlockSpec((1, count, width), lambda i: (i, 0, 0)),
        ),
    )


def spatial_backward(rows, weight, triple, upstream):
    lines, images, pixels, channels = rows.shape
    width = weight.shape[1] // 3
    count = lines * pixels

    def kernel(x_ref, w_ref, triple_ref, up_ref, grad_ref, dw_ref, grads_ref, total_ref):
        step = pl.program_id(0)
        x = x_ref[...].reshape(count, channels)
        for head in range(width // HDIM):
            at = head * HDIM
            query, key, value = (
                triple_ref[0, :, j * width + at : j * width + at + HDIM] for j in range(3)
            )
            grads = head_backward(query, key, value, None, None, up_ref[0, :, at : at + HDIM])
            for j in range(3):
                grads_ref[:, j * width + at : j * width + at + HDIM] = low(grads[j])
        part = dot_nt(grads_ref[...], w_ref[...])
        grad_ref[...] = low(part).reshape(lines, 1, pixels, channels)

        @pl.when(step == 0)
        def _():
            total_ref[...] = jnp.zeros_like(total_ref)

        total_ref[...] += dot_tn(x, grads_ref[...])

        @pl.when(step == images - 1)
        def _():
            dw_ref[...] = low(total_ref[...])

    return local(
        kernel,
        (
            jax.ShapeDtypeStruct((lines, images, pixels, channels), jnp.bfloat16),
            jax.ShapeDtypeStruct((channels, 3 * width), jnp.bfloat16),
        ),
        (rows, weight, triple, upstream),
        (images,),
        [
            pl.BlockSpec((lines, 1, pixels, channels), lambda i: (0, i, 0, 0)),
            pl.BlockSpec(weight.shape, lambda i: (0, 0)),
            pl.BlockSpec((1, count, 3 * width), lambda i: (i, 0, 0)),
            pl.BlockSpec((1, count, width), lambda i: (i, 0, 0)),
        ],
        (
            pl.BlockSpec((lines, 1, pixels, channels), lambda i: (0, i, 0, 0)),
            pl.BlockSpec((channels, 3 * width), lambda i: (0, 0)),
        ),
        [
            pltpu.VMEM((count, 3 * width), jnp.bfloat16),
            pltpu.VMEM((channels, 3 * width), jnp.float32),
        ],
    )


def dot_exact(a, b):
    return jnp.dot(a, b, preferred_element_type=jnp.float32, precision=highest)


def clip_masks(rows, few, ids_ref, turned_ref):
    across = lax.broadcasted_iota(jnp.int32, (rows, rows), 1)
    down = lax.broadcasted_iota(jnp.int32, (rows, rows), 0)
    return (lax.rem(across, few) == lax.rem(down, few)) & (ids_ref[0] == turned_ref[0])


def temporal_forward(clip, bias, ids, few):
    slots, rows, triple = clip.shape
    width = triple // 3

    def kernel(x_ref, bias_ref, ids_ref, turned_ref, mix_ref):
        valid = clip_masks(rows, few, ids_ref, turned_ref)
        for head in range(width // HDIM):
            at = head * HDIM
            query, key, value = (
                x_ref[0, :, j * width + at : j * width + at + HDIM] for j in range(3)
            )
            mix = head_forward(query, key, value, bias_ref[head], valid)
            mix_ref[0, :, at : at + HDIM] = low(mix)

    return local(
        kernel,
        jax.ShapeDtypeStruct((slots, rows, width), jnp.bfloat16),
        (clip, bias, ids[:, :, None], ids[:, None, :]),
        (slots,),
        [
            pl.BlockSpec((1, rows, triple), lambda i: (i, 0, 0)),
            pl.BlockSpec(bias.shape, lambda i: (0, 0, 0)),
            pl.BlockSpec((1, rows, 1), lambda i: (i, 0, 0)),
            pl.BlockSpec((1, 1, rows), lambda i: (i, 0, 0)),
        ],
        pl.BlockSpec((1, rows, width), lambda i: (i, 0, 0)),
    )


def temporal_backward(clip, bias, ids, few, upstream):
    slots, rows, triple = clip.shape
    width = triple // 3
    frames = rows // few

    def kernel(x_ref, bias_ref, ids_ref, turned_ref, up_ref, grad_ref, score_ref):
        step = pl.program_id(0)
        valid = clip_masks(rows, few, ids_ref, turned_ref)
        frame = lax.broadcasted_iota(jnp.int32, (frames, rows), 0)
        row = lax.broadcasted_iota(jnp.int32, (frames, rows), 1)
        gather = low((row // few == frame).astype(jnp.float32))

        @pl.when(step == 0)
        def _():
            score_ref[...] = jnp.zeros_like(score_ref)

        for head in range(width // HDIM):
            at = head * HDIM
            query, key, value = (
                x_ref[0, :, j * width + at : j * width + at + HDIM] for j in range(3)
            )
            grads = head_backward(
                query, key, value, bias_ref[head], valid, up_ref[0, :, at : at + HDIM]
            )
            for j in range(3):
                grad_ref[0, :, j * width + at : j * width + at + HDIM] = low(grads[j])
            score_ref[head] += dot(gather, grads[3])

    return local(
        kernel,
        (
            jax.ShapeDtypeStruct((slots, rows, triple), jnp.bfloat16),
            jax.ShapeDtypeStruct((bias.shape[0], frames, rows), jnp.float32),
        ),
        (clip, bias, ids[:, :, None], ids[:, None, :], upstream),
        (slots,),
        [
            pl.BlockSpec((1, rows, triple), lambda i: (i, 0, 0)),
            pl.BlockSpec(bias.shape, lambda i: (0, 0, 0)),
            pl.BlockSpec((1, rows, 1), lambda i: (i, 0, 0)),
            pl.BlockSpec((1, 1, rows), lambda i: (i, 0, 0)),
            pl.BlockSpec((1, rows, width), lambda i: (i, 0, 0)),
        ],
        (
            pl.BlockSpec((1, rows, triple), lambda i: (i, 0, 0)),
            pl.BlockSpec((bias.shape[0], frames, rows), lambda i: (0, 0, 0)),
        ),
    )


def later():
    pass


def like(*shape):
    return jax.ShapeDtypeStruct(shape, jnp.bfloat16)


def temporal_chain(triple, bias, ids, numbers, riders):
    slots, frames, pixels, channels = triple.shape
    width, count = channels // 3, lax.axis_size("tm")
    few, all_frames = pixels // count, frames * count
    rows = all_frames * few
    first = to_clips(like(*triple.shape), None)
    second = from_clips(like(slots, all_frames, few, width), None)
    if first is None or second is None:
        clip, done = to_clips(triple, numbers[0], riders)
        mix = temporal_forward(clip.reshape(slots, rows, channels), bias, ids, few)
        mix, _ = from_clips(mix.reshape(slots, all_frames, few, width), numbers[1])
        return clip, mix, done

    def kernel(hook, x_ref, bias_ref, ids_ref, turned_ref, clip_ref, out_ref, mix_ref, *scratch):
        first[0](later, x_ref, clip_ref, *scratch[: len(first[3])])
        for slot in range(slots):
            valid = clip_masks(rows, few, ids_ref.at[pl.ds(slot, 1)], turned_ref.at[pl.ds(slot, 1)])
            for head in range(width // HDIM):
                at = head * HDIM
                query, key, value = (
                    clip_ref[slot, :, :, j * width + at : j * width + at + HDIM].reshape(rows, HDIM)
                    for j in range(3)
                )
                mix = low(head_forward(query, key, value, bias_ref[head], valid))
                mix_ref[slot, :, :, at : at + HDIM] = mix.reshape(all_frames, few, HDIM)
        second[0](hook, mix_ref, out_ref, *scratch[len(first[3]) :])

    (clip, mix), done = talk_many(
        kernel,
        frame_peers,
        [first[2], second[2]],
        [triple, bias, ids[:, :, None], ids[:, None, :]],
        [pltpu.VMEM((slots, all_frames, few, width), jnp.bfloat16)] + first[3] + second[3],
        numbers[0],
        riders,
        [VMEM] * 4,
        [VMEM, VMEM],
        58,
    )
    return clip, mix, done


def temporal_back_chain(clip, bias, ids, upstream, numbers, riders):
    slots, all_frames, few, channels = clip.shape
    width, rows = channels // 3, all_frames * few
    first = to_clips(like(*upstream.shape), None)
    second = from_clips(like(*clip.shape), None)
    if first is None or second is None:
        up, done = to_clips(upstream, numbers[0], riders)
        grads, score = temporal_backward(
            clip.reshape(slots, rows, channels), bias, ids, few, up.reshape(slots, rows, width)
        )
        grads, _ = from_clips(grads.reshape(clip.shape), numbers[1])
        return grads, score, done

    def kernel(
        hook, up_ref, clip_ref, bias_ref, ids_ref, turned_ref, out_ref, score_ref, line_ref, grad_ref, *scratch
    ):
        first[0](later, up_ref, line_ref, *scratch[: len(first[3])])
        hook()
        frame = lax.broadcasted_iota(jnp.int32, (all_frames, rows), 0)
        row = lax.broadcasted_iota(jnp.int32, (all_frames, rows), 1)
        gather = low((row // few == frame).astype(jnp.float32))
        score_ref[...] = jnp.zeros_like(score_ref)
        for slot in range(slots):
            valid = clip_masks(rows, few, ids_ref.at[pl.ds(slot, 1)], turned_ref.at[pl.ds(slot, 1)])
            for head in range(width // HDIM):
                at = head * HDIM
                query, key, value = (
                    clip_ref[slot, :, :, j * width + at : j * width + at + HDIM].reshape(rows, HDIM)
                    for j in range(3)
                )
                up = line_ref[slot, :, :, at : at + HDIM].reshape(rows, HDIM)
                grads = head_backward(query, key, value, bias_ref[head], valid, up)
                for j in range(3):
                    grad_ref[slot, :, :, j * width + at : j * width + at + HDIM] = low(
                        grads[j]
                    ).reshape(all_frames, few, HDIM)
                score_ref[head] += dot(gather, grads[3])
        second[0](hook, grad_ref, out_ref, *scratch[len(first[3]) :])

    (grads, score), done = talk_many(
        kernel,
        frame_peers,
        [second[2], jax.ShapeDtypeStruct((bias.shape[0], all_frames, rows), jnp.float32)],
        [upstream, clip, bias, ids[:, :, None], ids[:, None, :]],
        [pltpu.VMEM(first[2].shape, jnp.bfloat16), pltpu.VMEM(clip.shape, jnp.bfloat16)]
        + first[3]
        + second[3],
        numbers[0],
        riders,
        [VMEM] * 5,
        [VMEM, VMEM],
        58,
    )
    return grads, score, done


def line_rows(line_ref, image, lines, images, pixels):
    return jnp.concatenate(
        [
            line_ref[0, (s * images + image) * pixels : (s * images + image + 1) * pixels, :]
            for s in range(lines)
        ],
        axis=0,
    )


def spatial_chain(rows, branch, gain, weight, images, numbers, riders):
    count, channels = rows.shape
    lines, width = lax.axis_size("space"), weight.shape[1] // 3
    pixels = count // images
    first = gather_tokens(like(*rows.shape), None)
    second = from_lines(like(images, lines * pixels, width), False, None)
    if second is None:
        stream, normed = first_norm(rows, branch, gain)
        line, done = gather_tokens(normed, numbers[0], riders)
        line = line[None]
        triple, mix = spatial_forward(line.reshape(lines, images, pixels, channels), weight)
        mix, _ = from_lines(mix, False, numbers[1])
        return stream, line, triple, mix, done

    def kernel(
        hook, branch_ref, gain_ref, w_ref, rows_ref, stream_ref, line_ref, triple_ref, out_ref,
        mix_ref, normed_ref, one_ref, here_ref, sem, *scratch,
    ):
        fetch = Fetch([rows_ref], [here_ref], sem)
        one = fetch(0)[...].astype(jnp.float32) + branch_ref[...].astype(jnp.float32)
        one_ref[...] = one
        written = keep(one_ref, stream_ref, sem.at[1])
        normed_ref[0] = low(norm_forward(one, gain_ref[...]))
        first[0](later, normed_ref, line_ref, *scratch[: len(first[3])])
        hook()
        for image in range(images):
            x = line_rows(line_ref, image, lines, images, pixels)
            triple_ref[image] = low(dot(x, w_ref[...]))
            for head in range(width // HDIM):
                at = head * HDIM
                query, key, value = (
                    triple_ref[image, :, j * width + at : j * width + at + HDIM] for j in range(3)
                )
                mix = low(head_forward(query, key, value, None, None))
                mix_ref[image, :, at : at + HDIM] = mix
        second[0](hook, mix_ref, out_ref, *scratch[len(first[3]) :])
        written.wait()

    (stream, line, triple, mix), done = talk_many(
        kernel,
        lambda: line_peers() + twin_peers(),
        [
            jax.ShapeDtypeStruct(rows.shape, jnp.float32),
            first[2],
            like(images, lines * pixels, 3 * width),
            second[2],
        ],
        [branch, gain, weight, rows],
        [
            pltpu.VMEM((images, lines * pixels, width), jnp.bfloat16),
            pltpu.VMEM((1,) + rows.shape, jnp.bfloat16),
            pltpu.VMEM(rows.shape, jnp.float32),
            pltpu.VMEM(rows.shape, rows.dtype),
        ]
        + dma_sems(2)
        + first[3]
        + second[3],
        numbers[0],
        riders,
        [VMEM, VMEM, VMEM, ANY],
        [ANY, VMEM, VMEM, VMEM],
        58,
    )
    return stream, line, triple, mix, done


def late_chain(mix, stream, out, gain, number, riders):
    rows, channels = stream.shape
    first = gather_tokens(like(*stream.shape), None)

    def kernel(
        hook, mix_ref, gain_ref, out_any, stream_any, four_any, line_ref,
        normed_ref, four_ref, mine_ref, theirs_ref, out_ref, stream_ref, sem, end_sem, send_sem, recv_sem, *scratch,
    ):
        fetch = Fetch([out_any, stream_any], [out_ref, stream_ref], sem)
        part = dot(mix_ref[...], out_weight(fetch(0), 0, 1))
        part = twin_sum(part, mine_ref, theirs_ref, send_sem.at[0], recv_sem.at[0])
        four = fetch(1)[...] + part
        four_ref[...] = four
        written = keep(four_ref, four_any, end_sem.at[0])
        normed_ref[0] = low(norm_forward(four, gain_ref[...]))
        first[0](hook, normed_ref, line_ref, *scratch)
        written.wait()

    (four, line), done = talk_many(
        kernel,
        lambda: line_peers() + twin_peers(),
        [jax.ShapeDtypeStruct(stream.shape, jnp.float32), first[2]],
        [mix, gain, out, stream],
        [
            pltpu.VMEM((1,) + stream.shape, jnp.bfloat16),
            pltpu.VMEM(stream.shape, jnp.float32),
            pltpu.VMEM(stream.shape, jnp.bfloat16),
            pltpu.VMEM(stream.shape, jnp.bfloat16),
            pltpu.VMEM(out.shape, out.dtype),
            pltpu.VMEM(stream.shape, jnp.float32),
        ]
        + dma_sems(2, 1, 1, 1)
        + first[3],
        number,
        riders,
        [VMEM, VMEM, ANY, ANY],
        [ANY, VMEM],
    )
    return four, line, done


def first_back_chain(stream, gain, normed_grad, upstream, owners, images, numbers, riders):
    count, channels = stream.shape
    lines, pixels = lax.axis_size("space"), count // images
    first = to_lines(like(2 * images, pixels, channels), False, None, join=True)
    if first is None or (channels // owners) % HDIM != 0:
        grad, both, gain_grad = first_norm_backward(
            stream, gain, normed_grad, upstream, owners, lines
        )
        line, done = to_lines(
            both.reshape(2 * images, pixels, channels), False, numbers[0], riders, join=True
        )
        return grad, line, gain_grad, done

    def kernel(
        hook, gain_ref, normed_ref, stream_any, up_any, grad_any, line_ref, dg_ref,
        both_ref, rows_ref, grad_ref, stream_ref, up_ref, sem, *scratch,
    ):
        fetch = Fetch([stream_any, up_any], [stream_ref, up_ref], sem)
        step, gain_grad = norm_backward(
            fetch(0)[...], gain_ref[...], normed_ref[...].astype(jnp.float32)
        )
        grad = fetch(1)[...] + step
        grad_ref[...] = grad
        written = keep(grad_ref, grad_any, sem.at[2])
        dg_ref[...] = gain_grad
        store_both(rows_ref, low(grad), owners, lines)
        for half in range(2):
            for image in range(images):
                both_ref[half * images + image] = rows_ref[
                    half, image * pixels : (image + 1) * pixels, :
                ]
        first[0](hook, both_ref, line_ref, *scratch)
        written.wait()

    (grad, line, gain_grad), done = talk_many(
        kernel,
        first[1],
        [
            jax.ShapeDtypeStruct(stream.shape, jnp.float32),
            first[2],
            jax.ShapeDtypeStruct(gain.shape, jnp.float32),
        ],
        [gain, normed_grad, stream, upstream],
        [
            pltpu.VMEM((2 * images, pixels, channels), jnp.bfloat16),
            pltpu.VMEM((2, count, channels), jnp.bfloat16),
            pltpu.VMEM(stream.shape, jnp.float32),
            pltpu.VMEM(stream.shape, jnp.float32),
            pltpu.VMEM(stream.shape, jnp.float32),
        ]
        + dma_sems(3)
        + first[3],
        numbers[0],
        riders,
        [VMEM, VMEM, ANY, ANY],
        [ANY, ANY, VMEM],
        58,
    )
    return grad, line, gain_grad, done


def spatial_back_chain(upstream, line, weight, triple, numbers, riders):
    images, pixels, _ = upstream.shape
    lines, (channels, width) = lax.axis_size("space"), weight.shape
    width = width // 3
    count = images * pixels
    first = to_lines(like(*upstream.shape), False, None)
    second = scatter_tokens(like(lines * count, channels), None)
    if first is None:
        up, done = to_lines(upstream, False, numbers[0], riders)
        part, grads = spatial_backward(
            line.reshape(lines, images, pixels, channels), weight, triple, up
        )
        normed, _ = scatter_tokens(part.reshape(lines * count, channels), numbers[1])
        return normed, jnp.stack(jnp.split(grads, 3, axis=1)), done

    def kernel(
        hook, up_ref, line_ref, w_ref, triple_ref, out_ref, dw_ref, upline_ref, part_ref, grads_ref, *scratch
    ):
        first[0](later, up_ref, upline_ref, *scratch[: len(first[3])])
        for image in range(images):
            for head in range(width // HDIM):
                at = head * HDIM
                query, key, value = (
                    triple_ref[image, :, j * width + at : j * width + at + HDIM] for j in range(3)
                )
                up = upline_ref[image, :, at : at + HDIM]
                grads = head_backward(query, key, value, None, None, up)
                for j in range(3):
                    grads_ref[image, :, j * width + at : j * width + at + HDIM] = low(grads[j])
            part = low(dot_nt(grads_ref[image], w_ref[...]))
            for s in range(lines):
                here = slice(image * pixels, (image + 1) * pixels)
                part_ref[s, here, :] = part[s * pixels : (s + 1) * pixels]

        def weights():
            total = None
            for image in range(images):
                x = line_rows(line_ref, image, lines, images, pixels)
                one = dot_tn(x, grads_ref[image])
                total = one if total is None else total + one
            for j in range(3):
                dw_ref[j] = low(total[:, j * width : (j + 1) * width])

        hook()
        second[0](weights, part_ref, out_ref, *scratch[len(first[3]) :])

    (normed, grads), done = talk_many(
        kernel,
        lambda: line_peers() + twin_peers(),
        [second[2], like(3, channels, width)],
        [upstream, line, weight, triple],
        [
            pltpu.VMEM((images, lines * pixels, width), jnp.bfloat16),
            pltpu.VMEM((lines, count, channels), jnp.bfloat16),
            pltpu.VMEM((images, lines * pixels, 3 * width), jnp.bfloat16),
        ]
        + first[3]
        + second[3],
        numbers[0],
        riders,
        [VMEM] * 4,
        [VMEM, VMEM],
        58,
    )
    return normed, grads, done


def gelu_pair(upper):
    rate = math.sqrt(2.0 / math.pi)
    square = upper * upper
    bend = jnp.tanh(rate * (upper + 0.044715 * square * upper))
    half = 0.5 * (1.0 + bend)
    slope = half + 0.5 * upper * (1.0 - bend * bend) * rate * (1.0 + 3.0 * 0.044715 * square)
    return upper * half, slope


def feed_both(rows, cot, w_in, w_out):
    lines, count, channels = rows.shape
    hidden = w_in.shape[1]

    def kernel(x_ref, cot_ref, in_ref, out_ref, y_ref, grad_ref, dw_ref, first_ref, second_ref):
        step = pl.program_id(0)
        x, up = x_ref[0], cot_ref[0]
        active, slope = gelu_pair(dot(x, in_ref[...]))
        active = low(active)
        upper_grad = low(dot_nt(up, out_ref[...]) * slope)
        y_ref[0] = low(dot(active, out_ref[...]))
        grad_ref[0] = low(dot_nt(upper_grad, in_ref[...]))

        @pl.when(step == 0)
        def _():
            first_ref[...] = dot_tn(x, upper_grad)
            second_ref[...] = dot_tn(up, active)

        @pl.when(step > 0)
        def _():
            first_ref[...] += dot_tn(x, upper_grad)
            second_ref[...] += dot_tn(up, active)

        @pl.when(step == lines - 1)
        def _():
            dw_ref[:, :hidden] = low(first_ref[...])
            dw_ref[:, hidden:] = low(second_ref[...])

    block = pl.BlockSpec((1, count, channels), lambda i: (i, 0, 0))
    return local(
        kernel,
        (
            jax.ShapeDtypeStruct(rows.shape, jnp.bfloat16),
            jax.ShapeDtypeStruct(rows.shape, jnp.bfloat16),
            jax.ShapeDtypeStruct((channels, 2 * hidden), jnp.bfloat16),
        ),
        (rows, cot, w_in, w_out),
        (lines,),
        [
            block,
            block,
            pl.BlockSpec(w_in.shape, lambda i: (0, 0)),
            pl.BlockSpec(w_out.shape, lambda i: (0, 0)),
        ],
        (block, block, pl.BlockSpec((channels, 2 * hidden), lambda i: (0, 0))),
        [
            pltpu.VMEM((channels, hidden), jnp.float32),
            pltpu.VMEM((channels, hidden), jnp.float32),
        ],
    )


def twin_sum(partial_sum, mine_ref, theirs_ref, send_sem, recv_sem, work=None):
    mine_ref[...] = low(partial_sum)
    copy = send(mine_ref, theirs_ref, send_sem, recv_sem, {"mp": 1 - lax.axis_index("mp")})
    if work is not None:
        work()
    copy.wait()
    return mine_ref[...].astype(jnp.float32) + theirs_ref[...].astype(jnp.float32)


def chat(kernel, results, operands, rows, channels, swaps, number, scratch=(), far=(), late=()):
    own = []
    if swaps > 0:
        own = [
            pltpu.VMEM((swaps, rows, channels), jnp.bfloat16),
            pltpu.VMEM((swaps, rows, channels), jnp.bfloat16),
        ] + dma_sems(swaps, swaps)
    near, fetched = len(operands), len(far)
    count = near + fetched + len(results)
    late = list(late)
    late_scratch = [pltpu.VMEM(results[i].shape, results[i].dtype) for i in late] + dma_sems(
        len(late)
    )

    def whole(*refs):
        ins, sources = refs[:near], refs[near : near + fetched]
        outs = list(refs[near + fetched : count])
        rest = refs[count:]
        swapped, rest = rest[: len(own)], rest[len(own) :]
        targets, sem, rest = rest[:fetched], rest[fetched], rest[fetched + 1 :]
        held, late_sem, rest = rest[: len(late)], rest[len(late)], rest[len(late) + 1 :]
        fetch = Fetch(sources, targets, sem)
        ends = {place: outs[place] for place in late}
        for place, ref in zip(late, held):
            outs[place] = ref
        written = []

        def flush(*places):
            for place in places:
                index = late.index(place)
                written.append(keep(held[index], ends[place], late_sem.at[index]))

        def swap(index, partial_sum, work=None):
            mine_ref, theirs_ref, send_sem, recv_sem = swapped
            return twin_sum(
                partial_sum,
                mine_ref.at[index],
                theirs_ref.at[index],
                send_sem.at[index],
                recv_sem.at[index],
                work,
            )

        if swaps > 0:
            meet(twin_peers())
        kernel(swap, fetch, flush, *ins, *outs, *rest)
        for copy in written:
            copy.wait()

    specs = [VMEM] * near + [ANY] * fetched
    out_specs = tuple(ANY if i in late else VMEM for i in range(len(results)))
    scratch = own + fetch_scratch(far) + late_scratch + list(scratch)
    if swaps > 0:
        return talk(
            whole, tuple(results), list(operands) + list(far), scratch, number, specs, out_specs, 56
        )
    return pl.pallas_call(
        whole,
        out_shape=tuple(results),
        in_specs=specs,
        out_specs=out_specs,
        scratch_shapes=scratch,
        compiler_params=pltpu.CompilerParams(vmem_limit_bytes=56 * 1024 * 1024),
    )(*operands, *far)


def group_means(totals, count):
    channels = totals.shape[1]
    down = lax.broadcasted_iota(jnp.int32, (channels, channels), 0)
    across = lax.broadcasted_iota(jnp.int32, (channels, channels), 1)
    size = D // G
    same = (down // size == across // size).astype(jnp.float32)
    return dot_exact(totals, same) * (1.0 / (count * size))


def group_normal(source):
    count = source.shape[0]
    centered = source - group_means(jnp.sum(source, axis=0, keepdims=True), count)
    spread = group_means(jnp.sum(centered * centered, axis=0, keepdims=True), count)
    inverse = lax.rsqrt(spread + epsilon)
    return centered * inverse, inverse


def group_step(upstream, normal, inverse):
    count = upstream.shape[0]
    first = group_means(jnp.sum(upstream, axis=0, keepdims=True), count)
    second = group_means(jnp.sum(upstream * normal, axis=0, keepdims=True), count)
    return inverse * (upstream - first - normal * second)


def silu(value):
    return value * jax.nn.sigmoid(value)


def silu_slope(value):
    gate = jax.nn.sigmoid(value)
    return gate * (1.0 + value * (1.0 - gate))


def image_block(shape):
    return pl.BlockSpec((1,) + shape[1:], lambda i: (i, 0, 0))


def group_forward(source, scale, shift):
    def kernel(x_ref, scale_ref, shift_ref, out_ref):
        normal, _ = group_normal(x_ref[0].astype(jnp.float32))
        out_ref[0] = low(silu(normal * scale_ref[0] + shift_ref[0]))

    return local(
        kernel,
        jax.ShapeDtypeStruct(source.shape, jnp.bfloat16),
        (source, scale, shift),
        (source.shape[0],),
        [image_block(source.shape), image_block(scale.shape), image_block(shift.shape)],
        image_block(source.shape),
    )


def group_backward(source, scale, shift, upstream):
    def kernel(x_ref, scale_ref, shift_ref, up_ref, grad_ref, scale_grad_ref, shift_grad_ref):
        normal, inverse = group_normal(x_ref[0].astype(jnp.float32))
        grad = up_ref[0] * silu_slope(normal * scale_ref[0] + shift_ref[0])
        scale_grad_ref[0] = jnp.sum(grad * normal, axis=0, keepdims=True)
        shift_grad_ref[0] = jnp.sum(grad, axis=0, keepdims=True)
        grad_ref[0] = low(group_step(grad * scale_ref[0], normal, inverse))

    return local(
        kernel,
        (
            jax.ShapeDtypeStruct(source.shape, jnp.bfloat16),
            jax.ShapeDtypeStruct(scale.shape, jnp.float32),
            jax.ShapeDtypeStruct(shift.shape, jnp.float32),
        ),
        (source, scale, shift, upstream),
        (source.shape[0],),
        [
            image_block(source.shape),
            image_block(scale.shape),
            image_block(shift.shape),
            image_block(upstream.shape),
        ],
        (image_block(source.shape), image_block(scale.shape), image_block(shift.shape)),
    )


def flat_call(kernel, results, operands):
    return pl.pallas_call(
        kernel,
        out_shape=tuple(results),
        in_specs=[VMEM] * len(operands),
        out_specs=tuple([VMEM] * len(results)),
        compiler_params=pltpu.CompilerParams(vmem_limit_bytes=32 * 1024 * 1024),
    )(*operands)


def store_both(both_ref, value, owners, lines):
    both_ref[0] = value
    if (value.shape[1] // owners) % HDIM != 0:
        return
    size = value.shape[1] // owners
    frames = owners // lines
    both_ref[1] = jnp.concatenate(
        [
            value[:, (t * lines + s) * size : (t * lines + s + 1) * size]
            for s in range(lines)
            for t in range(frames)
        ],
        axis=1,
    )


def both_orders(rows, owners, lines):
    if (rows.shape[1] // owners) % HDIM != 0:
        return jnp.stack([rows, by_owner_line(rows, owners, lines)])

    def kernel(x_ref, both_ref):
        store_both(both_ref, x_ref[...], owners, lines)

    return flat_call(kernel, [jax.ShapeDtypeStruct((2,) + rows.shape, rows.dtype)], [rows])[0]


def first_norm(rows, branch, gain):
    def kernel(swap, fetch, flush, branch_ref, gain_ref, one_ref, normed_ref):
        one = fetch(0)[...].astype(jnp.float32) + branch_ref[...].astype(jnp.float32)
        one_ref[...] = one
        flush(0)
        normed_ref[...] = low(norm_forward(one, gain_ref[...]))

    return chat(
        kernel,
        [
            jax.ShapeDtypeStruct(rows.shape, jnp.float32),
            jax.ShapeDtypeStruct(rows.shape, jnp.bfloat16),
        ],
        [branch, gain],
        *rows.shape,
        0,
        0,
        far=[rows],
        late=[0],
    )


def first_norm_backward(stream, gain, normed_grad, upstream, owners, lines):
    def kernel(swap, fetch, flush, gain_ref, normed_ref, grad_ref, both_ref, dg_ref):
        step, gain_grad = norm_backward(
            fetch(0)[...], gain_ref[...], normed_ref[...].astype(jnp.float32)
        )
        grad = fetch(1)[...] + step
        grad_ref[...] = grad
        flush(0)
        dg_ref[...] = gain_grad
        store_both(both_ref, low(grad), owners, lines)

    grad, both, gain_grad = chat(
        kernel,
        [
            jax.ShapeDtypeStruct(stream.shape, jnp.float32),
            jax.ShapeDtypeStruct((2,) + stream.shape, jnp.bfloat16),
            jax.ShapeDtypeStruct(gain.shape, jnp.float32),
        ],
        [gain, normed_grad],
        *stream.shape,
        0,
        0,
        far=[stream, upstream],
        late=[0],
    )
    if (stream.shape[1] // owners) % HDIM != 0:
        both = jnp.stack([both[0], by_owner_line(both[0], owners, lines)])
    return grad, both, gain_grad


def text_mask(rows, valid_ref):
    slots, keys = valid_ref.shape
    slot = lax.broadcasted_iota(jnp.int32, (rows, keys), 0) // (rows // slots)
    good = None
    for index in range(slots):
        own = (slot == index) & (valid_ref[index : index + 1, :] > 0.5)
        good = own if good is None else good | own
    return good


def middle_forward(mix, stream, outs, ins, pairs, valid, gains, number):
    rows, channels = stream.shape
    width = mix.shape[1]

    def kernel(
        swap, fetch, flush, mix_ref, x_ref, pairs_ref, valid_ref, gain_ref,
        two_ref, normed_ref, query_ref, cross_ref, three_ref, last_ref, triple_ref,
    ):
        two = x_ref[...] + swap(0, dot(mix_ref[...], out_weight(fetch(0), 0, 2)))
        two_ref[...] = two
        normed_ref[...] = low(norm_forward(two, gain_ref[0:1, :]))
        flush(0, 1)
        query_ref[...] = low(dot(normed_ref[...], in_weight((fetch(1), fetch(2)), 0, width)))
        good = text_mask(rows, valid_ref)
        for head in range(width // HDIM):
            at = head * HDIM
            cross = head_forward(
                query_ref[:, at : at + HDIM],
                pairs_ref[:, at : at + HDIM],
                pairs_ref[:, width + at : width + at + HDIM],
                None,
                good,
            )
            cross_ref[:, at : at + HDIM] = low(cross)
        flush(2, 3)
        three = two_ref[...] + swap(1, dot(cross_ref[...], out_weight(fetch(0), 1, 2)))
        three_ref[...] = three
        last_ref[...] = low(norm_forward(three, gain_ref[1:2, :]))
        flush(4, 5)
        for j in range(3):
            weight = in_weight((fetch(1), fetch(2)), 1 + j, width)
            triple_ref[:, j * width : (j + 1) * width] = low(dot(last_ref[...], weight))

    wide = jax.ShapeDtypeStruct((rows, channels), jnp.float32)
    wide_low = jax.ShapeDtypeStruct((rows, channels), jnp.bfloat16)
    thin = jax.ShapeDtypeStruct((rows, width), jnp.bfloat16)
    return chat(
        kernel,
        [wide, wide_low, thin, thin, wide, wide_low, jax.ShapeDtypeStruct((rows, 3 * width), jnp.bfloat16)],
        [mix, stream, pairs, valid, gains],
        rows,
        channels,
        2,
        number,
        far=[outs, *ins],
        late=range(6),
    )


def late_forward(mix, stream, out, gain, number):
    rows, channels = stream.shape

    def kernel(swap, fetch, flush, mix_ref, gain_ref, four_ref, normed_ref):
        part = swap(0, dot(mix_ref[...], out_weight(fetch(0), 0, 1)))
        four = fetch(1)[...] + part
        four_ref[...] = four
        flush(0)
        normed_ref[...] = low(norm_forward(four, gain_ref[...]))

    return chat(
        kernel,
        [
            jax.ShapeDtypeStruct((rows, channels), jnp.float32),
            jax.ShapeDtypeStruct((rows, channels), jnp.bfloat16),
        ],
        [mix, gain],
        rows,
        channels,
        1,
        number,
        far=[out, stream],
        late=[0],
    )


def late_backward(cot, normed_grad, stream, gain, mix, out):
    rows, channels = stream.shape
    width = mix.shape[1]

    def kernel(swap, fetch, flush, up_ref, gain_ref, grad_ref, mix_grad_ref, dw_ref, dg_ref):
        step, gain_grad = norm_backward(
            fetch(0)[...], gain_ref[...], up_ref[...].astype(jnp.float32)
        )
        grad = fetch(1)[...].astype(jnp.float32) + step
        grad_ref[...] = grad
        flush(0)
        dg_ref[...] = gain_grad
        branch = low(grad)
        dw_ref[...] = low(dot_tn(branch, fetch(3)[...]))
        flush(2)
        mix_grad_ref[...] = low(dot_nt(branch, out_weight(fetch(2), 0, 1)))

    return chat(
        kernel,
        [
            jax.ShapeDtypeStruct((rows, channels), jnp.float32),
            jax.ShapeDtypeStruct((rows, width), jnp.bfloat16),
            jax.ShapeDtypeStruct((channels, width), jnp.bfloat16),
            jax.ShapeDtypeStruct((1, channels), jnp.float32),
        ],
        [normed_grad, gain],
        rows,
        channels,
        0,
        0,
        far=[stream, cot, out, mix],
        late=[0, 2],
    )


def middle_backward(
    triple, upstream, three, two, last, normed, query, cross, mix, outs, ins, pairs, valid, gains, number
):
    rows, channels = three.shape
    width = mix.shape[1]

    def kernel(
        swap, fetch, flush, pairs_ref, valid_ref, gain_ref,
        grad_ref, mix_grad_ref, pair_grad_ref, query_dw_ref, pair_dw_ref, cross_dw_ref, outs_dw_ref, dg_ref,
        cross_up_ref, dq_ref,
    ):
        def weight_in(index):
            return in_weight((fetch(1), fetch(2)), index, width)

        def temporal_weights():
            last_ref = fetch(3)
            query_dw_ref[...] = low(dot_tn(last_ref[...], triple_ref[:, :width]))
            pair_dw_ref[...] = low(dot_tn(last_ref[...], triple_ref[:, width:]))
            flush(3, 4)

        triple_ref = fetch(9)
        part_sum = dot_nt(triple_ref[:, :width], weight_in(1))
        part_sum = part_sum + dot_nt(triple_ref[:, width : 2 * width], weight_in(2))
        part_sum = part_sum + dot_nt(triple_ref[:, 2 * width :], weight_in(3))
        normed_grad = swap(0, part_sum, temporal_weights)
        step, gain_grad = norm_backward(fetch(10)[...], gain_ref[1:2, :], normed_grad)
        dg_ref[1:2, :] = gain_grad
        grad = fetch(11)[...] + step
        grad_ref[...] = grad
        branch = low(grad)
        cross_up_ref[...] = low(dot_nt(branch, out_weight(fetch(0), 1, 2)))
        query_ref, cross_ref, two_ref = fetch(4), fetch(5), fetch(6)
        normed_ref, mix_ref = fetch(7), fetch(8)
        good = text_mask(rows, valid_ref)
        for head in range(width // HDIM):
            at = head * HDIM
            grads = head_backward(
                query_ref[:, at : at + HDIM],
                pairs_ref[:, at : at + HDIM],
                pairs_ref[:, width + at : width + at + HDIM],
                None,
                good,
                cross_up_ref[:, at : at + HDIM],
            )
            dq_ref[:, at : at + HDIM] = low(grads[0])
            pair_grad_ref[:, at : at + HDIM] = low(grads[1])
            pair_grad_ref[:, width + at : width + at + HDIM] = low(grads[2])
        flush(2)

        def cross_weights():
            cross_dw_ref[...] = low(dot_tn(normed_ref[...], dq_ref[...]))
            flush(5)
            outs_dw_ref[:, :width] = low(dot_tn(low(grad_ref[...]), cross_ref[...]))

        normed_grad = swap(1, dot_nt(dq_ref[...], weight_in(0)), cross_weights)
        step, gain_grad = norm_backward(two_ref[...], gain_ref[0:1, :], normed_grad)
        dg_ref[0:1, :] = gain_grad
        grad = grad_ref[...] + step
        grad_ref[...] = grad
        flush(0)
        branch = low(grad)
        outs_dw_ref[:, width:] = low(dot_tn(branch, mix_ref[...]))
        flush(6)
        mix_grad_ref[...] = low(dot_nt(branch, out_weight(fetch(0), 0, 2)))

    return chat(
        kernel,
        [
            jax.ShapeDtypeStruct((rows, channels), jnp.float32),
            jax.ShapeDtypeStruct((rows, width), jnp.bfloat16),
            jax.ShapeDtypeStruct(pairs.shape, jnp.bfloat16),
            jax.ShapeDtypeStruct((channels, width), jnp.bfloat16),
            jax.ShapeDtypeStruct((channels, 2 * width), jnp.bfloat16),
            jax.ShapeDtypeStruct((channels, width), jnp.bfloat16),
            jax.ShapeDtypeStruct((channels, 2 * width), jnp.bfloat16),
            jax.ShapeDtypeStruct((2, channels), jnp.float32),
        ],
        [pairs, valid, gains],
        rows,
        channels,
        2,
        number,
        [pltpu.VMEM((rows, width), jnp.bfloat16), pltpu.VMEM((rows, width), jnp.bfloat16)],
        [outs, *ins, last, query, cross, two, normed, mix, triple, three, upstream],
        [0, 2, 3, 4, 5, 6],
    )


def on_device(
    video,
    cotangent,
    text,
    video_ids,
    timesteps,
    text_lengths,
    group_gain,
    group_bias,
    first_conv,
    film_weight,
    second_conv,
    spatial_norm,
    spatial_qkv,
    spatial_out,
    cross_norm,
    cross_query,
    cross_kv,
    cross_out,
    temporal_norm,
    temporal_qkv,
    temporal_out,
    offset_bias,
    feed_norm,
    feed_in,
    feed_out,
):
    frames_axis, lines, cores = (lax.axis_size(name) for name in ("tm", "space", "mp"))
    slots, frame_dev, row_dev, columns, channels = video.shape
    half_width = first_conv.shape[2]
    head_local = half_width // HDIM
    pixels_dev = row_dev * columns
    frames_all = frame_dev * frames_axis
    token_rows = slots * frame_dev * pixels_dev
    text_local = text.shape[1]
    images = slots * frame_dev
    frame_shape = (-1, frame_dev, H, W)
    everyone = ("tm", "space")
    owners = frames_axis * lines
    line_half = lines // 2
    feed_width = feed_in.shape[1] // lines
    text_rows = slots * text_local

    def wide(source):
        return source.reshape(frame_shape + source.shape[2:])

    out_piece = part_of(jnp.concatenate([spatial_out, cross_out, temporal_out], axis=1), "tm", 0)
    if frames_axis == 4:
        in_piece = jnp.concatenate([cross_query[None], temporal_qkv.transpose(1, 0, 2)], axis=0)
        in_piece = lax.dynamic_index_in_dim(in_piece, lax.axis_index("tm"), 0, keepdims=False)
    else:
        in_piece = jnp.concatenate([cross_query, temporal_qkv.reshape(-1, 3 * half_width)], axis=1)
        in_piece = part_of(in_piece, "tm", 1)
    picks = channels % (16 * owners) == 0 and (half_width // lines) % lane == 0
    turned_qkv = spatial_qkv.transpose(1, 0, 2)

    def cut_qkv(whole):
        piece = part_of(whole, "tm", 1)
        return piece.reshape(3, -1, lines, half_width // lines).transpose(2, 0, 1, 3)

    def pick_qkv(ref, place):
        rows = span(lax.axis_index("tm"), channels // owners)
        return ref.at[:, rows, span(place, half_width // lines)]

    def cut_in(whole):
        return part_of(whole, "tm", 0).reshape(-1, lines, feed_width).transpose(1, 0, 2)

    def pick_in(ref, place):
        return ref.at[span(lax.axis_index("tm"), channels // owners), span(place, feed_width)]

    def cut_out(whole):
        return part_of(whole.reshape(lines, feed_width, -1), "tm", 1)

    def pick_out(ref, place):
        return ref.at[span(place * frames_axis + lax.axis_index("tm"), feed_width // frames_axis)]

    def cut_text(whole):
        return whole.reshape(text_rows, frames_axis, -1).transpose(1, 0, 2)

    def pick_text(ref, place):
        return ref.at[:, span(place, ref.shape[1] // frames_axis)]

    def cut_cols(whole):
        return whole.reshape(frames_axis, text_rows, lines, -1).transpose(2, 0, 1, 3)

    def pick_cols(ref, place):
        return ref.at[:, :, span(place, ref.shape[2] // lines)]

    def cut_and_send(source, axes, pick, cut):
        return Exchange(source, axes, pick, cut) if picks else Exchange(cut(source), axes)

    cot_rows = cotangent.reshape(token_rows, channels)
    text_flat = text.reshape(text_rows, -1)
    cross_kv = cross_kv.reshape(cross_kv.shape[0], -1)

    folds = in_piece.shape[0] // out_piece.shape[0]
    in_piece = jnp.concatenate(jnp.split(in_piece, folds, axis=0), axis=1)
    out_cols = out_piece.shape[1]
    pack = jnp.concatenate([out_piece, in_piece], axis=1)
    in_cols = (out_cols, pack.shape[1])
    embed = sinusoid(timesteps).astype(jnp.bfloat16)
    film_part = jnp.einsum(
        "bvc,cjk->bvjk", part_of(embed, "space", 2), film_weight, preferred_element_type=jnp.float32
    )
    film_part = film_part.reshape(slots * VIDS * 2, lines, -1).transpose(1, 0, 2)

    video_rows = video.reshape(token_rows, channels)
    in_groups = (channels // owners) % (D // G) == 0
    video_both = both_orders(video_rows, owners, lines) if in_groups else video_rows
    video_lines, (text_line, qkv_piece, film, pack) = to_lines(
        video_both.reshape(-1, pixels_dev, channels),
        True,
        1,
        [
            LineColumns(text_flat),
            cut_and_send(turned_qkv, ("space",), pick_qkv, cut_qkv),
            Exchange(film_part, ("space",)),
            Keep(pack),
        ],
    )
    pack = lax.all_gather(pack, "space", axis=0, tiled=False)

    def line_gains(whole):
        own = part_of(part_of(whole, "space", 0), "mp", 0)
        if not in_groups:
            return jnp.broadcast_to(own, (images, 1, own.shape[0]))
        owned = part_of(part_of(by_owner_line(whole, owners, lines), "space", 0), "mp", 0)
        return jnp.repeat(jnp.stack([own, owned]), images, axis=0)[:, None]

    gain_line, bias_line = line_gains(group_gain), line_gains(group_bias)
    first_in = group_forward(video_lines, gain_line, bias_line)
    text_part = jnp.dot(
        text_line.reshape(lines * text_rows, -1), cross_kv, preferred_element_type=jnp.float32
    )
    text_part = text_part.astype(jnp.bfloat16).reshape(lines, text_rows, -1)
    first_in, (text_part,) = gather_cores(first_in, 3, [Exchange(text_part, ("space",))])
    if in_groups:
        first_in, first_owned = first_in[:images], first_in[images:]
    else:
        blocks = first_in.reshape(first_in.shape[:2] + (-1, lines, channels // owners))
        blocks = blocks.swapaxes(2, 3).reshape(first_in.shape)
        first_owned = lax.all_to_all(blocks, "space", split_axis=2, concat_axis=2, tiled=True)
    text_part = jnp.sum(text_part.astype(jnp.float32), axis=0).astype(jnp.bfloat16)
    hidden_part = conv_frames(wide(first_in), first_conv, "IHWO", False).astype(jnp.bfloat16)
    hidden, (text_part, qkv_piece) = sum_lines(
        hidden_part.reshape(images, H * W, half_width),
        4,
        [Share(text_part, ("space",)), Share(qkv_piece, ("tm",))],
    )

    film = jnp.sum(film, axis=0).reshape(slots, VIDS, 2, -1)
    frame_ids = part_of(video_ids, "tm", 1)
    choose = (frame_ids[:, :, None] == jnp.arange(VIDS, dtype=jnp.int32)[None, None, :]).astype(
        jnp.float32
    )
    frame_film = jnp.einsum("bfv,bvjk->jbfk", choose, film, precision=highest)
    frame_film = frame_film.reshape(2, images, 1, -1)
    film_scale, film_shift = 1.0 + frame_film[0], frame_film[1]
    second_in = group_forward(hidden, film_scale, film_shift)
    second_wide, (text_pairs, in_first, cot_late) = gather_lines(
        second_in,
        5,
        [Share(text_part, ("tm",)), Share(pack, ("tm",), 0, line_half, in_cols), Keep(cot_rows)],
    )
    cot_half = lax.all_gather(part_of(cot_late, "mp", 1), "space", axis=0, tiled=True)
    text_pairs = text_pairs.reshape(owners * text_rows, 2 * half_width)
    conv_part = conv_frames(wide(second_wide), second_conv, "IHWO", False).astype(jnp.bfloat16)
    conv_half, _ = sum_cores(conv_part.reshape(images, H * W, -1), 6)
    conv_rows, (outs_all,) = from_lines(
        conv_half.astype(jnp.bfloat16),
        True,
        7,
        [Share(pack, ("tm",), cols=(0, out_cols // 3 * 2))],
    )
    spatial_qkv = qkv_piece.transpose(1, 0, 3, 2, 4).reshape(channels, -1)

    spatial_gain = spatial_norm[None]
    stream_one, spatial_line, spatial_triple, spatial_mix, (in_rest, out_last, text_cols) = (
        spatial_chain(
            video_rows,
            conv_rows.reshape(token_rows, channels),
            spatial_gain,
            spatial_qkv,
            images,
            (8, 9),
            [
                Share(pack, ("tm",), line_half, lines - line_half, in_cols),
                Share(pack, ("tm",), cols=(out_cols // 3 * 2, out_cols)),
                cut_and_send(text_flat, ("tm",), pick_text, cut_text),
            ],
        )
    )

    spatial_mix = spatial_mix.reshape(token_rows, half_width)
    in_all = (in_first, in_rest)
    key = jnp.arange(owners * text_rows, dtype=jnp.int32)[None, :]
    key_slot = key % text_rows // text_local
    key_place = key // text_rows * text_local + key % text_local
    own_slot = key_slot == jnp.arange(slots, dtype=jnp.int32)[:, None]
    text_valid = (own_slot & (key_place < text_lengths[:, None])).astype(jnp.float32)
    two_gains = jnp.stack([cross_norm, temporal_norm])
    stream_two, cross_in, cross_queries, cross_mix, stream_three, temporal_in, temporal_triple = (
        middle_forward(
            spatial_mix, stream_one, outs_all, in_all, text_pairs, text_valid, two_gains, 34
        )
    )

    clip_pixels = pixels_dev // frames_axis
    clip_rows = frames_all * clip_pixels
    offset_table = offset_onehot(0, frames_all, frames_all)
    clip_frames = jnp.arange(clip_rows, dtype=jnp.int32)[:, None] // clip_pixels
    clip_frames = (clip_frames == jnp.arange(frames_all, dtype=jnp.int32)[None, :]).astype(
        jnp.float32
    )
    clip_bias = jnp.einsum("qkr,rh->hqk", offset_table, offset_bias, precision=highest)
    clip_bias = jnp.einsum("hqk,ck->hqc", clip_bias, clip_frames, precision=highest)
    clip_bias = jnp.einsum("rq,hqc->hrc", clip_frames, clip_bias, precision=highest)
    clip_ids = jnp.repeat(video_ids, clip_pixels, axis=1)
    clip_triple, temporal_mix, (in_quarter, out_quarter, text_cols) = temporal_chain(
        temporal_triple.reshape(slots, frame_dev, pixels_dev, 3 * half_width),
        clip_bias,
        clip_ids,
        (10, 11),
        [
            cut_and_send(feed_in, ("space",), pick_in, cut_in),
            cut_and_send(feed_out, ("space",), pick_out, cut_out),
            cut_and_send(text_cols, ("space",), pick_cols, cut_cols),
        ],
    )
    temporal_mix = temporal_mix.reshape(token_rows, half_width)

    feed_gain = feed_norm[None]
    stream_four, feed_line, (feed_in, feed_out, cot_line) = late_chain(
        temporal_mix,
        stream_three,
        out_last,
        feed_gain,
        12,
        [Share(in_quarter, ("tm",)), Share(out_quarter, ("tm",)), JoinCores(cot_half)],
    )
    feed_in = feed_in.transpose(1, 0, 2, 3).reshape(channels, feed_width)
    feed_out = feed_out.transpose(0, 2, 1, 3).reshape(feed_width, channels)
    line_shape = (lines, token_rows, channels)
    final_part, feed_part, feed_grads = feed_both(
        feed_line.reshape(line_shape), cot_line.reshape(line_shape), feed_in, feed_out
    )
    normed_grad, (feed_grads, final_half) = scatter_tokens(
        feed_part.reshape(lines * token_rows, channels),
        14,
        [by_frames(feed_grads), CoreSum(final_part.reshape(lines * token_rows, channels))],
    )

    upstream, mix_grad, temporal_out_grad, feed_norm_grad = late_backward(
        cot_rows, normed_grad, stream_four, feed_gain, temporal_mix, out_last
    )

    def cut_feed(half):
        cols = slice(half * feed_width, (half + 1) * feed_width)
        return lambda whole: whole[:, cols].reshape(lines, -1, feed_width)

    def pick_feed(half):
        cols = pl.ds(half * feed_width, feed_width)
        return lambda ref, place: ref.at[span(place, channels // owners), cols]

    (
        triple_grad,
        score_total,
        (feed_in_grad, feed_out_grad, first_grads, final_half),
    ) = temporal_back_chain(
        clip_triple,
        clip_bias,
        clip_ids,
        mix_grad.reshape(slots, frame_dev, pixels_dev, half_width),
        (15, 16),
        [
            ColumnJoin(feed_grads, pick_feed(0), cut_feed(0)),
            ColumnJoin(feed_grads, pick_feed(1), cut_feed(1)),
            by_frames(temporal_out_grad),
            LineSum(final_half),
        ],
    )
    score_total = jnp.einsum("hqc,ck->hqk", score_total, clip_frames, precision=highest)
    offset_bias_grad = jnp.einsum("hqk,qkr->rh", score_total, offset_table, precision=highest)

    (
        upstream,
        mix_grad,
        pair_grad,
        temporal_query_grad,
        temporal_pair_grad,
        cross_query_grad,
        outs_grad,
        two_grads,
    ) = middle_backward(
        triple_grad.reshape(token_rows, 3 * half_width),
        upstream,
        stream_three,
        stream_two,
        temporal_in,
        cross_in,
        cross_queries,
        cross_mix,
        spatial_mix,
        outs_all,
        in_all,
        text_pairs,
        text_valid,
        two_gains,
        36,
    )
    pair_grad = pair_grad.reshape(frames_axis, lines * text_rows, 2 * half_width)

    (
        normed_grad,
        spatial_qkv_grad,
        (pair_grad, second_grads, final_rows, temporal_out_grad, third_grads),
    ) = spatial_back_chain(
        mix_grad.reshape(images, pixels_dev, half_width),
        spatial_line,
        spatial_qkv,
        spatial_triple,
        (17, 18),
        [
            FrameSum(pair_grad),
            by_frames(temporal_query_grad),
            JoinCores(final_half),
            LineSum(first_grads, jnp.float32),
            by_frames(temporal_pair_grad),
        ],
    )
    mixed = (stream_four + final_rows.astype(jnp.float32)).astype(jnp.bfloat16)
    (
        upstream,
        branch_line,
        spatial_norm_grad,
        (fourth_grads, pair_grad, temporal_query_grad),
    ) = first_back_chain(
        stream_one,
        spatial_gain,
        normed_grad,
        upstream,
        owners,
        images,
        (19,),
        [
            by_frames(cross_query_grad),
            Exchange(pair_grad.reshape(lines, text_rows, 2 * half_width), ("space",)),
            LineSum(second_grads, jnp.float32),
        ],
    )
    branch_line, branch_owned = branch_line[:images], branch_line[images:]
    pair_grad = jnp.sum(pair_grad.astype(jnp.float32), axis=0).astype(jnp.bfloat16)
    second_conv_grad = conv_weight_grad(wide(second_wide), wide(branch_owned), "kc")
    second_part = conv_frames(wide(branch_line), second_conv, "OHWI", True).astype(jnp.bfloat16)
    second_in_grad, (fifth_grads, pair_line) = sum_lines(
        second_part.reshape(images, H * W, half_width),
        20,
        [by_frames(outs_grad), Share(pair_grad, ("space",))],
    )
    hidden_grad, scale_grad, shift_grad = group_backward(
        hidden, film_scale, film_shift, second_in_grad
    )
    frame_grads = jnp.stack([scale_grad, shift_grad], axis=1).reshape(slots, frame_dev, 2, -1)
    film_rows = jnp.einsum("bfv,bfjk->bvjk", choose, frame_grads, precision=highest)
    film_rows = film_rows.reshape(slots * VIDS * 2, -1)
    text_part = jnp.dot(
        pair_line.reshape(lines * text_rows, -1), cross_kv.T, preferred_element_type=jnp.float32
    )
    text_part = text_part.astype(jnp.bfloat16).reshape(lines, text_rows, -1)

    hidden_wide, (second_conv_grad, film_shares, text_part, pair_all) = gather_lines(
        hidden_grad,
        21,
        [FrameSum(second_conv_grad, True, kind=jnp.float32), Share(film_rows, ("tm",)), Exchange(text_part, ("space",)), Share(pair_line, ("tm",))],
    )
    film_rows = jnp.sum(film_shares, axis=0)
    first_conv_grad = conv_weight_grad(wide(first_owned), wide(hidden_wide), "ck")
    first_part = conv_frames(wide(hidden_wide), first_conv, "OHWI", True).astype(jnp.bfloat16)
    (
        first_in_grad,
        (first_conv_some, spatial_qkv_grad, cross_query_grad, outs_grad, film_shares),
    ) = sum_cores(
        first_part.reshape(images, H * W, -1),
        22,
        [
            FrameSum(first_conv_grad, True, 0, 5),
            FrameSum(spatial_qkv_grad, True),
            LineSum(fourth_grads, jnp.float32),
            LineSum(fifth_grads, jnp.float32),
            Share(film_rows, ("space",)),
        ],
    )
    video_line_grad, gain_grad, bias_grad = group_backward(
        video_lines[:images], gain_line[:images], bias_line[:images], first_in_grad
    )

    def placed(line_grad):
        whole = jnp.zeros((channels,), jnp.float32)
        size = line_grad.shape[2]
        place = (lax.axis_index("space") * cores + lax.axis_index("mp")) * size
        return lax.dynamic_update_slice_in_dim(whole, jnp.sum(line_grad, axis=(0, 1)), place, 0)

    small = jnp.concatenate(
        [
            item.reshape(owners, -1)
            for item in (
                placed(gain_grad),
                placed(bias_grad),
                spatial_norm_grad,
                two_grads[0],
                two_grads[1],
                feed_norm_grad,
                offset_bias_grad,
            )
        ],
        axis=1,
    )
    owner_rows = channels // owners

    def cut_qkv_rows(whole):
        return whole.reshape(3, lines, owner_rows, -1).transpose(1, 0, 2, 3)

    video_rows_grad, (small, qkv_part, first_conv_rest, temporal_pair_grad) = from_lines(
        video_line_grad,
        True,
        23,
        [
            SmallSum(small.reshape(frames_axis, lines, 1, -1)),
            ColumnJoin(
                spatial_qkv_grad,
                lambda ref, place: ref.at[:, span(place, owner_rows)],
                cut_qkv_rows,
            ),
            FrameSum(first_conv_grad, True, 5, 4),
            LineSum(third_grads, jnp.float32),
        ],
    )
    video_grad = upstream + video_rows_grad.reshape(token_rows, channels).astype(jnp.float32)

    video_film_grad = (
        film_shares.reshape(lines, slots, VIDS, 2, -1)
        .transpose(1, 2, 3, 0, 4)
        .reshape(slots, VIDS, 2, half_width)
    )
    film_weight_grad = jnp.einsum(
        "bvc,bvjk->cjk",
        part_of(part_of(embed, "tm", 2), "space", 2).astype(jnp.float32),
        video_film_grad,
        precision=highest,
    )
    cross_kv_grad = jnp.einsum(
        "prc,prk->ck",
        text_cols.transpose(1, 0, 2, 3).reshape(owners, text_rows, -1),
        pair_all.reshape(owners, text_rows, 2 * half_width),
        preferred_element_type=jnp.float32,
    )
    text_half = part_of(
        twin_add(text_part.transpose(1, 0, 2).reshape(text_rows, -1)), "mp", 1
    )
    small = small[0]
    small_twin = lax.ppermute(small, "mp", [(0, 1), (1, 0)])
    gain_size = channels // owners
    gains = [small[i * gain_size : (i + 1) * gain_size] for i in range(6)]
    for i in range(2):
        gains[i] = gains[i] + small_twin[i * gain_size : (i + 1) * gain_size]
    first_conv_grad = jnp.concatenate([first_conv_some, first_conv_rest])
    temporal_triple_grad = jnp.stack(
        [temporal_query_grad, *jnp.split(temporal_pair_grad, 2, axis=1)], axis=1
    )
    return (
        mixed.reshape(video.shape),
        video_grad.reshape(video.shape),
        text_half.reshape(slots, text_local, -1),
        gains[0],
        gains[1],
        first_conv_grad.astype(jnp.float32).transpose(1, 0, 2),
        film_weight_grad,
        second_conv_grad.transpose(2, 0, 1),
        gains[2],
        qkv_part.astype(jnp.float32).transpose(1, 0, 2),
        outs_grad[:, half_width:].T,
        gains[3],
        cross_query_grad,
        cross_kv_grad.reshape(-1, 2, half_width),
        outs_grad[:, :half_width].T,
        gains[4],
        temporal_triple_grad,
        temporal_out_grad.T,
        small[6 * gain_size :].reshape(R // owners, head_local),
        gains[5],
        feed_in_grad.astype(jnp.float32),
        feed_out_grad.astype(jnp.float32).T,
    )


def solution(mesh):
    return jax.shard_map(
        on_device,
        mesh=mesh,
        in_specs=(
            P(None, "tm", "space", None, None),
            P(None, "tm", "space", None, None),
            P(None, ("tm", "space"), None),
            P(),
            P(),
            P(),
            P(),
            P(),
            P("space", None, "mp"),
            P("space", None, "mp"),
            P("mp", None, "space"),
            P(),
            P("space", None, "mp"),
            P("mp", "space"),
            P(),
            P("space", "mp"),
            P("space", None, "mp"),
            P("mp", "space"),
            P(),
            P("space", None, "mp"),
            P("mp", "space"),
            P(None, "mp"),
            P(),
            P("space", "mp"),
            P("mp", "space"),
        ),
        out_specs=(
            P(None, "tm", "space", None, None),
            P(None, "tm", "space", None, None),
            P(None, ("tm", "space"), "mp"),
            P(("tm", "space")),
            P(("tm", "space")),
            P(("tm", "space"), None, "mp"),
            P(("tm", "space"), None, "mp"),
            P("mp", None, ("tm", "space")),
            P(("tm", "space")),
            P(("tm", "space"), None, "mp"),
            P("mp", ("tm", "space")),
            P(("tm", "space")),
            P(("tm", "space"), "mp"),
            P(("tm", "space"), None, "mp"),
            P("mp", ("tm", "space")),
            P(("tm", "space")),
            P(("tm", "space"), None, "mp"),
            P("mp", ("tm", "space")),
            P(("tm", "space"), "mp"),
            P(("tm", "space")),
            P(("tm", "space"), "mp"),
            P("mp", ("tm", "space")),
        ),
        check_vma=False,
    )
```
